32 devices in a mesh: groups: 2 (over y), ep: 4 (over z), sub: 4 (over x, core).
Axes of the slice: x: 2, y: 2, z: 4, core: 2. Of those that a mesh axis runs over, the one named last changes fastest.
Arguments:
- grad_out: bfloat16 [1024, 2048], P(('groups', 'ep'), 'sub'), parts along dimension 0, may hold values from -6 to 6
- route_weight: bfloat16 [1024, 8], P(('groups', 'ep')), parts along dimension 0, may hold values from 0.049804688 to 0.59765625
- routes: int32 [1024, 8], P(('groups', 'ep')), parts along dimension 0, may hold values from 0 to 15, as said below
- replica: int32 [1024, 8], P(('groups', 'ep')), parts along dimension 0, may hold values from 0 to 3, as said below
- replica_slot: int32 [32, 4], P('groups'), parts along dimension 0, may hold values from 0 to 31, as said below
- token_count: int32 [8], P(('groups', 'ep')), parts along dimension 0, may hold values from 64 to 128, as said below
- saved_input: bfloat16 [64, 4, 32, 2048], P(('groups', 'ep'), None, None, 'sub'), parts along dimension 0, may hold values from -6 to 6
- saved_gate_up: bfloat16 [64, 128, 1536], P(('groups', 'ep')), parts along dimension 0, may hold values from -6 to 6
- weight_in: bfloat16 [64, 1536, 2048], P(('groups', 'ep'), None, 'sub'), parts along dimension 0
- weight_down: bfloat16 [64, 768, 2048], P(('groups', 'ep'), None, 'sub'), parts along dimension 0
Outputs:
- grad_tokens: bfloat16 [1024, 2048], P(('groups', 'ep'), 'sub'), parts along dimension 0
- grad_route_weight: bfloat16 [1024, 8], P(('groups', 'ep')), parts along dimension 0
- grad_weight_in: bfloat16 [32, 1536, 2048], P('groups', 'ep', 'sub'), parts along dimension 0
- grad_weight_down: bfloat16 [32, 768, 2048], P('groups', 'ep', 'sub'), parts along dimension 0
The draws below stay inside these ranges and needn't reach their ends.
There are 2 independent parts, one for each index of `groups`. The reference program is written for one: setup_inputs(seed, part) draws one part's arguments, and reference() takes and returns one part's arrays. A program takes and returns all parts, laid end to end along the dimension named above; each array names one. Nothing has to cross between parts.
Inputs may be any that keep to these rules, and one draw needn't show every extreme that they name: A token's 8 experts differ. Counting padding tokens too, each index of ep names expert e on c * 32 of its routes, c being the number of slots of e. A route's replica is below the number of slots of its expert. Counting padding tokens too, each index of ep sends exactly 32 of its routes to each slot. `replica_slot`: every slot appears in exactly one row. Expert e has 1 to 4 slots, listed first in its row; the rest of the row repeats the first of them. `token_count`: some index of ep has all 128 tokens valid.
All inputs are finite; a program needn't handle non-finite values.
Results may differ from the reference program's by a relative error of at most 0.018.
Values may be sent and summed in bfloat16 or wider, within the bound.
No kernel may reach another device: no remote copies, remote signals or barrier semaphores. Data moves between devices by JAX's collectives and lax.ppermute only.
A program may use at most 192 MiB of HBM per device.

```python
import math
import jax
import jax.numpy as jnp
from jax import lax

D = 2048
F = 768
TOPK = 8
EXPERTS = 16
SLOTS = 32
REP_MAX = 4
TOK_DEV = 128
CS = 32
SLOT_ROWS = 128
TOKENS = 512
N_EP = 4
N_SUB = 4


def shuffle_experts(device_key):
    return jax.random.permutation(device_key, EXPERTS)


def shuffle_tokens(device_key):
    return jax.random.permutation(device_key, TOK_DEV)


def layout(key):
    keys = jax.random.split(key, 8)
    base_counts = jnp.array([4, 4, 3, 3, 2, 2, 2, 2, 2, 2, 1, 1, 1, 1, 1, 1], jnp.int32)
    count_order = jax.random.permutation(keys[0], EXPERTS).astype(jnp.int32)
    counts = base_counts[count_order]
    slot_order = jax.random.permutation(keys[1], SLOTS).astype(jnp.int32)
    ends = jnp.cumsum(counts)
    starts = ends - counts
    ranks = jnp.arange(REP_MAX, dtype=jnp.int32)
    picks = starts[:, None] + jnp.where(ranks[None, :] < counts[:, None], ranks[None, :], 0)
    replica_table = slot_order[picks]
    order_index = jnp.arange(SLOTS, dtype=jnp.int32)
    owner_of_order = jnp.sum((order_index[:, None] >= ends[None, :]).astype(jnp.int32), axis=1)
    slot_owner = jnp.zeros((SLOTS,), jnp.int32).at[slot_order].set(owner_of_order)
    loads = counts * TOK_DEV // 4
    orders = jax.vmap(shuffle_experts)(jax.random.split(keys[2], N_EP)).astype(jnp.int32)
    run_loads = loads[orders]
    run_ends = jnp.cumsum(run_loads, axis=1)
    run_starts = run_ends - run_loads
    places = jnp.arange(TOPK * TOK_DEV, dtype=jnp.int32)
    run_index = jnp.sum((places[None, :, None] >= run_ends[:, None, :]).astype(jnp.int32), axis=2)
    expert_at = jnp.take_along_axis(orders, run_index, axis=1)
    offset = places[None, :] - jnp.take_along_axis(run_starts, run_index, axis=1)
    block_index = offset // (TOK_DEV // 8)
    shifts = jax.random.randint(keys[4], (N_EP, EXPERTS), 0, REP_MAX)
    expert_counts = counts[expert_at]
    chosen_shift = jnp.take_along_axis(shifts, expert_at, axis=1)
    replica_at = ((block_index + chosen_shift) % expert_counts).astype(jnp.int32)
    token_perms = jax.vmap(shuffle_tokens)(jax.random.split(keys[5], N_EP))
    inverse = jnp.argsort(token_perms, axis=1).astype(jnp.int32)
    gather_index = (jnp.arange(TOPK, dtype=jnp.int32)[None, None, :] * TOK_DEV + inverse[:, :, None]).reshape(N_EP, TOK_DEV * TOPK)
    routes = jnp.take_along_axis(expert_at, gather_index, axis=1).reshape(TOKENS, TOPK).astype(jnp.int32)
    replicas = jnp.take_along_axis(replica_at, gather_index, axis=1).reshape(TOKENS, TOPK).astype(jnp.int32)
    valid_counts = jax.random.randint(keys[6], (N_EP,), TOK_DEV // 2, TOK_DEV + 1)
    full_device = jax.random.randint(keys[7], (), 0, N_EP)
    valid_counts = jnp.where(jnp.arange(N_EP) == full_device, TOK_DEV, valid_counts).astype(jnp.int32)
    return (routes, replicas, replica_table, valid_counts, slot_owner)


def draw_routes(key, part):
    return layout(key)[0]


def draw_replica(key, part):
    return layout(key)[1]


def draw_replica_slot(key, part):
    return layout(key)[2]


def draw_token_count(key, part):
    return layout(key)[3]


def draw_weight_in(key, part):
    owners = layout(key)[4]
    key = jax.random.fold_in(key, 21)
    expert_weights = jax.random.normal(key, (EXPERTS, 2 * F, D), jnp.float32) * D ** (-0.5)
    return expert_weights[owners].astype(jnp.bfloat16)


def draw_weight_down(key, part):
    owners = layout(key)[4]
    key = jax.random.fold_in(key, 37)
    expert_weights = jax.random.normal(key, (EXPERTS, F, D), jnp.float32) * F ** (-0.5)
    return expert_weights[owners].astype(jnp.bfloat16)


def shard_levels(own_key, extent, cuts, smallest, high):
    loudness = 1.0
    for dim, blocks in cuts:
        draws = jax.random.uniform(jax.random.fold_in(jax.random.fold_in(own_key, 6), dim), (blocks,), jnp.float32, smallest / len(cuts), high / len(cuts))
        loudness = loudness * jnp.repeat(jnp.exp(draws), extent[dim] // blocks).reshape((-1,) + (1,) * (len(extent) - 1 - dim))
    return loudness


def centred(rng, extent, deviation, bound, cuts=(), kind=jnp.bfloat16):
    entries = jax.random.normal(rng, extent, jnp.float32) * deviation
    if len(cuts) > 0:
        entries = shard_levels(rng, extent, cuts, -0.22, 0.18) * entries
    return jnp.clip(entries, min=-bound, max=bound).astype(kind)


def setup_inputs(seed: int = 0, part: int = 0) -> dict:
    key_of = jax.random.split(jax.random.key(seed), 11)
    own_keys = jax.random.split(jax.random.fold_in(key_of[10], part), 11)
    grad_out = centred(own_keys[0], (TOKENS, D), 1.0, 6.0, ((0, 4), (1, 4)))
    route_weight = jnp.clip(jnp.exp(math.log(0.59765625) - 2.4849066 * jax.random.uniform(own_keys[1], (TOKENS, TOPK), jnp.float32) ** shard_levels(own_keys[1], (TOKENS, TOPK), ((0, 4),), -0.2, 0.2)), 0.049804688, 0.59765625).astype(jnp.bfloat16)
    routes = draw_routes(jax.random.fold_in(jax.random.fold_in(key_of[10], part), 71), part)
    replica = draw_replica(jax.random.fold_in(jax.random.fold_in(key_of[10], part), 71), part)
    replica_slot = draw_replica_slot(jax.random.fold_in(jax.random.fold_in(key_of[10], part), 71), part)
    token_count = draw_token_count(jax.random.fold_in(jax.random.fold_in(key_of[10], part), 71), part)
    saved_input = centred(own_keys[6], (SLOTS, N_EP, CS, D), 1.0, 6.0, ((0, 4), (3, 4)))
    saved_gate_up = centred(own_keys[7], (SLOTS, SLOT_ROWS, 2 * F), 1.0, 6.0, ((0, 4),))
    weight_in = draw_weight_in(jax.random.fold_in(jax.random.fold_in(key_of[10], part), 71), part)
    weight_down = draw_weight_down(jax.random.fold_in(jax.random.fold_in(key_of[10], part), 71), part)
    return {"grad_out": grad_out, "route_weight": route_weight, "routes": routes, "replica": replica, "replica_slot": replica_slot, "token_count": token_count, "saved_input": saved_input, "saved_gate_up": saved_gate_up, "weight_in": weight_in, "weight_down": weight_down}


def one_slot(operands):
    grad_rows, scale_rows, input_rows, gate_up, weight_pair, weight_proj = operands
    gate_pre = gate_up[:, :F].astype(jnp.float32)
    up_pre = gate_up[:, F:].astype(jnp.float32)
    sigmoid_gate = jax.nn.sigmoid(gate_pre)
    hidden = gate_pre * sigmoid_gate * up_pre
    hidden_b = hidden.astype(jnp.bfloat16)
    scale_wide = scale_rows.astype(jnp.float32)[:, None]
    scaled = (scale_wide * grad_rows.astype(jnp.float32)).astype(jnp.bfloat16)
    blocks = grad_rows.reshape(SLOT_ROWS, N_SUB, D // N_SUB).astype(jnp.float32)
    proj_blocks = weight_proj.reshape(F, N_SUB, D // N_SUB).astype(jnp.float32)
    partial_sums = jnp.einsum("rbd,fbd->brf", blocks, proj_blocks)
    rounded = lax.optimization_barrier(partial_sums.astype(jnp.bfloat16))
    grad_hidden = jnp.sum(rounded.astype(jnp.float32), axis=0)
    route_rows = jnp.sum(hidden * grad_hidden, axis=1).astype(jnp.bfloat16)
    scaled_grad = scale_wide * grad_hidden
    grad_gate = scaled_grad * up_pre * sigmoid_gate * (1.0 + gate_pre * (1.0 - sigmoid_gate))
    grad_up = scaled_grad * gate_pre * sigmoid_gate
    pre_grad = jnp.concatenate([grad_gate, grad_up], axis=1).astype(jnp.bfloat16)
    slot_down = jnp.dot(hidden_b.T, scaled, preferred_element_type=jnp.float32)
    slot_in = jnp.dot(pre_grad.T, input_rows, preferred_element_type=jnp.float32)
    row_grad = jnp.dot(pre_grad, weight_pair, preferred_element_type=jnp.float32).astype(jnp.bfloat16)
    return slot_in, slot_down, row_grad, route_rows


def reference(grad_out, route_weight, routes, replica, replica_slot, token_count, saved_input, saved_gate_up, weight_in, weight_down):
    route_slot = replica_slot[routes, replica]
    token_ids = jnp.arange(TOKENS, dtype=jnp.int32)
    live_token = (token_ids % TOK_DEV) < token_count[token_ids // TOK_DEV]
    live_flat = jnp.broadcast_to(live_token[:, None], (TOKENS, TOPK)).reshape(N_EP, TOK_DEV * TOPK)
    slot_flat = route_slot.reshape(N_EP, TOK_DEV * TOPK)
    slot_ids = jnp.arange(SLOTS, dtype=jnp.int32)
    hits = ((slot_flat[:, :, None] == slot_ids[None, None, :]) & live_flat[:, :, None]).astype(jnp.int32)
    earlier = jnp.cumsum(hits, axis=1) - hits
    position = jnp.sum(earlier * hits, axis=2)
    row_index = slot_flat * SLOT_ROWS + jnp.arange(N_EP, dtype=jnp.int32)[:, None] * CS + position
    live_all = live_flat.reshape(-1)
    total_rows = SLOTS * SLOT_ROWS
    target = jnp.where(live_all, row_index.reshape(-1), total_rows).astype(jnp.int32)
    source = jnp.arange(TOKENS * TOPK, dtype=jnp.int32) // TOPK
    dispatched = jnp.zeros((total_rows, D), jnp.bfloat16).at[target].set(grad_out[source], mode="drop")
    scale_all = jnp.zeros((total_rows,), jnp.bfloat16).at[target].set(route_weight.reshape(-1), mode="drop")
    slot_in, slot_down, row_grad, route_rows = lax.map(one_slot, (
        dispatched.reshape(SLOTS, SLOT_ROWS, D),
        scale_all.reshape(SLOTS, SLOT_ROWS),
        saved_input.reshape(SLOTS, SLOT_ROWS, D),
        saved_gate_up, weight_in, weight_down))
    members = jnp.any(replica_slot[:, :, None] == slot_ids[None, None, :], axis=1).astype(jnp.float32)
    grad_weight_in = jnp.einsum("es,sfd->efd", members, slot_in, precision=lax.Precision.HIGHEST).astype(jnp.bfloat16)
    grad_weight_down = jnp.einsum("es,sfd->efd", members, slot_down, precision=lax.Precision.HIGHEST).astype(jnp.bfloat16)
    safe = jnp.where(live_all, target, 0).astype(jnp.int32)
    routed = jnp.where(live_all[:, None], row_grad.reshape(total_rows, D)[safe], jnp.zeros((), jnp.bfloat16))
    grad_tokens = jnp.sum(routed.reshape(TOKENS, TOPK, D).astype(jnp.float32), axis=1).astype(jnp.bfloat16)
    grad_route_weight = jnp.where(live_all, route_rows.reshape(-1)[safe], jnp.zeros((), jnp.bfloat16)).reshape(TOKENS, TOPK)
    return grad_tokens, grad_route_weight, grad_weight_in, grad_weight_down
```

```python
import functools
import math

import jax
import jax.numpy as jnp
from jax import lax
from jax.experimental import pallas as pl
from jax.experimental.pallas import tpu as pltpu
from jax.sharding import PartitionSpec as P

BF = jnp.bfloat16
F32 = jnp.float32
VMEM_BYTES = 48 * 1024 * 1024


def nt(a, b):
    return lax.dot_general(a, b, (((1,), (1,)), ((), ())), preferred_element_type=F32)


def tn(a, b):
    return lax.dot_general(a, b, (((0,), (0,)), ((), ())), preferred_element_type=F32)


def nn(a, b):
    return jnp.dot(a, b, preferred_element_type=F32)


def whole(shape):
    zeros = (0,) * len(shape)
    return pl.BlockSpec(shape, lambda *_: zeros)


def smem():
    return pl.BlockSpec(memory_space=pltpu.SMEM)


def params(axes=1):
    return pltpu.CompilerParams(
        vmem_limit_bytes=VMEM_BYTES, dimension_semantics=("arbitrary",) * axes
    )


class Sizes:
    def __init__(self, grad_out, routes, replica_slot, saved_input, weight_in, weight_down):
        self.ep = lax.axis_size("ep")
        self.sub = lax.axis_size("sub")
        self.tokens, self.width = grad_out.shape
        self.top = routes.shape[1]
        self.experts, self.reps = replica_slot.shape
        self.local = weight_in.shape[0]
        self.slots = self.ep * self.local
        self.cap = saved_input.shape[2]
        self.rows = self.ep * self.cap
        self.hidden = weight_down.shape[1]
        self.pair = weight_in.shape[1]
        self.all_rows = self.local * self.rows
        self.part = self.all_rows // self.sub
        self.block = math.gcd(self.rows, self.part)
        self.sources = self.block // self.cap
        self.blocks = self.all_rows // self.block
        self.part_blocks = self.part // self.block
        self.slot_blocks = self.rows // self.block
        self.in_cols = self.pair // self.ep
        self.down_cols = self.hidden // self.ep
        self.cols = self.in_cols + self.down_cols
        self.folds = self.width // self.tokens
        self.tail = 2 * self.slots // self.folds


def key_columns(z, routes_ref, replica_ref):
    return routes_ref[...] * z.reps + replica_ref[...]


def slot_table(z, table_ref):
    ids = lax.broadcasted_iota(jnp.int32, (z.slots, z.experts * z.reps), 0)
    return (table_ref[...] == ids).astype(F32).astype(BF)


def route_kernel(z, count_ref, grad_ref, weight_ref, routes_ref, replica_ref, table_ref, out_ref):
    keys = key_columns(z, routes_ref, replica_ref)
    weights = weight_ref[...].astype(F32)
    width = z.experts * z.reps
    ids = lax.broadcasted_iota(jnp.int32, (z.tokens, width), 1)
    live = lax.broadcasted_iota(jnp.int32, (z.tokens, width), 0) < count_ref[0]
    hit = jnp.zeros((z.tokens, width), F32)
    load = jnp.zeros((z.tokens, width), F32)
    for k in range(z.top):
        same = (keys[:, k : k + 1] == ids) & live
        hit = jnp.where(same, 1.0, hit)
        load = jnp.where(same, weights[:, k : k + 1], load)
    table = slot_table(z, table_ref)
    hits = nt(table, hit.astype(BF))
    loads = nt(table, load.astype(BF))
    before = lax.broadcasted_iota(jnp.int32, (z.tokens, z.tokens), 0)
    after = lax.broadcasted_iota(jnp.int32, (z.tokens, z.tokens), 1)
    earlier = nn(hits.astype(BF), (before < after).astype(F32).astype(BF))
    code = jnp.where(hits > 0.5, earlier, -1.0)
    both = jnp.concatenate([code, loads], axis=0).astype(BF)
    out_ref[: z.tokens, :] = grad_ref[...]
    for b in range(z.folds):
        out_ref[z.tokens :, b * z.tokens : (b + 1) * z.tokens] = both[
            b * z.tail : (b + 1) * z.tail, :
        ]


def block_place(z, block):
    slot = block // z.slot_blocks
    first = (block % z.slot_blocks) * z.sources
    return slot, first


def block_picks(z, codes_ref, slot, first):
    rows = lax.broadcasted_iota(jnp.int32, (z.cap, z.tokens), 0).astype(F32)
    for a in range(z.sources):
        code = codes_ref[first + a, pl.ds(slot, 1), :]
        yield a, rows == code


def block_scale(z, codes_ref, slot, first):
    parts = []
    for a, pick in block_picks(z, codes_ref, slot, first):
        load = codes_ref[first + a, pl.ds(z.slots + slot, 1), :]
        parts.append(jnp.sum(jnp.where(pick, load, 0.0), axis=1, keepdims=True))
    return jnp.concatenate(parts, axis=0)


def block_rows(z, codes_ref, grads_ref, slot, first):
    parts = []
    for a, pick in block_picks(z, codes_ref, slot, first):
        parts.append(nn(pick.astype(F32).astype(BF), grads_ref[first + a]))
    return jnp.concatenate(parts, axis=0)


def down_kernel(z, ids_ref, *refs):
    bufs = refs[: z.ep]
    weight_ref = refs[z.ep]
    parts = refs[z.ep + 1 : z.ep + 1 + z.sub]
    grads_ref, codes_ref = refs[z.ep + 1 + z.sub :]
    me, mine = ids_ref[0], ids_ref[1]
    step = pl.program_id(0)

    @pl.when(step == 0)
    def _():
        for k in range(z.ep):
            source = me ^ k
            grads_ref[source] = bufs[k][: z.tokens, :]
            for b in range(z.folds):
                codes_ref[source, b * z.tail : (b + 1) * z.tail, :] = bufs[k][
                    z.tokens :, b * z.tokens : (b + 1) * z.tokens
                ].astype(F32)

    place = step // z.part_blocks
    block = (place ^ mine) * z.part_blocks + step % z.part_blocks
    slot, first = block_place(z, block)
    rows = block_rows(z, codes_ref, grads_ref, me * z.local + slot, first).astype(BF)
    partial = nt(rows, weight_ref[0]).astype(BF)
    spot = pl.multiple_of((step % z.part_blocks) * z.block, z.block)
    for k in range(z.sub):

        @pl.when(place == k)
        def _():
            parts[k][pl.ds(spot, z.block), :] = partial


def gate_terms(z, pair, grad, scale):
    gate = pair[:, : z.hidden].astype(F32)
    up = pair[:, z.hidden :].astype(F32)
    sig = 1.0 / (1.0 + jnp.exp(-gate))
    act = gate * sig
    hidden = act * up
    scaled = scale * grad
    grad_gate = scaled * up * sig * (1.0 + gate * (1.0 - sig))
    grad_up = scaled * act
    return hidden, grad_gate.astype(BF), grad_up.astype(BF)


def pre_kernel(z, ids_ref, *refs):
    parts = refs[: z.sub]
    pair_ref, codes_ref, out_ref, grad_ref = refs[z.sub :]
    block = ids_ref[1] * z.part_blocks + pl.program_id(0)
    slot, first = block_place(z, block)
    scale = block_scale(z, codes_ref, ids_ref[0] * z.local + slot, first)
    grad = parts[0][...].astype(F32)
    for k in range(1, z.sub):
        grad = grad + parts[k][...].astype(F32)
    grad_ref[...] = grad.astype(BF)
    hidden, grad_gate, grad_up = gate_terms(z, pair_ref[...], grad, scale)
    hidden = hidden.astype(BF)
    pre = jnp.concatenate([grad_gate, grad_up], axis=1)
    for q in range(z.ep):
        out_ref[q, :, : z.in_cols] = pre[:, q * z.in_cols : (q + 1) * z.in_cols]
        out_ref[q, :, z.in_cols :] = hidden[:, q * z.down_cols : (q + 1) * z.down_cols]


def row_kernel(z, ids_ref, *refs):
    grads = refs[: z.sub]
    pair_ref, weight_ref, codes_ref, out_ref, sums, marks, held = refs[z.sub :]
    me, mine = ids_ref[0], ids_ref[1]
    step = pl.program_id(0)
    place = step // z.part_blocks
    block = (place ^ mine) * z.part_blocks + step % z.part_blocks
    slot, first = block_place(z, block)

    @pl.when(step == 0)
    def _():
        sums[...] = jnp.zeros_like(sums)
        marks[...] = jnp.zeros_like(marks)

    spot = pl.multiple_of((step % z.part_blocks) * z.block, z.block)
    for k in range(z.sub):

        @pl.when(place == k)
        def _():
            held[...] = grads[k][pl.ds(spot, z.block), :]

    grad = held[...].astype(F32)
    scale = block_scale(z, codes_ref, me * z.local + slot, first)
    hidden, grad_gate, grad_up = gate_terms(z, pair_ref[...], grad, scale)
    route = jnp.sum(hidden * grad, axis=1, keepdims=True).astype(BF).astype(F32)
    rows = nn(grad_gate, weight_ref[0, : z.hidden, :]) + nn(grad_up, weight_ref[0, z.hidden :, :])
    rows = rows.astype(BF)
    for a, pick in block_picks(z, codes_ref, me * z.local + slot, first):
        lo, hi = a * z.cap, (a + 1) * z.cap
        sums[first + a] += tn(pick.astype(F32).astype(BF), rows[lo:hi, :])
        marks[first + a, pl.ds(slot, 1), :] = jnp.sum(
            jnp.where(pick, route[lo:hi, :], 0.0), axis=0, keepdims=True
        )

    @pl.when(step == z.blocks - 1)
    def _():
        for p in range(z.ep):
            out_ref[p ^ me, : z.tokens, :] = sums[p].astype(BF)
            tail = jnp.concatenate(
                [
                    marks[p],
                    jnp.zeros((marks.shape[1], z.width - z.tokens), F32),
                ],
                axis=1,
            )
            out_ref[p ^ me, z.tokens :, :] = tail.astype(BF)


def token_kernel(z, ids_ref, count_ref, *refs):
    got = refs[: z.ep]
    routes_ref, replica_ref, table_ref, tokens_ref, route_ref, marks = refs[z.ep :]
    me = ids_ref[0]
    total = got[0][: z.tokens, :].astype(F32)
    for k in range(1, z.ep):
        total = total + got[k][: z.tokens, :].astype(F32)
    tokens_ref[...] = total.astype(BF)
    for k in range(z.ep):
        marks[me ^ k] = got[k][z.tokens :, : z.tokens].astype(F32)
    rows = jnp.concatenate([marks[p][: z.local, :] for p in range(z.ep)], axis=0)
    spread = tn(rows.astype(BF), slot_table(z, table_ref))
    keys = key_columns(z, routes_ref, replica_ref)
    width = z.experts * z.reps
    ids = lax.broadcasted_iota(jnp.int32, (z.tokens, width), 1)
    live = lax.broadcasted_iota(jnp.int32, (z.tokens, width), 0) < count_ref[0]
    columns = []
    for k in range(z.top):
        same = (keys[:, k : k + 1] == ids) & live
        columns.append(jnp.sum(jnp.where(same, spread, 0.0), axis=1, keepdims=True))
    route_ref[...] = jnp.concatenate(columns, axis=1).astype(BF)


def total_kernel(z, ids_ref, table_ref, *refs):
    sides = refs[: z.sub]
    inputs_ref, grads_ref, codes_ref, in_ref, down_ref = refs[z.sub : z.sub + 5]
    held, in_sum, down_sum, sems = refs[z.sub + 5 :]
    mine = ids_ref[1]
    expert = pl.program_id(0)

    @pl.when(expert == 0)
    def _():
        copies = [
            pltpu.make_async_copy(sides[k], held.at[k], sems.at[k]) for k in range(z.sub)
        ]
        for copy in copies:
            copy.start()
        for copy in copies:
            copy.wait()

    first_slot = table_ref[expert, 0]

    def add(slot_id, fresh):
        source = slot_id // z.local
        for b in range(z.slot_blocks):
            block = (slot_id % z.local) * z.slot_blocks + b
            part = (block // z.part_blocks) ^ mine
            spot = pl.multiple_of((block % z.part_blocks) * z.block, z.block)
            left = held[part, source, pl.ds(spot, z.block), :]
            start = pl.multiple_of(block * z.block, z.block)
            right = inputs_ref[source, pl.ds(start, z.block), :]
            first = b * z.sources
            scale = block_scale(z, codes_ref, slot_id, first)
            rows = (block_rows(z, codes_ref, grads_ref, slot_id, first) * scale).astype(BF)
            grad_in = tn(left[:, : z.in_cols], right)
            grad_down = tn(left[:, z.in_cols :], rows)
            if fresh and b == 0:
                in_sum[...] = grad_in
                down_sum[...] = grad_down
            else:
                in_sum[...] += grad_in
                down_sum[...] += grad_down

    add(first_slot, True)
    for r in range(1, z.reps):
        slot_id = table_ref[expert, r]

        @pl.when(slot_id != first_slot)
        def _():
            add(slot_id, False)

    in_ref[0] = in_sum[...].astype(BF)
    down_ref[0] = down_sum[...].astype(BF)


def swap(x, axis, size, bit):
    return lax.ppermute(x, axis, [(i, i ^ bit) for i in range(size)])


def spread_over(x, axis, size):
    have = {0: x}
    bit = size // 2
    while bit:
        for k in list(have):
            have[k | bit] = swap(have[k], axis, size, bit)
        bit //= 2
    return [have[k] for k in range(size)]


def body(
    grad_out,
    route_weight,
    routes,
    replica,
    replica_slot,
    token_count,
    saved_input,
    saved_gate_up,
    weight_in,
    weight_down,
):
    z = Sizes(grad_out, routes, replica_slot, saved_input, weight_in, weight_down)
    n, m = z.ep, z.sub
    ids = jnp.stack([lax.axis_index("ep"), lax.axis_index("sub")]).astype(jnp.int32)
    table_row = replica_slot.reshape(1, -1)
    pair_rows = saved_gate_up.reshape(z.all_rows, z.pair)
    grad_shape = (z.tokens + z.tail, z.width)
    code_shape = (n, 2 * z.slots, z.tokens)

    inputs_all = lax.all_gather(saved_input.reshape(z.all_rows, z.width), "ep")

    buf = pl.pallas_call(
        functools.partial(route_kernel, z),
        out_shape=jax.ShapeDtypeStruct(grad_shape, BF),
        in_specs=[smem()]
        + [
            whole(a.shape) for a in (grad_out, route_weight, routes, replica, table_row)
        ],
        out_specs=whole(grad_shape),
        grid=(1,),
        compiler_params=params(),
        name="route",
    )(token_count, grad_out, route_weight, routes, replica, table_row)
    bufs = [buf] + [swap(buf, "ep", n, k) for k in range(1, n)]

    def down_slot(i, ids_ref):
        place = i // z.part_blocks
        block = (place ^ ids_ref[1]) * z.part_blocks + i % z.part_blocks
        return block // z.slot_blocks

    outs = pl.pallas_call(
        functools.partial(down_kernel, z),
        grid_spec=pltpu.PrefetchScalarGridSpec(
            num_scalar_prefetch=1,
            grid=(z.blocks,),
            in_specs=[whole(grad_shape)] * n
            + [pl.BlockSpec((1, z.hidden, z.width), lambda i, r: (down_slot(i, r), 0, 0))],
            out_specs=[whole((z.part, z.hidden))] * m
            + [whole((n, z.tokens, z.width)), whole(code_shape)],
        ),
        out_shape=[jax.ShapeDtypeStruct((z.part, z.hidden), BF)] * m
        + [
            jax.ShapeDtypeStruct((n, z.tokens, z.width), BF),
            jax.ShapeDtypeStruct(code_shape, F32),
        ],
        compiler_params=params(),
        name="hidden_partials",
    )(ids, *bufs, weight_down)
    parts, (grads_all, codes) = outs[:m], outs[m:]
    parts = [parts[0]] + [swap(parts[k], "sub", m, k) for k in range(1, m)]

    pre, grad_part = pl.pallas_call(
        functools.partial(pre_kernel, z),
        grid_spec=pltpu.PrefetchScalarGridSpec(
            num_scalar_prefetch=1,
            grid=(z.part_blocks,),
            in_specs=[pl.BlockSpec((z.block, z.hidden), lambda i, r: (i, 0))] * m
            + [
                pl.BlockSpec((z.block, z.pair), lambda i, r: (r[1] * z.part_blocks + i, 0)),
                whole(code_shape),
            ],
            out_specs=[
                pl.BlockSpec((n, z.block, z.cols), lambda i, r: (0, i, 0)),
                pl.BlockSpec((z.block, z.hidden), lambda i, r: (i, 0)),
            ],
        ),
        out_shape=[
            jax.ShapeDtypeStruct((n, z.part, z.cols), BF),
            jax.ShapeDtypeStruct((z.part, z.hidden), BF),
        ],
        compiler_params=params(),
        name="pre_grads",
    )(ids, *parts, pair_rows, codes)

    columns = lax.all_to_all(pre, "ep", split_axis=0, concat_axis=0, tiled=True)
    grad_parts = spread_over(grad_part, "sub", m)
    sides = spread_over(columns, "sub", m)

    def row_block(i, ids_ref):
        place = i // z.part_blocks
        return (place ^ ids_ref[1]) * z.part_blocks + i % z.part_blocks

    mark_rows = -(-z.local // 16) * 16
    back_shape = (n, z.tokens + mark_rows, z.width)
    back = pl.pallas_call(
        functools.partial(row_kernel, z),
        grid_spec=pltpu.PrefetchScalarGridSpec(
            num_scalar_prefetch=1,
            grid=(z.blocks,),
            in_specs=[whole((z.part, z.hidden))] * m
            + [
                pl.BlockSpec((z.block, z.pair), lambda i, r: (row_block(i, r), 0)),
                pl.BlockSpec((1, z.pair, z.width), lambda i, r: (down_slot(i, r), 0, 0)),
                whole(code_shape),
            ],
            out_specs=whole(back_shape),
            scratch_shapes=[
                pltpu.VMEM((n, z.tokens, z.width), F32),
                pltpu.VMEM((n, mark_rows, z.tokens), F32),
                pltpu.VMEM((z.block, z.hidden), BF),
            ],
        ),
        out_shape=jax.ShapeDtypeStruct(back_shape, BF),
        compiler_params=params(),
        name="row_grads",
    )(ids, *grad_parts, pair_rows, weight_in, codes)
    got = [back[0]] + [swap(back[k], "ep", n, k) for k in range(1, n)]

    grad_tokens, grad_routes = pl.pallas_call(
        functools.partial(token_kernel, z),
        out_shape=[
            jax.ShapeDtypeStruct((z.tokens, z.width), BF),
            jax.ShapeDtypeStruct((z.tokens, z.top), BF),
        ],
        in_specs=[smem(), smem()]
        + [whole(back_shape[1:])] * n
        + [whole(a.shape) for a in (routes, replica, table_row)],
        out_specs=[whole((z.tokens, z.width)), whole((z.tokens, z.top))],
        grid=(1,),
        scratch_shapes=[pltpu.VMEM((n, mark_rows, z.tokens), F32)],
        compiler_params=params(),
        name="token_grads",
    )(ids, token_count, *got, routes, replica, table_row)

    side_shape = (n, z.part, z.cols)
    grad_in, grad_down = pl.pallas_call(
        functools.partial(total_kernel, z),
        grid_spec=pltpu.PrefetchScalarGridSpec(
            num_scalar_prefetch=2,
            grid=(z.experts,),
            in_specs=[pl.BlockSpec(memory_space=pl.ANY)] * m
            + [
                whole((n, z.all_rows, z.width)),
                whole((n, z.tokens, z.width)),
                whole(code_shape),
            ],
            out_specs=[
                pl.BlockSpec((1, z.in_cols, z.width), lambda e, r, t: (e, 0, 0)),
                pl.BlockSpec((1, z.down_cols, z.width), lambda e, r, t: (e, 0, 0)),
            ],
            scratch_shapes=[
                pltpu.VMEM((m,) + side_shape, BF),
                pltpu.VMEM((z.in_cols, z.width), F32),
                pltpu.VMEM((z.down_cols, z.width), F32),
                pltpu.SemaphoreType.DMA((m,)),
            ],
        ),
        out_shape=[
            jax.ShapeDtypeStruct((z.experts, z.in_cols, z.width), BF),
            jax.ShapeDtypeStruct((z.experts, z.down_cols, z.width), BF),
        ],
        compiler_params=params(),
        name="weight_grads",
    )(ids, replica_slot, *sides, inputs_all, grads_all, codes)
    return grad_tokens, grad_routes, grad_in, grad_down


def solution(mesh):
    return jax.shard_map(
        body,
        mesh=mesh,
        in_specs=(
            P(("groups", "ep"), "sub"),
            P(("groups", "ep"), None),
            P(("groups", "ep"), None),
            P(("groups", "ep"), None),
            P("groups", None),
            P(("groups", "ep")),
            P(("groups", "ep"), None, None, "sub"),
            P(("groups", "ep"), None, None),
            P(("groups", "ep"), None, "sub"),
            P(("groups", "ep"), None, "sub"),
        ),
        out_specs=(
            P(("groups", "ep"), "sub"),
            P(("groups", "ep"), None),
            P("groups", "ep", "sub"),
            P("groups", "ep", "sub"),
        ),
        check_vma=False,
    )
```

```python
import functools
import math

import jax
import jax.numpy as jnp
from jax import lax
from jax.experimental import pallas as pl
from jax.experimental.pallas import tpu as pltpu
from jax.sharding import PartitionSpec as P

BF = jnp.bfloat16
F32 = jnp.float32
CUTS = 2


def nt(a, b):
    return lax.dot_general(a, b, (((1,), (1,)), ((), ())), preferred_element_type=F32)


def tn(a, b):
    return lax.dot_general(a, b, (((0,), (0,)), ((), ())), preferred_element_type=F32)


def nn(a, b):
    return jnp.dot(a, b, preferred_element_type=F32)


def whole(shape):
    zeros = (0,) * len(shape)
    return pl.BlockSpec(shape, lambda *_: zeros)


def smem():
    return pl.BlockSpec(memory_space=pltpu.SMEM)


def params(mib):
    return pltpu.CompilerParams(
        vmem_limit_bytes=mib * 1024 * 1024, dimension_semantics=("arbitrary",)
    )


class Sizes:
    def __init__(self, grad_out, routes, replica_slot, saved_input, weight_in, weight_down):
        self.ep = lax.axis_size("ep")
        self.sub = lax.axis_size("sub")
        self.tokens, self.width = grad_out.shape
        self.top = routes.shape[1]
        self.experts, self.reps = replica_slot.shape
        self.local = weight_in.shape[0]
        self.slots = self.ep * self.local
        self.cap = saved_input.shape[2]
        self.rows = self.ep * self.cap
        self.hidden = weight_down.shape[1]
        self.pair = weight_in.shape[1]
        self.all_rows = self.local * self.rows
        self.part = self.all_rows // self.sub
        self.block = math.gcd(self.rows, self.part)
        self.sources = self.block // self.cap
        self.blocks = self.all_rows // self.block
        self.part_blocks = self.part // self.block
        self.slot_blocks = self.rows // self.block
        self.in_cols = self.pair // self.ep
        self.down_cols = self.hidden // self.ep
        self.cols = self.in_cols + self.down_cols
        self.folds = self.width // self.tokens
        self.tail = 2 * self.slots // self.folds


def slot_table(z, table_ref, r):
    ids = lax.broadcasted_iota(jnp.int32, (z.slots, z.experts), 0)
    return (table_ref[r : r + 1, :] == ids).astype(F32).astype(BF)


def key_hits(z, count_ref, routes_ref, replica_ref, r, k):
    ids = lax.broadcasted_iota(jnp.int32, (z.experts, z.tokens), 0)
    live = lax.broadcasted_iota(jnp.int32, (1, z.tokens), 1) < count_ref[0]
    key = jnp.where(live & (replica_ref[k : k + 1, :] == r), routes_ref[k : k + 1, :], -1)
    return key == ids


def route_kernel(z, count_ref, grad_ref, weight_ref, routes_ref, replica_ref, table_ref, out_ref):
    weights = weight_ref[...].astype(F32)
    hits = jnp.zeros((z.slots, z.tokens), F32)
    loads = jnp.zeros((z.slots, z.tokens), F32)
    for r in range(z.reps):
        hit = jnp.zeros((z.experts, z.tokens), F32)
        load = jnp.zeros((z.experts, z.tokens), F32)
        for k in range(z.top):
            same = key_hits(z, count_ref, routes_ref, replica_ref, r, k)
            hit = jnp.where(same, 1.0, hit)
            load = jnp.where(same, weights[k : k + 1, :], load)
        table = slot_table(z, table_ref, r)
        hits = hits + nn(table, hit.astype(BF))
        loads = loads + nn(table, load.astype(BF))
    before = lax.broadcasted_iota(jnp.int32, (z.tokens, z.tokens), 0)
    after = lax.broadcasted_iota(jnp.int32, (z.tokens, z.tokens), 1)
    earlier = nn(hits.astype(BF), (before < after).astype(F32).astype(BF))
    code = jnp.where(hits > 0.5, earlier, -1.0)
    both = jnp.concatenate([code, loads], axis=0).astype(BF)
    out_ref[: z.tokens, :] = grad_ref[...]
    for b in range(z.folds):
        out_ref[z.tokens :, b * z.tokens : (b + 1) * z.tokens] = both[
            b * z.tail : (b + 1) * z.tail, :
        ]


def block_place(z, block):
    slot = block // z.slot_blocks
    first = (block % z.slot_blocks) * z.sources
    return slot, first


def block_picks(z, codes_ref, slot, first):
    rows = lax.broadcasted_iota(jnp.int32, (z.cap, z.tokens), 0).astype(F32)
    for a in range(z.sources):
        code = codes_ref[first + a, pl.ds(slot, 1), :]
        yield a, rows == code


def block_scale(z, codes_ref, slot, first):
    parts = []
    for a, pick in block_picks(z, codes_ref, slot, first):
        load = codes_ref[first + a, pl.ds(z.slots + slot, 1), :]
        parts.append(jnp.sum(jnp.where(pick, load, 0.0), axis=1, keepdims=True))
    return jnp.concatenate(parts, axis=0)


def scaled_rows(z, codes_ref, grads_ref, slot, first):
    parts = []
    for a, pick in block_picks(z, codes_ref, slot, first):
        load = codes_ref[first + a, pl.ds(z.slots + slot, 1), :]
        parts.append(nn(jnp.where(pick, load, 0.0).astype(BF), grads_ref[first + a]))
    return jnp.concatenate(parts, axis=0).astype(BF)


def local_picks(z, codes_ref, source, me):
    code = codes_ref[source, pl.ds(pl.multiple_of(me * z.local, z.local), z.local), :]
    rows = lax.broadcasted_iota(jnp.int32, (z.local, z.cap, z.tokens), 1).astype(F32)
    pick = (code[:, None, :] == rows).astype(F32)
    return pick.reshape(z.local * z.cap, z.tokens).astype(BF)


def down_kernel(z, ids_ref, *refs):
    bufs = refs[: z.ep]
    weight_ref = refs[z.ep]
    parts = refs[z.ep + 1 : z.ep + 1 + z.sub]
    grads_ref, codes_ref, rows_ref = refs[z.ep + 1 + z.sub :]
    me, mine = ids_ref[0], ids_ref[1]
    step = pl.program_id(0)

    @pl.when(step == 0)
    def _():
        for k in range(z.ep):
            source = me ^ k
            grads_ref[source] = bufs[k][: z.tokens, :]
            for b in range(z.folds):
                codes_ref[source, b * z.tail : (b + 1) * z.tail, :] = bufs[k][
                    z.tokens :, b * z.tokens : (b + 1) * z.tokens
                ].astype(F32)
        for p in range(z.ep):
            rows = nn(local_picks(z, codes_ref, p, me), grads_ref[p]).astype(BF)
            rows_ref[:, p * z.cap : (p + 1) * z.cap, :] = rows.reshape(z.local, z.cap, z.width)

    place = step // z.part_blocks
    block = (place ^ mine) * z.part_blocks + step % z.part_blocks
    slot, first = block_place(z, block)
    start = pl.multiple_of(first * z.cap, z.block)
    partial = nt(rows_ref[slot, pl.ds(start, z.block), :], weight_ref[0]).astype(BF)
    spot = pl.multiple_of((step % z.part_blocks) * z.block, z.block)
    for k in range(z.sub):

        @pl.when(place == k)
        def _():
            parts[k][pl.ds(spot, z.block), :] = partial


def gate_terms(z, pair, grad, scale):
    gate = pair[:, : z.hidden].astype(F32)
    up = pair[:, z.hidden :].astype(F32)
    sig = 1.0 / (1.0 + jnp.exp(-gate))
    act = gate * sig
    hidden = act * up
    scaled = scale * grad
    grad_gate = scaled * up * sig * (1.0 + gate * (1.0 - sig))
    grad_up = scaled * act
    return hidden, grad_gate.astype(BF), grad_up.astype(BF)


def pre_kernel(z, ids_ref, *refs):
    parts = refs[: z.sub]
    pair_ref, codes_ref, out_ref, grad_ref = refs[z.sub :]
    block = ids_ref[1] * z.part_blocks + pl.program_id(0)
    slot, first = block_place(z, block)
    scale = block_scale(z, codes_ref, ids_ref[0] * z.local + slot, first)
    grad = parts[0][...].astype(F32)
    for k in range(1, z.sub):
        grad = grad + parts[k][...].astype(F32)
    grad_ref[...] = grad.astype(BF)
    hidden, grad_gate, grad_up = gate_terms(z, pair_ref[...], grad, scale)
    hidden = hidden.astype(BF).T
    pre = jnp.concatenate([grad_gate.T, grad_up.T], axis=0)
    for q in range(z.ep):
        out_ref[q, : z.in_cols, :] = pre[q * z.in_cols : (q + 1) * z.in_cols, :]
        out_ref[q, z.in_cols :, :] = hidden[q * z.down_cols : (q + 1) * z.down_cols, :]


def row_kernel(z, ids_ref, *refs):
    grads = refs[: z.sub]
    pair_ref, weight_ref, codes_ref, out_ref, rows_ref, marks, held = refs[z.sub :]
    me, mine = ids_ref[0], ids_ref[1]
    step = pl.program_id(0)
    place = step // z.part_blocks
    block = (place ^ mine) * z.part_blocks + step % z.part_blocks
    slot, first = block_place(z, block)

    @pl.when(step == 0)
    def _():
        marks[...] = jnp.zeros_like(marks)

    spot = pl.multiple_of((step % z.part_blocks) * z.block, z.block)
    for k in range(z.sub):

        @pl.when(place == k)
        def _():
            held[...] = grads[k][pl.ds(spot, z.block), :]

    grad = held[...].astype(F32)
    scale = block_scale(z, codes_ref, me * z.local + slot, first)
    hidden, grad_gate, grad_up = gate_terms(z, pair_ref[...], grad, scale)
    route = jnp.sum(hidden * grad, axis=1, keepdims=True).astype(BF).astype(F32)
    rows = nn(grad_gate, weight_ref[0, : z.hidden, :]) + nn(grad_up, weight_ref[0, z.hidden :, :])
    start = pl.multiple_of(first * z.cap, z.block)
    rows_ref[slot, pl.ds(start, z.block), :] = rows.astype(BF)
    for a, pick in block_picks(z, codes_ref, me * z.local + slot, first):
        marks[first + a, pl.ds(slot, 1), :] = jnp.sum(
            jnp.where(pick, route[a * z.cap : (a + 1) * z.cap, :], 0.0), axis=0, keepdims=True
        )

    @pl.when(step == z.blocks - 1)
    def _():
        for p in range(z.ep):
            rows = rows_ref[:, p * z.cap : (p + 1) * z.cap, :].reshape(z.local * z.cap, z.width)
            out_ref[p ^ me, : z.tokens, :] = tn(local_picks(z, codes_ref, p, me), rows).astype(BF)
            out_ref[p ^ me, z.tokens :, : z.tokens] = marks[p].astype(BF)
            out_ref[p ^ me, z.tokens :, z.tokens :] = jnp.zeros(
                (marks.shape[1], z.width - z.tokens), BF
            )


def token_kernel(z, ids_ref, count_ref, *refs):
    got = refs[: z.ep]
    routes_ref, replica_ref, table_ref, tokens_ref, route_ref, marks = refs[z.ep :]
    me = ids_ref[0]
    total = got[0][: z.tokens, :].astype(F32)
    for k in range(1, z.ep):
        total = total + got[k][: z.tokens, :].astype(F32)
    tokens_ref[...] = total.astype(BF)
    for k in range(z.ep):
        marks[me ^ k] = got[k][z.tokens :, : z.tokens].astype(F32)
    rows = jnp.concatenate([marks[p][: z.local, :] for p in range(z.ep)], axis=0).astype(BF)
    totals = [jnp.zeros((1, z.tokens), F32)] * z.top
    for r in range(z.reps):
        spread = tn(slot_table(z, table_ref, r), rows)
        for k in range(z.top):
            same = key_hits(z, count_ref, routes_ref, replica_ref, r, k)
            totals[k] += jnp.sum(jnp.where(same, spread, 0.0), axis=0, keepdims=True)
    route_ref[...] = jnp.concatenate(totals, axis=0).astype(BF)


def total_kernel(z, down, ids_ref, table_ref, *refs):
    sides = refs[: z.sub]
    inputs_ref, grads_ref, codes_ref = refs[z.sub : z.sub + 3]
    if down:
        in_ref, down_ref, held, sems = refs[z.sub + 3 :]
    else:
        in_ref, held, sems = refs[z.sub + 4 :]
    mine = ids_ref[1]
    expert = pl.program_id(0)

    @pl.when(expert == 0)
    def _():
        copies = [
            pltpu.make_async_copy(sides[k], held.at[k], sems.at[k]) for k in range(z.sub)
        ]
        for copy in copies:
            copy.start()
        for copy in copies:
            copy.wait()

    slot_ids = [table_ref[r, expert] for r in range(z.reps)]
    count = 1
    for r in range(1, z.reps):
        count = count + (slot_ids[r] != slot_ids[0]).astype(jnp.int32)

    def add(used):
        lefts, rights, rows = [], [], []
        for slot_id in used:
            source = slot_id // z.local
            for b in range(z.slot_blocks):
                block = (slot_id % z.local) * z.slot_blocks + b
                part = (block // z.part_blocks) ^ mine
                spot = pl.multiple_of((block % z.part_blocks) * z.block, z.block)
                lefts.append(held[part, source, :, pl.ds(spot, z.block)])
                start = pl.multiple_of(block * z.block, z.block)
                rights.append(inputs_ref[source, pl.ds(start, z.block), :])
                if down:
                    rows.append(scaled_rows(z, codes_ref, grads_ref, slot_id, b * z.sources))
        left = jnp.concatenate(lefts, axis=1)
        in_ref[0] = nn(left[: z.in_cols, :], jnp.concatenate(rights, axis=0)).astype(BF)
        if down:
            down_ref[0] = nn(left[z.in_cols :, :], jnp.concatenate(rows, axis=0)).astype(BF)

    for c in range(1, z.reps + 1):

        @pl.when(count == c)
        def _():
            add(slot_ids[:c])


def swap(x, axis, size, bit):
    return lax.ppermute(x, axis, [(i, i ^ bit) for i in range(size)])


def spread_over(x, axis, size):
    have = {0: x}
    bit = size // 2
    while bit:
        for k in list(have):
            have[k | bit] = swap(have[k], axis, size, bit)
        bit //= 2
    return [have[k] for k in range(size)]


def body(
    grad_out,
    route_weight,
    routes,
    replica,
    replica_slot,
    token_count,
    saved_input,
    saved_gate_up,
    weight_in,
    weight_down,
):
    z = Sizes(grad_out, routes, replica_slot, saved_input, weight_in, weight_down)
    n, m = z.ep, z.sub
    ids = jnp.stack([lax.axis_index("ep"), lax.axis_index("sub")]).astype(jnp.int32)
    routes, replica, table = routes.T, replica.T, replica_slot.T
    route_weight = route_weight.T
    pair_rows = saved_gate_up.reshape(z.all_rows, z.pair)
    grad_shape = (z.tokens + z.tail, z.width)
    code_shape = (n, 2 * z.slots, z.tokens)
    chunk = z.width // CUTS
    inputs = saved_input.reshape(z.all_rows, z.width)
    inputs = [inputs[:, c * chunk : (c + 1) * chunk] for c in range(CUTS)]

    buf = pl.pallas_call(
        functools.partial(route_kernel, z),
        out_shape=jax.ShapeDtypeStruct(grad_shape, BF),
        in_specs=[smem()]
        + [whole(a.shape) for a in (grad_out, route_weight, routes, replica, table)],
        out_specs=whole(grad_shape),
        grid=(1,),
        compiler_params=params(4),
        name="route",
    )(token_count, grad_out, route_weight, routes, replica, table)
    bufs = [buf] + [swap(buf, "ep", n, k) for k in range(1, n)]
    bufs, inputs[0] = lax.optimization_barrier((bufs, inputs[0]))
    gathered = [lax.all_gather(inputs[0], "ep")]

    def row_block(i, ids_ref):
        place = i // z.part_blocks
        return (place ^ ids_ref[1]) * z.part_blocks + i % z.part_blocks

    def row_slot(i, ids_ref):
        return row_block(i, ids_ref) // z.slot_blocks

    outs = pl.pallas_call(
        functools.partial(down_kernel, z),
        grid_spec=pltpu.PrefetchScalarGridSpec(
            num_scalar_prefetch=1,
            grid=(z.blocks,),
            in_specs=[whole(grad_shape)] * n
            + [pl.BlockSpec((1, z.hidden, z.width), lambda i, r: (row_slot(i, r), 0, 0))],
            out_specs=[whole((z.part, z.hidden))] * m
            + [whole((n, z.tokens, z.width)), whole(code_shape)],
            scratch_shapes=[pltpu.VMEM((z.local, z.rows, z.width), BF)],
        ),
        out_shape=[jax.ShapeDtypeStruct((z.part, z.hidden), BF)] * m
        + [
            jax.ShapeDtypeStruct((n, z.tokens, z.width), BF),
            jax.ShapeDtypeStruct(code_shape, F32),
        ],
        compiler_params=params(16),
        name="hidden_partials",
    )(ids, *bufs, weight_down)
    parts, (grads_all, codes) = outs[:m], outs[m:]
    parts = [parts[0]] + [swap(parts[k], "sub", m, k) for k in range(1, m)]

    pre, grad_part = pl.pallas_call(
        functools.partial(pre_kernel, z),
        grid_spec=pltpu.PrefetchScalarGridSpec(
            num_scalar_prefetch=1,
            grid=(z.part_blocks,),
            in_specs=[pl.BlockSpec((z.block, z.hidden), lambda i, r: (i, 0))] * m
            + [
                pl.BlockSpec((z.block, z.pair), lambda i, r: (r[1] * z.part_blocks + i, 0)),
                whole(code_shape),
            ],
            out_specs=[
                pl.BlockSpec((n, z.cols, z.block), lambda i, r: (0, 0, i)),
                pl.BlockSpec((z.block, z.hidden), lambda i, r: (i, 0)),
            ],
        ),
        out_shape=[
            jax.ShapeDtypeStruct((n, z.cols, z.part), BF),
            jax.ShapeDtypeStruct((z.part, z.hidden), BF),
        ],
        compiler_params=params(16),
        name="pre_grads",
    )(ids, *parts, pair_rows, codes)

    grad_parts = spread_over(grad_part, "sub", m)
    columns = lax.all_to_all(pre, "ep", split_axis=0, concat_axis=0, tiled=True)
    columns, *inputs[1:] = lax.optimization_barrier((columns, *inputs[1:]))
    gathered += [lax.all_gather(a, "ep") for a in inputs[1:]]
    sides = spread_over(columns, "sub", m)

    mark_rows = -(-z.local // 16) * 16
    back_shape = (n, z.tokens + mark_rows, z.width)
    back = pl.pallas_call(
        functools.partial(row_kernel, z),
        grid_spec=pltpu.PrefetchScalarGridSpec(
            num_scalar_prefetch=1,
            grid=(z.blocks,),
            in_specs=[whole((z.part, z.hidden))] * m
            + [
                pl.BlockSpec((z.block, z.pair), lambda i, r: (row_block(i, r), 0)),
                pl.BlockSpec((1, z.pair, z.width), lambda i, r: (row_slot(i, r), 0, 0)),
                whole(code_shape),
            ],
            out_specs=whole(back_shape),
            scratch_shapes=[
                pltpu.VMEM((z.local, z.rows, z.width), BF),
                pltpu.VMEM((n, mark_rows, z.tokens), F32),
                pltpu.VMEM((z.block, z.hidden), BF),
            ],
        ),
        out_shape=jax.ShapeDtypeStruct(back_shape, BF),
        compiler_params=params(24),
        name="row_grads",
    )(ids, *grad_parts, pair_rows, weight_in, codes)
    got = [back[0]] + [swap(back[k], "ep", n, k) for k in range(1, n)]

    grad_tokens, grad_routes = pl.pallas_call(
        functools.partial(token_kernel, z),
        out_shape=[
            jax.ShapeDtypeStruct((z.tokens, z.width), BF),
            jax.ShapeDtypeStruct((z.top, z.tokens), BF),
        ],
        in_specs=[smem(), smem()]
        + [whole(back_shape[1:])] * n
        + [whole(a.shape) for a in (routes, replica, table)],
        out_specs=[whole((z.tokens, z.width)), whole((z.top, z.tokens))],
        grid=(1,),
        scratch_shapes=[pltpu.VMEM((n, mark_rows, z.tokens), F32)],
        compiler_params=params(8),
        name="token_grads",
    )(ids, token_count, *got, routes, replica, table)

    in_shape = jax.ShapeDtypeStruct((z.experts, z.in_cols, z.width), BF)
    down_shape = jax.ShapeDtypeStruct((z.experts, z.down_cols, z.width), BF)
    grad_in, grad_down = None, None
    for c in range(CUTS):
        first = c == 0
        in_spec = pl.BlockSpec((1, z.in_cols, chunk), lambda e, r, t, c=c: (e, 0, c))
        down_spec = pl.BlockSpec((1, z.down_cols, z.width), lambda e, r, t: (e, 0, 0))
        out = pl.pallas_call(
            functools.partial(total_kernel, z, first),
            grid_spec=pltpu.PrefetchScalarGridSpec(
                num_scalar_prefetch=2,
                grid=(z.experts,),
                in_specs=[pl.BlockSpec(memory_space=pl.ANY)] * m
                + [
                    whole((n, z.all_rows, chunk)),
                    whole((n, z.tokens, z.width)),
                    whole(code_shape),
                ]
                + ([] if first else [pl.BlockSpec(memory_space=pl.ANY)]),
                out_specs=[in_spec, down_spec] if first else [in_spec],
                scratch_shapes=[
                    pltpu.VMEM((m, n, z.cols, z.part), BF),
                    pltpu.SemaphoreType.DMA((m,)),
                ],
            ),
            out_shape=[in_shape, down_shape] if first else [in_shape],
            input_output_aliases={} if first else {2 + m + 3: 0},
            compiler_params=params(24),
            name="weight_grads",
        )(
            ids,
            table,
            *sides,
            gathered[c],
            grads_all,
            codes,
            *([] if first else [grad_in]),
        )
        grad_in = out[0]
        if first:
            grad_down = out[1]
    return grad_tokens, grad_routes.T, grad_in, grad_down


def solution(mesh):
    return jax.shard_map(
        body,
        mesh=mesh,
        in_specs=(
            P(("groups", "ep"), "sub"),
            P(("groups", "ep"), None),
            P(("groups", "ep"), None),
            P(("groups", "ep"), None),
            P("groups", None),
            P(("groups", "ep")),
            P(("groups", "ep"), None, None, "sub"),
            P(("groups", "ep"), None, None),
            P(("groups", "ep"), None, "sub"),
            P(("groups", "ep"), None, "sub"),
        ),
        out_specs=(
            P(("groups", "ep"), "sub"),
            P(("groups", "ep"), None),
            P("groups", "ep", "sub"),
            P("groups", "ep", "sub"),
        ),
        check_vma=False,
    )
```

```python
import functools
import math

import jax
import jax.numpy as jnp
from jax import lax
from jax.experimental import pallas as pl
from jax.experimental.pallas import tpu as pltpu
from jax.sharding import PartitionSpec as P

BF = jnp.bfloat16
F32 = jnp.float32
CUTS = 2
GROUPS = 2


def nt(a, b):
    return lax.dot_general(a, b, (((1,), (1,)), ((), ())), preferred_element_type=F32)


def tn(a, b):
    return lax.dot_general(a, b, (((0,), (0,)), ((), ())), preferred_element_type=F32)


def nn(a, b):
    return jnp.dot(a, b, preferred_element_type=F32)


def whole(shape):
    zeros = (0,) * len(shape)
    return pl.BlockSpec(shape, lambda *_: zeros)


def smem():
    return pl.BlockSpec(memory_space=pltpu.SMEM)


def params(mib):
    return pltpu.CompilerParams(
        vmem_limit_bytes=mib * 1024 * 1024, dimension_semantics=("arbitrary",)
    )


def cost(micros):
    return pl.CostEstimate(
        flops=int(micros * 1.1e9), bytes_accessed=int(micros * 3.6e6), transcendentals=0
    )


class Sizes:
    def __init__(self, grad_out, routes, replica_slot, saved_input, weight_in, weight_down):
        self.ep = lax.axis_size("ep")
        self.sub = lax.axis_size("sub")
        self.tokens, self.width = grad_out.shape
        self.top = routes.shape[1]
        self.experts, self.reps = replica_slot.shape
        self.local = weight_in.shape[0]
        self.slots = self.ep * self.local
        self.cap = saved_input.shape[2]
        self.rows = self.ep * self.cap
        self.hidden = weight_down.shape[1]
        self.pair = weight_in.shape[1]
        self.all_rows = self.local * self.rows
        self.part = self.all_rows // self.sub
        self.block = math.gcd(self.rows, self.part)
        self.sources = self.block // self.cap
        self.blocks = self.all_rows // self.block
        self.part_blocks = self.part // self.block
        self.slot_blocks = self.rows // self.block
        self.in_cols = self.pair // self.ep
        self.down_cols = self.hidden // self.ep
        self.cols = self.in_cols + self.down_cols
        self.folds = self.width // self.tokens
        self.tail = 2 * self.slots // self.folds


def slot_table(z, table_ref, r):
    ids = lax.broadcasted_iota(jnp.int32, (z.slots, z.experts), 0)
    return (table_ref[r : r + 1, :] == ids).astype(F32).astype(BF)


def key_hits(z, count_ref, routes_ref, replica_ref, r, k):
    ids = lax.broadcasted_iota(jnp.int32, (z.experts, z.tokens), 0)
    live = lax.broadcasted_iota(jnp.int32, (1, z.tokens), 1) < count_ref[0]
    key = jnp.where(live & (replica_ref[k : k + 1, :] == r), routes_ref[k : k + 1, :], -1)
    return key == ids


def route_kernel(z, count_ref, grad_ref, weight_ref, routes_ref, replica_ref, table_ref, out_ref):
    weights = weight_ref[...].astype(F32)
    hits = jnp.zeros((z.slots, z.tokens), F32)
    loads = jnp.zeros((z.slots, z.tokens), F32)
    for r in range(z.reps):
        hit = jnp.zeros((z.experts, z.tokens), F32)
        load = jnp.zeros((z.experts, z.tokens), F32)
        for k in range(z.top):
            same = key_hits(z, count_ref, routes_ref, replica_ref, r, k)
            hit = jnp.where(same, 1.0, hit)
            load = jnp.where(same, weights[k : k + 1, :], load)
        table = slot_table(z, table_ref, r)
        hits = hits + nn(table, hit.astype(BF))
        loads = loads + nn(table, load.astype(BF))
    before = lax.broadcasted_iota(jnp.int32, (z.tokens, z.tokens), 0)
    after = lax.broadcasted_iota(jnp.int32, (z.tokens, z.tokens), 1)
    earlier = nn(hits.astype(BF), (before < after).astype(F32).astype(BF))
    code = jnp.where(hits > 0.5, earlier, -1.0)
    both = jnp.concatenate([code, loads], axis=0).astype(BF)
    out_ref[: z.tokens, :] = grad_ref[...]
    for b in range(z.folds):
        out_ref[z.tokens :, b * z.tokens : (b + 1) * z.tokens] = both[
            b * z.tail : (b + 1) * z.tail, :
        ]


def block_place(z, block):
    slot = block // z.slot_blocks
    first = (block % z.slot_blocks) * z.sources
    return slot, first


def block_picks(z, codes_ref, slot, first):
    rows = lax.broadcasted_iota(jnp.int32, (z.cap, z.tokens), 0).astype(F32)
    for a in range(z.sources):
        code = codes_ref[first + a, pl.ds(slot, 1), :]
        yield a, rows == code


def block_scale(z, codes_ref, slot, first):
    parts = []
    for a, pick in block_picks(z, codes_ref, slot, first):
        load = codes_ref[first + a, pl.ds(z.slots + slot, 1), :]
        parts.append(jnp.sum(jnp.where(pick, load, 0.0), axis=1, keepdims=True))
    return jnp.concatenate(parts, axis=0)


def scaled_rows(z, codes_ref, grads_ref, slot, first):
    parts = []
    for a, pick in block_picks(z, codes_ref, slot, first):
        load = codes_ref[first + a, pl.ds(z.slots + slot, 1), :]
        parts.append(nn(jnp.where(pick, load, 0.0).astype(BF), grads_ref[first + a]))
    return jnp.concatenate(parts, axis=0).astype(BF)


def local_picks(z, codes_ref, source, me):
    code = codes_ref[source, pl.ds(pl.multiple_of(me * z.local, z.local), z.local), :]
    rows = lax.broadcasted_iota(jnp.int32, (z.local, z.cap, z.tokens), 1).astype(F32)
    pick = (code[:, None, :] == rows).astype(F32)
    return pick.reshape(z.local * z.cap, z.tokens).astype(BF)


def down_kernel(z, ids_ref, *refs):
    bufs = refs[: z.ep]
    weight_ref = refs[z.ep]
    parts = refs[z.ep + 1 : z.ep + 1 + z.sub]
    grads_ref, codes_ref, rows_ref = refs[z.ep + 1 + z.sub :]
    me, mine = ids_ref[0], ids_ref[1]
    step = pl.program_id(0)

    @pl.when(step == 0)
    def _():
        for k in range(z.ep):
            source = me ^ k
            grads_ref[source] = bufs[k][: z.tokens, :]
            for b in range(z.folds):
                codes_ref[source, b * z.tail : (b + 1) * z.tail, :] = bufs[k][
                    z.tokens :, b * z.tokens : (b + 1) * z.tokens
                ].astype(F32)
        for p in range(z.ep):
            rows = nn(local_picks(z, codes_ref, p, me), grads_ref[p]).astype(BF)
            rows_ref[:, p * z.cap : (p + 1) * z.cap, :] = rows.reshape(z.local, z.cap, z.width)

    place = step // z.part_blocks
    block = (place ^ mine) * z.part_blocks + step % z.part_blocks
    slot, first = block_place(z, block)
    start = pl.multiple_of(first * z.cap, z.block)
    partial = nt(rows_ref[slot, pl.ds(start, z.block), :], weight_ref[0]).astype(BF)
    spot = pl.multiple_of((step % z.part_blocks) * z.block, z.block)
    for k in range(z.sub):

        @pl.when(place == k)
        def _():
            parts[k][pl.ds(spot, z.block), :] = partial


def gate_terms(z, pair, grad, scale):
    gate = pair[:, : z.hidden].astype(F32)
    up = pair[:, z.hidden :].astype(F32)
    sig = 1.0 / (1.0 + jnp.exp(-gate))
    act = gate * sig
    hidden = act * up
    scaled = scale * grad
    grad_gate = scaled * up * sig * (1.0 + gate * (1.0 - sig))
    grad_up = scaled * act
    return hidden, grad_gate.astype(BF), grad_up.astype(BF)


def pre_kernel(z, ids_ref, *refs):
    parts = refs[: z.sub]
    pair_ref, codes_ref = refs[z.sub : z.sub + 2]
    outs = refs[z.sub + 2 : z.sub + 2 + z.ep]
    grad_ref, sides = refs[z.sub + 2 + z.ep :]
    me = ids_ref[0]
    block = ids_ref[1] * z.part_blocks + pl.program_id(0)
    slot, first = block_place(z, block)
    scale = block_scale(z, codes_ref, me * z.local + slot, first)
    grad = parts[0][...].astype(F32)
    for k in range(1, z.sub):
        grad = grad + parts[k][...].astype(F32)
    grad_ref[...] = grad.astype(BF)
    hidden, grad_gate, grad_up = gate_terms(z, pair_ref[...], grad, scale)
    hidden = hidden.astype(BF).T
    pre = jnp.concatenate([grad_gate.T, grad_up.T], axis=0)
    for q in range(z.ep):
        sides[q, : z.in_cols, :] = pre[q * z.in_cols : (q + 1) * z.in_cols, :]
        sides[q, z.in_cols :, :] = hidden[q * z.down_cols : (q + 1) * z.down_cols, :]
    for k in range(z.ep):
        outs[k][...] = sides[me ^ k]


def stack_kernel(count, extra, *refs):
    ins, outs = refs[: count + extra], refs[count + extra :]
    for i in range(count):
        outs[0][i] = ins[i][...]
    for i, out in enumerate(outs[1:]):
        out[...] = ins[count + i][...]


def row_kernel(z, ids_ref, *refs):
    grads = refs[: z.sub]
    pair_ref, weight_ref, codes_ref, out_ref, rows_ref, marks, held = refs[z.sub :]
    me, mine = ids_ref[0], ids_ref[1]
    step = pl.program_id(0)
    place = step // z.part_blocks
    block = (place ^ mine) * z.part_blocks + step % z.part_blocks
    slot, first = block_place(z, block)

    @pl.when(step == 0)
    def _():
        marks[...] = jnp.zeros_like(marks)

    spot = pl.multiple_of((step % z.part_blocks) * z.block, z.block)
    for k in range(z.sub):

        @pl.when(place == k)
        def _():
            held[...] = grads[k][pl.ds(spot, z.block), :]

    grad = held[...].astype(F32)
    scale = block_scale(z, codes_ref, me * z.local + slot, first)
    hidden, grad_gate, grad_up = gate_terms(z, pair_ref[...], grad, scale)
    route = jnp.sum(hidden * grad, axis=1, keepdims=True).astype(BF).astype(F32)
    rows = nn(grad_gate, weight_ref[0, : z.hidden, :]) + nn(grad_up, weight_ref[0, z.hidden :, :])
    start = pl.multiple_of(first * z.cap, z.block)
    rows_ref[slot, pl.ds(start, z.block), :] = rows.astype(BF)
    for a, pick in block_picks(z, codes_ref, me * z.local + slot, first):
        marks[first + a, pl.ds(slot, 1), :] = jnp.sum(
            jnp.where(pick, route[a * z.cap : (a + 1) * z.cap, :], 0.0), axis=0, keepdims=True
        )

    @pl.when(step == z.blocks - 1)
    def _():
        for p in range(z.ep):
            rows = rows_ref[:, p * z.cap : (p + 1) * z.cap, :].reshape(z.local * z.cap, z.width)
            out_ref[p ^ me, : z.tokens, :] = tn(local_picks(z, codes_ref, p, me), rows).astype(BF)
            out_ref[p ^ me, z.tokens :, : z.tokens] = marks[p].astype(BF)
            out_ref[p ^ me, z.tokens :, z.tokens :] = jnp.zeros(
                (marks.shape[1], z.width - z.tokens), BF
            )


def token_kernel(z, ids_ref, count_ref, *refs):
    got = refs[: z.ep]
    routes_ref, replica_ref, table_ref, tokens_ref, route_ref, marks = refs[z.ep :]
    me = ids_ref[0]
    total = got[0][: z.tokens, :].astype(F32)
    for k in range(1, z.ep):
        total = total + got[k][: z.tokens, :].astype(F32)
    tokens_ref[...] = total.astype(BF)
    for k in range(z.ep):
        marks[me ^ k] = got[k][z.tokens :, : z.tokens].astype(F32)
    rows = jnp.concatenate([marks[p][: z.local, :] for p in range(z.ep)], axis=0).astype(BF)
    totals = [jnp.zeros((1, z.tokens), F32)] * z.top
    for r in range(z.reps):
        spread = tn(slot_table(z, table_ref, r), rows)
        for k in range(z.top):
            same = key_hits(z, count_ref, routes_ref, replica_ref, r, k)
            totals[k] += jnp.sum(jnp.where(same, spread, 0.0), axis=0, keepdims=True)
    route_ref[...] = jnp.concatenate(totals, axis=0).astype(BF)


def total_kernel(z, down, groups, ids_ref, table_ref, *refs):
    sides, refs = refs[: groups * z.sub], refs[groups * z.sub :]
    own_ref, rights, lefts = refs[0], refs[1 : z.ep], refs[z.ep : 2 * z.ep - 1]
    grads_ref, codes_ref = refs[2 * z.ep - 1 : 2 * z.ep + 1]
    refs = refs[2 * z.ep + 1 :]
    if down:
        in_ref, down_ref, held, inputs_ref, sems, own_sem, right_sems, left_sems = refs
    else:
        in_ref, held, inputs_ref, sems, own_sem, right_sems, left_sems = refs[1:]
    me, mine = ids_ref[0], ids_ref[1]
    expert = pl.program_id(0)
    size = z.ep // groups

    def moves(act):
        for g in range(groups):
            for k in range(z.sub):
                act(
                    pltpu.make_async_copy(
                        sides[g * z.sub + k],
                        held.at[k, pl.ds(g * size, size)],
                        sems.at[g * z.sub + k],
                    )
                )
        act(pltpu.make_async_copy(own_ref, inputs_ref.at[me], own_sem))
        for d in range(1, z.ep):

            @pl.when(me >= d)
            def _():
                act(
                    pltpu.make_async_copy(
                        rights[d - 1], inputs_ref.at[me - d], right_sems.at[d - 1]
                    )
                )

            @pl.when(me + d < z.ep)
            def _():
                act(
                    pltpu.make_async_copy(
                        lefts[d - 1], inputs_ref.at[me + d], left_sems.at[d - 1]
                    )
                )

    @pl.when(expert == 0)
    def _():
        moves(lambda copy: copy.start())
        moves(lambda copy: copy.wait())

    slot_ids = [table_ref[r, expert] for r in range(z.reps)]
    count = 1
    for r in range(1, z.reps):
        count = count + (slot_ids[r] != slot_ids[0]).astype(jnp.int32)

    def add(used):
        left_parts, right_parts, rows = [], [], []
        for slot_id in used:
            source = slot_id // z.local
            for b in range(z.slot_blocks):
                block = (slot_id % z.local) * z.slot_blocks + b
                part = (block // z.part_blocks) ^ mine
                spot = pl.multiple_of((block % z.part_blocks) * z.block, z.block)
                left_parts.append(held[part, source ^ me, :, pl.ds(spot, z.block)])
                start = pl.multiple_of(block * z.block, z.block)
                right_parts.append(inputs_ref[source, pl.ds(start, z.block), :])
                if down:
                    rows.append(scaled_rows(z, codes_ref, grads_ref, slot_id, b * z.sources))
        left = jnp.concatenate(left_parts, axis=1)
        in_ref[0] = nn(left[: z.in_cols, :], jnp.concatenate(right_parts, axis=0)).astype(BF)
        if down:
            down_ref[0] = nn(left[z.in_cols :, :], jnp.concatenate(rows, axis=0)).astype(BF)

    for c in range(1, z.reps + 1):

        @pl.when(count == c)
        def _():
            add(slot_ids[:c])


def swap(x, axis, size, bit):
    return lax.ppermute(x, axis, [(i, i ^ bit) for i in range(size)])


def spread_over(x, axis, size):
    have = {0: x}
    bit = size // 2
    while bit:
        for k in list(have):
            have[k | bit] = swap(have[k], axis, size, bit)
        bit //= 2
    return [have[k] for k in range(size)]


def chain_gather(x, axis, size):
    rights, lefts = [], []
    go, back = x, x
    for d in range(1, size):
        go = lax.ppermute(go, axis, [(i, i + 1) for i in range(d - 1, size - 1)])
        back = lax.ppermute(back, axis, [(i, i - 1) for i in range(size - d, 0, -1)])
        rights.append(go)
        lefts.append(back)
    return [x] + rights + lefts


def body(
    grad_out,
    route_weight,
    routes,
    replica,
    replica_slot,
    token_count,
    saved_input,
    saved_gate_up,
    weight_in,
    weight_down,
):
    z = Sizes(grad_out, routes, replica_slot, saved_input, weight_in, weight_down)
    n, m = z.ep, z.sub
    ids = jnp.stack([lax.axis_index("ep"), lax.axis_index("sub")]).astype(jnp.int32)
    routes, replica, table = routes.T, replica.T, replica_slot.T
    route_weight = route_weight.T
    pair_rows = saved_gate_up.reshape(z.all_rows, z.pair)
    grad_shape = (z.tokens + z.tail, z.width)
    code_shape = (n, 2 * z.slots, z.tokens)
    chunk = z.width // CUTS
    inputs = saved_input.reshape(z.all_rows, z.width)
    gathered = [chain_gather(inputs[:, :chunk], "ep", n)]

    buf = pl.pallas_call(
        functools.partial(route_kernel, z),
        out_shape=jax.ShapeDtypeStruct(grad_shape, BF),
        in_specs=[smem()]
        + [whole(a.shape) for a in (grad_out, route_weight, routes, replica, table)],
        out_specs=whole(grad_shape),
        grid=(1,),
        compiler_params=params(60),
        cost_estimate=cost(1),
        name="route",
    )(token_count, grad_out, route_weight, routes, replica, table)
    bufs = [buf] + [swap(buf, "ep", n, k) for k in range(1, n)]

    def row_block(i, ids_ref):
        place = i // z.part_blocks
        return (place ^ ids_ref[1]) * z.part_blocks + i % z.part_blocks

    def row_slot(i, ids_ref):
        return row_block(i, ids_ref) // z.slot_blocks

    outs = pl.pallas_call(
        functools.partial(down_kernel, z),
        grid_spec=pltpu.PrefetchScalarGridSpec(
            num_scalar_prefetch=1,
            grid=(z.blocks,),
            in_specs=[whole(grad_shape)] * n
            + [pl.BlockSpec((1, z.hidden, z.width), lambda i, r: (row_slot(i, r), 0, 0))],
            out_specs=[whole((z.part, z.hidden))] * m
            + [whole((n, z.tokens, z.width)), whole(code_shape)],
            scratch_shapes=[pltpu.VMEM((z.local, z.rows, z.width), BF)],
        ),
        out_shape=[jax.ShapeDtypeStruct((z.part, z.hidden), BF)] * m
        + [
            jax.ShapeDtypeStruct((n, z.tokens, z.width), BF),
            jax.ShapeDtypeStruct(code_shape, F32),
        ],
        compiler_params=params(56),
        cost_estimate=cost(6),
        name="hidden_partials",
    )(ids, *bufs, weight_down)
    parts, (grads_all, codes) = outs[:m], outs[m:]
    parts = [parts[0]] + [swap(parts[k], "sub", m, k) for k in range(1, m)]

    outs = pl.pallas_call(
        functools.partial(pre_kernel, z),
        grid_spec=pltpu.PrefetchScalarGridSpec(
            num_scalar_prefetch=1,
            grid=(z.part_blocks,),
            in_specs=[pl.BlockSpec((z.block, z.hidden), lambda i, r: (i, 0))] * m
            + [
                pl.BlockSpec((z.block, z.pair), lambda i, r: (r[1] * z.part_blocks + i, 0)),
                whole(code_shape),
            ],
            out_specs=[
                pl.BlockSpec((z.cols, z.block), lambda i, r: (0, i))
            ]
            * n
            + [pl.BlockSpec((z.block, z.hidden), lambda i, r: (i, 0))],
            scratch_shapes=[pltpu.VMEM((n, z.cols, z.block), BF)],
        ),
        out_shape=[jax.ShapeDtypeStruct((z.cols, z.part), BF)] * n
        + [jax.ShapeDtypeStruct((z.part, z.hidden), BF)],
        compiler_params=params(16),
        cost_estimate=cost(2),
        name="pre_grads",
    )(ids, *parts, pair_rows, codes)

    pieces, grad_part = outs[:n], outs[n]
    pieces = [pieces[0]] + [swap(pieces[k], "ep", n, k) for k in range(1, n)]
    grad_parts = spread_over(grad_part, "sub", m)
    size = n // GROUPS
    sides = []
    for g in range(GROUPS):
        extra = CUTS - 1 if g == GROUPS - 1 else 0
        outs = pl.pallas_call(
            functools.partial(stack_kernel, size, extra),
            in_specs=[whole((z.cols, z.part))] * size
            + [
                pl.BlockSpec((z.all_rows, chunk), lambda i, c=c: (0, c + 1))
                for c in range(extra)
            ],
            out_specs=[whole((size, z.cols, z.part))] + [whole((z.all_rows, chunk))] * extra,
            out_shape=[jax.ShapeDtypeStruct((size, z.cols, z.part), BF)]
            + [jax.ShapeDtypeStruct((z.all_rows, chunk), BF)] * extra,
            grid=(1,),
            compiler_params=params(16),
            cost_estimate=cost(1),
            name="stack_columns",
        )(*pieces[g * size : (g + 1) * size], *[inputs] * extra)
        sides += spread_over(outs[0], "sub", m)
        gathered += [chain_gather(a, "ep", n) for a in outs[1:]]

    mark_rows = -(-z.local // 16) * 16
    back_shape = (n, z.tokens + mark_rows, z.width)
    back = pl.pallas_call(
        functools.partial(row_kernel, z),
        grid_spec=pltpu.PrefetchScalarGridSpec(
            num_scalar_prefetch=1,
            grid=(z.blocks,),
            in_specs=[whole((z.part, z.hidden))] * m
            + [
                pl.BlockSpec((z.block, z.pair), lambda i, r: (row_block(i, r), 0)),
                pl.BlockSpec((1, z.pair, z.width), lambda i, r: (row_slot(i, r), 0, 0)),
                whole(code_shape),
            ],
            out_specs=whole(back_shape),
            scratch_shapes=[
                pltpu.VMEM((z.local, z.rows, z.width), BF),
                pltpu.VMEM((n, mark_rows, z.tokens), F32),
                pltpu.VMEM((z.block, z.hidden), BF),
            ],
        ),
        out_shape=jax.ShapeDtypeStruct(back_shape, BF),
        compiler_params=params(54),
        cost_estimate=cost(7),
        name="row_grads",
    )(ids, *grad_parts, pair_rows, weight_in, codes)
    got = [back[0]] + [swap(back[k], "ep", n, k) for k in range(1, n)]

    grad_tokens, grad_routes = pl.pallas_call(
        functools.partial(token_kernel, z),
        out_shape=[
            jax.ShapeDtypeStruct((z.tokens, z.width), BF),
            jax.ShapeDtypeStruct((z.top, z.tokens), BF),
        ],
        in_specs=[smem(), smem()]
        + [whole(back_shape[1:])] * n
        + [whole(a.shape) for a in (routes, replica, table)],
        out_specs=[whole((z.tokens, z.width)), whole((z.top, z.tokens))],
        grid=(1,),
        scratch_shapes=[pltpu.VMEM((n, mark_rows, z.tokens), F32)],
        compiler_params=params(60),
        cost_estimate=cost(2),
        name="token_grads",
    )(ids, token_count, *got, routes, replica, table)

    in_shape = jax.ShapeDtypeStruct((z.experts, z.in_cols, z.width), BF)
    down_shape = jax.ShapeDtypeStruct((z.experts, z.down_cols, z.width), BF)
    grad_in, grad_down = None, None
    for c in range(CUTS):
        first = c == 0
        in_spec = pl.BlockSpec((1, z.in_cols, chunk), lambda e, r, t, c=c: (e, 0, c))
        down_spec = pl.BlockSpec((1, z.down_cols, z.width), lambda e, r, t: (e, 0, 0))
        out = pl.pallas_call(
            functools.partial(total_kernel, z, first, GROUPS),
            grid_spec=pltpu.PrefetchScalarGridSpec(
                num_scalar_prefetch=2,
                grid=(z.experts,),
                in_specs=[pl.BlockSpec(memory_space=pl.ANY)] * (GROUPS * m + 2 * n - 1)
                + [whole((n, z.tokens, z.width)), whole(code_shape)]
                + ([] if first else [pl.BlockSpec(memory_space=pl.ANY)]),
                out_specs=[in_spec, down_spec] if first else [in_spec],
                scratch_shapes=[
                    pltpu.VMEM((m, n, z.cols, z.part), BF),
                    pltpu.VMEM((n, z.all_rows, chunk), BF),
                    pltpu.SemaphoreType.DMA((GROUPS * m,)),
                    pltpu.SemaphoreType.DMA,
                    pltpu.SemaphoreType.DMA((n - 1,)),
                    pltpu.SemaphoreType.DMA((n - 1,)),
                ],
            ),
            out_shape=[in_shape, down_shape] if first else [in_shape],
            input_output_aliases={} if first else {2 + GROUPS * m + 2 * n + 1: 0},
            compiler_params=params(32),
            cost_estimate=cost(12 if first else 8),
            name="weight_grads",
        )(
            ids,
            table,
            *sides,
            *gathered[c],
            grads_all,
            codes,
            *([] if first else [grad_in]),
        )
        grad_in = out[0]
        if first:
            grad_down = out[1]
    return grad_tokens, grad_routes.T, grad_in, grad_down


def solution(mesh):
    return jax.shard_map(
        body,
        mesh=mesh,
        in_specs=(
            P(("groups", "ep"), "sub"),
            P(("groups", "ep"), None),
            P(("groups", "ep"), None),
            P(("groups", "ep"), None),
            P("groups", None),
            P(("groups", "ep")),
            P(("groups", "ep"), None, None, "sub"),
            P(("groups", "ep"), None, None),
            P(("groups", "ep"), None, "sub"),
            P(("groups", "ep"), None, "sub"),
        ),
        out_specs=(
            P(("groups", "ep"), "sub"),
            P(("groups", "ep"), None),
            P("groups", "ep", "sub"),
            P("groups", "ep", "sub"),
        ),
        check_vma=False,
    )
```

```python
import functools
import math

import jax
import jax.numpy as jnp
from jax import lax
from jax.experimental import pallas as pl
from jax.experimental.pallas import tpu as pltpu
from jax.sharding import PartitionSpec as P

BF = jnp.bfloat16
F32 = jnp.float32
GROUPS = 2
PER = 2


def nt(a, b):
    return lax.dot_general(a, b, (((1,), (1,)), ((), ())), preferred_element_type=F32)


def tn(a, b):
    return lax.dot_general(a, b, (((0,), (0,)), ((), ())), preferred_element_type=F32)


def nn(a, b):
    return jnp.dot(a, b, preferred_element_type=F32)


def whole(shape):
    zeros = (0,) * len(shape)
    return pl.BlockSpec(shape, lambda *_: zeros)


def smem():
    return pl.BlockSpec(memory_space=pltpu.SMEM)


def params(mib):
    return pltpu.CompilerParams(
        vmem_limit_bytes=mib * 1024 * 1024, dimension_semantics=("arbitrary",)
    )


class Sizes:
    def __init__(self, grad_out, routes, replica_slot, saved_input, weight_in, weight_down):
        self.ep = lax.axis_size("ep")
        self.sub = lax.axis_size("sub")
        self.tokens, self.width = grad_out.shape
        self.top = routes.shape[1]
        self.experts, self.reps = replica_slot.shape
        self.local = weight_in.shape[0]
        self.slots = self.ep * self.local
        self.cap = saved_input.shape[2]
        self.rows = self.ep * self.cap
        self.hidden = weight_down.shape[1]
        self.pair = weight_in.shape[1]
        self.all_rows = self.local * self.rows
        self.part = self.all_rows // self.sub
        self.block = math.gcd(self.rows, self.part)
        self.sources = self.block // self.cap
        self.blocks = self.all_rows // self.block
        self.part_blocks = self.part // self.block
        self.slot_blocks = self.rows // self.block
        self.in_cols = self.pair // self.ep
        self.down_cols = self.hidden // self.ep
        self.cols = self.in_cols + self.down_cols
        self.folds = self.width // self.tokens
        self.tail = 2 * self.slots // self.folds
        self.side_folds = self.width // self.part
        self.side_rows = self.down_cols // self.side_folds
        self.side_start = self.tokens + self.tail


def slot_table(z, table_ref, r):
    ids = lax.broadcasted_iota(jnp.int32, (z.slots, z.experts), 0)
    return (table_ref[r : r + 1, :] == ids).astype(F32).astype(BF)


def key_hits(z, count_ref, routes_ref, replica_ref, r, k):
    ids = lax.broadcasted_iota(jnp.int32, (z.experts, z.tokens), 0)
    live = lax.broadcasted_iota(jnp.int32, (1, z.tokens), 1) < count_ref[0]
    key = jnp.where(live & (replica_ref[k : k + 1, :] == r), routes_ref[k : k + 1, :], -1)
    return key == ids


def route_kernel(z, ids_ref, count_ref, *refs):
    grad_ref, weight_ref, routes_ref, replica_ref, table_ref, pair_ref = refs[:6]
    outs, sides = refs[6:-1], refs[-1]
    weights = weight_ref[...].astype(F32)
    hits = jnp.zeros((z.slots, z.tokens), F32)
    loads = jnp.zeros((z.slots, z.tokens), F32)
    for r in range(z.reps):
        hit = jnp.zeros((z.experts, z.tokens), F32)
        load = jnp.zeros((z.experts, z.tokens), F32)
        for k in range(z.top):
            same = key_hits(z, count_ref, routes_ref, replica_ref, r, k)
            hit = jnp.where(same, 1.0, hit)
            load = jnp.where(same, weights[k : k + 1, :], load)
        table = slot_table(z, table_ref, r)
        hits = hits + nn(table, hit.astype(BF))
        loads = loads + nn(table, load.astype(BF))
    before = lax.broadcasted_iota(jnp.int32, (z.tokens, z.tokens), 0)
    after = lax.broadcasted_iota(jnp.int32, (z.tokens, z.tokens), 1)
    earlier = nn(hits.astype(BF), (before < after).astype(F32).astype(BF))
    code = jnp.where(hits > 0.5, earlier, -1.0)
    both = jnp.concatenate([code, loads], axis=0).astype(BF)
    pair = pair_ref[...]
    gate = pair[:, : z.hidden].astype(F32)
    up = pair[:, z.hidden :].astype(F32)
    hidden = (gate * (1.0 / (1.0 + jnp.exp(-gate))) * up).astype(BF).T
    for q in range(z.ep):
        for f in range(z.side_folds):
            lo = q * z.down_cols + f * z.side_rows
            sides[q, :, f * z.part : (f + 1) * z.part] = hidden[lo : lo + z.side_rows, :]
    for k in range(z.ep):
        outs[k][: z.tokens, :] = grad_ref[...]
        for b in range(z.folds):
            outs[k][z.tokens : z.side_start, b * z.tokens : (b + 1) * z.tokens] = both[
                b * z.tail : (b + 1) * z.tail, :
            ]
        outs[k][z.side_start :, :] = sides[ids_ref[0] ^ k]


def block_place(z, block):
    slot = block // z.slot_blocks
    first = (block % z.slot_blocks) * z.sources
    return slot, first


def block_picks(z, codes_ref, slot, first):
    rows = lax.broadcasted_iota(jnp.int32, (z.cap, z.tokens), 0).astype(F32)
    for a in range(z.sources):
        code = codes_ref[first + a, pl.ds(slot, 1), :]
        yield a, rows == code


def block_scale(z, codes_ref, slot, first):
    parts = []
    for a, pick in block_picks(z, codes_ref, slot, first):
        load = codes_ref[first + a, pl.ds(z.slots + slot, 1), :]
        parts.append(jnp.sum(jnp.where(pick, load, 0.0), axis=1, keepdims=True))
    return jnp.concatenate(parts, axis=0)


def scaled_rows(z, codes_ref, grads_ref, slot, first):
    parts = []
    for a, pick in block_picks(z, codes_ref, slot, first):
        load = codes_ref[first + a, pl.ds(z.slots + slot, 1), :]
        parts.append(nn(jnp.where(pick, load, 0.0).astype(BF), grads_ref[first + a]))
    return jnp.concatenate(parts, axis=0).astype(BF)


def local_picks(z, codes_ref, source, me):
    code = codes_ref[source, pl.ds(pl.multiple_of(me * z.local, z.local), z.local), :]
    rows = lax.broadcasted_iota(jnp.int32, (z.local, z.cap, z.tokens), 1).astype(F32)
    pick = (code[:, None, :] == rows).astype(F32)
    return pick.reshape(z.local * z.cap, z.tokens).astype(BF)


def block_slot(z, mine, step):
    place = step // z.part_blocks
    return ((place ^ mine) * z.part_blocks + step % z.part_blocks) // z.slot_blocks


def weight_copy(weight_ref, held, sems, slot):
    return pltpu.make_async_copy(weight_ref.at[slot], held.at[slot], sems.at[slot])


def down_kernel(z, ids_ref, *refs):
    bufs = refs[: z.ep]
    weight_ref = refs[z.ep]
    parts = refs[z.ep + 1 : z.ep + 1 + z.sub]
    grads_ref, codes_ref, rows_ref, held, sems = refs[z.ep + 1 + z.sub :]
    me, mine = ids_ref[0], ids_ref[1]
    step = pl.program_id(0)

    @pl.when(step == 0)
    def _():
        for s in range(z.local):
            weight_copy(weight_ref, held, sems, s).start()
        for k in range(z.ep):
            source = me ^ k
            grads_ref[source] = bufs[k][: z.tokens, :]
            for b in range(z.folds):
                codes_ref[source, b * z.tail : (b + 1) * z.tail, :] = bufs[k][
                    z.tokens : z.side_start, b * z.tokens : (b + 1) * z.tokens
                ].astype(F32)
        for p in range(z.ep):
            rows = nn(local_picks(z, codes_ref, p, me), grads_ref[p]).astype(BF)
            rows_ref[:, p * z.cap : (p + 1) * z.cap, :] = rows.reshape(z.local, z.cap, z.width)

    place = step // z.part_blocks
    block = (place ^ mine) * z.part_blocks + step % z.part_blocks
    slot, first = block_place(z, block)
    start = pl.multiple_of(first * z.cap, z.block)

    @pl.when((step == 0) | (slot != block_slot(z, mine, step - 1)))
    def _():
        weight_copy(weight_ref, held, sems, slot).wait()

    partial = nt(rows_ref[slot, pl.ds(start, z.block), :], held[slot]).astype(BF)
    spot = pl.multiple_of((step % z.part_blocks) * z.block, z.block)
    for k in range(z.sub):

        @pl.when(place == k)
        def _():
            parts[k][pl.ds(spot, z.block), :] = partial


def gate_terms(z, pair, grad, scale):
    gate = pair[:, : z.hidden].astype(F32)
    up = pair[:, z.hidden :].astype(F32)
    sig = 1.0 / (1.0 + jnp.exp(-gate))
    act = gate * sig
    hidden = act * up
    scaled = scale * grad
    grad_gate = scaled * up * sig * (1.0 + gate * (1.0 - sig))
    grad_up = scaled * act
    return hidden, grad_gate.astype(BF), grad_up.astype(BF)


def pre_kernel(z, ids_ref, *refs):
    parts = refs[: z.sub]
    pair_ref, codes_ref = refs[z.sub : z.sub + 2]
    bufs, refs = refs[z.sub + 2 : z.sub + 2 + z.ep], refs[z.sub + 2 + z.ep :]
    outs = refs[: z.ep]
    grad_ref, down_ref, sides = refs[z.ep :]

    @pl.when(pl.program_id(0) == 0)
    def _():
        for k in range(z.ep):
            for f in range(z.side_folds):
                down_ref[k, f * z.side_rows : (f + 1) * z.side_rows, :] = bufs[k][
                    z.side_start :, f * z.part : (f + 1) * z.part
                ]

    me = ids_ref[0]
    block = ids_ref[1] * z.part_blocks + pl.program_id(0)
    slot, first = block_place(z, block)
    scale = block_scale(z, codes_ref, me * z.local + slot, first)
    grad = parts[0][...].astype(F32)
    for k in range(1, z.sub):
        grad = grad + parts[k][...].astype(F32)
    grad_ref[...] = grad.astype(BF)
    _, grad_gate, grad_up = gate_terms(z, pair_ref[...], grad, scale)
    pre = jnp.concatenate([grad_gate.T, grad_up.T], axis=0)
    for q in range(z.ep):
        sides[q] = pre[q * z.in_cols : (q + 1) * z.in_cols, :]
    for k in range(z.ep):
        outs[k][...] = sides[me ^ k]


def stack_kernel(*refs):
    for i, ref in enumerate(refs[:-1]):
        refs[-1][i] = ref[...]


def row_kernel(z, ids_ref, *refs):
    grads = refs[: z.sub]
    pair_ref, weight_ref, codes_ref, out_ref, rows_ref, marks, held, weights, sems = refs[z.sub :]
    me, mine = ids_ref[0], ids_ref[1]
    step = pl.program_id(0)
    place = step // z.part_blocks
    block = (place ^ mine) * z.part_blocks + step % z.part_blocks
    slot, first = block_place(z, block)

    @pl.when(step == 0)
    def _():
        for s in range(z.local):
            weight_copy(weight_ref, weights, sems, s).start()
        marks[...] = jnp.zeros_like(marks)

    spot = pl.multiple_of((step % z.part_blocks) * z.block, z.block)
    for k in range(z.sub):

        @pl.when(place == k)
        def _():
            held[...] = grads[k][pl.ds(spot, z.block), :]

    grad = held[...].astype(F32)
    scale = block_scale(z, codes_ref, me * z.local + slot, first)
    hidden, grad_gate, grad_up = gate_terms(z, pair_ref[...], grad, scale)
    route = jnp.sum(hidden * grad, axis=1, keepdims=True).astype(BF).astype(F32)

    @pl.when((step == 0) | (slot != block_slot(z, mine, step - 1)))
    def _():
        weight_copy(weight_ref, weights, sems, slot).wait()

    rows = nn(grad_gate, weights[slot, : z.hidden, :]) + nn(grad_up, weights[slot, z.hidden :, :])
    start = pl.multiple_of(first * z.cap, z.block)
    rows_ref[slot, pl.ds(start, z.block), :] = rows.astype(BF)
    for a, pick in block_picks(z, codes_ref, me * z.local + slot, first):
        marks[first + a, pl.ds(slot, 1), :] = jnp.sum(
            jnp.where(pick, route[a * z.cap : (a + 1) * z.cap, :], 0.0), axis=0, keepdims=True
        )

    @pl.when(step == z.blocks - 1)
    def _():
        for p in range(z.ep):
            rows = rows_ref[:, p * z.cap : (p + 1) * z.cap, :].reshape(z.local * z.cap, z.width)
            out_ref[p ^ me, : z.tokens, :] = tn(local_picks(z, codes_ref, p, me), rows).astype(BF)
            out_ref[p ^ me, z.tokens :, : z.tokens] = marks[p].astype(BF)
            out_ref[p ^ me, z.tokens :, z.tokens :] = jnp.zeros(
                (marks.shape[1], z.width - z.tokens), BF
            )


def token_kernel(z, ids_ref, count_ref, *refs):
    got = refs[: z.ep]
    routes_ref, replica_ref, table_ref, tokens_ref, route_ref, marks = refs[z.ep :]
    me = ids_ref[0]
    total = got[0][: z.tokens, :].astype(F32)
    for k in range(1, z.ep):
        total = total + got[k][: z.tokens, :].astype(F32)
    tokens_ref[...] = total.astype(BF)
    for k in range(z.ep):
        marks[me ^ k] = got[k][z.tokens :, : z.tokens].astype(F32)
    rows = jnp.concatenate([marks[p][: z.local, :] for p in range(z.ep)], axis=0).astype(BF)
    totals = [jnp.zeros((1, z.tokens), F32)] * z.top
    for r in range(z.reps):
        spread = tn(slot_table(z, table_ref, r), rows)
        for k in range(z.top):
            same = key_hits(z, count_ref, routes_ref, replica_ref, r, k)
            totals[k] += jnp.sum(jnp.where(same, spread, 0.0), axis=0, keepdims=True)
    route_ref[...] = jnp.concatenate(totals, axis=0).astype(BF)


def side_moves(z, groups, sides, held, sems, act):
    size = z.ep // groups
    for g in range(groups):
        for k in range(z.sub):
            i = g * z.sub + k
            act(pltpu.make_async_copy(sides[i], held.at[k, pl.ds(g * size, size)], sems.at[i]))


def input_moves(z, me, own_ref, rights, lefts, inputs_ref, own_sem, right_sems, left_sems, act):
    act(pltpu.make_async_copy(own_ref, inputs_ref.at[me], own_sem))
    for d in range(1, z.ep):

        @pl.when(me >= d)
        def _():
            act(
                pltpu.make_async_copy(
                    rights[d - 1], inputs_ref.at[me - d], right_sems.at[d - 1]
                )
            )

        @pl.when(me + d < z.ep)
        def _():
            act(
                pltpu.make_async_copy(
                    lefts[d - 1], inputs_ref.at[me + d], left_sems.at[d - 1]
                )
            )


def expert_products(z, ids_ref, table_ref, held, right_rows, out_ref):
    me, mine = ids_ref[0], ids_ref[1]

    def one(i, carry):
        expert = pl.program_id(0) * PER + i
        slot_ids = [table_ref[r, expert] for r in range(z.reps)]
        count = 1
        for r in range(1, z.reps):
            count = count + (slot_ids[r] != slot_ids[0]).astype(jnp.int32)
        for c in range(1, z.reps + 1):

            @pl.when(count == c)
            def _():
                left, right = [], []
                for slot_id in slot_ids[:c]:
                    source = slot_id // z.local
                    for b in range(z.slot_blocks):
                        block = (slot_id % z.local) * z.slot_blocks + b
                        part = (block // z.part_blocks) ^ mine
                        spot = pl.multiple_of((block % z.part_blocks) * z.block, z.block)
                        left.append(held[part, source ^ me, :, pl.ds(spot, z.block)])
                        right.append(right_rows(slot_id, b))
                left = jnp.concatenate(left, axis=1)
                out_ref[i] = nn(left, jnp.concatenate(right, axis=0)).astype(BF)

        return carry

    lax.fori_loop(0, PER, one, 0)


def total_down_kernel(z, ids_ref, table_ref, *refs):
    sides = refs[: z.sub]
    grads_ref, codes_ref, out_ref, held, sems = refs[z.sub :]

    @pl.when(pl.program_id(0) == 0)
    def _():
        side_moves(z, 1, sides, held, sems, lambda copy: copy.start())
        side_moves(z, 1, sides, held, sems, lambda copy: copy.wait())

    def right_rows(slot_id, b):
        return scaled_rows(z, codes_ref, grads_ref, slot_id, b * z.sources)

    expert_products(z, ids_ref, table_ref, held, right_rows, out_ref)


def total_in_kernel(z, ids_ref, table_ref, *refs):
    sides, refs = refs[: GROUPS * z.sub], refs[GROUPS * z.sub :]
    own_ref, rights, lefts = refs[0], refs[1 : z.ep], refs[z.ep : 2 * z.ep - 1]
    out_ref, held, inputs_ref, sems, *other_sems = refs[2 * z.ep - 1 :]

    @pl.when(pl.program_id(0) == 0)
    def _():
        def moves(act):
            side_moves(z, GROUPS, sides, held, sems, act)
            input_moves(z, ids_ref[0], own_ref, rights, lefts, inputs_ref, *other_sems, act)

        moves(lambda copy: copy.start())
        moves(lambda copy: copy.wait())

    def right_rows(slot_id, b):
        block = (slot_id % z.local) * z.slot_blocks + b
        start = pl.multiple_of(block * z.block, z.block)
        return inputs_ref[slot_id // z.local, pl.ds(start, z.block), :]

    expert_products(z, ids_ref, table_ref, held, right_rows, out_ref)


def swap(x, axis, size, bit):
    return lax.ppermute(x, axis, [(i, i ^ bit) for i in range(size)])


def spread_over(x, axis, size):
    have = {0: x}
    bit = size // 2
    while bit:
        for k in list(have):
            have[k | bit] = swap(have[k], axis, size, bit)
        bit //= 2
    return [have[k] for k in range(size)]


def chain_gather(x, axis, size):
    rights, lefts = [], []
    go, back = x, x
    for d in range(1, size):
        go = lax.ppermute(go, axis, [(i, i + 1) for i in range(d - 1, size - 1)])
        back = lax.ppermute(back, axis, [(i, i - 1) for i in range(size - d, 0, -1)])
        rights.append(go)
        lefts.append(back)
    return [x] + rights + lefts


def body(
    grad_out,
    route_weight,
    routes,
    replica,
    replica_slot,
    token_count,
    saved_input,
    saved_gate_up,
    weight_in,
    weight_down,
):
    z = Sizes(grad_out, routes, replica_slot, saved_input, weight_in, weight_down)
    n, m = z.ep, z.sub
    ids = jnp.stack([lax.axis_index("ep"), lax.axis_index("sub")]).astype(jnp.int32)
    routes, replica, table = routes.T, replica.T, replica_slot.T
    route_weight = route_weight.T
    pair_rows = saved_gate_up.reshape(z.all_rows, z.pair)
    grad_shape = (z.side_start + z.side_rows, z.width)
    code_shape = (n, 2 * z.slots, z.tokens)
    inputs = saved_input.reshape(z.all_rows, z.width)
    gathered = chain_gather(inputs, "ep", n)

    routing = (grad_out, route_weight, routes, replica, table)
    bufs = pl.pallas_call(
        functools.partial(route_kernel, z),
        grid_spec=pltpu.PrefetchScalarGridSpec(
            num_scalar_prefetch=1,
            grid=(1,),
            in_specs=[smem()]
            + [whole(a.shape) for a in routing]
            + [pl.BlockSpec((z.part, z.pair), lambda i, r: (r[1], 0))],
            out_specs=[whole(grad_shape)] * n,
            scratch_shapes=[pltpu.VMEM((n, z.side_rows, z.width), BF)],
        ),
        out_shape=[jax.ShapeDtypeStruct(grad_shape, BF)] * n,
        compiler_params=params(60),
        name="route",
    )(ids, token_count, *routing, pair_rows)
    bufs = [bufs[0]] + [swap(bufs[k], "ep", n, k) for k in range(1, n)]

    def stack(pieces):
        shape = pieces[0].shape
        return pl.pallas_call(
            stack_kernel,
            in_specs=[whole(shape)] * len(pieces),
            out_specs=whole((len(pieces),) + shape),
            out_shape=jax.ShapeDtypeStruct((len(pieces),) + shape, BF),
            grid=(1,),
            compiler_params=params(8),
            name="stack_columns",
        )(*pieces)

    def row_block(i, ids_ref):
        place = i // z.part_blocks
        return (place ^ ids_ref[1]) * z.part_blocks + i % z.part_blocks

    outs = pl.pallas_call(
        functools.partial(down_kernel, z),
        grid_spec=pltpu.PrefetchScalarGridSpec(
            num_scalar_prefetch=1,
            grid=(z.blocks,),
            in_specs=[whole(grad_shape)] * n + [pl.BlockSpec(memory_space=pltpu.HBM)],
            out_specs=[whole((z.part, z.hidden))] * m
            + [whole((n, z.tokens, z.width)), whole(code_shape)],
            scratch_shapes=[
                pltpu.VMEM((z.local, z.rows, z.width), BF),
                pltpu.VMEM((z.local, z.hidden, z.width), BF),
                pltpu.SemaphoreType.DMA((z.local,)),
            ],
        ),
        out_shape=[jax.ShapeDtypeStruct((z.part, z.hidden), BF)] * m
        + [
            jax.ShapeDtypeStruct((n, z.tokens, z.width), BF),
            jax.ShapeDtypeStruct(code_shape, F32),
        ],
        compiler_params=params(52),
        name="hidden_partials",
    )(ids, *bufs, weight_down)
    parts, (grads_all, codes) = outs[:m], outs[m:]
    parts = [parts[0]] + [swap(parts[k], "sub", m, k) for k in range(1, m)]

    outs = pl.pallas_call(
        functools.partial(pre_kernel, z),
        grid_spec=pltpu.PrefetchScalarGridSpec(
            num_scalar_prefetch=1,
            grid=(z.part_blocks,),
            in_specs=[pl.BlockSpec((z.block, z.hidden), lambda i, r: (i, 0))] * m
            + [
                pl.BlockSpec((z.block, z.pair), lambda i, r: (r[1] * z.part_blocks + i, 0)),
                whole(code_shape),
            ]
            + [whole(grad_shape)] * n,
            out_specs=[pl.BlockSpec((z.in_cols, z.block), lambda i, r: (0, i))] * n
            + [
                pl.BlockSpec((z.block, z.hidden), lambda i, r: (i, 0)),
                whole((n, z.down_cols, z.part)),
            ],
            scratch_shapes=[pltpu.VMEM((n, z.in_cols, z.block), BF)],
        ),
        out_shape=[jax.ShapeDtypeStruct((z.in_cols, z.part), BF)] * n
        + [
            jax.ShapeDtypeStruct((z.part, z.hidden), BF),
            jax.ShapeDtypeStruct((n, z.down_cols, z.part), BF),
        ],
        compiler_params=params(16),
        name="pre_grads",
    )(ids, *parts, pair_rows, codes, *bufs)
    pieces, grad_part = outs[:n], outs[n]
    pieces = [pieces[0]] + [swap(pieces[k], "ep", n, k) for k in range(1, n)]
    grad_parts = spread_over(grad_part, "sub", m)
    down_sides = spread_over(outs[n + 1], "sub", m)
    size = n // GROUPS
    sides = []
    for g in range(GROUPS):
        sides += spread_over(stack(pieces[g * size : (g + 1) * size]), "sub", m)

    mark_rows = -(-z.local // 16) * 16
    back_shape = (n, z.tokens + mark_rows, z.width)
    back = pl.pallas_call(
        functools.partial(row_kernel, z),
        grid_spec=pltpu.PrefetchScalarGridSpec(
            num_scalar_prefetch=1,
            grid=(z.blocks,),
            in_specs=[whole((z.part, z.hidden))] * m
            + [
                pl.BlockSpec((z.block, z.pair), lambda i, r: (row_block(i, r), 0)),
                pl.BlockSpec(memory_space=pltpu.HBM),
                whole(code_shape),
            ],
            out_specs=whole(back_shape),
            scratch_shapes=[
                pltpu.VMEM((z.local, z.rows, z.width), BF),
                pltpu.VMEM((n, mark_rows, z.tokens), F32),
                pltpu.VMEM((z.block, z.hidden), BF),
                pltpu.VMEM((z.local, z.pair, z.width), BF),
                pltpu.SemaphoreType.DMA((z.local,)),
            ],
        ),
        out_shape=jax.ShapeDtypeStruct(back_shape, BF),
        compiler_params=params(32),
        name="row_grads",
    )(ids, *grad_parts, pair_rows, weight_in, codes)
    got = [back[0]] + [swap(back[k], "ep", n, k) for k in range(1, n)]

    grad_tokens, grad_routes = pl.pallas_call(
        functools.partial(token_kernel, z),
        out_shape=[
            jax.ShapeDtypeStruct((z.tokens, z.width), BF),
            jax.ShapeDtypeStruct((z.top, z.tokens), BF),
        ],
        in_specs=[smem(), smem()]
        + [whole(back_shape[1:])] * n
        + [whole(a.shape) for a in (routes, replica, table)],
        out_specs=[whole((z.tokens, z.width)), whole((z.top, z.tokens))],
        grid=(1,),
        scratch_shapes=[pltpu.VMEM((n, mark_rows, z.tokens), F32)],
        compiler_params=params(16),
        name="token_grads",
    )(ids, token_count, *got, routes, replica, table)

    def total_call(kernel, operands, specs, cols, scratch, name):
        return pl.pallas_call(
            functools.partial(kernel, z),
            grid_spec=pltpu.PrefetchScalarGridSpec(
                num_scalar_prefetch=2,
                grid=(z.experts // PER,),
                in_specs=specs,
                out_specs=pl.BlockSpec((PER, cols, z.width), lambda e, r, t: (e, 0, 0)),
                scratch_shapes=[pltpu.VMEM((m, n, cols, z.part), BF)] + scratch,
            ),
            out_shape=jax.ShapeDtypeStruct((z.experts, cols, z.width), BF),
            compiler_params=params(32),
            name=name,
        )(ids, table, *operands)

    anywhere = pl.BlockSpec(memory_space=pl.ANY)
    pinned = pl.BlockSpec(memory_space=pltpu.HBM)
    grad_down = total_call(
        total_down_kernel,
        [*down_sides, grads_all, codes],
        [anywhere] * m + [whole((n, z.tokens, z.width)), whole(code_shape)],
        z.down_cols,
        [pltpu.SemaphoreType.DMA((m,))],
        "down_grads",
    )
    grad_in = total_call(
        total_in_kernel,
        [*sides, *gathered],
        [anywhere] * (GROUPS * m) + [pinned] * (2 * n - 1),
        z.in_cols,
        [
            pltpu.VMEM((n, z.all_rows, z.width), BF),
            pltpu.SemaphoreType.DMA((GROUPS * m,)),
            pltpu.SemaphoreType.DMA,
            pltpu.SemaphoreType.DMA((n - 1,)),
            pltpu.SemaphoreType.DMA((n - 1,)),
        ],
        "in_grads",
    )
    return grad_tokens, grad_routes.T, grad_in, grad_down


def solution(mesh):
    return jax.shard_map(
        body,
        mesh=mesh,
        in_specs=(
            P(("groups", "ep"), "sub"),
            P(("groups", "ep"), None),
            P(("groups", "ep"), None),
            P(("groups", "ep"), None),
            P("groups", None),
            P(("groups", "ep")),
            P(("groups", "ep"), None, None, "sub"),
            P(("groups", "ep"), None, None),
            P(("groups", "ep"), None, "sub"),
            P(("groups", "ep"), None, "sub"),
        ),
        out_specs=(
            P(("groups", "ep"), "sub"),
            P(("groups", "ep"), None),
            P("groups", "ep", "sub"),
            P("groups", "ep", "sub"),
        ),
        check_vma=False,
    )
```

```python
import functools
import math

import jax
import jax.numpy as jnp
from jax import lax
from jax.experimental import pallas as pl
from jax.experimental.pallas import tpu as pltpu
from jax.sharding import PartitionSpec as P

BF = jnp.bfloat16
F32 = jnp.float32
GROUPS = 2
PER = 2


def nt(a, b):
    return lax.dot_general(a, b, (((1,), (1,)), ((), ())), preferred_element_type=F32)


def tn(a, b):
    return lax.dot_general(a, b, (((0,), (0,)), ((), ())), preferred_element_type=F32)


def nn(a, b):
    return jnp.dot(a, b, preferred_element_type=F32)


def whole(shape):
    zeros = (0,) * len(shape)
    return pl.BlockSpec(shape, lambda *_: zeros)


def smem():
    return pl.BlockSpec(memory_space=pltpu.SMEM)


def params(mib):
    return pltpu.CompilerParams(
        vmem_limit_bytes=mib * 1024 * 1024, dimension_semantics=("arbitrary",)
    )


class Sizes:
    def __init__(self, grad_out, routes, replica_slot, saved_input, weight_in, weight_down):
        self.ep = lax.axis_size("ep")
        self.sub = lax.axis_size("sub")
        self.tokens, self.width = grad_out.shape
        self.top = routes.shape[1]
        self.experts, self.reps = replica_slot.shape
        self.local = weight_in.shape[0]
        self.slots = self.ep * self.local
        self.cap = saved_input.shape[2]
        self.rows = self.ep * self.cap
        self.hidden = weight_down.shape[1]
        self.pair = weight_in.shape[1]
        self.all_rows = self.local * self.rows
        self.part = self.all_rows // self.sub
        self.block = math.gcd(self.rows, self.part)
        self.sources = self.block // self.cap
        self.blocks = self.all_rows // self.block
        self.part_blocks = self.part // self.block
        self.slot_blocks = self.rows // self.block
        self.in_cols = self.pair // self.ep
        self.down_cols = self.hidden // self.ep
        self.cols = self.in_cols + self.down_cols
        self.folds = self.width // self.tokens
        self.tail = 2 * self.slots // self.folds


def slot_table(z, table_ref, r):
    ids = lax.broadcasted_iota(jnp.int32, (z.slots, z.experts), 0)
    return (table_ref[r : r + 1, :] == ids).astype(F32).astype(BF)


def key_hits(z, count_ref, routes_ref, replica_ref, r, k):
    ids = lax.broadcasted_iota(jnp.int32, (z.experts, z.tokens), 0)
    live = lax.broadcasted_iota(jnp.int32, (1, z.tokens), 1) < count_ref[0]
    key = jnp.where(live & (replica_ref[k : k + 1, :] == r), routes_ref[k : k + 1, :], -1)
    return key == ids


def route_kernel(z, count_ref, grad_ref, weight_ref, routes_ref, replica_ref, table_ref, out_ref):
    weights = weight_ref[...].astype(F32)
    hits = jnp.zeros((z.slots, z.tokens), F32)
    loads = jnp.zeros((z.slots, z.tokens), F32)
    for r in range(z.reps):
        hit = jnp.zeros((z.experts, z.tokens), F32)
        load = jnp.zeros((z.experts, z.tokens), F32)
        for k in range(z.top):
            same = key_hits(z, count_ref, routes_ref, replica_ref, r, k)
            hit = jnp.where(same, 1.0, hit)
            load = jnp.where(same, weights[k : k + 1, :], load)
        table = slot_table(z, table_ref, r)
        hits = hits + nn(table, hit.astype(BF))
        loads = loads + nn(table, load.astype(BF))
    before = lax.broadcasted_iota(jnp.int32, (z.tokens, z.tokens), 0)
    after = lax.broadcasted_iota(jnp.int32, (z.tokens, z.tokens), 1)
    earlier = nn(hits.astype(BF), (before < after).astype(F32).astype(BF))
    code = jnp.where(hits > 0.5, earlier, -1.0)
    both = jnp.concatenate([code, loads], axis=0).astype(BF)
    out_ref[: z.tokens, :] = grad_ref[...]
    for b in range(z.folds):
        out_ref[z.tokens :, b * z.tokens : (b + 1) * z.tokens] = both[
            b * z.tail : (b + 1) * z.tail, :
        ]


def hidden_kernel(z, ids_ref, pair_ref, after_ref, *refs):
    outs, sides = refs[:-1], refs[-1]
    pair = pair_ref[...]
    gate_pre = pair[:, : z.hidden].astype(F32)
    up = pair[:, z.hidden :].astype(F32)
    hidden = (gate_pre * (1.0 / (1.0 + jnp.exp(-gate_pre))) * up).astype(BF).T
    for q in range(z.ep):
        sides[q] = hidden[q * z.down_cols : (q + 1) * z.down_cols, :]
    for k in range(z.ep):
        outs[k][...] = sides[ids_ref[0] ^ k]


def block_place(z, block):
    slot = block // z.slot_blocks
    first = (block % z.slot_blocks) * z.sources
    return slot, first


def block_picks(z, codes_ref, slot, first):
    rows = lax.broadcasted_iota(jnp.int32, (z.cap, z.tokens), 0).astype(F32)
    for a in range(z.sources):
        code = codes_ref[first + a, pl.ds(slot, 1), :]
        yield a, rows == code


def block_scale(z, codes_ref, slot, first):
    parts = []
    for a, pick in block_picks(z, codes_ref, slot, first):
        load = codes_ref[first + a, pl.ds(z.slots + slot, 1), :]
        parts.append(jnp.sum(jnp.where(pick, load, 0.0), axis=1, keepdims=True))
    return jnp.concatenate(parts, axis=0)


def local_picks(z, codes_ref, source, me):
    code = codes_ref[source, pl.ds(pl.multiple_of(me * z.local, z.local), z.local), :]
    rows = lax.broadcasted_iota(jnp.int32, (z.local, z.cap, z.tokens), 1).astype(F32)
    pick = (code[:, None, :] == rows).astype(F32)
    return pick.reshape(z.local * z.cap, z.tokens).astype(BF)


def block_slot(z, mine, step):
    place = step // z.part_blocks
    return ((place ^ mine) * z.part_blocks + step % z.part_blocks) // z.slot_blocks


def weight_copy(weight_ref, held, sems, slot):
    return pltpu.make_async_copy(weight_ref.at[slot], held.at[slot], sems.at[slot])


def down_kernel(z, ids_ref, *refs):
    bufs = refs[: z.ep]
    weight_ref = refs[z.ep]
    parts = refs[z.ep + 1 : z.ep + 1 + z.sub]
    grads_ref, codes_ref, rows_ref, held, sems = refs[z.ep + 1 + z.sub :]
    me, mine = ids_ref[0], ids_ref[1]
    step = pl.program_id(0)

    @pl.when(step == 0)
    def _():
        for s in range(z.local):
            weight_copy(weight_ref, held, sems, s).start()
        for k in range(z.ep):
            source = me ^ k
            grads_ref[source] = bufs[k][: z.tokens, :]
            for b in range(z.folds):
                codes_ref[source, b * z.tail : (b + 1) * z.tail, :] = bufs[k][
                    z.tokens :, b * z.tokens : (b + 1) * z.tokens
                ].astype(F32)
        for p in range(z.ep):
            rows = nn(local_picks(z, codes_ref, p, me), grads_ref[p]).astype(BF)
            rows_ref[:, p * z.cap : (p + 1) * z.cap, :] = rows.reshape(z.local, z.cap, z.width)

    place = step // z.part_blocks
    block = (place ^ mine) * z.part_blocks + step % z.part_blocks
    slot, first = block_place(z, block)
    start = pl.multiple_of(first * z.cap, z.block)

    @pl.when((step == 0) | (slot != block_slot(z, mine, step - 1)))
    def _():
        weight_copy(weight_ref, held, sems, slot).wait()

    partial = nt(rows_ref[slot, pl.ds(start, z.block), :], held[slot]).astype(BF)
    spot = pl.multiple_of((step % z.part_blocks) * z.block, z.block)
    for k in range(z.sub):

        @pl.when(place == k)
        def _():
            parts[k][pl.ds(spot, z.block), :] = partial


def gate_terms(z, pair, grad, scale):
    gate = pair[:, : z.hidden].astype(F32)
    up = pair[:, z.hidden :].astype(F32)
    sig = 1.0 / (1.0 + jnp.exp(-gate))
    act = gate * sig
    hidden = act * up
    scaled = scale * grad
    grad_gate = scaled * up * sig * (1.0 + gate * (1.0 - sig))
    grad_up = scaled * act
    return hidden, grad_gate.astype(BF), grad_up.astype(BF)


def pre_kernel(z, ids_ref, *refs):
    parts = refs[: z.sub]
    pair_ref, codes_ref = refs[z.sub : z.sub + 2]
    downs, refs = refs[z.sub + 2 : z.sub + 2 + z.ep], refs[z.sub + 2 + z.ep :]
    outs = refs[: z.ep]
    grad_ref, down_ref, sides = refs[z.ep :]

    @pl.when(pl.program_id(0) == 0)
    def _():
        for k in range(z.ep):
            down_ref[k] = downs[k][...]

    me = ids_ref[0]
    block = ids_ref[1] * z.part_blocks + pl.program_id(0)
    slot, first = block_place(z, block)
    scale = block_scale(z, codes_ref, me * z.local + slot, first)
    grad = parts[0][...].astype(F32)
    for k in range(1, z.sub):
        grad = grad + parts[k][...].astype(F32)
    grad_ref[...] = grad.astype(BF)
    _, grad_gate, grad_up = gate_terms(z, pair_ref[...], grad, scale)
    pre = jnp.concatenate([grad_gate.T, grad_up.T], axis=0)
    for q in range(z.ep):
        sides[q] = pre[q * z.in_cols : (q + 1) * z.in_cols, :]
    for k in range(z.ep):
        outs[k][...] = sides[me ^ k]


def stack_kernel(*refs):
    for i, ref in enumerate(refs[:-1]):
        refs[-1][i] = ref[...]


def row_kernel(z, ids_ref, *refs):
    grads = refs[: z.sub]
    pair_ref, weight_ref, codes_ref = refs[z.sub : z.sub + 3]
    out_ref, rows_ref, marks, held, weights, sems = refs[-6:]
    me, mine = ids_ref[0], ids_ref[1]
    step = pl.program_id(0)
    place = step // z.part_blocks
    block = (place ^ mine) * z.part_blocks + step % z.part_blocks
    slot, first = block_place(z, block)

    @pl.when(step == 0)
    def _():
        for s in range(z.local):
            weight_copy(weight_ref, weights, sems, s).start()
        marks[...] = jnp.zeros_like(marks)

    spot = pl.multiple_of((step % z.part_blocks) * z.block, z.block)
    for k in range(z.sub):

        @pl.when(place == k)
        def _():
            held[...] = grads[k][pl.ds(spot, z.block), :]

    grad = held[...].astype(F32)
    scale = block_scale(z, codes_ref, me * z.local + slot, first)
    hidden, grad_gate, grad_up = gate_terms(z, pair_ref[...], grad, scale)
    route = jnp.sum(hidden * grad, axis=1, keepdims=True).astype(BF).astype(F32)

    @pl.when((step == 0) | (slot != block_slot(z, mine, step - 1)))
    def _():
        weight_copy(weight_ref, weights, sems, slot).wait()

    rows = nn(grad_gate, weights[slot, : z.hidden, :]) + nn(grad_up, weights[slot, z.hidden :, :])
    start = pl.multiple_of(first * z.cap, z.block)
    rows_ref[slot, pl.ds(start, z.block), :] = rows.astype(BF)
    for a, pick in block_picks(z, codes_ref, me * z.local + slot, first):
        marks[first + a, pl.ds(slot, 1), :] = jnp.sum(
            jnp.where(pick, route[a * z.cap : (a + 1) * z.cap, :], 0.0), axis=0, keepdims=True
        )

    @pl.when(step == z.blocks - 1)
    def _():
        for p in range(z.ep):
            rows = rows_ref[:, p * z.cap : (p + 1) * z.cap, :].reshape(z.local * z.cap, z.width)
            out_ref[p ^ me, : z.tokens, :] = tn(local_picks(z, codes_ref, p, me), rows).astype(BF)
            out_ref[p ^ me, z.tokens :, : z.tokens] = marks[p].astype(BF)
            out_ref[p ^ me, z.tokens :, z.tokens :] = jnp.zeros(
                (marks.shape[1], z.width - z.tokens), BF
            )


def token_kernel(z, ids_ref, count_ref, *refs):
    got = refs[: z.ep]
    routes_ref, replica_ref, table_ref, tokens_ref, route_ref, marks = refs[z.ep :]
    me = ids_ref[0]
    total = got[0][: z.tokens, :].astype(F32)
    for k in range(1, z.ep):
        total = total + got[k][: z.tokens, :].astype(F32)
    tokens_ref[...] = total.astype(BF)
    for k in range(z.ep):
        marks[me ^ k] = got[k][z.tokens :, : z.tokens].astype(F32)
    rows = jnp.concatenate([marks[p][: z.local, :] for p in range(z.ep)], axis=0).astype(BF)
    totals = [jnp.zeros((1, z.tokens), F32)] * z.top
    for r in range(z.reps):
        spread = tn(slot_table(z, table_ref, r), rows)
        for k in range(z.top):
            same = key_hits(z, count_ref, routes_ref, replica_ref, r, k)
            totals[k] += jnp.sum(jnp.where(same, spread, 0.0), axis=0, keepdims=True)
    route_ref[...] = jnp.concatenate(totals, axis=0).astype(BF)


def side_moves(z, groups, sides, held, sems, act):
    size = z.ep // groups
    for g in range(groups):
        for k in range(z.sub):
            i = g * z.sub + k
            act(pltpu.make_async_copy(sides[i], held.at[k, pl.ds(g * size, size)], sems.at[i]))


def input_moves(z, me, own_ref, rights, lefts, inputs_ref, own_sem, right_sems, left_sems, act):
    act(pltpu.make_async_copy(own_ref, inputs_ref.at[me], own_sem))
    for d in range(1, z.ep):

        @pl.when(me >= d)
        def _():
            act(
                pltpu.make_async_copy(
                    rights[d - 1], inputs_ref.at[me - d], right_sems.at[d - 1]
                )
            )

        @pl.when(me + d < z.ep)
        def _():
            act(
                pltpu.make_async_copy(
                    lefts[d - 1], inputs_ref.at[me + d], left_sems.at[d - 1]
                )
            )


def expert_products(z, ids_ref, table_ref, held, right_rows, out_ref):
    me, mine = ids_ref[0], ids_ref[1]
    for i in range(PER):
        expert = pl.program_id(0) * PER + i
        first = table_ref[0, expert]
        left, right = [], []
        for r in range(z.reps):
            slot_id = table_ref[r, expert]
            source = slot_id // z.local
            for b in range(z.slot_blocks):
                block = (slot_id % z.local) * z.slot_blocks + b
                part = (block // z.part_blocks) ^ mine
                spot = pl.multiple_of((block % z.part_blocks) * z.block, z.block)
                side = jnp.where(slot_id == first, z.ep, source ^ me) if r else source ^ me
                left.append(held[part, side, :, pl.ds(spot, z.block)])
                right.append(right_rows(slot_id, block, b))
        left = jnp.concatenate(left, axis=1)
        out_ref[i] = nn(left, jnp.concatenate(right, axis=0)).astype(BF)


def total_down_kernel(z, ids_ref, table_ref, *refs):
    sides = refs[: z.sub]
    grads_ref, codes_ref, out_ref, held, scaled, sems = refs[z.sub :]

    @pl.when(pl.program_id(0) == 0)
    def _():
        side_moves(z, 1, sides, held, sems, lambda copy: copy.start())
        held[:, z.ep] = jnp.zeros_like(held[:, z.ep])
        rows = lax.broadcasted_iota(jnp.int32, (z.slots, z.cap, z.tokens), 1).astype(F32)
        for p in range(z.ep):
            code = codes_ref[p, : z.slots, :][:, None, :]
            load = codes_ref[p, z.slots :, :][:, None, :]
            pick = jnp.where(rows == code, load, 0.0).reshape(z.slots * z.cap, z.tokens)
            made = nn(pick.astype(BF), grads_ref[p]).astype(BF)
            scaled[:, p * z.cap : (p + 1) * z.cap, :] = made.reshape(z.slots, z.cap, z.width)
        side_moves(z, 1, sides, held, sems, lambda copy: copy.wait())

    def right_rows(slot_id, block, b):
        return scaled[slot_id, b * z.block : (b + 1) * z.block, :]

    expert_products(z, ids_ref, table_ref, held, right_rows, out_ref)


def total_in_kernel(z, ids_ref, table_ref, *refs):
    sides, refs = refs[: GROUPS * z.sub], refs[GROUPS * z.sub :]
    own_ref, rights, lefts = refs[0], refs[1 : z.ep], refs[z.ep : 2 * z.ep - 1]
    out_ref, held, inputs_ref, sems, *other_sems = refs[2 * z.ep - 1 :]

    @pl.when(pl.program_id(0) == 0)
    def _():
        def moves(act):
            side_moves(z, GROUPS, sides, held, sems, act)
            input_moves(z, ids_ref[0], own_ref, rights, lefts, inputs_ref, *other_sems, act)

        moves(lambda copy: copy.start())
        held[:, z.ep] = jnp.zeros_like(held[:, z.ep])
        moves(lambda copy: copy.wait())

    def right_rows(slot_id, block, b):
        start = pl.multiple_of(block * z.block, z.block)
        return inputs_ref[slot_id // z.local, pl.ds(start, z.block), :]

    expert_products(z, ids_ref, table_ref, held, right_rows, out_ref)


def swap(x, axis, size, bit):
    return lax.ppermute(x, axis, [(i, i ^ bit) for i in range(size)])


def spread_over(x, axis, size):
    have = {0: x}
    bit = size // 2
    while bit:
        for k in list(have):
            have[k | bit] = swap(have[k], axis, size, bit)
        bit //= 2
    return [have[k] for k in range(size)]


def nothing(*refs):
    pass


def gate(values, after):
    anywhere = pl.BlockSpec(memory_space=pl.ANY)
    return pl.pallas_call(
        nothing,
        in_specs=[anywhere] * (len(values) + len(after)),
        out_specs=[anywhere] * len(values),
        out_shape=[jax.ShapeDtypeStruct(v.shape, v.dtype) for v in values],
        input_output_aliases={i: i for i in range(len(values))},
        name="gate",
    )(*values, *after)


def chain_step(go, back, axis, size, d):
    go = lax.ppermute(go, axis, [(i, i + 1) for i in range(d - 1, size - 1)])
    back = lax.ppermute(back, axis, [(i, i - 1) for i in range(size - d, 0, -1)])
    return go, back


def body(
    grad_out,
    route_weight,
    routes,
    replica,
    replica_slot,
    token_count,
    saved_input,
    saved_gate_up,
    weight_in,
    weight_down,
):
    z = Sizes(grad_out, routes, replica_slot, saved_input, weight_in, weight_down)
    n, m = z.ep, z.sub
    ids = jnp.stack([lax.axis_index("ep"), lax.axis_index("sub")]).astype(jnp.int32)
    routes, replica, table = routes.T, replica.T, replica_slot.T
    route_weight = route_weight.T
    pair_rows = saved_gate_up.reshape(z.all_rows, z.pair)
    grad_shape = (z.tokens + z.tail, z.width)
    code_shape = (n, 2 * z.slots, z.tokens)
    inputs = saved_input.reshape(z.all_rows, z.width)

    routing = (grad_out, route_weight, routes, replica, table)
    buf = pl.pallas_call(
        functools.partial(route_kernel, z),
        out_shape=jax.ShapeDtypeStruct(grad_shape, BF),
        in_specs=[smem()] + [whole(a.shape) for a in routing],
        out_specs=whole(grad_shape),
        grid=(1,),
        compiler_params=params(60),
        name="route",
    )(token_count, *routing)
    bufs = [buf] + [swap(buf, "ep", n, k) for k in range(1, n)]

    downs = pl.pallas_call(
        functools.partial(hidden_kernel, z),
        grid_spec=pltpu.PrefetchScalarGridSpec(
            num_scalar_prefetch=1,
            grid=(z.part_blocks,),
            in_specs=[
                pl.BlockSpec((z.block, z.pair), lambda i, r: (r[1] * z.part_blocks + i, 0)),
                pl.BlockSpec(memory_space=pl.ANY),
            ],
            out_specs=[pl.BlockSpec((z.down_cols, z.block), lambda i, r: (0, i))] * n,
            scratch_shapes=[pltpu.VMEM((n, z.down_cols, z.block), BF)],
        ),
        out_shape=[jax.ShapeDtypeStruct((z.down_cols, z.part), BF)] * n,
        compiler_params=params(16),
        name="hidden_columns",
    )(ids, pair_rows, bufs[1])
    downs = [downs[0]] + [swap(downs[k], "ep", n, k) for k in range(1, n)]

    def stack(pieces):
        shape = pieces[0].shape
        return pl.pallas_call(
            stack_kernel,
            in_specs=[whole(shape)] * len(pieces),
            out_specs=whole((len(pieces),) + shape),
            out_shape=jax.ShapeDtypeStruct((len(pieces),) + shape, BF),
            grid=(1,),
            compiler_params=params(8),
            name="stack_columns",
        )(*pieces)

    def row_block(i, ids_ref):
        place = i // z.part_blocks
        return (place ^ ids_ref[1]) * z.part_blocks + i % z.part_blocks

    outs = pl.pallas_call(
        functools.partial(down_kernel, z),
        grid_spec=pltpu.PrefetchScalarGridSpec(
            num_scalar_prefetch=1,
            grid=(z.blocks,),
            in_specs=[whole(grad_shape)] * n + [pl.BlockSpec(memory_space=pltpu.HBM)],
            out_specs=[whole((z.part, z.hidden))] * m
            + [whole((n, z.tokens, z.width)), whole(code_shape)],
            scratch_shapes=[
                pltpu.VMEM((z.local, z.rows, z.width), BF),
                pltpu.VMEM((z.local, z.hidden, z.width), BF),
                pltpu.SemaphoreType.DMA((z.local,)),
            ],
        ),
        out_shape=[jax.ShapeDtypeStruct((z.part, z.hidden), BF)] * m
        + [
            jax.ShapeDtypeStruct((n, z.tokens, z.width), BF),
            jax.ShapeDtypeStruct(code_shape, F32),
        ],
        compiler_params=params(48),
        name="hidden_partials",
    )(ids, *bufs, weight_down)
    parts, (grads_all, codes) = outs[:m], outs[m:]
    chain = gate([inputs], downs[1:] + [codes])
    steps = [chain_step(chain[0], chain[0], "ep", n, 1)]
    parts = [parts[0]] + [swap(parts[k], "sub", m, k) for k in range(1, m)]

    outs = pl.pallas_call(
        functools.partial(pre_kernel, z),
        grid_spec=pltpu.PrefetchScalarGridSpec(
            num_scalar_prefetch=1,
            grid=(z.part_blocks,),
            in_specs=[pl.BlockSpec((z.block, z.hidden), lambda i, r: (i, 0))] * m
            + [
                pl.BlockSpec((z.block, z.pair), lambda i, r: (r[1] * z.part_blocks + i, 0)),
                whole(code_shape),
            ]
            + [whole((z.down_cols, z.part))] * n,
            out_specs=[pl.BlockSpec((z.in_cols, z.block), lambda i, r: (0, i))] * n
            + [
                pl.BlockSpec((z.block, z.hidden), lambda i, r: (i, 0)),
                whole((n, z.down_cols, z.part)),
            ],
            scratch_shapes=[pltpu.VMEM((n, z.in_cols, z.block), BF)],
        ),
        out_shape=[jax.ShapeDtypeStruct((z.in_cols, z.part), BF)] * n
        + [
            jax.ShapeDtypeStruct((z.part, z.hidden), BF),
            jax.ShapeDtypeStruct((n, z.down_cols, z.part), BF),
        ],
        compiler_params=params(16),
        name="pre_grads",
    )(ids, *parts, pair_rows, codes, *downs)
    pieces, grad_part = outs[:n], outs[n]
    pieces = [pieces[0]] + [swap(pieces[k], "ep", n, k) for k in range(1, n)]
    grad_parts = spread_over(grad_part, "sub", m)
    steps[0] = gate(steps[0], pieces[1:])
    for d in range(2, n):
        steps.append(chain_step(*steps[-1], "ep", n, d))
    gathered = [inputs] + [go for go, _ in steps] + [back for _, back in steps]
    down_sides = spread_over(outs[n + 1], "sub", m)
    size = n // GROUPS
    sides = []
    for g in range(GROUPS):
        sides += spread_over(stack(pieces[g * size : (g + 1) * size]), "sub", m)

    mark_rows = -(-z.local // 16) * 16
    back_shape = (n, z.tokens + mark_rows, z.width)
    back = pl.pallas_call(
        functools.partial(row_kernel, z),
        grid_spec=pltpu.PrefetchScalarGridSpec(
            num_scalar_prefetch=1,
            grid=(z.blocks,),
            in_specs=[whole((z.part, z.hidden))] * m
            + [
                pl.BlockSpec((z.block, z.pair), lambda i, r: (row_block(i, r), 0)),
                pl.BlockSpec(memory_space=pltpu.HBM),
                whole(code_shape),
            ]
            + [pl.BlockSpec(memory_space=pl.ANY)] * (m - 1),
            out_specs=whole(back_shape),
            scratch_shapes=[
                pltpu.VMEM((z.local, z.rows, z.width), BF),
                pltpu.VMEM((n, mark_rows, z.tokens), F32),
                pltpu.VMEM((z.block, z.hidden), BF),
                pltpu.VMEM((z.local, z.pair, z.width), BF),
                pltpu.SemaphoreType.DMA((z.local,)),
            ],
        ),
        out_shape=jax.ShapeDtypeStruct(back_shape, BF),
        compiler_params=params(46),
        name="row_grads",
    )(ids, *grad_parts, pair_rows, weight_in, codes, *sides[1 - m :])
    got = [back[0]] + [swap(back[k], "ep", n, k) for k in range(1, n)]

    grad_tokens, grad_routes = pl.pallas_call(
        functools.partial(token_kernel, z),
        out_shape=[
            jax.ShapeDtypeStruct((z.tokens, z.width), BF),
            jax.ShapeDtypeStruct((z.top, z.tokens), BF),
        ],
        in_specs=[smem(), smem()]
        + [whole(back_shape[1:])] * n
        + [whole(a.shape) for a in (routes, replica, table)],
        out_specs=[whole((z.tokens, z.width)), whole((z.top, z.tokens))],
        grid=(1,),
        scratch_shapes=[pltpu.VMEM((n, mark_rows, z.tokens), F32)],
        compiler_params=params(16),
        name="token_grads",
    )(ids, token_count, *got, routes, replica, table)

    def total_call(kernel, operands, specs, cols, scratch, name):
        return pl.pallas_call(
            functools.partial(kernel, z),
            grid_spec=pltpu.PrefetchScalarGridSpec(
                num_scalar_prefetch=2,
                grid=(z.experts // PER,),
                in_specs=specs,
                out_specs=pl.BlockSpec((PER, cols, z.width), lambda e, r, t: (e, 0, 0)),
                scratch_shapes=[pltpu.VMEM((m, n + 1, cols, z.part), BF)] + scratch,
            ),
            out_shape=jax.ShapeDtypeStruct((z.experts, cols, z.width), BF),
            compiler_params=params(32),
            name=name,
        )(ids, table, *operands)

    anywhere = pl.BlockSpec(memory_space=pl.ANY)
    pinned = pl.BlockSpec(memory_space=pltpu.HBM)
    grad_down = total_call(
        total_down_kernel,
        [*down_sides, grads_all, codes],
        [anywhere] * m + [whole((n, z.tokens, z.width)), whole(code_shape)],
        z.down_cols,
        [pltpu.VMEM((z.slots, z.rows, z.width), BF), pltpu.SemaphoreType.DMA((m,))],
        "down_grads",
    )
    grad_in = total_call(
        total_in_kernel,
        [*sides, *gathered],
        [anywhere] * (GROUPS * m) + [pinned] * (2 * n - 1),
        z.in_cols,
        [
            pltpu.VMEM((n, z.all_rows, z.width), BF),
            pltpu.SemaphoreType.DMA((GROUPS * m,)),
            pltpu.SemaphoreType.DMA,
            pltpu.SemaphoreType.DMA((n - 1,)),
            pltpu.SemaphoreType.DMA((n - 1,)),
        ],
        "in_grads",
    )
    return grad_tokens, grad_routes.T, grad_in, grad_down


def solution(mesh):
    return jax.shard_map(
        body,
        mesh=mesh,
        in_specs=(
            P(("groups", "ep"), "sub"),
            P(("groups", "ep"), None),
            P(("groups", "ep"), None),
            P(("groups", "ep"), None),
            P("groups", None),
            P(("groups", "ep")),
            P(("groups", "ep"), None, None, "sub"),
            P(("groups", "ep"), None, None),
            P(("groups", "ep"), None, "sub"),
            P(("groups", "ep"), None, "sub"),
        ),
        out_specs=(
            P(("groups", "ep"), "sub"),
            P(("groups", "ep"), None),
            P("groups", "ep", "sub"),
            P("groups", "ep", "sub"),
        ),
        check_vma=False,
    )
```

```python
import functools
import math

import jax
import jax.numpy as jnp
from jax import lax
from jax.experimental import pallas as pl
from jax.experimental.pallas import tpu as pltpu
from jax.sharding import PartitionSpec as P

BF = jnp.bfloat16
F32 = jnp.float32
PER = 2


def nt(a, b):
    return lax.dot_general(a, b, (((1,), (1,)), ((), ())), preferred_element_type=F32)


def tn(a, b):
    return lax.dot_general(a, b, (((0,), (0,)), ((), ())), preferred_element_type=F32)


def nn(a, b):
    return jnp.dot(a, b, preferred_element_type=F32)


def whole(shape):
    zeros = (0,) * len(shape)
    return pl.BlockSpec(shape, lambda *_: zeros)


def smem():
    return pl.BlockSpec(memory_space=pltpu.SMEM)


def params(mib):
    return pltpu.CompilerParams(
        vmem_limit_bytes=mib * 1024 * 1024, dimension_semantics=("arbitrary",)
    )


class Sizes:
    def __init__(self, grad_out, routes, replica_slot, saved_input, weight_in, weight_down):
        self.ep = lax.axis_size("ep")
        self.sub = lax.axis_size("sub")
        self.tokens, self.width = grad_out.shape
        self.top = routes.shape[1]
        self.experts, self.reps = replica_slot.shape
        self.local = weight_in.shape[0]
        self.slots = self.ep * self.local
        self.cap = saved_input.shape[2]
        self.rows = self.ep * self.cap
        self.hidden = weight_down.shape[1]
        self.pair = weight_in.shape[1]
        self.all_rows = self.local * self.rows
        self.part = self.all_rows // self.sub
        self.block = math.gcd(self.rows, self.part)
        self.sources = self.block // self.cap
        self.blocks = self.all_rows // self.block
        self.part_blocks = self.part // self.block
        self.slot_blocks = self.rows // self.block
        self.in_cols = self.pair // self.ep
        self.down_cols = self.hidden // self.ep
        self.cols = self.in_cols + self.down_cols
        self.folds = self.width // self.tokens
        self.tail = 2 * self.slots // self.folds


def slot_table(z, table_ref, r):
    ids = lax.broadcasted_iota(jnp.int32, (z.slots, z.experts), 0)
    return (table_ref[r : r + 1, :] == ids).astype(F32).astype(BF)


def key_hits(z, count_ref, routes_ref, replica_ref, r, k):
    ids = lax.broadcasted_iota(jnp.int32, (z.experts, z.tokens), 0)
    live = lax.broadcasted_iota(jnp.int32, (1, z.tokens), 1) < count_ref[0]
    key = jnp.where(live & (replica_ref[k : k + 1, :] == r), routes_ref[k : k + 1, :], -1)
    return key == ids


def route_kernel(z, count_ref, grad_ref, weight_ref, routes_ref, replica_ref, table_ref, out_ref):
    weights = weight_ref[...].astype(F32)
    hits = jnp.zeros((z.slots, z.tokens), F32)
    loads = jnp.zeros((z.slots, z.tokens), F32)
    for r in range(z.reps):
        hit = jnp.zeros((z.experts, z.tokens), F32)
        load = jnp.zeros((z.experts, z.tokens), F32)
        for k in range(z.top):
            same = key_hits(z, count_ref, routes_ref, replica_ref, r, k)
            hit = jnp.where(same, 1.0, hit)
            load = jnp.where(same, weights[k : k + 1, :], load)
        table = slot_table(z, table_ref, r)
        hits = hits + nn(table, hit.astype(BF))
        loads = loads + nn(table, load.astype(BF))
    before = lax.broadcasted_iota(jnp.int32, (z.tokens, z.tokens), 0)
    after = lax.broadcasted_iota(jnp.int32, (z.tokens, z.tokens), 1)
    earlier = nn(hits.astype(BF), (before < after).astype(F32).astype(BF))
    code = jnp.where(hits > 0.5, earlier, -1.0)
    both = jnp.concatenate([code, loads], axis=0).astype(BF)
    out_ref[: z.tokens, :] = grad_ref[...]
    for b in range(z.folds):
        out_ref[z.tokens :, b * z.tokens : (b + 1) * z.tokens] = both[
            b * z.tail : (b + 1) * z.tail, :
        ]


def hidden_kernel(z, ids_ref, pair_ref, after_ref, *refs):
    outs, sides = refs[:-1], refs[-1]
    pair = pair_ref[...]
    gate_pre = pair[:, : z.hidden].astype(F32)
    up = pair[:, z.hidden :].astype(F32)
    hidden = (gate_pre * (1.0 / (1.0 + jnp.exp(-gate_pre))) * up).astype(BF).T
    for q in range(z.ep):
        sides[q] = hidden[q * z.down_cols : (q + 1) * z.down_cols, :]
    for k in range(z.ep):
        outs[k][...] = sides[ids_ref[0] ^ k]


def block_place(z, block):
    slot = block // z.slot_blocks
    first = (block % z.slot_blocks) * z.sources
    return slot, first


def block_picks(z, codes_ref, slot, first):
    rows = lax.broadcasted_iota(jnp.int32, (z.cap, z.tokens), 0).astype(F32)
    for a in range(z.sources):
        code = codes_ref[first + a, pl.ds(slot, 1), :]
        yield a, rows == code


def block_scale(z, codes_ref, slot, first):
    parts = []
    for a, pick in block_picks(z, codes_ref, slot, first):
        load = codes_ref[first + a, pl.ds(z.slots + slot, 1), :]
        parts.append(jnp.sum(jnp.where(pick, load, 0.0), axis=1, keepdims=True))
    return jnp.concatenate(parts, axis=0)


def local_picks(z, codes_ref, source, me):
    code = codes_ref[source, pl.ds(pl.multiple_of(me * z.local, z.local), z.local), :]
    rows = lax.broadcasted_iota(jnp.int32, (z.local, z.cap, z.tokens), 1).astype(F32)
    pick = (code[:, None, :] == rows).astype(F32)
    return pick.reshape(z.local * z.cap, z.tokens).astype(BF)


def block_slot(z, mine, step):
    place = step // z.part_blocks
    return ((place ^ mine) * z.part_blocks + step % z.part_blocks) // z.slot_blocks


def weight_copy(weight_ref, held, sems, slot):
    return pltpu.make_async_copy(weight_ref.at[slot], held.at[slot], sems.at[slot])


def down_kernel(z, ids_ref, *refs):
    bufs = refs[: z.ep]
    weight_ref = refs[z.ep]
    parts = refs[z.ep + 2 : z.ep + 4]
    grads_ref, codes_ref, rows_ref, held, sems = refs[z.ep + 4 :]
    me, mine = ids_ref[0], ids_ref[1]
    step = pl.program_id(0)

    @pl.when(step == 0)
    def _():
        for s in range(z.local):
            weight_copy(weight_ref, held, sems, s).start()
        for k in range(z.ep):
            source = me ^ k
            grads_ref[source] = bufs[k][: z.tokens, :]
            for b in range(z.folds):
                codes_ref[source, b * z.tail : (b + 1) * z.tail, :] = bufs[k][
                    z.tokens :, b * z.tokens : (b + 1) * z.tokens
                ].astype(F32)
        for p in range(z.ep):
            rows = nn(local_picks(z, codes_ref, p, me), grads_ref[p]).astype(BF)
            rows_ref[:, p * z.cap : (p + 1) * z.cap, :] = rows.reshape(z.local, z.cap, z.width)

    place = step // z.part_blocks
    block = (place ^ mine) * z.part_blocks + step % z.part_blocks
    slot, first = block_place(z, block)
    start = pl.multiple_of(first * z.cap, z.block)

    @pl.when((step == 0) | (slot != block_slot(z, mine, step - 1)))
    def _():
        weight_copy(weight_ref, held, sems, slot).wait()

    partial = nt(rows_ref[slot, pl.ds(start, z.block), :], held[slot]).astype(BF)
    spot = pl.multiple_of((step % z.part_blocks) * z.block, z.block)
    for k in range(z.sub):

        @pl.when(place == k)
        def _():
            parts[k % 2][k // 2, pl.ds(spot, z.block), :] = partial


def gate_terms(z, pair, grad, scale):
    gate = pair[:, : z.hidden].astype(F32)
    up = pair[:, z.hidden :].astype(F32)
    sig = 1.0 / (1.0 + jnp.exp(-gate))
    act = gate * sig
    hidden = act * up
    scaled = scale * grad
    grad_gate = scaled * up * sig * (1.0 + gate * (1.0 - sig))
    grad_up = scaled * act
    return hidden, grad_gate.astype(BF), grad_up.astype(BF)


def pre_kernel(z, ids_ref, keep_ref, got_ref, pair_ref, codes_ref, *refs):
    downs = refs[: z.ep]
    out_ref, bundle_ref = refs[-2:]

    @pl.when(pl.program_id(0) == 0)
    def _():
        for k in range(z.ep):
            bundle_ref[k] = downs[k][...]

    me = ids_ref[0]
    block = ids_ref[1] * z.part_blocks + pl.program_id(0)
    slot, first = block_place(z, block)
    scale = block_scale(z, codes_ref, me * z.local + slot, first)
    grad = keep_ref[0].astype(F32) + got_ref[0].astype(F32)
    turned = grad.astype(BF).T
    spot = pl.multiple_of(pl.program_id(0) * z.block, z.block)
    for q in range(z.ep):
        bundle_ref[z.ep + q, :, pl.ds(spot, z.block)] = turned[
            q * z.down_cols : (q + 1) * z.down_cols, :
        ]
    _, grad_gate, grad_up = gate_terms(z, pair_ref[...], grad, scale)
    pre = jnp.concatenate([grad_gate.T, grad_up.T], axis=0)
    for q in range(z.ep):
        out_ref[q] = pre[q * z.in_cols : (q + 1) * z.in_cols, :]


def row_kernel(z, ids_ref, *refs):
    grads = refs[: z.sub]
    pair_ref, weight_ref, codes_ref, keep_ref, send_ref = refs[z.sub : z.sub + 5]
    rows_ref, marks, held, weights, sems = refs[z.sub + 5 :]
    me, mine = ids_ref[0], ids_ref[1]
    step = pl.program_id(0)
    place = step // z.part_blocks
    block = (place ^ mine) * z.part_blocks + step % z.part_blocks
    slot, first = block_place(z, block)

    @pl.when(step == 0)
    def _():
        for s in range(z.local):
            weight_copy(weight_ref, weights, sems, s).start()
        marks[...] = jnp.zeros_like(marks)

    spot = pl.multiple_of((step % z.part_blocks) * z.block, z.block)
    for k in range(z.sub):

        @pl.when(place == k)
        def _():
            turned = [grads[k][z.ep + q, :, pl.ds(spot, z.block)] for q in range(z.ep)]
            held[...] = jnp.concatenate(turned, axis=0).T

    grad = held[...].astype(F32)
    scale = block_scale(z, codes_ref, me * z.local + slot, first)
    hidden, grad_gate, grad_up = gate_terms(z, pair_ref[...], grad, scale)
    route = jnp.sum(hidden * grad, axis=1, keepdims=True).astype(BF).astype(F32)

    @pl.when((step == 0) | (slot != block_slot(z, mine, step - 1)))
    def _():
        weight_copy(weight_ref, weights, sems, slot).wait()

    rows = nn(grad_gate, weights[slot, : z.hidden, :]) + nn(grad_up, weights[slot, z.hidden :, :])
    start = pl.multiple_of(first * z.cap, z.block)
    rows_ref[slot, pl.ds(start, z.block), :] = rows.astype(BF)
    for a, pick in block_picks(z, codes_ref, me * z.local + slot, first):
        marks[first + a, pl.ds(me * z.local + slot, 1), :] = jnp.sum(
            jnp.where(pick, route[a * z.cap : (a + 1) * z.cap, :], 0.0), axis=0, keepdims=True
        )

    @pl.when(step == z.blocks - 1)
    def _():
        blank = jnp.zeros((z.slots, z.width - z.tokens), BF)
        for k in range(z.ep):
            source = me ^ k
            start = pl.multiple_of(source * z.cap, z.cap)
            rows = rows_ref[:, pl.ds(start, z.cap), :].reshape(z.local * z.cap, z.width)
            out_ref = send_ref if k % 2 else keep_ref
            picks = local_picks(z, codes_ref, source, me)
            out_ref[k // 2, : z.tokens, :] = tn(picks, rows).astype(BF)
            out_ref[k // 2, z.tokens :, : z.tokens] = marks[source].astype(BF)
            out_ref[k // 2, z.tokens :, z.tokens :] = blank


def halve_kernel(keep_ref, got_ref, out_keep, out_send):
    for i in range(out_keep.shape[0]):
        for j, out in enumerate((out_keep, out_send)):
            total = keep_ref[2 * i + j].astype(F32) + got_ref[2 * i + j].astype(F32)
            out[i] = total.astype(BF)


def token_kernel(z, count_ref, *refs):
    keep_ref, got_ref, routes_ref, replica_ref, table_ref, tokens_ref, route_ref = refs
    total = keep_ref[0].astype(F32) + got_ref[0].astype(F32)
    tokens_ref[...] = total[: z.tokens, :].astype(BF)
    rows = total[z.tokens :, : z.tokens].astype(BF)
    totals = [jnp.zeros((1, z.tokens), F32)] * z.top
    for r in range(z.reps):
        spread = tn(slot_table(z, table_ref, r), rows)
        for k in range(z.top):
            same = key_hits(z, count_ref, routes_ref, replica_ref, r, k)
            totals[k] += jnp.sum(jnp.where(same, spread, 0.0), axis=0, keepdims=True)
    route_ref[...] = jnp.concatenate(totals, axis=0).astype(BF)


def input_moves(z, me, own_ref, rights, lefts, inputs_ref, own_sem, right_sems, left_sems, act):
    act(pltpu.make_async_copy(own_ref, inputs_ref.at[me], own_sem))
    for d in range(1, z.ep):

        @pl.when(me >= d)
        def _():
            act(
                pltpu.make_async_copy(
                    rights[d - 1], inputs_ref.at[me - d], right_sems.at[d - 1]
                )
            )

        @pl.when(me + d < z.ep)
        def _():
            act(
                pltpu.make_async_copy(
                    lefts[d - 1], inputs_ref.at[me + d], left_sems.at[d - 1]
                )
            )


def expert_products(z, ids_ref, table_ref, turn, held, right_rows, out_ref, made, out_sems):
    mine = ids_ref[1]

    def out_copy(expert):
        return pltpu.make_async_copy(made.at[expert], out_ref.at[expert], out_sems.at[expert])

    def some(step, carry):
        for i in range(PER):
            expert = step * PER + i
            first = table_ref[0, expert]
            left, right = [], []
            for r in range(z.reps):
                slot_id = table_ref[r, expert]
                source = slot_id // z.local
                for b in range(z.slot_blocks):
                    block = (slot_id % z.local) * z.slot_blocks + b
                    part = (block // z.part_blocks) ^ mine
                    spot = pl.multiple_of((block % z.part_blocks) * z.block, z.block)
                    side = source ^ turn
                    if r:
                        side = jnp.where(slot_id == first, z.ep, side)
                    left.append(held[part, side, :, pl.ds(spot, z.block)])
                    right.append(right_rows(slot_id, block, b))
            left = jnp.concatenate(left, axis=1)
            made[expert] = nn(left, jnp.concatenate(right, axis=0)).astype(BF)
            out_copy(expert).start()
        return carry

    lax.fori_loop(0, z.experts // PER, some, 0)
    for expert in range(z.experts):
        out_copy(expert).wait()


def total_down_kernel(z, ids_ref, table_ref, *refs):
    sides = refs[: z.sub]
    grads_ref, codes_ref, out_ref, held, made, out_sems, scaled, sems = refs[z.sub :]

    def moves(act):
        for k in range(z.sub):
            act(
                pltpu.make_async_copy(
                    sides[k].at[pl.ds(0, z.ep)], held.at[k, pl.ds(0, z.ep)], sems.at[k]
                )
            )

    moves(lambda copy: copy.start())
    held[:, z.ep] = jnp.zeros_like(held[:, z.ep])
    rows = lax.broadcasted_iota(jnp.int32, (z.slots, z.cap, z.tokens), 1).astype(F32)
    for p in range(z.ep):
        code = codes_ref[p, : z.slots, :][:, None, :]
        load = codes_ref[p, z.slots :, :][:, None, :]
        pick = jnp.where(rows == code, load, 0.0).reshape(z.slots * z.cap, z.tokens)
        result = nn(pick.astype(BF), grads_ref[p]).astype(BF)
        scaled[:, p * z.cap : (p + 1) * z.cap, :] = result.reshape(z.slots, z.cap, z.width)
    moves(lambda copy: copy.wait())

    def right_rows(slot_id, block, b):
        return scaled[slot_id, b * z.block : (b + 1) * z.block, :]

    expert_products(z, ids_ref, table_ref, ids_ref[0], held, right_rows, out_ref, made, out_sems)


def total_in_kernel(z, ids_ref, table_ref, *refs):
    sides, refs = refs[: z.sub], refs[z.sub :]
    own_ref, rights, lefts = refs[0], refs[1 : z.ep], refs[z.ep : 2 * z.ep - 1]
    out_ref, held, made, out_sems, inputs_ref, sems, *other_sems = refs[2 * z.ep - 1 :]

    def moves(act):
        for k in range(z.sub):
            act(pltpu.make_async_copy(sides[k], held.at[k, pl.ds(0, z.ep)], sems.at[k]))
        input_moves(z, ids_ref[0], own_ref, rights, lefts, inputs_ref, *other_sems, act)

    moves(lambda copy: copy.start())
    held[:, z.ep] = jnp.zeros_like(held[:, z.ep])
    moves(lambda copy: copy.wait())

    def right_rows(slot_id, block, b):
        start = pl.multiple_of(block * z.block, z.block)
        return inputs_ref[slot_id // z.local, pl.ds(start, z.block), :]

    expert_products(z, ids_ref, table_ref, 0, held, right_rows, out_ref, made, out_sems)


def swap(x, axis, size, bit):
    return lax.ppermute(x, axis, [(i, i ^ bit) for i in range(size)])


def spread_over(have, axis, size, bit):
    have = dict(have)
    while bit:
        for k in list(have):
            if k | bit not in have:
                have[k | bit] = swap(have[k], axis, size, bit)
        bit //= 2
    return [have[k] for k in range(size)]


def nothing(*refs):
    pass


def gate(values, after):
    anywhere = pl.BlockSpec(memory_space=pl.ANY)
    return pl.pallas_call(
        nothing,
        in_specs=[anywhere] * (len(values) + len(after)),
        out_specs=[anywhere] * len(values),
        out_shape=[jax.ShapeDtypeStruct(v.shape, v.dtype) for v in values],
        input_output_aliases={i: i for i in range(len(values))},
        compiler_params=pltpu.CompilerParams(vmem_limit_bytes=1024 * 1024),
        name="gate",
    )(*values, *after)


def chain_step(go, back, axis, size, d):
    go = lax.ppermute(go, axis, [(i, i + 1) for i in range(d - 1, size - 1)])
    back = lax.ppermute(back, axis, [(i, i - 1) for i in range(size - d, 0, -1)])
    return go, back


def body(
    grad_out,
    route_weight,
    routes,
    replica,
    replica_slot,
    token_count,
    saved_input,
    saved_gate_up,
    weight_in,
    weight_down,
):
    z = Sizes(grad_out, routes, replica_slot, saved_input, weight_in, weight_down)
    n, m = z.ep, z.sub
    ids = jnp.stack([lax.axis_index("ep"), lax.axis_index("sub")]).astype(jnp.int32)
    routes, replica, table = routes.T, replica.T, replica_slot.T
    route_weight = route_weight.T
    pair_rows = saved_gate_up.reshape(z.all_rows, z.pair)
    grad_shape = (z.tokens + z.tail, z.width)
    code_shape = (n, 2 * z.slots, z.tokens)
    inputs = saved_input.reshape(z.all_rows, z.width)

    routing = (grad_out, route_weight, routes, replica, table)
    buf = pl.pallas_call(
        functools.partial(route_kernel, z),
        out_shape=jax.ShapeDtypeStruct(grad_shape, BF),
        in_specs=[smem()] + [whole(a.shape) for a in routing],
        out_specs=whole(grad_shape),
        grid=(1,),
        compiler_params=params(60),
        name="route",
    )(token_count, *routing)
    bufs = [buf] + [swap(buf, "ep", n, k) for k in range(1, n)]

    downs = pl.pallas_call(
        functools.partial(hidden_kernel, z),
        grid_spec=pltpu.PrefetchScalarGridSpec(
            num_scalar_prefetch=1,
            grid=(z.part_blocks,),
            in_specs=[
                pl.BlockSpec((z.block, z.pair), lambda i, r: (r[1] * z.part_blocks + i, 0)),
                pl.BlockSpec(memory_space=pl.ANY),
            ],
            out_specs=[pl.BlockSpec((z.down_cols, z.block), lambda i, r: (0, i))] * n,
            scratch_shapes=[pltpu.VMEM((n, z.down_cols, z.block), BF)],
        ),
        out_shape=[jax.ShapeDtypeStruct((z.down_cols, z.part), BF)] * n,
        compiler_params=params(16),
        name="hidden_columns",
    )(ids, pair_rows, bufs[1])
    downs = [downs[0]] + [swap(downs[k], "ep", n, k) for k in range(1, n)]

    def halve(keep, got):
        half = (keep.shape[0] // 2,) + keep.shape[1:]
        return pl.pallas_call(
            halve_kernel,
            in_specs=[whole(keep.shape)] * 2,
            out_specs=[whole(half)] * 2,
            out_shape=[jax.ShapeDtypeStruct(half, BF)] * 2,
            grid=(1,),
            compiler_params=params(16),
            name="halve",
        )(keep, got)

    def row_block(i, ids_ref):
        place = i // z.part_blocks
        return (place ^ ids_ref[1]) * z.part_blocks + i % z.part_blocks

    chain = gate([inputs], bufs[1:] + downs[1:])
    steps = [chain_step(chain[0], chain[0], "ep", n, 1)]

    part_shape = (m // 2, z.part, z.hidden)
    outs = pl.pallas_call(
        functools.partial(down_kernel, z),
        grid_spec=pltpu.PrefetchScalarGridSpec(
            num_scalar_prefetch=1,
            grid=(z.blocks,),
            in_specs=[whole(grad_shape)] * n
            + [pl.BlockSpec(memory_space=pltpu.HBM), pl.BlockSpec(memory_space=pl.ANY)],
            out_specs=[whole(part_shape)] * 2
            + [whole((n, z.tokens, z.width)), whole(code_shape)],
            scratch_shapes=[
                pltpu.VMEM((z.local, z.rows, z.width), BF),
                pltpu.VMEM((z.local, z.hidden, z.width), BF),
                pltpu.SemaphoreType.DMA((z.local,)),
            ],
        ),
        out_shape=[jax.ShapeDtypeStruct(part_shape, BF)] * 2
        + [
            jax.ShapeDtypeStruct((n, z.tokens, z.width), BF),
            jax.ShapeDtypeStruct(code_shape, F32),
        ],
        compiler_params=params(48),
        name="hidden_partials",
    )(ids, *bufs, weight_down, chain[0])
    keep, send, grads_all, codes = outs
    got = swap(send, "sub", m, 1)
    bit = 2
    while bit < m:
        keep, send = halve(keep, got)
        got = swap(send, "sub", m, bit)
        bit *= 2
    pre, bundle = pl.pallas_call(
        functools.partial(pre_kernel, z),
        grid_spec=pltpu.PrefetchScalarGridSpec(
            num_scalar_prefetch=1,
            grid=(z.part_blocks,),
            in_specs=[pl.BlockSpec((1, z.block, z.hidden), lambda i, r: (0, i, 0))] * 2
            + [
                pl.BlockSpec((z.block, z.pair), lambda i, r: (r[1] * z.part_blocks + i, 0)),
                whole(code_shape),
            ]
            + [whole((z.down_cols, z.part))] * n
            + [pl.BlockSpec(memory_space=pl.ANY)] * 2,
            out_specs=[
                pl.BlockSpec((n, z.in_cols, z.block), lambda i, r: (0, 0, i)),
                whole((2 * n, z.down_cols, z.part)),
            ],
        ),
        out_shape=[
            jax.ShapeDtypeStruct((n, z.in_cols, z.part), BF),
            jax.ShapeDtypeStruct((2 * n, z.down_cols, z.part), BF),
        ],
        compiler_params=params(16),
        name="pre_grads",
    )(ids, keep, got, pair_rows, codes, *downs, *steps[0])
    columns = lax.all_to_all(pre, "ep", split_axis=0, concat_axis=0, tiled=True)
    steps[0] = gate(steps[0], [columns])
    for d in range(2, n):
        steps.append(chain_step(*steps[-1], "ep", n, d))
    bundles = spread_over({0: bundle}, "sub", m, m // 2)
    sides = {0: gate([columns], [bundles[m // 2]])[0]}
    sides[m // 2] = swap(sides[0], "sub", m, m // 2)
    gathered = [inputs] + [go for go, _ in steps] + [back for _, back in steps]

    back_shape = (n // 2, z.tokens + z.slots, z.width)
    keep, send = pl.pallas_call(
        functools.partial(row_kernel, z),
        grid_spec=pltpu.PrefetchScalarGridSpec(
            num_scalar_prefetch=1,
            grid=(z.blocks,),
            in_specs=[whole(bundle.shape)] * m
            + [
                pl.BlockSpec((z.block, z.pair), lambda i, r: (row_block(i, r), 0)),
                pl.BlockSpec(memory_space=pltpu.HBM),
                whole(code_shape),
            ],
            out_specs=[whole(back_shape)] * 2,
            scratch_shapes=[
                pltpu.VMEM((z.local, z.rows, z.width), BF),
                pltpu.VMEM((n, z.slots, z.tokens), F32),
                pltpu.VMEM((z.block, z.hidden), BF),
                pltpu.VMEM((z.local, z.pair, z.width), BF),
                pltpu.SemaphoreType.DMA((z.local,)),
            ],
        ),
        out_shape=[jax.ShapeDtypeStruct(back_shape, BF)] * 2,
        compiler_params=params(46),
        name="row_grads",
    )(ids, *bundles, pair_rows, weight_in, codes)
    sides[m // 2] = gate([sides[m // 2]], [keep])[0]
    sides = spread_over(sides, "sub", m, m // 4)
    got = swap(send, "ep", n, 1)
    bit = 2
    while bit < n:
        keep, send = halve(keep, got)
        got = swap(send, "ep", n, bit)
        bit *= 2

    grad_tokens, grad_routes = pl.pallas_call(
        functools.partial(token_kernel, z),
        out_shape=[
            jax.ShapeDtypeStruct((z.tokens, z.width), BF),
            jax.ShapeDtypeStruct((z.top, z.tokens), BF),
        ],
        in_specs=[smem()] + [whole(a.shape) for a in (keep, got, routes, replica, table)],
        out_specs=[whole((z.tokens, z.width)), whole((z.top, z.tokens))],
        grid=(1,),
        compiler_params=params(16),
        name="token_grads",
    )(token_count, keep, got, routes, replica, table)

    def total_call(kernel, operands, specs, cols, scratch, name):
        return pl.pallas_call(
            functools.partial(kernel, z),
            grid_spec=pltpu.PrefetchScalarGridSpec(
                num_scalar_prefetch=2,
                grid=(1,),
                in_specs=specs,
                out_specs=pl.BlockSpec(memory_space=pl.ANY),
                scratch_shapes=[
                    pltpu.VMEM((m, n + 1, cols, z.part), BF),
                    pltpu.VMEM((z.experts, cols, z.width), BF),
                    pltpu.SemaphoreType.DMA((z.experts,)),
                ]
                + scratch,
            ),
            out_shape=jax.ShapeDtypeStruct((z.experts, cols, z.width), BF),
            compiler_params=params(32),
            name=name,
        )(ids, table, *operands)

    anywhere = pl.BlockSpec(memory_space=pl.ANY)
    grad_down = total_call(
        total_down_kernel,
        [*bundles, grads_all, codes],
        [anywhere] * m + [whole((n, z.tokens, z.width)), whole(code_shape)],
        z.down_cols,
        [pltpu.VMEM((z.slots, z.rows, z.width), BF), pltpu.SemaphoreType.DMA((m,))],
        "down_grads",
    )
    grad_in = total_call(
        total_in_kernel,
        [*sides, *gathered],
        [anywhere] * (m + 2 * n - 1),
        z.in_cols,
        [
            pltpu.VMEM((n, z.all_rows, z.width), BF),
            pltpu.SemaphoreType.DMA((m,)),
            pltpu.SemaphoreType.DMA,
            pltpu.SemaphoreType.DMA((n - 1,)),
            pltpu.SemaphoreType.DMA((n - 1,)),
        ],
        "in_grads",
    )
    return grad_tokens, grad_routes.T, grad_in, grad_down


def solution(mesh):
    return jax.shard_map(
        body,
        mesh=mesh,
        in_specs=(
            P(("groups", "ep"), "sub"),
            P(("groups", "ep"), None),
            P(("groups", "ep"), None),
            P(("groups", "ep"), None),
            P("groups", None),
            P(("groups", "ep")),
            P(("groups", "ep"), None, None, "sub"),
            P(("groups", "ep"), None, None),
            P(("groups", "ep"), None, "sub"),
            P(("groups", "ep"), None, "sub"),
        ),
        out_specs=(
            P(("groups", "ep"), "sub"),
            P(("groups", "ep"), None),
            P("groups", "ep", "sub"),
            P("groups", "ep", "sub"),
        ),
        check_vma=False,
    )
```

```python
import functools
import math

import jax
import jax.numpy as jnp
from jax import lax
from jax.experimental import pallas as pl
from jax.experimental.pallas import tpu as pltpu
from jax.sharding import PartitionSpec as P

BF = jnp.bfloat16
F32 = jnp.float32
PER = 2


def nt(a, b):
    return lax.dot_general(a, b, (((1,), (1,)), ((), ())), preferred_element_type=F32)


def tn(a, b):
    return lax.dot_general(a, b, (((0,), (0,)), ((), ())), preferred_element_type=F32)


def nn(a, b):
    return jnp.dot(a, b, preferred_element_type=F32)


def whole(shape):
    zeros = (0,) * len(shape)
    return pl.BlockSpec(shape, lambda *_: zeros)


def smem():
    return pl.BlockSpec(memory_space=pltpu.SMEM)


def params(mib):
    return pltpu.CompilerParams(
        vmem_limit_bytes=mib * 1024 * 1024, dimension_semantics=("arbitrary",)
    )


class Sizes:
    def __init__(self, grad_out, routes, replica_slot, saved_input, weight_in, weight_down):
        self.ep = lax.axis_size("ep")
        self.sub = lax.axis_size("sub")
        self.tokens, self.width = grad_out.shape
        self.top = routes.shape[1]
        self.experts, self.reps = replica_slot.shape
        self.local = weight_in.shape[0]
        self.slots = self.ep * self.local
        self.cap = saved_input.shape[2]
        self.rows = self.ep * self.cap
        self.hidden = weight_down.shape[1]
        self.pair = weight_in.shape[1]
        self.all_rows = self.local * self.rows
        self.part = self.all_rows // self.sub
        self.block = math.gcd(self.rows, self.part)
        self.sources = self.block // self.cap
        self.blocks = self.all_rows // self.block
        self.part_blocks = self.part // self.block
        self.slot_blocks = self.rows // self.block
        self.in_cols = self.pair // self.ep
        self.down_cols = self.hidden // self.ep
        self.cols = self.in_cols + self.down_cols
        self.folds = self.width // self.tokens
        self.tail = 2 * self.slots // self.folds


def slot_table(z, table_ref, r):
    ids = lax.broadcasted_iota(jnp.int32, (z.slots, z.experts), 0)
    return (table_ref[r : r + 1, :] == ids).astype(F32).astype(BF)


def key_hits(z, count_ref, routes_ref, replica_ref, r, k):
    ids = lax.broadcasted_iota(jnp.int32, (z.experts, z.tokens), 0)
    live = lax.broadcasted_iota(jnp.int32, (1, z.tokens), 1) < count_ref[0]
    key = jnp.where(live & (replica_ref[k : k + 1, :] == r), routes_ref[k : k + 1, :], -1)
    return key == ids


def route_kernel(z, count_ref, grad_ref, weight_ref, routes_ref, replica_ref, table_ref, out_ref):
    weights = weight_ref[...].astype(F32)
    hits = jnp.zeros((z.slots, z.tokens), F32)
    loads = jnp.zeros((z.slots, z.tokens), F32)
    for r in range(z.reps):
        hit = jnp.zeros((z.experts, z.tokens), F32)
        load = jnp.zeros((z.experts, z.tokens), F32)
        for k in range(z.top):
            same = key_hits(z, count_ref, routes_ref, replica_ref, r, k)
            hit = jnp.where(same, 1.0, hit)
            load = jnp.where(same, weights[k : k + 1, :], load)
        table = slot_table(z, table_ref, r)
        hits = hits + nn(table, hit.astype(BF))
        loads = loads + nn(table, load.astype(BF))
    before = lax.broadcasted_iota(jnp.int32, (z.tokens, z.tokens), 0)
    after = lax.broadcasted_iota(jnp.int32, (z.tokens, z.tokens), 1)
    earlier = nn(hits.astype(BF), (before < after).astype(F32).astype(BF))
    code = jnp.where(hits > 0.5, earlier, -1.0)
    both = jnp.concatenate([code, loads], axis=0).astype(BF)
    out_ref[: z.tokens, :] = grad_ref[...]
    for b in range(z.folds):
        out_ref[z.tokens :, b * z.tokens : (b + 1) * z.tokens] = both[
            b * z.tail : (b + 1) * z.tail, :
        ]


def hidden_kernel(z, ids_ref, pair_ref, after_ref, other_ref, *refs):
    outs, sides = refs[:-1], refs[-1]
    pair = pair_ref[...]
    gate_pre = pair[:, : z.hidden].astype(F32)
    up = pair[:, z.hidden :].astype(F32)
    hidden = (gate_pre * (1.0 / (1.0 + jnp.exp(-gate_pre))) * up).astype(BF).T
    for q in range(z.ep):
        sides[q] = hidden[q * z.down_cols : (q + 1) * z.down_cols, :]
    for k in range(z.ep):
        outs[k][...] = sides[ids_ref[0] ^ k]


def block_place(z, block):
    slot = block // z.slot_blocks
    first = (block % z.slot_blocks) * z.sources
    return slot, first


def block_picks(z, codes_ref, slot, first):
    rows = lax.broadcasted_iota(jnp.int32, (z.cap, z.tokens), 0).astype(F32)
    for a in range(z.sources):
        code = codes_ref[first + a, pl.ds(slot, 1), :]
        yield a, rows == code


def block_scale(z, codes_ref, slot, first):
    parts = []
    for a, pick in block_picks(z, codes_ref, slot, first):
        load = codes_ref[first + a, pl.ds(z.slots + slot, 1), :]
        parts.append(jnp.sum(jnp.where(pick, load, 0.0), axis=1, keepdims=True))
    return jnp.concatenate(parts, axis=0)


def local_picks(z, codes_ref, source, me):
    code = codes_ref[source, pl.ds(pl.multiple_of(me * z.local, z.local), z.local), :]
    rows = lax.broadcasted_iota(jnp.int32, (z.local, z.cap, z.tokens), 1).astype(F32)
    pick = (code[:, None, :] == rows).astype(F32)
    return pick.reshape(z.local * z.cap, z.tokens).astype(BF)


def block_slot(z, mine, step):
    place = step // z.part_blocks
    return ((place ^ mine) * z.part_blocks + step % z.part_blocks) // z.slot_blocks


def weight_copy(weight_ref, held, sems, slot):
    return pltpu.make_async_copy(weight_ref.at[slot], held.at[slot], sems.at[slot])


def down_kernel(z, ids_ref, *refs):
    bufs = refs[: z.ep]
    weight_ref = refs[z.ep]
    parts = refs[2 * z.ep : 2 * z.ep + 2]
    grads_ref, codes_ref, rows_ref, held, sems = refs[2 * z.ep + 2 :]
    me, mine = ids_ref[0], ids_ref[1]
    step = pl.program_id(0)

    @pl.when(step == 0)
    def _():
        for s in range(z.local):
            weight_copy(weight_ref, held, sems, s).start()
        for k in range(z.ep):
            source = me ^ k
            grads_ref[source] = bufs[k][: z.tokens, :]
            for b in range(z.folds):
                codes_ref[source, b * z.tail : (b + 1) * z.tail, :] = bufs[k][
                    z.tokens :, b * z.tokens : (b + 1) * z.tokens
                ].astype(F32)
        for p in range(z.ep):
            rows = nn(local_picks(z, codes_ref, p, me), grads_ref[p]).astype(BF)
            rows_ref[:, p * z.cap : (p + 1) * z.cap, :] = rows.reshape(z.local, z.cap, z.width)

    place = step // z.part_blocks
    block = (place ^ mine) * z.part_blocks + step % z.part_blocks
    slot, first = block_place(z, block)
    start = pl.multiple_of(first * z.cap, z.block)

    @pl.when((step == 0) | (slot != block_slot(z, mine, step - 1)))
    def _():
        weight_copy(weight_ref, held, sems, slot).wait()

    partial = nt(rows_ref[slot, pl.ds(start, z.block), :], held[slot]).astype(BF)
    spot = pl.multiple_of((step % z.part_blocks) * z.block, z.block)
    for k in range(z.sub):

        @pl.when(place == k)
        def _():
            parts[k % 2][k // 2, pl.ds(spot, z.block), :] = partial


def gate_terms(z, pair, grad, scale):
    gate = pair[:, : z.hidden].astype(F32)
    up = pair[:, z.hidden :].astype(F32)
    sig = 1.0 / (1.0 + jnp.exp(-gate))
    act = gate * sig
    hidden = act * up
    scaled = scale * grad
    grad_gate = scaled * up * sig * (1.0 + gate * (1.0 - sig))
    grad_up = scaled * act
    return hidden, grad_gate.astype(BF), grad_up.astype(BF)


def pre_kernel(z, ids_ref, keep_ref, got_ref, pair_ref, codes_ref, *refs):
    downs, outs = refs[: z.ep], refs[z.ep : 2 * z.ep]
    bundle_ref, sides = refs[2 * z.ep :]

    @pl.when(pl.program_id(0) == 0)
    def _():
        for k in range(z.ep):
            bundle_ref[k] = downs[k][...]

    me = ids_ref[0]
    block = ids_ref[1] * z.part_blocks + pl.program_id(0)
    slot, first = block_place(z, block)
    scale = block_scale(z, codes_ref, me * z.local + slot, first)
    grad = keep_ref[0].astype(F32) + got_ref[0].astype(F32)
    turned = grad.astype(BF).T
    spot = pl.multiple_of(pl.program_id(0) * z.block, z.block)
    for q in range(z.ep):
        bundle_ref[z.ep + q, :, pl.ds(spot, z.block)] = turned[
            q * z.down_cols : (q + 1) * z.down_cols, :
        ]
    _, grad_gate, grad_up = gate_terms(z, pair_ref[...], grad, scale)
    pre = jnp.concatenate([grad_gate.T, grad_up.T], axis=0)
    for q in range(z.ep):
        sides[q] = pre[q * z.in_cols : (q + 1) * z.in_cols, :]
    for k in range(z.ep):
        outs[k][...] = sides[me ^ k]


def stack_kernel(*refs):
    for i, ref in enumerate(refs[:-1]):
        refs[-1][i] = ref[...]


def row_kernel(z, ids_ref, *refs):
    grads = refs[: z.sub]
    pair_ref, weight_ref, codes_ref, keep_ref, send_ref = refs[z.sub : z.sub + 5]
    rows_ref, marks, held, weights, sems = refs[z.sub + 5 :]
    me, mine = ids_ref[0], ids_ref[1]
    step = pl.program_id(0)
    place = step // z.part_blocks
    block = (place ^ mine) * z.part_blocks + step % z.part_blocks
    slot, first = block_place(z, block)

    @pl.when(step == 0)
    def _():
        for s in range(z.local):
            weight_copy(weight_ref, weights, sems, s).start()
        marks[...] = jnp.zeros_like(marks)

    spot = pl.multiple_of((step % z.part_blocks) * z.block, z.block)
    for k in range(z.sub):

        @pl.when(place == k)
        def _():
            turned = [grads[k][z.ep + q, :, pl.ds(spot, z.block)] for q in range(z.ep)]
            held[...] = jnp.concatenate(turned, axis=0).T

    grad = held[...].astype(F32)
    scale = block_scale(z, codes_ref, me * z.local + slot, first)
    hidden, grad_gate, grad_up = gate_terms(z, pair_ref[...], grad, scale)
    route = jnp.sum(hidden * grad, axis=1, keepdims=True).astype(BF).astype(F32)

    @pl.when((step == 0) | (slot != block_slot(z, mine, step - 1)))
    def _():
        weight_copy(weight_ref, weights, sems, slot).wait()

    rows = nn(grad_gate, weights[slot, : z.hidden, :]) + nn(grad_up, weights[slot, z.hidden :, :])
    start = pl.multiple_of(first * z.cap, z.block)
    rows_ref[slot, pl.ds(start, z.block), :] = rows.astype(BF)
    for a, pick in block_picks(z, codes_ref, me * z.local + slot, first):
        marks[first + a, pl.ds(me * z.local + slot, 1), :] = jnp.sum(
            jnp.where(pick, route[a * z.cap : (a + 1) * z.cap, :], 0.0), axis=0, keepdims=True
        )

    @pl.when(step == z.blocks - 1)
    def _():
        blank = jnp.zeros((z.slots, z.width - z.tokens), BF)
        for k in range(z.ep):
            source = me ^ k
            start = pl.multiple_of(source * z.cap, z.cap)
            rows = rows_ref[:, pl.ds(start, z.cap), :].reshape(z.local * z.cap, z.width)
            out_ref = send_ref if k % 2 else keep_ref
            picks = local_picks(z, codes_ref, source, me)
            out_ref[k // 2, : z.tokens, :] = tn(picks, rows).astype(BF)
            out_ref[k // 2, z.tokens :, : z.tokens] = marks[source].astype(BF)
            out_ref[k // 2, z.tokens :, z.tokens :] = blank


def halve_kernel(keep_ref, got_ref, out_keep, out_send):
    for i in range(out_keep.shape[0]):
        for j, out in enumerate((out_keep, out_send)):
            total = keep_ref[2 * i + j].astype(F32) + got_ref[2 * i + j].astype(F32)
            out[i] = total.astype(BF)


def token_kernel(z, count_ref, *refs):
    keep_ref, got_ref, routes_ref, replica_ref, table_ref, tokens_ref, route_ref = refs
    total = keep_ref[0].astype(F32) + got_ref[0].astype(F32)
    tokens_ref[...] = total[: z.tokens, :].astype(BF)
    rows = total[z.tokens :, : z.tokens].astype(BF)
    totals = [jnp.zeros((1, z.tokens), F32)] * z.top
    for r in range(z.reps):
        spread = tn(slot_table(z, table_ref, r), rows)
        for k in range(z.top):
            same = key_hits(z, count_ref, routes_ref, replica_ref, r, k)
            totals[k] += jnp.sum(jnp.where(same, spread, 0.0), axis=0, keepdims=True)
    route_ref[...] = jnp.concatenate(totals, axis=0).astype(BF)


def input_moves(z, me, own_ref, rights, lefts, inputs_ref, own_sem, right_sems, left_sems, act):
    act(pltpu.make_async_copy(own_ref, inputs_ref.at[me], own_sem))
    for d in range(1, z.ep):

        @pl.when(me >= d)
        def _():
            act(
                pltpu.make_async_copy(
                    rights[d - 1], inputs_ref.at[me - d], right_sems.at[d - 1]
                )
            )

        @pl.when(me + d < z.ep)
        def _():
            act(
                pltpu.make_async_copy(
                    lefts[d - 1], inputs_ref.at[me + d], left_sems.at[d - 1]
                )
            )


def expert_products(z, ids_ref, table_ref, turn, held, right_rows, out_ref, made, out_sems):
    mine = ids_ref[1]

    def out_copy(expert):
        return pltpu.make_async_copy(made.at[expert], out_ref.at[expert], out_sems.at[expert])

    def some(step, carry):
        for i in range(PER):
            expert = step * PER + i
            first = table_ref[0, expert]
            left, right = [], []
            for r in range(z.reps):
                slot_id = table_ref[r, expert]
                source = slot_id // z.local
                for b in range(z.slot_blocks):
                    block = (slot_id % z.local) * z.slot_blocks + b
                    part = (block // z.part_blocks) ^ mine
                    spot = pl.multiple_of((block % z.part_blocks) * z.block, z.block)
                    side = source ^ turn
                    if r:
                        side = jnp.where(slot_id == first, z.ep, side)
                    left.append(held[part, side, :, pl.ds(spot, z.block)])
                    right.append(right_rows(slot_id, block, b))
            left = jnp.concatenate(left, axis=1)
            made[expert] = nn(left, jnp.concatenate(right, axis=0)).astype(BF)
            out_copy(expert).start()
        return carry

    lax.fori_loop(0, z.experts // PER, some, 0)
    for expert in range(z.experts):
        out_copy(expert).wait()


def total_down_kernel(z, ids_ref, table_ref, *refs):
    sides = refs[: z.sub]
    grads_ref, codes_ref, out_ref, held, made, out_sems, scaled, sems = refs[z.sub :]

    def moves(act):
        for k in range(z.sub):
            act(
                pltpu.make_async_copy(
                    sides[k].at[pl.ds(0, z.ep)], held.at[k, pl.ds(0, z.ep)], sems.at[k]
                )
            )

    moves(lambda copy: copy.start())
    held[:, z.ep] = jnp.zeros_like(held[:, z.ep])
    rows = lax.broadcasted_iota(jnp.int32, (z.slots, z.cap, z.tokens), 1).astype(F32)
    for p in range(z.ep):
        code = codes_ref[p, : z.slots, :][:, None, :]
        load = codes_ref[p, z.slots :, :][:, None, :]
        pick = jnp.where(rows == code, load, 0.0).reshape(z.slots * z.cap, z.tokens)
        result = nn(pick.astype(BF), grads_ref[p]).astype(BF)
        scaled[:, p * z.cap : (p + 1) * z.cap, :] = result.reshape(z.slots, z.cap, z.width)
    moves(lambda copy: copy.wait())

    def right_rows(slot_id, block, b):
        return scaled[slot_id, b * z.block : (b + 1) * z.block, :]

    expert_products(z, ids_ref, table_ref, ids_ref[0], held, right_rows, out_ref, made, out_sems)


def total_in_kernel(z, ids_ref, table_ref, *refs):
    sides, refs = refs[: z.sub], refs[z.sub :]
    own_ref, rights, lefts = refs[0], refs[1 : z.ep], refs[z.ep : 2 * z.ep - 1]
    out_ref, held, made, out_sems, inputs_ref, sems, *other_sems = refs[2 * z.ep - 1 :]

    def moves(act):
        for k in range(z.sub):
            act(pltpu.make_async_copy(sides[k], held.at[k, pl.ds(0, z.ep)], sems.at[k]))
        input_moves(z, ids_ref[0], own_ref, rights, lefts, inputs_ref, *other_sems, act)

    moves(lambda copy: copy.start())
    held[:, z.ep] = jnp.zeros_like(held[:, z.ep])
    moves(lambda copy: copy.wait())

    def right_rows(slot_id, block, b):
        start = pl.multiple_of(block * z.block, z.block)
        return inputs_ref[slot_id // z.local, pl.ds(start, z.block), :]

    expert_products(z, ids_ref, table_ref, ids_ref[0], held, right_rows, out_ref, made, out_sems)


def swap(x, axis, size, bit):
    return lax.ppermute(x, axis, [(i, i ^ bit) for i in range(size)])


def spread_over(have, axis, size, bit):
    have = dict(have)
    while bit:
        for k in list(have):
            if k | bit not in have:
                have[k | bit] = swap(have[k], axis, size, bit)
        bit //= 2
    return [have[k] for k in range(size)]


def nothing(*refs):
    pass


def gate(values, after):
    anywhere = pl.BlockSpec(memory_space=pl.ANY)
    return pl.pallas_call(
        nothing,
        in_specs=[anywhere] * (len(values) + len(after)),
        out_specs=[anywhere] * len(values),
        out_shape=[jax.ShapeDtypeStruct(v.shape, v.dtype) for v in values],
        input_output_aliases={i: i for i in range(len(values))},
        compiler_params=pltpu.CompilerParams(vmem_limit_bytes=1024 * 1024),
        name="gate",
    )(*values, *after)


def chain_step(go, back, axis, size, d):
    go = lax.ppermute(go, axis, [(i, i + 1) for i in range(d - 1, size - 1)])
    back = lax.ppermute(back, axis, [(i, i - 1) for i in range(size - d, 0, -1)])
    return go, back


def body(
    grad_out,
    route_weight,
    routes,
    replica,
    replica_slot,
    token_count,
    saved_input,
    saved_gate_up,
    weight_in,
    weight_down,
):
    z = Sizes(grad_out, routes, replica_slot, saved_input, weight_in, weight_down)
    n, m = z.ep, z.sub
    ids = jnp.stack([lax.axis_index("ep"), lax.axis_index("sub")]).astype(jnp.int32)
    routes, replica, table = routes.T, replica.T, replica_slot.T
    route_weight = route_weight.T
    pair_rows = saved_gate_up.reshape(z.all_rows, z.pair)
    grad_shape = (z.tokens + z.tail, z.width)
    code_shape = (n, 2 * z.slots, z.tokens)
    inputs = saved_input.reshape(z.all_rows, z.width)

    routing = (grad_out, route_weight, routes, replica, table)
    buf = pl.pallas_call(
        functools.partial(route_kernel, z),
        out_shape=jax.ShapeDtypeStruct(grad_shape, BF),
        in_specs=[smem()] + [whole(a.shape) for a in routing],
        out_specs=whole(grad_shape),
        grid=(1,),
        compiler_params=params(60),
        name="route",
    )(token_count, *routing)
    bufs = [buf] + [swap(buf, "ep", n, k) for k in range(1, n)]

    chain = gate([inputs], [buf])
    downs = pl.pallas_call(
        functools.partial(hidden_kernel, z),
        grid_spec=pltpu.PrefetchScalarGridSpec(
            num_scalar_prefetch=1,
            grid=(z.part_blocks,),
            in_specs=[
                pl.BlockSpec((z.block, z.pair), lambda i, r: (r[1] * z.part_blocks + i, 0)),
                pl.BlockSpec(memory_space=pl.ANY),
                pl.BlockSpec(memory_space=pl.ANY),
            ],
            out_specs=[pl.BlockSpec((z.down_cols, z.block), lambda i, r: (0, i))] * n,
            scratch_shapes=[pltpu.VMEM((n, z.down_cols, z.block), BF)],
        ),
        out_shape=[jax.ShapeDtypeStruct((z.down_cols, z.part), BF)] * n,
        compiler_params=params(16),
        name="hidden_columns",
    )(ids, pair_rows, bufs[1], chain[0])
    downs = [downs[0]] + [swap(downs[k], "ep", n, k) for k in range(1, n)]

    def stack(pieces):
        shape = pieces[0].shape
        return pl.pallas_call(
            stack_kernel,
            in_specs=[whole(shape)] * n,
            out_specs=whole((n,) + shape),
            out_shape=jax.ShapeDtypeStruct((n,) + shape, BF),
            grid=(1,),
            compiler_params=params(8),
            name="stack_columns",
        )(*pieces)

    def halve(keep, got):
        half = (keep.shape[0] // 2,) + keep.shape[1:]
        return pl.pallas_call(
            halve_kernel,
            in_specs=[whole(keep.shape)] * 2,
            out_specs=[whole(half)] * 2,
            out_shape=[jax.ShapeDtypeStruct(half, BF)] * 2,
            grid=(1,),
            compiler_params=params(16),
            name="halve",
        )(keep, got)

    def row_block(i, ids_ref):
        place = i // z.part_blocks
        return (place ^ ids_ref[1]) * z.part_blocks + i % z.part_blocks

    part_shape = (m // 2, z.part, z.hidden)
    outs = pl.pallas_call(
        functools.partial(down_kernel, z),
        grid_spec=pltpu.PrefetchScalarGridSpec(
            num_scalar_prefetch=1,
            grid=(z.blocks,),
            in_specs=[whole(grad_shape)] * n
            + [pl.BlockSpec(memory_space=pltpu.HBM)]
            + [pl.BlockSpec(memory_space=pl.ANY)] * (n - 1),
            out_specs=[whole(part_shape)] * 2
            + [whole((n, z.tokens, z.width)), whole(code_shape)],
            scratch_shapes=[
                pltpu.VMEM((z.local, z.rows, z.width), BF),
                pltpu.VMEM((z.local, z.hidden, z.width), BF),
                pltpu.SemaphoreType.DMA((z.local,)),
            ],
        ),
        out_shape=[jax.ShapeDtypeStruct(part_shape, BF)] * 2
        + [
            jax.ShapeDtypeStruct((n, z.tokens, z.width), BF),
            jax.ShapeDtypeStruct(code_shape, F32),
        ],
        compiler_params=params(48),
        name="hidden_partials",
    )(ids, *bufs, weight_down, *downs[1:])
    keep, send, grads_all, codes = outs
    chain = gate(chain, downs[1:])
    steps = [chain_step(chain[0], chain[0], "ep", n, 1)]
    got = swap(send, "sub", m, 1)
    bit = 2
    while bit < m:
        keep, send = halve(keep, got)
        got = swap(send, "sub", m, bit)
        bit *= 2
    *pieces, bundle = pl.pallas_call(
        functools.partial(pre_kernel, z),
        grid_spec=pltpu.PrefetchScalarGridSpec(
            num_scalar_prefetch=1,
            grid=(z.part_blocks,),
            in_specs=[pl.BlockSpec((1, z.block, z.hidden), lambda i, r: (0, i, 0))] * 2
            + [
                pl.BlockSpec((z.block, z.pair), lambda i, r: (r[1] * z.part_blocks + i, 0)),
                whole(code_shape),
            ]
            + [whole((z.down_cols, z.part))] * n,
            out_specs=[pl.BlockSpec((z.in_cols, z.block), lambda i, r: (0, i))] * n
            + [whole((2 * n, z.down_cols, z.part))],
            scratch_shapes=[pltpu.VMEM((n, z.in_cols, z.block), BF)],
        ),
        out_shape=[jax.ShapeDtypeStruct((z.in_cols, z.part), BF)] * n
        + [jax.ShapeDtypeStruct((2 * n, z.down_cols, z.part), BF)],
        compiler_params=params(16),
        name="pre_grads",
    )(ids, keep, got, pair_rows, codes, *downs)
    pieces = [pieces[0]] + [swap(pieces[k], "ep", n, k) for k in range(1, n)]
    columns = stack(pieces)
    bundle = gate([bundle], pieces[1:2])[0]
    steps[0] = gate(steps[0], pieces[1:])
    steps.append(chain_step(*steps[0], "ep", n, 2))
    bundles = spread_over({0: bundle}, "sub", m, m // 2)
    sides = {0: gate([columns], [bundles[m // 2]])[0]}
    sides[m // 2] = swap(sides[0], "sub", m, m // 2)

    back_shape = (n // 2, z.tokens + z.slots, z.width)
    keep, send = pl.pallas_call(
        functools.partial(row_kernel, z),
        grid_spec=pltpu.PrefetchScalarGridSpec(
            num_scalar_prefetch=1,
            grid=(z.blocks,),
            in_specs=[whole(bundle.shape)] * m
            + [
                pl.BlockSpec((z.block, z.pair), lambda i, r: (row_block(i, r), 0)),
                pl.BlockSpec(memory_space=pltpu.HBM),
                whole(code_shape),
            ],
            out_specs=[whole(back_shape)] * 2,
            scratch_shapes=[
                pltpu.VMEM((z.local, z.rows, z.width), BF),
                pltpu.VMEM((n, z.slots, z.tokens), F32),
                pltpu.VMEM((z.block, z.hidden), BF),
                pltpu.VMEM((z.local, z.pair, z.width), BF),
                pltpu.SemaphoreType.DMA((z.local,)),
            ],
        ),
        out_shape=[jax.ShapeDtypeStruct(back_shape, BF)] * 2,
        compiler_params=params(46),
        name="row_grads",
    )(ids, *bundles, pair_rows, weight_in, codes)
    steps[1] = gate(steps[1], [keep])
    for d in range(3, n):
        steps.append(chain_step(*steps[-1], "ep", n, d))
    gathered = [inputs] + [go for go, _ in steps] + [back for _, back in steps]
    sides[m // 2] = gate([sides[m // 2]], [keep])[0]
    sides = spread_over(sides, "sub", m, m // 4)
    got = swap(send, "ep", n, 1)
    bit = 2
    while bit < n:
        keep, send = halve(keep, got)
        got = swap(send, "ep", n, bit)
        bit *= 2

    grad_tokens, grad_routes = pl.pallas_call(
        functools.partial(token_kernel, z),
        out_shape=[
            jax.ShapeDtypeStruct((z.tokens, z.width), BF),
            jax.ShapeDtypeStruct((z.top, z.tokens), BF),
        ],
        in_specs=[smem()] + [whole(a.shape) for a in (keep, got, routes, replica, table)],
        out_specs=[whole((z.tokens, z.width)), whole((z.top, z.tokens))],
        grid=(1,),
        compiler_params=params(16),
        name="token_grads",
    )(token_count, keep, got, routes, replica, table)

    def total_call(kernel, operands, specs, cols, scratch, name):
        return pl.pallas_call(
            functools.partial(kernel, z),
            grid_spec=pltpu.PrefetchScalarGridSpec(
                num_scalar_prefetch=2,
                grid=(1,),
                in_specs=specs,
                out_specs=pl.BlockSpec(memory_space=pl.ANY),
                scratch_shapes=[
                    pltpu.VMEM((m, n + 1, cols, z.part), BF),
                    pltpu.VMEM((z.experts, cols, z.width), BF),
                    pltpu.SemaphoreType.DMA((z.experts,)),
                ]
                + scratch,
            ),
            out_shape=jax.ShapeDtypeStruct((z.experts, cols, z.width), BF),
            compiler_params=params(32),
            name=name,
        )(ids, table, *operands)

    anywhere = pl.BlockSpec(memory_space=pl.ANY)
    grad_down = total_call(
        total_down_kernel,
        [*bundles, grads_all, codes],
        [anywhere] * m + [whole((n, z.tokens, z.width)), whole(code_shape)],
        z.down_cols,
        [pltpu.VMEM((z.slots, z.rows, z.width), BF), pltpu.SemaphoreType.DMA((m,))],
        "down_grads",
    )
    grad_in = total_call(
        total_in_kernel,
        [*sides, *gathered],
        [anywhere] * (m + 2 * n - 1),
        z.in_cols,
        [
            pltpu.VMEM((n, z.all_rows, z.width), BF),
            pltpu.SemaphoreType.DMA((m,)),
            pltpu.SemaphoreType.DMA,
            pltpu.SemaphoreType.DMA((n - 1,)),
            pltpu.SemaphoreType.DMA((n - 1,)),
        ],
        "in_grads",
    )
    return grad_tokens, grad_routes.T, grad_in, grad_down


def solution(mesh):
    return jax.shard_map(
        body,
        mesh=mesh,
        in_specs=(
            P(("groups", "ep"), "sub"),
            P(("groups", "ep"), None),
            P(("groups", "ep"), None),
            P(("groups", "ep"), None),
            P("groups", None),
            P(("groups", "ep")),
            P(("groups", "ep"), None, None, "sub"),
            P(("groups", "ep"), None, None),
            P(("groups", "ep"), None, "sub"),
            P(("groups", "ep"), None, "sub"),
        ),
        out_specs=(
            P(("groups", "ep"), "sub"),
            P(("groups", "ep"), None),
            P("groups", "ep", "sub"),
            P("groups", "ep", "sub"),
        ),
        check_vma=False,
    )
```

```python
import functools
import math

import jax
import jax.numpy as jnp
from jax import lax
from jax.experimental import pallas as pl
from jax.experimental.pallas import tpu as pltpu
from jax.sharding import PartitionSpec as P

BF = jnp.bfloat16
F32 = jnp.float32
PER = 2


def nt(a, b):
    return lax.dot_general(a, b, (((1,), (1,)), ((), ())), preferred_element_type=F32)


def tn(a, b):
    return lax.dot_general(a, b, (((0,), (0,)), ((), ())), preferred_element_type=F32)


def nn(a, b):
    return jnp.dot(a, b, preferred_element_type=F32)


def whole(shape):
    zeros = (0,) * len(shape)
    return pl.BlockSpec(shape, lambda *_: zeros)


def smem():
    return pl.BlockSpec(memory_space=pltpu.SMEM)


def params(mib):
    return pltpu.CompilerParams(
        vmem_limit_bytes=mib * 1024 * 1024, dimension_semantics=("arbitrary",)
    )


class Sizes:
    def __init__(self, grad_out, routes, replica_slot, saved_input, weight_in, weight_down):
        self.ep = lax.axis_size("ep")
        self.sub = lax.axis_size("sub")
        self.tokens, self.width = grad_out.shape
        self.top = routes.shape[1]
        self.experts, self.reps = replica_slot.shape
        self.local = weight_in.shape[0]
        self.slots = self.ep * self.local
        self.cap = saved_input.shape[2]
        self.rows = self.ep * self.cap
        self.hidden = weight_down.shape[1]
        self.pair = weight_in.shape[1]
        self.all_rows = self.local * self.rows
        self.part = self.all_rows // self.sub
        self.block = math.gcd(self.rows, self.part)
        self.sources = self.block // self.cap
        self.blocks = self.all_rows // self.block
        self.part_blocks = self.part // self.block
        self.slot_blocks = self.rows // self.block
        self.in_cols = self.pair // self.ep
        self.down_cols = self.hidden // self.ep
        self.cols = self.in_cols + self.down_cols
        self.folds = self.width // self.tokens
        self.tail = 2 * self.slots // self.folds


def slot_table(z, table_ref, r):
    ids = lax.broadcasted_iota(jnp.int32, (z.slots, z.experts), 0)
    return (table_ref[r : r + 1, :] == ids).astype(F32).astype(BF)


def key_hits(z, count_ref, routes_ref, replica_ref, r, k):
    ids = lax.broadcasted_iota(jnp.int32, (z.experts, z.tokens), 0)
    live = lax.broadcasted_iota(jnp.int32, (1, z.tokens), 1) < count_ref[0]
    key = jnp.where(live & (replica_ref[k : k + 1, :] == r), routes_ref[k : k + 1, :], -1)
    return key == ids


def route_kernel(z, count_ref, grad_ref, weight_ref, routes_ref, replica_ref, table_ref, out_ref):
    weights = weight_ref[...].astype(F32)
    hits = jnp.zeros((z.slots, z.tokens), F32)
    loads = jnp.zeros((z.slots, z.tokens), F32)
    for r in range(z.reps):
        hit = jnp.zeros((z.experts, z.tokens), F32)
        load = jnp.zeros((z.experts, z.tokens), F32)
        for k in range(z.top):
            same = key_hits(z, count_ref, routes_ref, replica_ref, r, k)
            hit = jnp.where(same, 1.0, hit)
            load = jnp.where(same, weights[k : k + 1, :], load)
        table = slot_table(z, table_ref, r)
        hits = hits + nn(table, hit.astype(BF))
        loads = loads + nn(table, load.astype(BF))
    before = lax.broadcasted_iota(jnp.int32, (z.tokens, z.tokens), 0)
    after = lax.broadcasted_iota(jnp.int32, (z.tokens, z.tokens), 1)
    earlier = nn(hits.astype(BF), (before < after).astype(F32).astype(BF))
    code = jnp.where(hits > 0.5, earlier, -1.0)
    both = jnp.concatenate([code, loads], axis=0).astype(BF)
    out_ref[: z.tokens, :] = grad_ref[...]
    for b in range(z.folds):
        out_ref[z.tokens :, b * z.tokens : (b + 1) * z.tokens] = both[
            b * z.tail : (b + 1) * z.tail, :
        ]


def block_place(z, block):
    slot = block // z.slot_blocks
    first = (block % z.slot_blocks) * z.sources
    return slot, first


def block_picks(z, codes_ref, slot, first):
    rows = lax.broadcasted_iota(jnp.int32, (z.cap, z.tokens), 0).astype(F32)
    for a in range(z.sources):
        code = codes_ref[first + a, pl.ds(slot, 1), :]
        yield a, rows == code


def block_scale(z, codes_ref, slot, first):
    parts = []
    for a, pick in block_picks(z, codes_ref, slot, first):
        load = codes_ref[first + a, pl.ds(z.slots + slot, 1), :]
        parts.append(jnp.sum(jnp.where(pick, load, 0.0), axis=1, keepdims=True))
    return jnp.concatenate(parts, axis=0)


def local_picks(z, codes_ref, source, me):
    code = codes_ref[source, pl.ds(pl.multiple_of(me * z.local, z.local), z.local), :]
    rows = lax.broadcasted_iota(jnp.int32, (z.local, z.cap, z.tokens), 1).astype(F32)
    pick = (code[:, None, :] == rows).astype(F32)
    return pick.reshape(z.local * z.cap, z.tokens).astype(BF)


def block_slot(z, mine, step):
    place = step // z.part_blocks
    return ((place ^ mine) * z.part_blocks + step % z.part_blocks) // z.slot_blocks


def weight_copy(weight_ref, held, sems, slot):
    return pltpu.make_async_copy(weight_ref.at[slot], held.at[slot], sems.at[slot])


def down_kernel(z, ids_ref, *refs):
    bufs = refs[: z.ep]
    weight_ref = refs[z.ep]
    parts = refs[z.ep + 1 : z.ep + 3]
    grads_ref, codes_ref, rows_ref, held, sems = refs[z.ep + 3 :]
    me, mine = ids_ref[0], ids_ref[1]
    step = pl.program_id(0)

    @pl.when(step == 0)
    def _():
        for s in range(z.local):
            weight_copy(weight_ref, held, sems, s).start()
        for k in range(z.ep):
            source = me ^ k
            grads_ref[source] = bufs[k][: z.tokens, :]
            for b in range(z.folds):
                codes_ref[source, b * z.tail : (b + 1) * z.tail, :] = bufs[k][
                    z.tokens :, b * z.tokens : (b + 1) * z.tokens
                ].astype(F32)
        for p in range(z.ep):
            rows = nn(local_picks(z, codes_ref, p, me), grads_ref[p]).astype(BF)
            rows_ref[:, p * z.cap : (p + 1) * z.cap, :] = rows.reshape(z.local, z.cap, z.width)

    place = step // z.part_blocks
    block = (place ^ mine) * z.part_blocks + step % z.part_blocks
    slot, first = block_place(z, block)
    start = pl.multiple_of(first * z.cap, z.block)

    @pl.when((step == 0) | (slot != block_slot(z, mine, step - 1)))
    def _():
        weight_copy(weight_ref, held, sems, slot).wait()

    partial = nt(rows_ref[slot, pl.ds(start, z.block), :], held[slot]).astype(BF)
    spot = pl.multiple_of((step % z.part_blocks) * z.block, z.block)
    for k in range(z.sub):

        @pl.when(place == k)
        def _():
            parts[k % 2][k // 2, pl.ds(spot, z.block), :] = partial


def gate_terms(z, pair, grad, scale):
    gate = pair[:, : z.hidden].astype(F32)
    up = pair[:, z.hidden :].astype(F32)
    sig = 1.0 / (1.0 + jnp.exp(-gate))
    act = gate * sig
    hidden = act * up
    scaled = scale * grad
    grad_gate = scaled * up * sig * (1.0 + gate * (1.0 - sig))
    grad_up = scaled * act
    return hidden, grad_gate.astype(BF), grad_up.astype(BF)


def pre_kernel(z, ids_ref, keep_ref, got_ref, pair_ref, codes_ref, *refs):
    outs, (grad_ref, sides) = refs[: z.ep], refs[z.ep :]
    me = ids_ref[0]
    block = ids_ref[1] * z.part_blocks + pl.program_id(0)
    slot, first = block_place(z, block)
    scale = block_scale(z, codes_ref, me * z.local + slot, first)
    grad = keep_ref[0].astype(F32) + got_ref[0].astype(F32)
    grad_ref[...] = grad.astype(BF)
    hidden, grad_gate, grad_up = gate_terms(z, pair_ref[...], grad, scale)
    hidden = hidden.astype(BF).T
    pre = jnp.concatenate([grad_gate.T, grad_up.T], axis=0)
    for q in range(z.ep):
        sides[q, : z.in_cols, :] = pre[q * z.in_cols : (q + 1) * z.in_cols, :]
        sides[q, z.in_cols :, :] = hidden[q * z.down_cols : (q + 1) * z.down_cols, :]
    for k in range(z.ep):
        outs[k][...] = sides[me ^ k]


def stack_kernel(z, *refs):
    refs = refs[: z.ep] + refs[-2:]
    for k in range(z.ep):
        refs[-2][k] = refs[k][: z.in_cols, :]
        refs[-1][k] = refs[k][z.in_cols :, :]


def row_kernel(z, ids_ref, *refs):
    grads = refs[: z.sub]
    pair_ref, weight_ref, codes_ref, keep_ref, send_ref = refs[z.sub : z.sub + 5]
    rows_ref, marks, held, weights, sems = refs[z.sub + 5 :]
    me, mine = ids_ref[0], ids_ref[1]
    step = pl.program_id(0)
    place = step // z.part_blocks
    block = (place ^ mine) * z.part_blocks + step % z.part_blocks
    slot, first = block_place(z, block)

    @pl.when(step == 0)
    def _():
        for s in range(z.local):
            weight_copy(weight_ref, weights, sems, s).start()
        marks[...] = jnp.zeros_like(marks)

    spot = pl.multiple_of((step % z.part_blocks) * z.block, z.block)
    for k in range(z.sub):

        @pl.when(place == k)
        def _():
            held[...] = grads[k][pl.ds(spot, z.block), :]

    grad = held[...].astype(F32)
    scale = block_scale(z, codes_ref, me * z.local + slot, first)
    hidden, grad_gate, grad_up = gate_terms(z, pair_ref[...], grad, scale)
    route = jnp.sum(hidden * grad, axis=1, keepdims=True).astype(BF).astype(F32)

    @pl.when((step == 0) | (slot != block_slot(z, mine, step - 1)))
    def _():
        weight_copy(weight_ref, weights, sems, slot).wait()

    rows = nn(grad_gate, weights[slot, : z.hidden, :]) + nn(grad_up, weights[slot, z.hidden :, :])
    start = pl.multiple_of(first * z.cap, z.block)
    rows_ref[slot, pl.ds(start, z.block), :] = rows.astype(BF)
    for a, pick in block_picks(z, codes_ref, me * z.local + slot, first):
        marks[first + a, pl.ds(me * z.local + slot, 1), :] = jnp.sum(
            jnp.where(pick, route[a * z.cap : (a + 1) * z.cap, :], 0.0), axis=0, keepdims=True
        )

    @pl.when(step == z.blocks - 1)
    def _():
        blank = jnp.zeros((z.slots, z.width - z.tokens), BF)
        for k in range(z.ep):
            source = me ^ k
            start = pl.multiple_of(source * z.cap, z.cap)
            rows = rows_ref[:, pl.ds(start, z.cap), :].reshape(z.local * z.cap, z.width)
            out_ref = send_ref if k % 2 else keep_ref
            picks = local_picks(z, codes_ref, source, me)
            out_ref[k // 2, : z.tokens, :] = tn(picks, rows).astype(BF)
            out_ref[k // 2, z.tokens :, : z.tokens] = marks[source].astype(BF)
            out_ref[k // 2, z.tokens :, z.tokens :] = blank


def halve_kernel(keep_ref, got_ref, out_keep, out_send):
    for i in range(out_keep.shape[0]):
        for j, out in enumerate((out_keep, out_send)):
            total = keep_ref[2 * i + j].astype(F32) + got_ref[2 * i + j].astype(F32)
            out[i] = total.astype(BF)


def token_kernel(z, count_ref, *refs):
    keep_ref, got_ref, routes_ref, replica_ref, table_ref, tokens_ref, route_ref = refs
    total = keep_ref[0].astype(F32) + got_ref[0].astype(F32)
    tokens_ref[...] = total[: z.tokens, :].astype(BF)
    rows = total[z.tokens :, : z.tokens].astype(BF)
    totals = [jnp.zeros((1, z.tokens), F32)] * z.top
    for r in range(z.reps):
        spread = tn(slot_table(z, table_ref, r), rows)
        for k in range(z.top):
            same = key_hits(z, count_ref, routes_ref, replica_ref, r, k)
            totals[k] += jnp.sum(jnp.where(same, spread, 0.0), axis=0, keepdims=True)
    route_ref[...] = jnp.concatenate(totals, axis=0).astype(BF)


def input_moves(z, me, own_ref, rights, lefts, inputs_ref, own_sem, right_sems, left_sems, act):
    act(pltpu.make_async_copy(own_ref, inputs_ref.at[me], own_sem))
    for d in range(1, z.ep):

        @pl.when(me >= d)
        def _():
            act(
                pltpu.make_async_copy(
                    rights[d - 1], inputs_ref.at[me - d], right_sems.at[d - 1]
                )
            )

        @pl.when(me + d < z.ep)
        def _():
            act(
                pltpu.make_async_copy(
                    lefts[d - 1], inputs_ref.at[me + d], left_sems.at[d - 1]
                )
            )


def expert_products(z, ids_ref, table_ref, turn, held, right_rows, out_ref, made, out_sems):
    mine = ids_ref[1]

    def out_copy(expert):
        return pltpu.make_async_copy(made.at[expert], out_ref.at[expert], out_sems.at[expert])

    def some(step, carry):
        for i in range(PER):
            expert = step * PER + i
            first = table_ref[0, expert]
            left, right = [], []
            for r in range(z.reps):
                slot_id = table_ref[r, expert]
                source = slot_id // z.local
                for b in range(z.slot_blocks):
                    block = (slot_id % z.local) * z.slot_blocks + b
                    part = (block // z.part_blocks) ^ mine
                    spot = pl.multiple_of((block % z.part_blocks) * z.block, z.block)
                    side = source ^ turn
                    if r:
                        side = jnp.where(slot_id == first, z.ep, side)
                    left.append(held[part, side, :, pl.ds(spot, z.block)])
                    right.append(right_rows(slot_id, block, b))
            left = jnp.concatenate(left, axis=1)
            made[expert] = nn(left, jnp.concatenate(right, axis=0)).astype(BF)
            out_copy(expert).start()
        return carry

    lax.fori_loop(0, z.experts // PER, some, 0)
    for expert in range(z.experts):
        out_copy(expert).wait()


def total_down_kernel(z, ids_ref, table_ref, *refs):
    sides = refs[: z.sub]
    grads_ref, codes_ref, out_ref, token_ref, held, made, out_sems, scaled, sems = refs[z.sub :]
    token_ref[...] = jnp.zeros_like(token_ref)

    def moves(act):
        for k in range(z.sub):
            act(
                pltpu.make_async_copy(
                    sides[k], held.at[k, pl.ds(0, z.ep)], sems.at[k]
                )
            )

    moves(lambda copy: copy.start())
    held[:, z.ep] = jnp.zeros_like(held[:, z.ep])
    rows = lax.broadcasted_iota(jnp.int32, (z.slots, z.cap, z.tokens), 1).astype(F32)
    for p in range(z.ep):
        code = codes_ref[p, : z.slots, :][:, None, :]
        load = codes_ref[p, z.slots :, :][:, None, :]
        pick = jnp.where(rows == code, load, 0.0).reshape(z.slots * z.cap, z.tokens)
        result = nn(pick.astype(BF), grads_ref[p]).astype(BF)
        scaled[:, p * z.cap : (p + 1) * z.cap, :] = result.reshape(z.slots, z.cap, z.width)
    moves(lambda copy: copy.wait())

    def right_rows(slot_id, block, b):
        return scaled[slot_id, b * z.block : (b + 1) * z.block, :]

    expert_products(z, ids_ref, table_ref, ids_ref[0], held, right_rows, out_ref, made, out_sems)


def total_in_kernel(z, ids_ref, table_ref, *refs):
    sides, refs = refs[: z.sub], refs[z.sub :]
    own_ref, rights, lefts = refs[0], refs[1 : z.ep], refs[z.ep : 2 * z.ep - 1]
    out_ref, token_ref, held, made, out_sems, inputs_ref, sems, *other_sems = refs[2 * z.ep - 1 :]
    token_ref[...] = jnp.zeros_like(token_ref)

    def moves(act):
        for k in range(z.sub):
            act(pltpu.make_async_copy(sides[k], held.at[k, pl.ds(0, z.ep)], sems.at[k]))
        input_moves(z, ids_ref[0], own_ref, rights, lefts, inputs_ref, *other_sems, act)

    moves(lambda copy: copy.start())
    held[:, z.ep] = jnp.zeros_like(held[:, z.ep])
    moves(lambda copy: copy.wait())

    def right_rows(slot_id, block, b):
        start = pl.multiple_of(block * z.block, z.block)
        return inputs_ref[slot_id // z.local, pl.ds(start, z.block), :]

    expert_products(z, ids_ref, table_ref, ids_ref[0], held, right_rows, out_ref, made, out_sems)


def swap(x, axis, size, bit):
    return lax.ppermute(x, axis, [(i, i ^ bit) for i in range(size)])


def spread_over(have, axis, size, bit):
    have = dict(have)
    while bit:
        for k in list(have):
            if k | bit not in have:
                have[k | bit] = swap(have[k], axis, size, bit)
        bit //= 2
    return [have[k] for k in range(size)]


def nothing(*refs):
    pass


def gate(values, after):
    anywhere = pl.BlockSpec(memory_space=pl.ANY)
    return pl.pallas_call(
        nothing,
        in_specs=[anywhere] * (len(values) + len(after)),
        out_specs=[anywhere] * len(values),
        out_shape=[jax.ShapeDtypeStruct(v.shape, v.dtype) for v in values],
        input_output_aliases={i: i for i in range(len(values))},
        compiler_params=pltpu.CompilerParams(vmem_limit_bytes=1024 * 1024),
        name="gate",
    )(*values, *after)


def chain_step(go, back, axis, size, d):
    go = lax.ppermute(go, axis, [(i, i + 1) for i in range(d - 1, size - 1)])
    back = lax.ppermute(back, axis, [(i, i - 1) for i in range(size - d, 0, -1)])
    return go, back


def body(
    grad_out,
    route_weight,
    routes,
    replica,
    replica_slot,
    token_count,
    saved_input,
    saved_gate_up,
    weight_in,
    weight_down,
):
    z = Sizes(grad_out, routes, replica_slot, saved_input, weight_in, weight_down)
    n, m = z.ep, z.sub
    ids = jnp.stack([lax.axis_index("ep"), lax.axis_index("sub")]).astype(jnp.int32)
    routes, replica, table = routes.T, replica.T, replica_slot.T
    route_weight = route_weight.T
    pair_rows = saved_gate_up.reshape(z.all_rows, z.pair)
    grad_shape = (z.tokens + z.tail, z.width)
    code_shape = (n, 2 * z.slots, z.tokens)
    inputs = saved_input.reshape(z.all_rows, z.width)

    routing = (grad_out, route_weight, routes, replica, table)
    buf = pl.pallas_call(
        functools.partial(route_kernel, z),
        out_shape=jax.ShapeDtypeStruct(grad_shape, BF),
        in_specs=[smem()] + [whole(a.shape) for a in routing],
        out_specs=whole(grad_shape),
        grid=(1,),
        compiler_params=params(60),
        name="route",
    )(token_count, *routing)
    bufs = [buf] + [swap(buf, "ep", n, k) for k in range(1, n)]

    chain = gate([inputs], bufs[1:])
    steps = [chain_step(chain[0], chain[0], "ep", n, 1)]
    steps.append(chain_step(*steps[0], "ep", n, 2))

    def stack(pieces, after):
        shapes = [(n, z.in_cols, z.part), (n, z.down_cols, z.part)]
        return pl.pallas_call(
            functools.partial(stack_kernel, z),
            in_specs=[whole((z.cols, z.part))] * n + [pl.BlockSpec(memory_space=pl.ANY)],
            out_specs=[whole(shape) for shape in shapes],
            out_shape=[jax.ShapeDtypeStruct(shape, BF) for shape in shapes],
            grid=(1,),
            compiler_params=params(12),
            name="stack_columns",
        )(*pieces, after)

    def halve(keep, got):
        half = (keep.shape[0] // 2,) + keep.shape[1:]
        return pl.pallas_call(
            halve_kernel,
            in_specs=[whole(keep.shape)] * 2,
            out_specs=[whole(half)] * 2,
            out_shape=[jax.ShapeDtypeStruct(half, BF)] * 2,
            grid=(1,),
            compiler_params=params(16),
            name="halve",
        )(keep, got)

    def row_block(i, ids_ref):
        place = i // z.part_blocks
        return (place ^ ids_ref[1]) * z.part_blocks + i % z.part_blocks

    part_shape = (m // 2, z.part, z.hidden)
    outs = pl.pallas_call(
        functools.partial(down_kernel, z),
        grid_spec=pltpu.PrefetchScalarGridSpec(
            num_scalar_prefetch=1,
            grid=(z.blocks,),
            in_specs=[whole(grad_shape)] * n + [pl.BlockSpec(memory_space=pltpu.HBM)],
            out_specs=[whole(part_shape)] * 2
            + [whole((n, z.tokens, z.width)), whole(code_shape)],
            scratch_shapes=[
                pltpu.VMEM((z.local, z.rows, z.width), BF),
                pltpu.VMEM((z.local, z.hidden, z.width), BF),
                pltpu.SemaphoreType.DMA((z.local,)),
            ],
        ),
        out_shape=[jax.ShapeDtypeStruct(part_shape, BF)] * 2
        + [
            jax.ShapeDtypeStruct((n, z.tokens, z.width), BF),
            jax.ShapeDtypeStruct(code_shape, F32),
        ],
        compiler_params=params(48),
        name="hidden_partials",
    )(ids, *bufs, weight_down)
    keep, send, grads_all, codes = outs
    send = gate([send], steps[0])[0]
    got = swap(send, "sub", m, 1)
    bit = 2
    while bit < m:
        keep, send = halve(keep, got)
        got = swap(send, "sub", m, bit)
        bit *= 2
    *pieces, grad_part = pl.pallas_call(
        functools.partial(pre_kernel, z),
        grid_spec=pltpu.PrefetchScalarGridSpec(
            num_scalar_prefetch=1,
            grid=(z.part_blocks,),
            in_specs=[pl.BlockSpec((1, z.block, z.hidden), lambda i, r: (0, i, 0))] * 2
            + [
                pl.BlockSpec((z.block, z.pair), lambda i, r: (r[1] * z.part_blocks + i, 0)),
                whole(code_shape),
            ],
            out_specs=[pl.BlockSpec((z.cols, z.block), lambda i, r: (0, i))] * n
            + [pl.BlockSpec((z.block, z.hidden), lambda i, r: (i, 0))],
            scratch_shapes=[pltpu.VMEM((n, z.cols, z.block), BF)],
        ),
        out_shape=[jax.ShapeDtypeStruct((z.cols, z.part), BF)] * n
        + [jax.ShapeDtypeStruct((z.part, z.hidden), BF)],
        compiler_params=params(16),
        name="pre_grads",
    )(ids, keep, got, pair_rows, codes)
    late = gate(pieces[1:], steps[1])
    pieces = pieces[:1] + [swap(a, "ep", n, k) for k, a in enumerate(late, 1)]
    grad_parts = spread_over({0: grad_part}, "sub", m, m // 2)

    back_shape = (n // 2, z.tokens + z.slots, z.width)
    keep, send = pl.pallas_call(
        functools.partial(row_kernel, z),
        grid_spec=pltpu.PrefetchScalarGridSpec(
            num_scalar_prefetch=1,
            grid=(z.blocks,),
            in_specs=[whole((z.part, z.hidden))] * m
            + [
                pl.BlockSpec((z.block, z.pair), lambda i, r: (row_block(i, r), 0)),
                pl.BlockSpec(memory_space=pltpu.HBM),
                whole(code_shape),
            ],
            out_specs=[whole(back_shape)] * 2,
            scratch_shapes=[
                pltpu.VMEM((z.local, z.rows, z.width), BF),
                pltpu.VMEM((n, z.slots, z.tokens), F32),
                pltpu.VMEM((z.block, z.hidden), BF),
                pltpu.VMEM((z.local, z.pair, z.width), BF),
                pltpu.SemaphoreType.DMA((z.local,)),
            ],
        ),
        out_shape=[jax.ShapeDtypeStruct(back_shape, BF)] * 2,
        compiler_params=params(46),
        name="row_grads",
    )(ids, *grad_parts, pair_rows, weight_in, codes)
    columns, down_columns = stack(pieces, keep)
    down_sides = spread_over({0: down_columns}, "sub", m, m // 2)
    got = swap(send, "ep", n, 1)
    sides = {0: gate([columns], [down_sides[m // 2], got])[0]}
    sides[m // 2] = swap(sides[0], "sub", m, m // 2)
    steps[1] = gate(steps[1], [got])
    for d in range(3, n):
        steps.append(chain_step(*steps[-1], "ep", n, d))
    gathered = [inputs] + [go for go, _ in steps] + [back for _, back in steps]
    def total_call(kernel, operands, specs, cols, scratch, name):
        return pl.pallas_call(
            functools.partial(kernel, z),
            grid_spec=pltpu.PrefetchScalarGridSpec(
                num_scalar_prefetch=2,
                grid=(1,),
                in_specs=specs,
                out_specs=[pl.BlockSpec(memory_space=pl.ANY), whole((8, 128))],
                scratch_shapes=[
                    pltpu.VMEM((m, n + 1, cols, z.part), BF),
                    pltpu.VMEM((z.experts, cols, z.width), BF),
                    pltpu.SemaphoreType.DMA((z.experts,)),
                ]
                + scratch,
            ),
            out_shape=[
                jax.ShapeDtypeStruct((z.experts, cols, z.width), BF),
                jax.ShapeDtypeStruct((8, 128), F32),
            ],
            compiler_params=params(32),
            name=name,
        )(ids, table, *operands)

    anywhere = pl.BlockSpec(memory_space=pl.ANY)
    grad_down, down_made = total_call(
        total_down_kernel,
        [*down_sides, grads_all, codes],
        [anywhere] * m + [whole((n, z.tokens, z.width)), whole(code_shape)],
        z.down_cols,
        [pltpu.VMEM((z.slots, z.rows, z.width), BF), pltpu.SemaphoreType.DMA((m,))],
        "down_grads",
    )
    sides[0], sides[m // 2] = gate([sides[0], sides[m // 2]], [down_made])
    sides = spread_over(sides, "sub", m, m // 4)
    bit = 2
    while bit < n:
        keep, send = halve(keep, got)
        send = gate([send], [down_made])[0]
        got = swap(send, "ep", n, bit)
        bit *= 2

    grad_tokens, grad_routes = pl.pallas_call(
        functools.partial(token_kernel, z),
        out_shape=[
            jax.ShapeDtypeStruct((z.tokens, z.width), BF),
            jax.ShapeDtypeStruct((z.top, z.tokens), BF),
        ],
        in_specs=[smem()] + [whole(a.shape) for a in (keep, got, routes, replica, table)],
        out_specs=[whole((z.tokens, z.width)), whole((z.top, z.tokens))],
        grid=(1,),
        compiler_params=params(16),
        name="token_grads",
    )(token_count, keep, got, routes, replica, table)

    grad_in, _ = total_call(
        total_in_kernel,
        [*sides, *gathered],
        [anywhere] * (m + 2 * n - 1),
        z.in_cols,
        [
            pltpu.VMEM((n, z.all_rows, z.width), BF),
            pltpu.SemaphoreType.DMA((m,)),
            pltpu.SemaphoreType.DMA,
            pltpu.SemaphoreType.DMA((n - 1,)),
            pltpu.SemaphoreType.DMA((n - 1,)),
        ],
        "in_grads",
    )
    return grad_tokens, grad_routes.T, grad_in, grad_down


def solution(mesh):
    return jax.shard_map(
        body,
        mesh=mesh,
        in_specs=(
            P(("groups", "ep"), "sub"),
            P(("groups", "ep"), None),
            P(("groups", "ep"), None),
            P(("groups", "ep"), None),
            P("groups", None),
            P(("groups", "ep")),
            P(("groups", "ep"), None, None, "sub"),
            P(("groups", "ep"), None, None),
            P(("groups", "ep"), None, "sub"),
            P(("groups", "ep"), None, "sub"),
        ),
        out_specs=(
            P(("groups", "ep"), "sub"),
            P(("groups", "ep"), None),
            P("groups", "ep", "sub"),
            P("groups", "ep", "sub"),
        ),
        check_vma=False,
    )
```

```python
import functools
import math

import jax
import jax.numpy as jnp
from jax import lax
from jax.experimental import pallas as pl
from jax.experimental.pallas import tpu as pltpu
from jax.sharding import PartitionSpec as P

BF = jnp.bfloat16
F32 = jnp.float32
PER = 2


def nt(a, b):
    return lax.dot_general(a, b, (((1,), (1,)), ((), ())), preferred_element_type=F32)


def tn(a, b):
    return lax.dot_general(a, b, (((0,), (0,)), ((), ())), preferred_element_type=F32)


def nn(a, b):
    return jnp.dot(a, b, preferred_element_type=F32)


def whole(shape):
    zeros = (0,) * len(shape)
    return pl.BlockSpec(shape, lambda *_: zeros)


def smem():
    return pl.BlockSpec(memory_space=pltpu.SMEM)


def params(mib):
    return pltpu.CompilerParams(
        vmem_limit_bytes=mib * 1024 * 1024, dimension_semantics=("arbitrary",)
    )


class Sizes:
    def __init__(self, grad_out, routes, replica_slot, saved_input, weight_in, weight_down):
        self.ep = lax.axis_size("ep")
        self.sub = lax.axis_size("sub")
        self.tokens, self.width = grad_out.shape
        self.top = routes.shape[1]
        self.experts, self.reps = replica_slot.shape
        self.local = weight_in.shape[0]
        self.slots = self.ep * self.local
        self.cap = saved_input.shape[2]
        self.rows = self.ep * self.cap
        self.hidden = weight_down.shape[1]
        self.pair = weight_in.shape[1]
        self.all_rows = self.local * self.rows
        self.part = self.all_rows // self.sub
        self.block = math.gcd(self.rows, self.part)
        self.sources = self.block // self.cap
        self.blocks = self.all_rows // self.block
        self.part_blocks = self.part // self.block
        self.slot_blocks = self.rows // self.block
        self.in_cols = self.pair // self.ep
        self.down_cols = self.hidden // self.ep
        self.cols = self.in_cols + self.down_cols
        self.folds = self.width // self.tokens
        self.tail = 2 * self.slots // self.folds


def slot_table(z, table_ref, r):
    ids = lax.broadcasted_iota(jnp.int32, (z.slots, z.experts), 0)
    return (table_ref[r : r + 1, :] == ids).astype(F32).astype(BF)


def key_hits(z, count_ref, routes_ref, replica_ref, r, k):
    ids = lax.broadcasted_iota(jnp.int32, (z.experts, z.tokens), 0)
    live = lax.broadcasted_iota(jnp.int32, (1, z.tokens), 1) < count_ref[0]
    key = jnp.where(live & (replica_ref[k : k + 1, :] == r), routes_ref[k : k + 1, :], -1)
    return key == ids


def route_kernel(z, count_ref, grad_ref, weight_ref, routes_ref, replica_ref, table_ref, out_ref):
    weights = weight_ref[...].astype(F32)
    hits = jnp.zeros((z.slots, z.tokens), F32)
    loads = jnp.zeros((z.slots, z.tokens), F32)
    for r in range(z.reps):
        hit = jnp.zeros((z.experts, z.tokens), F32)
        load = jnp.zeros((z.experts, z.tokens), F32)
        for k in range(z.top):
            same = key_hits(z, count_ref, routes_ref, replica_ref, r, k)
            hit = jnp.where(same, 1.0, hit)
            load = jnp.where(same, weights[k : k + 1, :], load)
        table = slot_table(z, table_ref, r)
        hits = hits + nn(table, hit.astype(BF))
        loads = loads + nn(table, load.astype(BF))
    before = lax.broadcasted_iota(jnp.int32, (z.tokens, z.tokens), 0)
    after = lax.broadcasted_iota(jnp.int32, (z.tokens, z.tokens), 1)
    earlier = nn(hits.astype(BF), (before < after).astype(F32).astype(BF))
    code = jnp.where(hits > 0.5, earlier, -1.0)
    both = jnp.concatenate([code, loads], axis=0).astype(BF)
    out_ref[: z.tokens, :] = grad_ref[...]
    for b in range(z.folds):
        out_ref[z.tokens :, b * z.tokens : (b + 1) * z.tokens] = both[
            b * z.tail : (b + 1) * z.tail, :
        ]


def block_place(z, block):
    slot = block // z.slot_blocks
    first = (block % z.slot_blocks) * z.sources
    return slot, first


def block_picks(z, codes_ref, slot, first):
    rows = lax.broadcasted_iota(jnp.int32, (z.cap, z.tokens), 0).astype(F32)
    for a in range(z.sources):
        code = codes_ref[first + a, pl.ds(slot, 1), :]
        yield a, rows == code


def block_scale(z, codes_ref, slot, first):
    parts = []
    for a, pick in block_picks(z, codes_ref, slot, first):
        load = codes_ref[first + a, pl.ds(z.slots + slot, 1), :]
        parts.append(jnp.sum(jnp.where(pick, load, 0.0), axis=1, keepdims=True))
    return jnp.concatenate(parts, axis=0)


def local_picks(z, codes_ref, source, me):
    code = codes_ref[source, pl.ds(pl.multiple_of(me * z.local, z.local), z.local), :]
    rows = lax.broadcasted_iota(jnp.int32, (z.local, z.cap, z.tokens), 1).astype(F32)
    pick = (code[:, None, :] == rows).astype(F32)
    return pick.reshape(z.local * z.cap, z.tokens).astype(BF)


def block_slot(z, mine, step):
    place = step // z.part_blocks
    return ((place ^ mine) * z.part_blocks + step % z.part_blocks) // z.slot_blocks


def weight_copy(weight_ref, held, sems, slot):
    return pltpu.make_async_copy(weight_ref.at[slot], held.at[slot], sems.at[slot])


def down_kernel(z, ids_ref, *refs):
    bufs = refs[: z.ep]
    weight_ref = refs[z.ep]
    parts = refs[z.ep + 2 : z.ep + 4]
    grads_ref, codes_ref, rows_ref, held, sems = refs[z.ep + 4 :]
    me, mine = ids_ref[0], ids_ref[1]
    step = pl.program_id(0)

    @pl.when(step == 0)
    def _():
        for s in range(z.local):
            weight_copy(weight_ref, held, sems, s).start()
        for k in range(z.ep):
            source = me ^ k
            grads_ref[source] = bufs[k][: z.tokens, :]
            for b in range(z.folds):
                codes_ref[source, b * z.tail : (b + 1) * z.tail, :] = bufs[k][
                    z.tokens :, b * z.tokens : (b + 1) * z.tokens
                ].astype(F32)
        for p in range(z.ep):
            rows = nn(local_picks(z, codes_ref, p, me), grads_ref[p]).astype(BF)
            rows_ref[:, p * z.cap : (p + 1) * z.cap, :] = rows.reshape(z.local, z.cap, z.width)

    place = step // z.part_blocks
    block = (place ^ mine) * z.part_blocks + step % z.part_blocks
    slot, first = block_place(z, block)
    start = pl.multiple_of(first * z.cap, z.block)

    @pl.when((step == 0) | (slot != block_slot(z, mine, step - 1)))
    def _():
        weight_copy(weight_ref, held, sems, slot).wait()

    partial = nt(rows_ref[slot, pl.ds(start, z.block), :], held[slot]).astype(BF)
    spot = pl.multiple_of((step % z.part_blocks) * z.block, z.block)
    for k in range(z.sub):

        @pl.when(place == k)
        def _():
            parts[k % 2][k // 2, pl.ds(spot, z.block), :] = partial


def gate_terms(z, pair, grad, scale):
    gate = pair[:, : z.hidden].astype(F32)
    up = pair[:, z.hidden :].astype(F32)
    sig = 1.0 / (1.0 + jnp.exp(-gate))
    act = gate * sig
    hidden = act * up
    scaled = scale * grad
    grad_gate = scaled * up * sig * (1.0 + gate * (1.0 - sig))
    grad_up = scaled * act
    return hidden, grad_gate.astype(BF), grad_up.astype(BF)


def pre_kernel(z, ids_ref, keep_ref, got_ref, pair_ref, codes_ref, *refs):
    outs, (grad_ref, sides) = refs[: z.ep], refs[z.ep :]
    me = ids_ref[0]
    block = ids_ref[1] * z.part_blocks + pl.program_id(0)
    slot, first = block_place(z, block)
    scale = block_scale(z, codes_ref, me * z.local + slot, first)
    grad = keep_ref[0].astype(F32) + got_ref[0].astype(F32)
    grad_ref[...] = grad.astype(BF)
    _, grad_gate, grad_up = gate_terms(z, pair_ref[...], grad, scale)
    send_columns(z, me, jnp.concatenate([grad_gate.T, grad_up.T], axis=0), sides, outs)


def send_columns(z, me, columns, sides, outs):
    size = columns.shape[0] // z.ep
    for q in range(z.ep):
        sides[q] = columns[q * size : (q + 1) * size, :]
    for k in range(z.ep):
        outs[k][...] = sides[me ^ k]


def hidden_kernel(z, ids_ref, pair_ref, after_ref, other_ref, *refs):
    pair = pair_ref[...]
    gate_pre = pair[:, : z.hidden].astype(F32)
    up = pair[:, z.hidden :].astype(F32)
    hidden = gate_pre * (1.0 / (1.0 + jnp.exp(-gate_pre))) * up
    send_columns(z, ids_ref[0], hidden.astype(BF).T, refs[-1], refs[:-1])


def stack_kernel(z, *refs):
    for k in range(z.ep):
        refs[-1][k] = refs[k][...]


def row_kernel(z, ids_ref, *refs):
    grads = refs[: z.sub]
    pair_ref, weight_ref, codes_ref, keep_ref, send_ref = refs[z.sub : z.sub + 5]
    rows_ref, marks, held, weights, sems = refs[z.sub + 5 :]
    me, mine = ids_ref[0], ids_ref[1]
    step = pl.program_id(0)
    place = step // z.part_blocks
    block = (place ^ mine) * z.part_blocks + step % z.part_blocks
    slot, first = block_place(z, block)

    @pl.when(step == 0)
    def _():
        for s in range(z.local):
            weight_copy(weight_ref, weights, sems, s).start()
        marks[...] = jnp.zeros_like(marks)

    spot = pl.multiple_of((step % z.part_blocks) * z.block, z.block)
    for k in range(z.sub):

        @pl.when(place == k)
        def _():
            held[...] = grads[k][pl.ds(spot, z.block), :]

    grad = held[...].astype(F32)
    scale = block_scale(z, codes_ref, me * z.local + slot, first)
    hidden, grad_gate, grad_up = gate_terms(z, pair_ref[...], grad, scale)
    route = jnp.sum(hidden * grad, axis=1, keepdims=True).astype(BF).astype(F32)

    @pl.when((step == 0) | (slot != block_slot(z, mine, step - 1)))
    def _():
        weight_copy(weight_ref, weights, sems, slot).wait()

    rows = nn(grad_gate, weights[slot, : z.hidden, :]) + nn(grad_up, weights[slot, z.hidden :, :])
    start = pl.multiple_of(first * z.cap, z.block)
    rows_ref[slot, pl.ds(start, z.block), :] = rows.astype(BF)
    for a, pick in block_picks(z, codes_ref, me * z.local + slot, first):
        marks[first + a, pl.ds(me * z.local + slot, 1), :] = jnp.sum(
            jnp.where(pick, route[a * z.cap : (a + 1) * z.cap, :], 0.0), axis=0, keepdims=True
        )

    @pl.when(step == z.blocks - 1)
    def _():
        blank = jnp.zeros((z.slots, z.width - z.tokens), BF)
        for k in range(z.ep):
            source = me ^ k
            start = pl.multiple_of(source * z.cap, z.cap)
            rows = rows_ref[:, pl.ds(start, z.cap), :].reshape(z.local * z.cap, z.width)
            out_ref = send_ref if k % 2 else keep_ref
            picks = local_picks(z, codes_ref, source, me)
            out_ref[k // 2, : z.tokens, :] = tn(picks, rows).astype(BF)
            out_ref[k // 2, z.tokens :, : z.tokens] = marks[source].astype(BF)
            out_ref[k // 2, z.tokens :, z.tokens :] = blank


def halve_kernel(keep_ref, got_ref, out_keep, out_send):
    for i in range(out_keep.shape[0]):
        for j, out in enumerate((out_keep, out_send)):
            total = keep_ref[2 * i + j].astype(F32) + got_ref[2 * i + j].astype(F32)
            out[i] = total.astype(BF)


def token_kernel(z, count_ref, *refs):
    keep_ref, got_ref, routes_ref, replica_ref, table_ref, tokens_ref, route_ref = refs
    total = keep_ref[0].astype(F32) + got_ref[0].astype(F32)
    tokens_ref[...] = total[: z.tokens, :].astype(BF)
    rows = total[z.tokens :, : z.tokens].astype(BF)
    totals = [jnp.zeros((1, z.tokens), F32)] * z.top
    for r in range(z.reps):
        spread = tn(slot_table(z, table_ref, r), rows)
        for k in range(z.top):
            same = key_hits(z, count_ref, routes_ref, replica_ref, r, k)
            totals[k] += jnp.sum(jnp.where(same, spread, 0.0), axis=0, keepdims=True)
    route_ref[...] = jnp.concatenate(totals, axis=0).astype(BF)


def input_moves(z, me, own_ref, rights, lefts, inputs_ref, own_sem, right_sems, left_sems, act):
    act(pltpu.make_async_copy(own_ref, inputs_ref.at[me], own_sem))
    for d in range(1, z.ep):

        @pl.when(me >= d)
        def _():
            act(
                pltpu.make_async_copy(
                    rights[d - 1], inputs_ref.at[me - d], right_sems.at[d - 1]
                )
            )

        @pl.when(me + d < z.ep)
        def _():
            act(
                pltpu.make_async_copy(
                    lefts[d - 1], inputs_ref.at[me + d], left_sems.at[d - 1]
                )
            )


def left_rows(held, part, side, spot, size):
    return held[part, side, :, pl.ds(spot, size)]


def expert_products(z, ids_ref, table_ref, turn, held, right_rows, out_ref, made, out_sems):
    mine = ids_ref[1]

    def out_copy(expert):
        return pltpu.make_async_copy(made.at[expert], out_ref.at[expert], out_sems.at[expert])

    def some(step, carry):
        for i in range(PER):
            expert = step * PER + i
            first = table_ref[0, expert]
            left, right = [], []
            for r in range(z.reps):
                slot_id = table_ref[r, expert]
                source = slot_id // z.local
                for b in range(z.slot_blocks):
                    block = (slot_id % z.local) * z.slot_blocks + b
                    part = (block // z.part_blocks) ^ mine
                    spot = pl.multiple_of((block % z.part_blocks) * z.block, z.block)
                    side = source ^ turn
                    if r:
                        side = jnp.where(slot_id == first, z.ep, side)
                    left.append(functools.partial(left_rows, held, part, side, spot, z.block))
                    right.append(functools.partial(right_rows, slot_id, block, b))
            half = len(left) // 2

            def product(lo, hi):
                return nn(
                    jnp.concatenate([f() for f in left[lo:hi]], axis=1),
                    jnp.concatenate([f() for f in right[lo:hi]], axis=0),
                )

            few = table_ref[z.reps // 2, expert] == first

            @pl.when(few)
            def _():
                made[expert] = product(0, half).astype(BF)

            @pl.when(jnp.logical_not(few))
            def _():
                made[expert] = product(0, 2 * half).astype(BF)

            out_copy(expert).start()
        return carry

    lax.fori_loop(0, z.experts // PER, some, 0)
    for expert in range(z.experts):
        out_copy(expert).wait()


def total_down_kernel(z, ids_ref, table_ref, *refs):
    sides = refs[: z.sub]
    grads_ref, codes_ref, out_ref, token_ref, held, made, out_sems, scaled, sems = refs[z.sub :]
    token_ref[...] = jnp.zeros_like(token_ref)

    def moves(act):
        for k in range(z.sub):
            act(
                pltpu.make_async_copy(
                    sides[k], held.at[k, pl.ds(0, z.ep)], sems.at[k]
                )
            )

    moves(lambda copy: copy.start())
    held[:, z.ep] = jnp.zeros_like(held[:, z.ep])
    rows = lax.broadcasted_iota(jnp.int32, (z.slots, z.cap, z.tokens), 1).astype(F32)
    for p in range(z.ep):
        code = codes_ref[p, : z.slots, :][:, None, :]
        load = codes_ref[p, z.slots :, :][:, None, :]
        pick = jnp.where(rows == code, load, 0.0).reshape(z.slots * z.cap, z.tokens)
        result = nn(pick.astype(BF), grads_ref[p]).astype(BF)
        scaled[:, p * z.cap : (p + 1) * z.cap, :] = result.reshape(z.slots, z.cap, z.width)
    moves(lambda copy: copy.wait())

    def right_rows(slot_id, block, b):
        return scaled[slot_id, b * z.block : (b + 1) * z.block, :]

    expert_products(z, ids_ref, table_ref, ids_ref[0], held, right_rows, out_ref, made, out_sems)


def total_in_kernel(z, ids_ref, table_ref, *refs):
    sides, refs = refs[: z.sub], refs[z.sub :]
    own_ref, rights, lefts = refs[0], refs[1 : z.ep], refs[z.ep : 2 * z.ep - 1]
    out_ref, token_ref, held, made, out_sems, inputs_ref, sems, *other_sems = refs[2 * z.ep - 1 :]
    token_ref[...] = jnp.zeros_like(token_ref)

    def moves(act):
        for k in range(z.sub):
            act(pltpu.make_async_copy(sides[k], held.at[k, pl.ds(0, z.ep)], sems.at[k]))
        input_moves(z, ids_ref[0], own_ref, rights, lefts, inputs_ref, *other_sems, act)

    moves(lambda copy: copy.start())
    held[:, z.ep] = jnp.zeros_like(held[:, z.ep])
    moves(lambda copy: copy.wait())

    def right_rows(slot_id, block, b):
        start = pl.multiple_of(block * z.block, z.block)
        return inputs_ref[slot_id // z.local, pl.ds(start, z.block), :]

    expert_products(z, ids_ref, table_ref, ids_ref[0], held, right_rows, out_ref, made, out_sems)


def swap(x, axis, size, bit):
    return lax.ppermute(x, axis, [(i, i ^ bit) for i in range(size)])


def spread_over(have, axis, size, bit):
    have = dict(have)
    while bit:
        for k in list(have):
            if k | bit not in have:
                have[k | bit] = swap(have[k], axis, size, bit)
        bit //= 2
    return [have[k] for k in range(size)]


def nothing(*refs):
    pass


def gate(values, after):
    anywhere = pl.BlockSpec(memory_space=pl.ANY)
    return pl.pallas_call(
        nothing,
        in_specs=[anywhere] * (len(values) + len(after)),
        out_specs=[anywhere] * len(values),
        out_shape=[jax.ShapeDtypeStruct(v.shape, v.dtype) for v in values],
        input_output_aliases={i: i for i in range(len(values))},
        compiler_params=pltpu.CompilerParams(vmem_limit_bytes=1024 * 1024),
        name="gate",
    )(*values, *after)


def chain_step(go, back, axis, size, d):
    go = lax.ppermute(go, axis, [(i, i + 1) for i in range(d - 1, size - 1)])
    back = lax.ppermute(back, axis, [(i, i - 1) for i in range(size - d, 0, -1)])
    return go, back


def body(
    grad_out,
    route_weight,
    routes,
    replica,
    replica_slot,
    token_count,
    saved_input,
    saved_gate_up,
    weight_in,
    weight_down,
):
    z = Sizes(grad_out, routes, replica_slot, saved_input, weight_in, weight_down)
    n, m = z.ep, z.sub
    ids = jnp.stack([lax.axis_index("ep"), lax.axis_index("sub")]).astype(jnp.int32)
    routes, replica, table = routes.T, replica.T, replica_slot.T
    route_weight = route_weight.T
    pair_rows = saved_gate_up.reshape(z.all_rows, z.pair)
    grad_shape = (z.tokens + z.tail, z.width)
    code_shape = (n, 2 * z.slots, z.tokens)
    inputs = saved_input.reshape(z.all_rows, z.width)

    routing = (grad_out, route_weight, routes, replica, table)
    buf = pl.pallas_call(
        functools.partial(route_kernel, z),
        out_shape=jax.ShapeDtypeStruct(grad_shape, BF),
        in_specs=[smem()] + [whole(a.shape) for a in routing],
        out_specs=whole(grad_shape),
        grid=(1,),
        compiler_params=params(60),
        name="route",
    )(token_count, *routing)
    bufs = [buf] + [swap(buf, "ep", n, k) for k in range(1, n)]

    chain = gate([inputs], [buf])
    downs = pl.pallas_call(
        functools.partial(hidden_kernel, z),
        grid_spec=pltpu.PrefetchScalarGridSpec(
            num_scalar_prefetch=1,
            grid=(z.part_blocks,),
            in_specs=[
                pl.BlockSpec((z.block, z.pair), lambda i, r: (r[1] * z.part_blocks + i, 0)),
                pl.BlockSpec(memory_space=pl.ANY),
                pl.BlockSpec(memory_space=pl.ANY),
            ],
            out_specs=[pl.BlockSpec((z.down_cols, z.block), lambda i, r: (0, i))] * n,
            scratch_shapes=[pltpu.VMEM((n, z.down_cols, z.block), BF)],
        ),
        out_shape=[jax.ShapeDtypeStruct((z.down_cols, z.part), BF)] * n,
        compiler_params=params(16),
        name="hidden_columns",
    )(ids, pair_rows, bufs[1], chain[0])
    downs = [downs[0]] + [swap(downs[k], "ep", n, k) for k in range(1, n)]
    chain = gate(chain, bufs[1:] + downs[1:])
    steps = [chain_step(chain[0], chain[0], "ep", n, 1)]

    def stack(pieces):
        shape = pieces[0].shape
        return pl.pallas_call(
            functools.partial(stack_kernel, z),
            in_specs=[whole(shape)] * n,
            out_specs=whole((n,) + shape),
            out_shape=jax.ShapeDtypeStruct((n,) + shape, BF),
            grid=(1,),
            compiler_params=params(12),
            name="stack_columns",
        )(*pieces)

    def halve(keep, got):
        half = (keep.shape[0] // 2,) + keep.shape[1:]
        return pl.pallas_call(
            halve_kernel,
            in_specs=[whole(keep.shape)] * 2,
            out_specs=[whole(half)] * 2,
            out_shape=[jax.ShapeDtypeStruct(half, BF)] * 2,
            grid=(1,),
            compiler_params=params(16),
            name="halve",
        )(keep, got)

    def row_block(i, ids_ref):
        place = i // z.part_blocks
        return (place ^ ids_ref[1]) * z.part_blocks + i % z.part_blocks

    part_shape = (m // 2, z.part, z.hidden)
    outs = pl.pallas_call(
        functools.partial(down_kernel, z),
        grid_spec=pltpu.PrefetchScalarGridSpec(
            num_scalar_prefetch=1,
            grid=(z.blocks,),
            in_specs=[whole(grad_shape)] * n
            + [pl.BlockSpec(memory_space=pltpu.HBM), pl.BlockSpec(memory_space=pl.ANY)],
            out_specs=[whole(part_shape)] * 2
            + [whole((n, z.tokens, z.width)), whole(code_shape)],
            scratch_shapes=[
                pltpu.VMEM((z.local, z.rows, z.width), BF),
                pltpu.VMEM((z.local, z.hidden, z.width), BF),
                pltpu.SemaphoreType.DMA((z.local,)),
            ],
        ),
        out_shape=[jax.ShapeDtypeStruct(part_shape, BF)] * 2
        + [
            jax.ShapeDtypeStruct((n, z.tokens, z.width), BF),
            jax.ShapeDtypeStruct(code_shape, F32),
        ],
        compiler_params=params(48),
        name="hidden_partials",
    )(ids, *bufs, weight_down, *downs[:1])
    keep, send, grads_all, codes = outs
    down_sides = spread_over({0: stack(downs)}, "sub", m, m // 2)
    def total_call(kernel, operands, specs, cols, scratch, name):
        return pl.pallas_call(
            functools.partial(kernel, z),
            grid_spec=pltpu.PrefetchScalarGridSpec(
                num_scalar_prefetch=2,
                grid=(1,),
                in_specs=specs,
                out_specs=[pl.BlockSpec(memory_space=pl.ANY), whole((8, 128))],
                scratch_shapes=[
                    pltpu.VMEM((m, n + 1, cols, z.part), BF),
                    pltpu.VMEM((z.experts, cols, z.width), BF),
                    pltpu.SemaphoreType.DMA((z.experts,)),
                ]
                + scratch,
            ),
            out_shape=[
                jax.ShapeDtypeStruct((z.experts, cols, z.width), BF),
                jax.ShapeDtypeStruct((8, 128), F32),
            ],
            compiler_params=params(32),
            name=name,
        )(ids, table, *operands)

    anywhere = pl.BlockSpec(memory_space=pl.ANY)
    grad_down, down_made = total_call(
        total_down_kernel,
        [*down_sides, grads_all, codes],
        [anywhere] * m + [whole((n, z.tokens, z.width)), whole(code_shape)],
        z.down_cols,
        [pltpu.VMEM((z.slots, z.rows, z.width), BF), pltpu.SemaphoreType.DMA((m,))],
        "down_grads",
    )
    steps[0] = gate(steps[0], [down_made])
    steps.append(chain_step(*steps[0], "ep", n, 2))
    got = swap(send, "sub", m, 1)
    bit = 2
    while bit < m:
        keep, send = halve(keep, got)
        got = swap(send, "sub", m, bit)
        bit *= 2
    *pieces, grad_part = pl.pallas_call(
        functools.partial(pre_kernel, z),
        grid_spec=pltpu.PrefetchScalarGridSpec(
            num_scalar_prefetch=1,
            grid=(z.part_blocks,),
            in_specs=[pl.BlockSpec((1, z.block, z.hidden), lambda i, r: (0, i, 0))] * 2
            + [
                pl.BlockSpec((z.block, z.pair), lambda i, r: (r[1] * z.part_blocks + i, 0)),
                whole(code_shape),
            ],
            out_specs=[pl.BlockSpec((z.in_cols, z.block), lambda i, r: (0, i))] * n
            + [pl.BlockSpec((z.block, z.hidden), lambda i, r: (i, 0))],
            scratch_shapes=[pltpu.VMEM((n, z.in_cols, z.block), BF)],
        ),
        out_shape=[jax.ShapeDtypeStruct((z.in_cols, z.part), BF)] * n
        + [jax.ShapeDtypeStruct((z.part, z.hidden), BF)],
        compiler_params=params(16),
        name="pre_grads",
    )(ids, keep, got, pair_rows, codes)
    late = gate(pieces[1:], steps[1])
    pieces = pieces[:1] + [swap(a, "ep", n, k) for k, a in enumerate(late, 1)]
    grad_parts = spread_over({0: grad_part}, "sub", m, m // 2)

    back_shape = (n // 2, z.tokens + z.slots, z.width)
    keep, send = pl.pallas_call(
        functools.partial(row_kernel, z),
        grid_spec=pltpu.PrefetchScalarGridSpec(
            num_scalar_prefetch=1,
            grid=(z.blocks,),
            in_specs=[whole((z.part, z.hidden))] * m
            + [
                pl.BlockSpec((z.block, z.pair), lambda i, r: (row_block(i, r), 0)),
                pl.BlockSpec(memory_space=pltpu.HBM),
                whole(code_shape),
            ],
            out_specs=[whole(back_shape)] * 2,
            scratch_shapes=[
                pltpu.VMEM((z.local, z.rows, z.width), BF),
                pltpu.VMEM((n, z.slots, z.tokens), F32),
                pltpu.VMEM((z.block, z.hidden), BF),
                pltpu.VMEM((z.local, z.pair, z.width), BF),
                pltpu.SemaphoreType.DMA((z.local,)),
            ],
        ),
        out_shape=[jax.ShapeDtypeStruct(back_shape, BF)] * 2,
        compiler_params=params(46),
        name="row_grads",
    )(ids, *grad_parts, pair_rows, weight_in, codes)
    for d in range(3, n):
        steps.append(chain_step(*steps[-1], "ep", n, d))
    gathered = [inputs] + [go for go, _ in steps] + [back for _, back in steps]
    got = swap(send, "ep", n, 1)
    pieces[:1] = gate(pieces[:1], [got])
    sides = spread_over({0: stack(pieces)}, "sub", m, m // 2)
    bit = 2
    while bit < n:
        keep, send = halve(keep, got)
        got = swap(send, "ep", n, bit)
        bit *= 2

    grad_in, in_made = total_call(
        total_in_kernel,
        [*sides, *gathered],
        [anywhere] * (m + 2 * n - 1),
        z.in_cols,
        [
            pltpu.VMEM((n, z.all_rows, z.width), BF),
            pltpu.SemaphoreType.DMA((m,)),
            pltpu.SemaphoreType.DMA,
            pltpu.SemaphoreType.DMA((n - 1,)),
            pltpu.SemaphoreType.DMA((n - 1,)),
        ],
        "in_grads",
    )
    got = gate([got], [in_made])[0]
    grad_tokens, grad_routes = pl.pallas_call(
        functools.partial(token_kernel, z),
        out_shape=[
            jax.ShapeDtypeStruct((z.tokens, z.width), BF),
            jax.ShapeDtypeStruct((z.top, z.tokens), BF),
        ],
        in_specs=[smem()] + [whole(a.shape) for a in (keep, got, routes, replica, table)],
        out_specs=[whole((z.tokens, z.width)), whole((z.top, z.tokens))],
        grid=(1,),
        compiler_params=params(16),
        name="token_grads",
    )(token_count, keep, got, routes, replica, table)

    return grad_tokens, grad_routes.T, grad_in, grad_down


def solution(mesh):
    return jax.shard_map(
        body,
        mesh=mesh,
        in_specs=(
            P(("groups", "ep"), "sub"),
            P(("groups", "ep"), None),
            P(("groups", "ep"), None),
            P(("groups", "ep"), None),
            P("groups", None),
            P(("groups", "ep")),
            P(("groups", "ep"), None, None, "sub"),
            P(("groups", "ep"), None, None),
            P(("groups", "ep"), None, "sub"),
            P(("groups", "ep"), None, "sub"),
        ),
        out_specs=(
            P(("groups", "ep"), "sub"),
            P(("groups", "ep"), None),
            P("groups", "ep", "sub"),
            P("groups", "ep", "sub"),
        ),
        check_vma=False,
    )
```

```python
import functools
import math

import jax
import jax.numpy as jnp
from jax import lax
from jax.experimental import pallas as pl
from jax.experimental.pallas import tpu as pltpu
from jax.sharding import PartitionSpec as P

BF = jnp.bfloat16
F32 = jnp.float32
PER = 2


def nt(a, b):
    return lax.dot_general(a, b, (((1,), (1,)), ((), ())), preferred_element_type=F32)


def tn(a, b):
    return lax.dot_general(a, b, (((0,), (0,)), ((), ())), preferred_element_type=F32)


def nn(a, b):
    return jnp.dot(a, b, preferred_element_type=F32)


def whole(shape):
    zeros = (0,) * len(shape)
    return pl.BlockSpec(shape, lambda *_: zeros)


def smem():
    return pl.BlockSpec(memory_space=pltpu.SMEM)


def params(mib):
    return pltpu.CompilerParams(
        vmem_limit_bytes=mib * 1024 * 1024, dimension_semantics=("arbitrary",)
    )


class Sizes:
    def __init__(self, grad_out, routes, replica_slot, saved_input, weight_in, weight_down):
        self.ep = lax.axis_size("ep")
        self.sub = lax.axis_size("sub")
        self.tokens, self.width = grad_out.shape
        self.top = routes.shape[1]
        self.experts, self.reps = replica_slot.shape
        self.local = weight_in.shape[0]
        self.slots = self.ep * self.local
        self.cap = saved_input.shape[2]
        self.rows = self.ep * self.cap
        self.hidden = weight_down.shape[1]
        self.pair = weight_in.shape[1]
        self.all_rows = self.local * self.rows
        self.part = self.all_rows // self.sub
        self.block = math.gcd(self.rows, self.part)
        self.sources = self.block // self.cap
        self.blocks = self.all_rows // self.block
        self.part_blocks = self.part // self.block
        self.slot_blocks = self.rows // self.block
        self.in_cols = self.pair // self.ep
        self.down_cols = self.hidden // self.ep
        self.cols = self.in_cols + self.down_cols
        self.folds = self.width // self.tokens
        self.tail = 2 * self.slots // self.folds


def slot_table(z, table_ref, r):
    ids = lax.broadcasted_iota(jnp.int32, (z.slots, z.experts), 0)
    return (table_ref[r : r + 1, :] == ids).astype(F32).astype(BF)


def key_hits(z, count_ref, routes_ref, replica_ref, r, k):
    ids = lax.broadcasted_iota(jnp.int32, (z.experts, z.tokens), 0)
    live = lax.broadcasted_iota(jnp.int32, (1, z.tokens), 1) < count_ref[0]
    key = jnp.where(live & (replica_ref[k : k + 1, :] == r), routes_ref[k : k + 1, :], -1)
    return key == ids


def route_kernel(z, count_ref, grad_ref, weight_ref, routes_ref, replica_ref, table_ref, out_ref):
    weights = weight_ref[...].astype(F32)
    hits = jnp.zeros((z.slots, z.tokens), F32)
    loads = jnp.zeros((z.slots, z.tokens), F32)
    for r in range(z.reps):
        hit = jnp.zeros((z.experts, z.tokens), F32)
        load = jnp.zeros((z.experts, z.tokens), F32)
        for k in range(z.top):
            same = key_hits(z, count_ref, routes_ref, replica_ref, r, k)
            hit = jnp.where(same, 1.0, hit)
            load = jnp.where(same, weights[k : k + 1, :], load)
        table = slot_table(z, table_ref, r)
        hits = hits + nn(table, hit.astype(BF))
        loads = loads + nn(table, load.astype(BF))
    before = lax.broadcasted_iota(jnp.int32, (z.tokens, z.tokens), 0)
    after = lax.broadcasted_iota(jnp.int32, (z.tokens, z.tokens), 1)
    earlier = nn(hits.astype(BF), (before < after).astype(F32).astype(BF))
    code = jnp.where(hits > 0.5, earlier, -1.0)
    both = jnp.concatenate([code, loads], axis=0).astype(BF)
    out_ref[: z.tokens, :] = grad_ref[...]
    for b in range(z.folds):
        out_ref[z.tokens :, b * z.tokens : (b + 1) * z.tokens] = both[
            b * z.tail : (b + 1) * z.tail, :
        ]


def block_place(z, block):
    slot = block // z.slot_blocks
    first = (block % z.slot_blocks) * z.sources
    return slot, first


def block_picks(z, codes_ref, slot, first):
    rows = lax.broadcasted_iota(jnp.int32, (z.cap, z.tokens), 0).astype(F32)
    for a in range(z.sources):
        code = codes_ref[first + a, pl.ds(slot, 1), :]
        yield a, rows == code


def block_scale(z, codes_ref, slot, first):
    parts = []
    for a, pick in block_picks(z, codes_ref, slot, first):
        load = codes_ref[first + a, pl.ds(z.slots + slot, 1), :]
        parts.append(jnp.sum(jnp.where(pick, load, 0.0), axis=1, keepdims=True))
    return jnp.concatenate(parts, axis=0)


def local_picks(z, codes_ref, source, me):
    code = codes_ref[source, pl.ds(pl.multiple_of(me * z.local, z.local), z.local), :]
    rows = lax.broadcasted_iota(jnp.int32, (z.local, z.cap, z.tokens), 1).astype(F32)
    pick = (code[:, None, :] == rows).astype(F32)
    return pick.reshape(z.local * z.cap, z.tokens).astype(BF)


def block_slot(z, mine, step):
    place = step // z.part_blocks
    return ((place ^ mine) * z.part_blocks + step % z.part_blocks) // z.slot_blocks


def weight_copy(weight_ref, held, sems, slot):
    return pltpu.make_async_copy(weight_ref.at[slot], held.at[slot], sems.at[slot])


def down_kernel(z, ids_ref, *refs):
    bufs = refs[: z.ep]
    weight_ref = refs[z.ep]
    parts = refs[z.ep + 2 : z.ep + 4]
    grads_ref, codes_ref, rows_ref, held, sems = refs[z.ep + 4 :]
    me, mine = ids_ref[0], ids_ref[1]
    step = pl.program_id(0)

    @pl.when(step == 0)
    def _():
        for s in range(z.local):
            weight_copy(weight_ref, held, sems, s).start()
        for k in range(z.ep):
            source = me ^ k
            grads_ref[source] = bufs[k][: z.tokens, :]
            for b in range(z.folds):
                codes_ref[source, b * z.tail : (b + 1) * z.tail, :] = bufs[k][
                    z.tokens :, b * z.tokens : (b + 1) * z.tokens
                ].astype(F32)
        for p in range(z.ep):
            rows = nn(local_picks(z, codes_ref, p, me), grads_ref[p]).astype(BF)
            rows_ref[:, p * z.cap : (p + 1) * z.cap, :] = rows.reshape(z.local, z.cap, z.width)

    place = step // z.part_blocks
    block = (place ^ mine) * z.part_blocks + step % z.part_blocks
    slot, first = block_place(z, block)
    start = pl.multiple_of(first * z.cap, z.block)

    @pl.when((step == 0) | (slot != block_slot(z, mine, step - 1)))
    def _():
        weight_copy(weight_ref, held, sems, slot).wait()

    partial = nt(rows_ref[slot, pl.ds(start, z.block), :], held[slot]).astype(BF)
    spot = pl.multiple_of((step % z.part_blocks) * z.block, z.block)
    for k in range(z.sub):

        @pl.when(place == k)
        def _():
            parts[k % 2][k // 2, pl.ds(spot, z.block), :] = partial


def gate_terms(z, pair, grad, scale):
    gate = pair[:, : z.hidden].astype(F32)
    up = pair[:, z.hidden :].astype(F32)
    sig = 1.0 / (1.0 + jnp.exp(-gate))
    act = gate * sig
    hidden = act * up
    scaled = scale * grad
    grad_gate = scaled * up * sig * (1.0 + gate * (1.0 - sig))
    grad_up = scaled * act
    return hidden, grad_gate.astype(BF), grad_up.astype(BF)


def pre_kernel(z, ids_ref, keep_ref, got_ref, pair_ref, codes_ref, *refs):
    outs, (grad_ref, sides) = refs[: z.ep], refs[z.ep :]
    me = ids_ref[0]
    block = ids_ref[1] * z.part_blocks + pl.program_id(0)
    slot, first = block_place(z, block)
    scale = block_scale(z, codes_ref, me * z.local + slot, first)
    grad = keep_ref[0].astype(F32) + got_ref[0].astype(F32)
    grad_ref[...] = grad.astype(BF)
    _, grad_gate, grad_up = gate_terms(z, pair_ref[...], grad, scale)
    send_columns(z, me, jnp.concatenate([grad_gate.T, grad_up.T], axis=0), sides, outs)


def send_columns(z, me, columns, sides, outs):
    size = columns.shape[0] // z.ep
    for q in range(z.ep):
        sides[q] = columns[q * size : (q + 1) * size, :]
    for k in range(z.ep):
        outs[k][...] = sides[me ^ k]


def hidden_kernel(z, ids_ref, pair_ref, *refs):
    refs = refs[z.ep :]
    pair = pair_ref[...]
    gate_pre = pair[:, : z.hidden].astype(F32)
    up = pair[:, z.hidden :].astype(F32)
    hidden = gate_pre * (1.0 / (1.0 + jnp.exp(-gate_pre))) * up
    send_columns(z, ids_ref[0], hidden.astype(BF).T, refs[-1], refs[:-1])


def stack_kernel(z, *refs):
    for k in range(z.ep):
        refs[-1][k] = refs[k][...]


def row_kernel(z, ids_ref, *refs):
    grads = refs[: z.sub]
    pair_ref, weight_ref, codes_ref, keep_ref, send_ref = refs[z.sub : z.sub + 5]
    rows_ref, marks, held, weights, sems = refs[z.sub + 5 :]
    me, mine = ids_ref[0], ids_ref[1]
    step = pl.program_id(0)
    place = step // z.part_blocks
    block = (place ^ mine) * z.part_blocks + step % z.part_blocks
    slot, first = block_place(z, block)

    @pl.when(step == 0)
    def _():
        for s in range(z.local):
            weight_copy(weight_ref, weights, sems, s).start()
        marks[...] = jnp.zeros_like(marks)

    spot = pl.multiple_of((step % z.part_blocks) * z.block, z.block)
    for k in range(z.sub):

        @pl.when(place == k)
        def _():
            held[...] = grads[k][pl.ds(spot, z.block), :]

    grad = held[...].astype(F32)
    scale = block_scale(z, codes_ref, me * z.local + slot, first)
    hidden, grad_gate, grad_up = gate_terms(z, pair_ref[...], grad, scale)
    route = jnp.sum(hidden * grad, axis=1, keepdims=True).astype(BF).astype(F32)

    @pl.when((step == 0) | (slot != block_slot(z, mine, step - 1)))
    def _():
        weight_copy(weight_ref, weights, sems, slot).wait()

    rows = nn(grad_gate, weights[slot, : z.hidden, :]) + nn(grad_up, weights[slot, z.hidden :, :])
    start = pl.multiple_of(first * z.cap, z.block)
    rows_ref[slot, pl.ds(start, z.block), :] = rows.astype(BF)
    for a, pick in block_picks(z, codes_ref, me * z.local + slot, first):
        marks[first + a, pl.ds(me * z.local + slot, 1), :] = jnp.sum(
            jnp.where(pick, route[a * z.cap : (a + 1) * z.cap, :], 0.0), axis=0, keepdims=True
        )

    @pl.when(step == z.blocks - 1)
    def _():
        blank = jnp.zeros((z.slots, z.width - z.tokens), BF)
        for k in range(z.ep):
            source = me ^ k
            start = pl.multiple_of(source * z.cap, z.cap)
            rows = rows_ref[:, pl.ds(start, z.cap), :].reshape(z.local * z.cap, z.width)
            out_ref = send_ref if k % 2 else keep_ref
            picks = local_picks(z, codes_ref, source, me)
            out_ref[k // 2, : z.tokens, :] = tn(picks, rows).astype(BF)
            out_ref[k // 2, z.tokens :, : z.tokens] = marks[source].astype(BF)
            out_ref[k // 2, z.tokens :, z.tokens :] = blank


def halve_kernel(keep_ref, got_ref, out_keep, out_send):
    for i in range(out_keep.shape[0]):
        for j, out in enumerate((out_keep, out_send)):
            total = keep_ref[2 * i + j].astype(F32) + got_ref[2 * i + j].astype(F32)
            out[i] = total.astype(BF)


def token_kernel(z, count_ref, *refs):
    keep_ref, got_ref, routes_ref, replica_ref, table_ref, tokens_ref, route_ref = refs
    total = keep_ref[0].astype(F32) + got_ref[0].astype(F32)
    tokens_ref[...] = total[: z.tokens, :].astype(BF)
    rows = total[z.tokens :, : z.tokens].astype(BF)
    totals = [jnp.zeros((1, z.tokens), F32)] * z.top
    for r in range(z.reps):
        spread = tn(slot_table(z, table_ref, r), rows)
        for k in range(z.top):
            same = key_hits(z, count_ref, routes_ref, replica_ref, r, k)
            totals[k] += jnp.sum(jnp.where(same, spread, 0.0), axis=0, keepdims=True)
    route_ref[...] = jnp.concatenate(totals, axis=0).astype(BF)


def input_moves(z, me, own_ref, rights, lefts, inputs_ref, own_sem, right_sems, left_sems, act):
    act(pltpu.make_async_copy(own_ref, inputs_ref.at[me], own_sem))
    for d in range(1, z.ep):

        @pl.when(me >= d)
        def _():
            act(
                pltpu.make_async_copy(
                    rights[d - 1], inputs_ref.at[me - d], right_sems.at[d - 1]
                )
            )

        @pl.when(me + d < z.ep)
        def _():
            act(
                pltpu.make_async_copy(
                    lefts[d - 1], inputs_ref.at[me + d], left_sems.at[d - 1]
                )
            )


def left_rows(held, part, side, spot, size):
    return held[part, side, :, pl.ds(spot, size)]


def expert_products(z, ids_ref, table_ref, turn, held, right_rows, out_ref, made, out_sems):
    mine = ids_ref[1]

    def out_copy(expert):
        return pltpu.make_async_copy(made.at[expert], out_ref.at[expert], out_sems.at[expert])

    def some(step, carry):
        for i in range(PER):
            expert = step * PER + i
            first = table_ref[0, expert]
            left, right = [], []
            for r in range(z.reps):
                slot_id = table_ref[r, expert]
                source = slot_id // z.local
                for b in range(z.slot_blocks):
                    block = (slot_id % z.local) * z.slot_blocks + b
                    part = (block // z.part_blocks) ^ mine
                    spot = pl.multiple_of((block % z.part_blocks) * z.block, z.block)
                    side = source ^ turn
                    if r:
                        side = jnp.where(slot_id == first, z.ep, side)
                    left.append(functools.partial(left_rows, held, part, side, spot, z.block))
                    right.append(functools.partial(right_rows, slot_id, block, b))
            half = len(left) // 2

            def product(lo, hi):
                return nn(
                    jnp.concatenate([f() for f in left[lo:hi]], axis=1),
                    jnp.concatenate([f() for f in right[lo:hi]], axis=0),
                )

            few = table_ref[z.reps // 2, expert] == first

            @pl.when(few)
            def _():
                made[expert] = product(0, half).astype(BF)

            @pl.when(jnp.logical_not(few))
            def _():
                made[expert] = product(0, 2 * half).astype(BF)

            out_copy(expert).start()
        return carry

    lax.fori_loop(0, z.experts // PER, some, 0)
    for expert in range(z.experts):
        out_copy(expert).wait()


def total_down_kernel(z, ids_ref, table_ref, *refs):
    sides = refs[: z.sub]
    grads_ref, codes_ref, _, out_ref, token_ref, held, made, out_sems, scaled, sems = refs[z.sub :]
    token_ref[...] = jnp.zeros_like(token_ref)

    def moves(act):
        for k in range(z.sub):
            act(
                pltpu.make_async_copy(
                    sides[k], held.at[k, pl.ds(0, z.ep)], sems.at[k]
                )
            )

    moves(lambda copy: copy.start())
    held[:, z.ep] = jnp.zeros_like(held[:, z.ep])
    rows = lax.broadcasted_iota(jnp.int32, (z.slots, z.cap, z.tokens), 1).astype(F32)
    for p in range(z.ep):
        code = codes_ref[p, : z.slots, :][:, None, :]
        load = codes_ref[p, z.slots :, :][:, None, :]
        pick = jnp.where(rows == code, load, 0.0).reshape(z.slots * z.cap, z.tokens)
        result = nn(pick.astype(BF), grads_ref[p]).astype(BF)
        scaled[:, p * z.cap : (p + 1) * z.cap, :] = result.reshape(z.slots, z.cap, z.width)
    moves(lambda copy: copy.wait())

    def right_rows(slot_id, block, b):
        return scaled[slot_id, b * z.block : (b + 1) * z.block, :]

    expert_products(z, ids_ref, table_ref, ids_ref[0], held, right_rows, out_ref, made, out_sems)


def total_in_kernel(z, ids_ref, table_ref, *refs):
    sides, refs = refs[: z.sub], refs[z.sub :]
    own_ref, rights, lefts = refs[0], refs[1 : z.ep], refs[z.ep : 2 * z.ep - 1]
    out_ref, token_ref, held, made, out_sems, inputs_ref, sems, *other_sems = refs[2 * z.ep - 1 :]
    token_ref[...] = jnp.zeros_like(token_ref)

    def moves(act):
        for k in range(z.sub):
            act(pltpu.make_async_copy(sides[k], held.at[k, pl.ds(0, z.ep)], sems.at[k]))
        input_moves(z, ids_ref[0], own_ref, rights, lefts, inputs_ref, *other_sems, act)

    moves(lambda copy: copy.start())
    held[:, z.ep] = jnp.zeros_like(held[:, z.ep])
    moves(lambda copy: copy.wait())

    def right_rows(slot_id, block, b):
        start = pl.multiple_of(block * z.block, z.block)
        return inputs_ref[slot_id // z.local, pl.ds(start, z.block), :]

    expert_products(z, ids_ref, table_ref, ids_ref[0], held, right_rows, out_ref, made, out_sems)


def swap(x, axis, size, bit):
    return lax.ppermute(x, axis, [(i, i ^ bit) for i in range(size)])


def spread_over(have, axis, size, bit):
    have = dict(have)
    while bit:
        for k in list(have):
            if k | bit not in have:
                have[k | bit] = swap(have[k], axis, size, bit)
        bit //= 2
    return [have[k] for k in range(size)]


def nothing(*refs):
    pass


def gate(values, after):
    anywhere = pl.BlockSpec(memory_space=pl.ANY)
    return pl.pallas_call(
        nothing,
        in_specs=[anywhere] * (len(values) + len(after)),
        out_specs=[anywhere] * len(values),
        out_shape=[jax.ShapeDtypeStruct(v.shape, v.dtype) for v in values],
        input_output_aliases={i: i for i in range(len(values))},
        compiler_params=pltpu.CompilerParams(vmem_limit_bytes=1024 * 1024),
        name="gate",
    )(*values, *after)


def chain_step(go, back, axis, size, d):
    go = lax.ppermute(go, axis, [(i, i + 1) for i in range(d - 1, size - 1)])
    back = lax.ppermute(back, axis, [(i, i - 1) for i in range(size - d, 0, -1)])
    return go, back


def body(
    grad_out,
    route_weight,
    routes,
    replica,
    replica_slot,
    token_count,
    saved_input,
    saved_gate_up,
    weight_in,
    weight_down,
):
    z = Sizes(grad_out, routes, replica_slot, saved_input, weight_in, weight_down)
    n, m = z.ep, z.sub
    ids = jnp.stack([lax.axis_index("ep"), lax.axis_index("sub")]).astype(jnp.int32)
    routes, replica, table = routes.T, replica.T, replica_slot.T
    route_weight = route_weight.T
    pair_rows = saved_gate_up.reshape(z.all_rows, z.pair)
    grad_shape = (z.tokens + z.tail, z.width)
    code_shape = (n, 2 * z.slots, z.tokens)
    inputs = saved_input.reshape(z.all_rows, z.width)

    routing = (grad_out, route_weight, routes, replica, table)
    buf = pl.pallas_call(
        functools.partial(route_kernel, z),
        out_shape=jax.ShapeDtypeStruct(grad_shape, BF),
        in_specs=[smem()] + [whole(a.shape) for a in routing],
        out_specs=whole(grad_shape),
        grid=(1,),
        compiler_params=params(60),
        name="route",
    )(token_count, *routing)
    bufs = [buf] + [swap(buf, "ep", n, k) for k in range(1, n)]

    chain = gate([inputs], [buf])
    downs = pl.pallas_call(
        functools.partial(hidden_kernel, z),
        grid_spec=pltpu.PrefetchScalarGridSpec(
            num_scalar_prefetch=1,
            grid=(z.part_blocks,),
            in_specs=[
                pl.BlockSpec((z.block, z.pair), lambda i, r: (r[1] * z.part_blocks + i, 0))
            ]
            + [pl.BlockSpec(memory_space=pl.ANY)] * n,
            out_specs=[pl.BlockSpec((z.down_cols, z.block), lambda i, r: (0, i))] * n,
            scratch_shapes=[pltpu.VMEM((n, z.down_cols, z.block), BF)],
        ),
        out_shape=[jax.ShapeDtypeStruct((z.down_cols, z.part), BF)] * n,
        compiler_params=params(16),
        name="hidden_columns",
    )(ids, pair_rows, *bufs[1:], chain[0])
    chain = gate(chain, [*bufs[1:], downs[0]])
    downs = [downs[0]] + [swap(downs[k], "ep", n, k) for k in range(1, n)]
    steps = [chain_step(chain[0], chain[0], "ep", n, 1)]

    def stack(pieces):
        shape = pieces[0].shape
        return pl.pallas_call(
            functools.partial(stack_kernel, z),
            in_specs=[whole(shape)] * n,
            out_specs=whole((n,) + shape),
            out_shape=jax.ShapeDtypeStruct((n,) + shape, BF),
            grid=(1,),
            compiler_params=params(12),
            name="stack_columns",
        )(*pieces)

    def halve(keep, got):
        half = (keep.shape[0] // 2,) + keep.shape[1:]
        return pl.pallas_call(
            halve_kernel,
            in_specs=[whole(keep.shape)] * 2,
            out_specs=[whole(half)] * 2,
            out_shape=[jax.ShapeDtypeStruct(half, BF)] * 2,
            grid=(1,),
            compiler_params=params(16),
            name="halve",
        )(keep, got)

    def row_block(i, ids_ref):
        place = i // z.part_blocks
        return (place ^ ids_ref[1]) * z.part_blocks + i % z.part_blocks

    part_shape = (m // 2, z.part, z.hidden)
    outs = pl.pallas_call(
        functools.partial(down_kernel, z),
        grid_spec=pltpu.PrefetchScalarGridSpec(
            num_scalar_prefetch=1,
            grid=(z.blocks,),
            in_specs=[whole(grad_shape)] * n
            + [pl.BlockSpec(memory_space=pltpu.HBM), pl.BlockSpec(memory_space=pl.ANY)],
            out_specs=[whole(part_shape)] * 2
            + [whole((n, z.tokens, z.width)), whole(code_shape)],
            scratch_shapes=[
                pltpu.VMEM((z.local, z.rows, z.width), BF),
                pltpu.VMEM((z.local, z.hidden, z.width), BF),
                pltpu.SemaphoreType.DMA((z.local,)),
            ],
        ),
        out_shape=[jax.ShapeDtypeStruct(part_shape, BF)] * 2
        + [
            jax.ShapeDtypeStruct((n, z.tokens, z.width), BF),
            jax.ShapeDtypeStruct(code_shape, F32),
        ],
        compiler_params=params(48),
        name="hidden_partials",
    )(ids, *bufs, weight_down, chain[0])
    keep, send, grads_all, codes = outs
    got = swap(send, "sub", m, 1)
    bit = 2
    while bit < m:
        keep, send = halve(keep, got)
        got = swap(send, "sub", m, bit)
        bit *= 2
    down_sides = spread_over({0: stack(downs)}, "sub", m, m // 2)
    def total_call(kernel, operands, specs, cols, scratch, name):
        return pl.pallas_call(
            functools.partial(kernel, z),
            grid_spec=pltpu.PrefetchScalarGridSpec(
                num_scalar_prefetch=2,
                grid=(1,),
                in_specs=specs,
                out_specs=[pl.BlockSpec(memory_space=pl.ANY), whole((8, 128))],
                scratch_shapes=[
                    pltpu.VMEM((m, n + 1, cols, z.part), BF),
                    pltpu.VMEM((z.experts, cols, z.width), BF),
                    pltpu.SemaphoreType.DMA((z.experts,)),
                ]
                + scratch,
            ),
            out_shape=[
                jax.ShapeDtypeStruct((z.experts, cols, z.width), BF),
                jax.ShapeDtypeStruct((8, 128), F32),
            ],
            compiler_params=params(32),
            name=name,
        )(ids, table, *operands)

    anywhere = pl.BlockSpec(memory_space=pl.ANY)
    grad_down, down_made = total_call(
        total_down_kernel,
        [*down_sides, grads_all, codes, send],
        [anywhere] * m + [whole((n, z.tokens, z.width)), whole(code_shape), anywhere],
        z.down_cols,
        [pltpu.VMEM((z.slots, z.rows, z.width), BF), pltpu.SemaphoreType.DMA((m,))],
        "down_grads",
    )
    steps[0] = gate(steps[0], [down_made])
    steps.append(chain_step(*steps[0], "ep", n, 2))
    *pieces, grad_part = pl.pallas_call(
        functools.partial(pre_kernel, z),
        grid_spec=pltpu.PrefetchScalarGridSpec(
            num_scalar_prefetch=1,
            grid=(z.part_blocks,),
            in_specs=[pl.BlockSpec((1, z.block, z.hidden), lambda i, r: (0, i, 0))] * 2
            + [
                pl.BlockSpec((z.block, z.pair), lambda i, r: (r[1] * z.part_blocks + i, 0)),
                whole(code_shape),
            ],
            out_specs=[pl.BlockSpec((z.in_cols, z.block), lambda i, r: (0, i))] * n
            + [pl.BlockSpec((z.block, z.hidden), lambda i, r: (i, 0))],
            scratch_shapes=[pltpu.VMEM((n, z.in_cols, z.block), BF)],
        ),
        out_shape=[jax.ShapeDtypeStruct((z.in_cols, z.part), BF)] * n
        + [jax.ShapeDtypeStruct((z.part, z.hidden), BF)],
        compiler_params=params(16),
        name="pre_grads",
    )(ids, keep, got, pair_rows, codes)
    late = gate(pieces[1:], steps[1])
    pieces = pieces[:1] + [swap(a, "ep", n, k) for k, a in enumerate(late, 1)]
    grad_parts = spread_over({0: grad_part}, "sub", m, m // 2)

    back_shape = (n // 2, z.tokens + z.slots, z.width)
    keep, send = pl.pallas_call(
        functools.partial(row_kernel, z),
        grid_spec=pltpu.PrefetchScalarGridSpec(
            num_scalar_prefetch=1,
            grid=(z.blocks,),
            in_specs=[whole((z.part, z.hidden))] * m
            + [
                pl.BlockSpec((z.block, z.pair), lambda i, r: (row_block(i, r), 0)),
                pl.BlockSpec(memory_space=pltpu.HBM),
                whole(code_shape),
            ],
            out_specs=[whole(back_shape)] * 2,
            scratch_shapes=[
                pltpu.VMEM((z.local, z.rows, z.width), BF),
                pltpu.VMEM((n, z.slots, z.tokens), F32),
                pltpu.VMEM((z.block, z.hidden), BF),
                pltpu.VMEM((z.local, z.pair, z.width), BF),
                pltpu.SemaphoreType.DMA((z.local,)),
            ],
        ),
        out_shape=[jax.ShapeDtypeStruct(back_shape, BF)] * 2,
        compiler_params=params(46),
        name="row_grads",
    )(ids, *grad_parts, pair_rows, weight_in, codes)
    steps[1] = gate(steps[1], pieces[1:])
    for d in range(3, n):
        steps.append(chain_step(*steps[-1], "ep", n, d))
    gathered = [inputs] + [go for go, _ in steps] + [back for _, back in steps]
    got = swap(send, "ep", n, 1)
    pieces[:1] = gate(pieces[:1], [got])
    columns = stack(pieces)
    sides = spread_over({0: columns}, "sub", m, m // 2)
    bit = 2
    while bit < n:
        keep, send = halve(keep, got)
        got = swap(send, "ep", n, bit)
        bit *= 2

    grad_in, in_made = total_call(
        total_in_kernel,
        [*sides, *gathered],
        [anywhere] * (m + 2 * n - 1),
        z.in_cols,
        [
            pltpu.VMEM((n, z.all_rows, z.width), BF),
            pltpu.SemaphoreType.DMA((m,)),
            pltpu.SemaphoreType.DMA,
            pltpu.SemaphoreType.DMA((n - 1,)),
            pltpu.SemaphoreType.DMA((n - 1,)),
        ],
        "in_grads",
    )
    got = gate([got], [in_made])[0]
    grad_tokens, grad_routes = pl.pallas_call(
        functools.partial(token_kernel, z),
        out_shape=[
            jax.ShapeDtypeStruct((z.tokens, z.width), BF),
            jax.ShapeDtypeStruct((z.top, z.tokens), BF),
        ],
        in_specs=[smem()] + [whole(a.shape) for a in (keep, got, routes, replica, table)],
        out_specs=[whole((z.tokens, z.width)), whole((z.top, z.tokens))],
        grid=(1,),
        compiler_params=params(16),
        name="token_grads",
    )(token_count, keep, got, routes, replica, table)

    return grad_tokens, grad_routes.T, grad_in, grad_down


def solution(mesh):
    return jax.shard_map(
        body,
        mesh=mesh,
        in_specs=(
            P(("groups", "ep"), "sub"),
            P(("groups", "ep"), None),
            P(("groups", "ep"), None),
            P(("groups", "ep"), None),
            P("groups", None),
            P(("groups", "ep")),
            P(("groups", "ep"), None, None, "sub"),
            P(("groups", "ep"), None, None),
            P(("groups", "ep"), None, "sub"),
            P(("groups", "ep"), None, "sub"),
        ),
        out_specs=(
            P(("groups", "ep"), "sub"),
            P(("groups", "ep"), None),
            P("groups", "ep", "sub"),
            P("groups", "ep", "sub"),
        ),
        check_vma=False,
    )
```

```python
import functools
import math

import jax
import jax.numpy as jnp
from jax import lax
from jax.experimental import pallas as pl
from jax.experimental.pallas import tpu as pltpu
from jax.sharding import PartitionSpec as P

BF = jnp.bfloat16
F32 = jnp.float32
PER = 2
GROUPS = 2


def nt(a, b):
    return lax.dot_general(a, b, (((1,), (1,)), ((), ())), preferred_element_type=F32)


def tn(a, b):
    return lax.dot_general(a, b, (((0,), (0,)), ((), ())), preferred_element_type=F32)


def nn(a, b):
    return jnp.dot(a, b, preferred_element_type=F32)


def whole(shape):
    zeros = (0,) * len(shape)
    return pl.BlockSpec(shape, lambda *_: zeros)


def smem():
    return pl.BlockSpec(memory_space=pltpu.SMEM)


def params(mib):
    return pltpu.CompilerParams(
        vmem_limit_bytes=mib * 1024 * 1024, dimension_semantics=("arbitrary",)
    )


class Sizes:
    def __init__(self, grad_out, routes, replica_slot, saved_input, weight_in, weight_down):
        self.ep = lax.axis_size("ep")
        self.sub = lax.axis_size("sub")
        self.tokens, self.width = grad_out.shape
        self.top = routes.shape[1]
        self.experts, self.reps = replica_slot.shape
        self.local = weight_in.shape[0]
        self.slots = self.ep * self.local
        self.cap = saved_input.shape[2]
        self.rows = self.ep * self.cap
        self.hidden = weight_down.shape[1]
        self.pair = weight_in.shape[1]
        self.all_rows = self.local * self.rows
        self.part = self.all_rows // self.sub
        self.block = math.gcd(self.rows, self.part)
        self.sources = self.block // self.cap
        self.blocks = self.all_rows // self.block
        self.part_blocks = self.part // self.block
        self.slot_blocks = self.rows // self.block
        self.in_cols = self.pair // self.ep
        self.down_cols = self.hidden // self.ep
        self.cols = self.in_cols + self.down_cols
        self.folds = self.width // self.tokens
        self.tail = 2 * self.slots // self.folds


def slot_table(z, table_ref, r):
    ids = lax.broadcasted_iota(jnp.int32, (z.slots, z.experts), 0)
    return (table_ref[r : r + 1, :] == ids).astype(F32).astype(BF)


def key_hits(z, count_ref, routes_ref, replica_ref, r, k):
    ids = lax.broadcasted_iota(jnp.int32, (z.experts, z.tokens), 0)
    live = lax.broadcasted_iota(jnp.int32, (1, z.tokens), 1) < count_ref[0]
    key = jnp.where(live & (replica_ref[k : k + 1, :] == r), routes_ref[k : k + 1, :], -1)
    return key == ids


def route_kernel(z, count_ref, grad_ref, weight_ref, routes_ref, replica_ref, table_ref, out_ref):
    weights = weight_ref[...].astype(F32)
    hits = jnp.zeros((z.slots, z.tokens), F32)
    loads = jnp.zeros((z.slots, z.tokens), F32)
    for r in range(z.reps):
        hit = jnp.zeros((z.experts, z.tokens), F32)
        load = jnp.zeros((z.experts, z.tokens), F32)
        for k in range(z.top):
            same = key_hits(z, count_ref, routes_ref, replica_ref, r, k)
            hit = jnp.where(same, 1.0, hit)
            load = jnp.where(same, weights[k : k + 1, :], load)
        table = slot_table(z, table_ref, r)
        hits = hits + nn(table, hit.astype(BF))
        loads = loads + nn(table, load.astype(BF))
    before = lax.broadcasted_iota(jnp.int32, (z.tokens, z.tokens), 0)
    after = lax.broadcasted_iota(jnp.int32, (z.tokens, z.tokens), 1)
    earlier = nn(hits.astype(BF), (before < after).astype(F32).astype(BF))
    code = jnp.where(hits > 0.5, earlier, -1.0)
    both = jnp.concatenate([code, loads], axis=0).astype(BF)
    out_ref[: z.tokens, :] = grad_ref[...]
    for b in range(z.folds):
        out_ref[z.tokens :, b * z.tokens : (b + 1) * z.tokens] = both[
            b * z.tail : (b + 1) * z.tail, :
        ]


def block_place(z, block):
    slot = block // z.slot_blocks
    first = (block % z.slot_blocks) * z.sources
    return slot, first


def block_picks(z, codes_ref, slot, first):
    rows = lax.broadcasted_iota(jnp.int32, (z.cap, z.tokens), 0).astype(F32)
    for a in range(z.sources):
        code = codes_ref[first + a, pl.ds(slot, 1), :]
        yield a, rows == code


def block_scale(z, codes_ref, slot, first):
    parts = []
    for a, pick in block_picks(z, codes_ref, slot, first):
        load = codes_ref[first + a, pl.ds(z.slots + slot, 1), :]
        parts.append(jnp.sum(jnp.where(pick, load, 0.0), axis=1, keepdims=True))
    return jnp.concatenate(parts, axis=0)


def local_picks(z, codes_ref, source, me):
    code = codes_ref[source, pl.ds(pl.multiple_of(me * z.local, z.local), z.local), :]
    rows = lax.broadcasted_iota(jnp.int32, (z.local, z.cap, z.tokens), 1).astype(F32)
    pick = (code[:, None, :] == rows).astype(F32)
    return pick.reshape(z.local * z.cap, z.tokens).astype(BF)


def block_slot(z, mine, step):
    place = step // z.part_blocks
    return ((place ^ mine) * z.part_blocks + step % z.part_blocks) // z.slot_blocks


def weight_copy(weight_ref, held, sems, slot):
    return pltpu.make_async_copy(weight_ref.at[slot], held.at[slot], sems.at[slot])


def down_kernel(z, ids_ref, *refs):
    bufs = refs[: z.ep]
    weight_ref = refs[z.ep]
    parts = refs[z.ep + 2 : z.ep + 4]
    grads_ref, codes_ref, rows_ref, held, sems = refs[z.ep + 4 :]
    me, mine = ids_ref[0], ids_ref[1]
    step = pl.program_id(0)

    @pl.when(step == 0)
    def _():
        for s in range(z.local):
            weight_copy(weight_ref, held, sems, s).start()
        for k in range(z.ep):
            source = me ^ k
            grads_ref[source] = bufs[k][: z.tokens, :]
            for b in range(z.folds):
                codes_ref[source, b * z.tail : (b + 1) * z.tail, :] = bufs[k][
                    z.tokens :, b * z.tokens : (b + 1) * z.tokens
                ].astype(F32)
        for p in range(z.ep):
            rows = nn(local_picks(z, codes_ref, p, me), grads_ref[p]).astype(BF)
            rows_ref[:, p * z.cap : (p + 1) * z.cap, :] = rows.reshape(z.local, z.cap, z.width)

    place = step // z.part_blocks
    block = (place ^ mine) * z.part_blocks + step % z.part_blocks
    slot, first = block_place(z, block)
    start = pl.multiple_of(first * z.cap, z.block)

    @pl.when((step == 0) | (slot != block_slot(z, mine, step - 1)))
    def _():
        weight_copy(weight_ref, held, sems, slot).wait()

    partial = nt(rows_ref[slot, pl.ds(start, z.block), :], held[slot]).astype(BF)
    spot = pl.multiple_of((step % z.part_blocks) * z.block, z.block)
    for k in range(z.sub):

        @pl.when(place == k)
        def _():
            parts[k % 2][k // 2, pl.ds(spot, z.block), :] = partial


def gate_terms(z, pair, grad, scale):
    gate = pair[:, : z.hidden].astype(F32)
    up = pair[:, z.hidden :].astype(F32)
    sig = 1.0 / (1.0 + jnp.exp(-gate))
    act = gate * sig
    hidden = act * up
    scaled = scale * grad
    grad_gate = scaled * up * sig * (1.0 + gate * (1.0 - sig))
    grad_up = scaled * act
    return hidden, grad_gate.astype(BF), grad_up.astype(BF)


def pre_kernel(z, ids_ref, keep_ref, got_ref, pair_ref, codes_ref, *refs):
    refs = refs[z.ep - 1 :]
    outs, (grad_ref, sides) = refs[: z.ep], refs[z.ep :]
    me = ids_ref[0]
    block = ids_ref[1] * z.part_blocks + pl.program_id(0)
    slot, first = block_place(z, block)
    scale = block_scale(z, codes_ref, me * z.local + slot, first)
    grad = keep_ref[0].astype(F32) + got_ref[0].astype(F32)
    grad_ref[...] = grad.astype(BF)
    _, grad_gate, grad_up = gate_terms(z, pair_ref[...], grad, scale)
    send_columns(z, me, jnp.concatenate([grad_gate.T, grad_up.T], axis=0), sides, outs)


def send_columns(z, me, columns, sides, outs):
    size = columns.shape[0] // z.ep
    for q in range(z.ep):
        sides[q] = columns[q * size : (q + 1) * size, :]
    for k in range(z.ep):
        outs[k][...] = sides[me ^ k]


def hidden_kernel(z, ids_ref, pair_ref, *refs):
    refs = refs[z.ep - 1 :]
    pair = pair_ref[...]
    gate_pre = pair[:, : z.hidden].astype(F32)
    up = pair[:, z.hidden :].astype(F32)
    hidden = gate_pre * (1.0 / (1.0 + jnp.exp(-gate_pre))) * up
    send_columns(z, ids_ref[0], hidden.astype(BF).T, refs[-1], refs[:-1])


def stack_kernel(*refs):
    for k, ref in enumerate(refs[:-1]):
        refs[-1][k] = ref[...]


def row_kernel(z, ids_ref, *refs):
    grads = refs[: z.sub]
    pair_ref, weight_ref, codes_ref, keep_ref, send_ref = refs[z.sub : z.sub + 5]
    rows_ref, marks, held, weights, sems = refs[z.sub + 5 :]
    me, mine = ids_ref[0], ids_ref[1]
    step = pl.program_id(0)
    place = step // z.part_blocks
    block = (place ^ mine) * z.part_blocks + step % z.part_blocks
    slot, first = block_place(z, block)

    @pl.when(step == 0)
    def _():
        for s in range(z.local):
            weight_copy(weight_ref, weights, sems, s).start()
        marks[...] = jnp.zeros_like(marks)

    spot = pl.multiple_of((step % z.part_blocks) * z.block, z.block)
    for k in range(z.sub):

        @pl.when(place == k)
        def _():
            held[...] = grads[k][pl.ds(spot, z.block), :]

    grad = held[...].astype(F32)
    scale = block_scale(z, codes_ref, me * z.local + slot, first)
    hidden, grad_gate, grad_up = gate_terms(z, pair_ref[...], grad, scale)
    route = jnp.sum(hidden * grad, axis=1, keepdims=True).astype(BF).astype(F32)

    @pl.when((step == 0) | (slot != block_slot(z, mine, step - 1)))
    def _():
        weight_copy(weight_ref, weights, sems, slot).wait()

    rows = nn(grad_gate, weights[slot, : z.hidden, :]) + nn(grad_up, weights[slot, z.hidden :, :])
    start = pl.multiple_of(first * z.cap, z.block)
    rows_ref[slot, pl.ds(start, z.block), :] = rows.astype(BF)
    for a, pick in block_picks(z, codes_ref, me * z.local + slot, first):
        marks[first + a, pl.ds(me * z.local + slot, 1), :] = jnp.sum(
            jnp.where(pick, route[a * z.cap : (a + 1) * z.cap, :], 0.0), axis=0, keepdims=True
        )

    @pl.when(step == z.blocks - 1)
    def _():
        blank = jnp.zeros((z.slots, z.width - z.tokens), BF)
        for k in range(z.ep):
            source = me ^ k
            start = pl.multiple_of(source * z.cap, z.cap)
            rows = rows_ref[:, pl.ds(start, z.cap), :].reshape(z.local * z.cap, z.width)
            out_ref = send_ref if k % 2 else keep_ref
            picks = local_picks(z, codes_ref, source, me)
            out_ref[k // 2, : z.tokens, :] = tn(picks, rows).astype(BF)
            out_ref[k // 2, z.tokens :, : z.tokens] = marks[source].astype(BF)
            out_ref[k // 2, z.tokens :, z.tokens :] = blank


def halve_kernel(keep_ref, got_ref, out_keep, out_send):
    for i in range(out_keep.shape[0]):
        for j, out in enumerate((out_keep, out_send)):
            total = keep_ref[2 * i + j].astype(F32) + got_ref[2 * i + j].astype(F32)
            out[i] = total.astype(BF)


def token_kernel(z, count_ref, *refs):
    keep_ref, got_ref, routes_ref, replica_ref, table_ref, tokens_ref, route_ref = refs
    total = keep_ref[0].astype(F32) + got_ref[0].astype(F32)
    tokens_ref[...] = total[: z.tokens, :].astype(BF)
    rows = total[z.tokens :, : z.tokens].astype(BF)
    totals = [jnp.zeros((1, z.tokens), F32)] * z.top
    for r in range(z.reps):
        spread = tn(slot_table(z, table_ref, r), rows)
        for k in range(z.top):
            same = key_hits(z, count_ref, routes_ref, replica_ref, r, k)
            totals[k] += jnp.sum(jnp.where(same, spread, 0.0), axis=0, keepdims=True)
    route_ref[...] = jnp.concatenate(totals, axis=0).astype(BF)


def left_rows(held, part, side, spot, size):
    return held[part, side, :, pl.ds(spot, size)]


def expert_products(z, ids_ref, table_ref, turn, held, right_rows, out_ref, made, out_sems):
    mine = ids_ref[1]

    def out_copy(expert):
        return pltpu.make_async_copy(made.at[expert], out_ref.at[expert], out_sems.at[expert])

    def some(step, carry):
        for i in range(PER):
            expert = step * PER + i
            first = table_ref[0, expert]
            left, right = [], []
            for r in range(z.reps):
                slot_id = table_ref[r, expert]
                source = slot_id // z.local
                for b in range(z.slot_blocks):
                    block = (slot_id % z.local) * z.slot_blocks + b
                    part = (block // z.part_blocks) ^ mine
                    spot = pl.multiple_of((block % z.part_blocks) * z.block, z.block)
                    side = source ^ turn
                    if r:
                        side = jnp.where(slot_id == first, z.ep, side)
                    left.append(functools.partial(left_rows, held, part, side, spot, z.block))
                    right.append(functools.partial(right_rows, slot_id, block, b))
            half = len(left) // 2

            def product(lo, hi):
                return nn(
                    jnp.concatenate([f() for f in left[lo:hi]], axis=1),
                    jnp.concatenate([f() for f in right[lo:hi]], axis=0),
                )

            few = table_ref[z.reps // 2, expert] == first

            @pl.when(few)
            def _():
                made[expert] = product(0, half).astype(BF)

            @pl.when(jnp.logical_not(few))
            def _():
                made[expert] = product(0, 2 * half).astype(BF)

            out_copy(expert).start()
        return carry

    lax.fori_loop(0, z.experts // PER, some, 0)
    for expert in range(z.experts):
        out_copy(expert).wait()


def total_down_kernel(z, ids_ref, table_ref, *refs):
    sides = refs[: z.sub]
    grads_ref, codes_ref, _, out_ref, token_ref, held, made, out_sems, scaled, sems = refs[z.sub :]
    token_ref[...] = jnp.zeros_like(token_ref)

    def moves(act):
        for k in range(z.sub):
            act(
                pltpu.make_async_copy(
                    sides[k], held.at[k, pl.ds(0, z.ep)], sems.at[k]
                )
            )

    moves(lambda copy: copy.start())
    held[:, z.ep] = jnp.zeros_like(held[:, z.ep])
    rows = lax.broadcasted_iota(jnp.int32, (z.slots, z.cap, z.tokens), 1).astype(F32)
    for p in range(z.ep):
        code = codes_ref[p, : z.slots, :][:, None, :]
        load = codes_ref[p, z.slots :, :][:, None, :]
        pick = jnp.where(rows == code, load, 0.0).reshape(z.slots * z.cap, z.tokens)
        result = nn(pick.astype(BF), grads_ref[p]).astype(BF)
        scaled[:, p * z.cap : (p + 1) * z.cap, :] = result.reshape(z.slots, z.cap, z.width)
    moves(lambda copy: copy.wait())

    def right_rows(slot_id, block, b):
        return scaled[slot_id, b * z.block : (b + 1) * z.block, :]

    expert_products(z, ids_ref, table_ref, ids_ref[0], held, right_rows, out_ref, made, out_sems)


def total_in_kernel(z, ids_ref, table_ref, *refs):
    sides, refs = refs[: GROUPS * z.sub], refs[GROUPS * z.sub :]
    size = z.ep // GROUPS
    gathered_ref, out_ref, token_ref, held, made, out_sems, inputs_ref, sems, in_sems = refs
    token_ref[...] = jnp.zeros_like(token_ref)

    def moves(act):
        for i in range(GROUPS * z.sub):
            g, k = divmod(i, z.sub)
            spots = held.at[k, pl.ds(g * size, size)]
            act(pltpu.make_async_copy(sides[i], spots, sems.at[i]))
        for p in range(z.ep):
            act(pltpu.make_async_copy(gathered_ref.at[p], inputs_ref.at[p], in_sems.at[p]))

    moves(lambda copy: copy.start())
    held[:, z.ep] = jnp.zeros_like(held[:, z.ep])
    moves(lambda copy: copy.wait())

    def right_rows(slot_id, block, b):
        start = pl.multiple_of(block * z.block, z.block)
        return inputs_ref[slot_id // z.local, pl.ds(start, z.block), :]

    expert_products(z, ids_ref, table_ref, ids_ref[0], held, right_rows, out_ref, made, out_sems)


def swap(x, axis, size, bit):
    return lax.ppermute(x, axis, [(i, i ^ bit) for i in range(size)])


def spread_over(have, axis, size, bit):
    have = dict(have)
    while bit:
        for k in list(have):
            if k | bit not in have:
                have[k | bit] = swap(have[k], axis, size, bit)
        bit //= 2
    return [have[k] for k in range(size)]


def nothing(*refs):
    pass


def gate(values, after):
    anywhere = pl.BlockSpec(memory_space=pl.ANY)
    return pl.pallas_call(
        nothing,
        in_specs=[anywhere] * (len(values) + len(after)),
        out_specs=[anywhere] * len(values),
        out_shape=[jax.ShapeDtypeStruct(v.shape, v.dtype) for v in values],
        input_output_aliases={i: i for i in range(len(values))},
        compiler_params=pltpu.CompilerParams(vmem_limit_bytes=1024 * 1024),
        name="gate",
    )(*values, *after)


def body(
    grad_out,
    route_weight,
    routes,
    replica,
    replica_slot,
    token_count,
    saved_input,
    saved_gate_up,
    weight_in,
    weight_down,
):
    z = Sizes(grad_out, routes, replica_slot, saved_input, weight_in, weight_down)
    n, m = z.ep, z.sub
    ids = jnp.stack([lax.axis_index("ep"), lax.axis_index("sub")]).astype(jnp.int32)
    routes, replica, table = routes.T, replica.T, replica_slot.T
    route_weight = route_weight.T
    pair_rows = saved_gate_up.reshape(z.all_rows, z.pair)
    grad_shape = (z.tokens + z.tail, z.width)
    code_shape = (n, 2 * z.slots, z.tokens)
    inputs = saved_input.reshape(z.all_rows, z.width)

    routing = (grad_out, route_weight, routes, replica, table)
    buf = pl.pallas_call(
        functools.partial(route_kernel, z),
        out_shape=jax.ShapeDtypeStruct(grad_shape, BF),
        in_specs=[smem()] + [whole(a.shape) for a in routing],
        out_specs=whole(grad_shape),
        grid=(1,),
        compiler_params=params(60),
        name="route",
    )(token_count, *routing)
    bufs = [buf] + [swap(buf, "ep", n, k) for k in range(1, n)]

    gathered = lax.all_gather(inputs, "ep")
    downs = pl.pallas_call(
        functools.partial(hidden_kernel, z),
        grid_spec=pltpu.PrefetchScalarGridSpec(
            num_scalar_prefetch=1,
            grid=(z.part_blocks,),
            in_specs=[
                pl.BlockSpec((z.block, z.pair), lambda i, r: (r[1] * z.part_blocks + i, 0))
            ]
            + [pl.BlockSpec(memory_space=pl.ANY)] * (n - 1),
            out_specs=[pl.BlockSpec((z.down_cols, z.block), lambda i, r: (0, i))] * n,
            scratch_shapes=[pltpu.VMEM((n, z.down_cols, z.block), BF)],
        ),
        out_shape=[jax.ShapeDtypeStruct((z.down_cols, z.part), BF)] * n,
        compiler_params=params(16),
        name="hidden_columns",
    )(ids, pair_rows, *bufs[1:])
    downs = [downs[0]] + [swap(downs[k], "ep", n, k) for k in range(1, n)]

    def stack(pieces):
        shape, count = pieces[0].shape, len(pieces)
        return pl.pallas_call(
            stack_kernel,
            in_specs=[whole(shape)] * count,
            out_specs=whole((count,) + shape),
            out_shape=jax.ShapeDtypeStruct((count,) + shape, BF),
            grid=(1,),
            compiler_params=params(12),
            name="stack_columns",
        )(*pieces)

    def halve(keep, got):
        half = (keep.shape[0] // 2,) + keep.shape[1:]
        return pl.pallas_call(
            halve_kernel,
            in_specs=[whole(keep.shape)] * 2,
            out_specs=[whole(half)] * 2,
            out_shape=[jax.ShapeDtypeStruct(half, BF)] * 2,
            grid=(1,),
            compiler_params=params(16),
            name="halve",
        )(keep, got)

    def row_block(i, ids_ref):
        place = i // z.part_blocks
        return (place ^ ids_ref[1]) * z.part_blocks + i % z.part_blocks

    part_shape = (m // 2, z.part, z.hidden)
    outs = pl.pallas_call(
        functools.partial(down_kernel, z),
        grid_spec=pltpu.PrefetchScalarGridSpec(
            num_scalar_prefetch=1,
            grid=(z.blocks,),
            in_specs=[whole(grad_shape)] * n
            + [pl.BlockSpec(memory_space=pltpu.HBM), pl.BlockSpec(memory_space=pl.ANY)],
            out_specs=[whole(part_shape)] * 2
            + [whole((n, z.tokens, z.width)), whole(code_shape)],
            scratch_shapes=[
                pltpu.VMEM((z.local, z.rows, z.width), BF),
                pltpu.VMEM((z.local, z.hidden, z.width), BF),
                pltpu.SemaphoreType.DMA((z.local,)),
            ],
        ),
        out_shape=[jax.ShapeDtypeStruct(part_shape, BF)] * 2
        + [
            jax.ShapeDtypeStruct((n, z.tokens, z.width), BF),
            jax.ShapeDtypeStruct(code_shape, F32),
        ],
        compiler_params=params(48),
        name="hidden_partials",
    )(ids, *bufs, weight_down, downs[0])
    keep, send, grads_all, codes = outs
    got = swap(send, "sub", m, 1)
    bit = 2
    while bit < m:
        keep, send = halve(keep, got)
        got = swap(send, "sub", m, bit)
        bit *= 2
    down_sides = spread_over({0: stack(downs)}, "sub", m, m // 2)
    def total_call(kernel, operands, specs, cols, scratch, name):
        return pl.pallas_call(
            functools.partial(kernel, z),
            grid_spec=pltpu.PrefetchScalarGridSpec(
                num_scalar_prefetch=2,
                grid=(1,),
                in_specs=specs,
                out_specs=[pl.BlockSpec(memory_space=pl.ANY), whole((8, 128))],
                scratch_shapes=[
                    pltpu.VMEM((m, n + 1, cols, z.part), BF),
                    pltpu.VMEM((z.experts, cols, z.width), BF),
                    pltpu.SemaphoreType.DMA((z.experts,)),
                ]
                + scratch,
            ),
            out_shape=[
                jax.ShapeDtypeStruct((z.experts, cols, z.width), BF),
                jax.ShapeDtypeStruct((8, 128), F32),
            ],
            compiler_params=params(32),
            name=name,
        )(ids, table, *operands)

    anywhere = pl.BlockSpec(memory_space=pl.ANY)
    grad_down, down_made = total_call(
        total_down_kernel,
        [*down_sides, grads_all, codes, send],
        [anywhere] * m + [whole((n, z.tokens, z.width)), whole(code_shape), anywhere],
        z.down_cols,
        [pltpu.VMEM((z.slots, z.rows, z.width), BF), pltpu.SemaphoreType.DMA((m,))],
        "down_grads",
    )
    *pieces, grad_part = pl.pallas_call(
        functools.partial(pre_kernel, z),
        grid_spec=pltpu.PrefetchScalarGridSpec(
            num_scalar_prefetch=1,
            grid=(z.part_blocks,),
            in_specs=[pl.BlockSpec((1, z.block, z.hidden), lambda i, r: (0, i, 0))] * 2
            + [
                pl.BlockSpec((z.block, z.pair), lambda i, r: (r[1] * z.part_blocks + i, 0)),
                whole(code_shape),
            ]
            + [pl.BlockSpec(memory_space=pl.ANY)] * (n - 1),
            out_specs=[pl.BlockSpec((z.in_cols, z.block), lambda i, r: (0, i))] * n
            + [pl.BlockSpec((z.block, z.hidden), lambda i, r: (i, 0))],
            scratch_shapes=[pltpu.VMEM((n, z.in_cols, z.block), BF)],
        ),
        out_shape=[jax.ShapeDtypeStruct((z.in_cols, z.part), BF)] * n
        + [jax.ShapeDtypeStruct((z.part, z.hidden), BF)],
        compiler_params=params(16),
        name="pre_grads",
    )(ids, keep, got, pair_rows, codes, *downs[1:])
    pieces = [pieces[0]] + [swap(pieces[k], "ep", n, k) for k in range(1, n)]
    grad_parts = spread_over({0: grad_part}, "sub", m, m // 2)

    back_shape = (n // 2, z.tokens + z.slots, z.width)
    keep, send = pl.pallas_call(
        functools.partial(row_kernel, z),
        grid_spec=pltpu.PrefetchScalarGridSpec(
            num_scalar_prefetch=1,
            grid=(z.blocks,),
            in_specs=[whole((z.part, z.hidden))] * m
            + [
                pl.BlockSpec((z.block, z.pair), lambda i, r: (row_block(i, r), 0)),
                pl.BlockSpec(memory_space=pltpu.HBM),
                whole(code_shape),
            ],
            out_specs=[whole(back_shape)] * 2,
            scratch_shapes=[
                pltpu.VMEM((z.local, z.rows, z.width), BF),
                pltpu.VMEM((n, z.slots, z.tokens), F32),
                pltpu.VMEM((z.block, z.hidden), BF),
                pltpu.VMEM((z.local, z.pair, z.width), BF),
                pltpu.SemaphoreType.DMA((z.local,)),
            ],
        ),
        out_shape=[jax.ShapeDtypeStruct(back_shape, BF)] * 2,
        compiler_params=params(46),
        name="row_grads",
    )(ids, *grad_parts, pair_rows, weight_in, codes)
    got = swap(send, "ep", n, 1)
    sides = []
    for g in range(0, n, n // GROUPS):
        stacked = stack(pieces[g : g + n // GROUPS])
        sides += spread_over({0: stacked}, "sub", m, m // 2)
    bit = 2
    while bit < n:
        keep, send = halve(keep, got)
        got = swap(send, "ep", n, bit)
        bit *= 2

    grad_in, in_made = total_call(
        total_in_kernel,
        [*sides, gathered],
        [anywhere] * (GROUPS * m + 1),
        z.in_cols,
        [
            pltpu.VMEM((n, z.all_rows, z.width), BF),
            pltpu.SemaphoreType.DMA((GROUPS * m,)),
            pltpu.SemaphoreType.DMA((n,)),
        ],
        "in_grads",
    )
    got = gate([got], [in_made])[0]
    grad_tokens, grad_routes = pl.pallas_call(
        functools.partial(token_kernel, z),
        out_shape=[
            jax.ShapeDtypeStruct((z.tokens, z.width), BF),
            jax.ShapeDtypeStruct((z.top, z.tokens), BF),
        ],
        in_specs=[smem()] + [whole(a.shape) for a in (keep, got, routes, replica, table)],
        out_specs=[whole((z.tokens, z.width)), whole((z.top, z.tokens))],
        grid=(1,),
        compiler_params=params(16),
        name="token_grads",
    )(token_count, keep, got, routes, replica, table)

    return grad_tokens, grad_routes.T, grad_in, grad_down


def solution(mesh):
    return jax.shard_map(
        body,
        mesh=mesh,
        in_specs=(
            P(("groups", "ep"), "sub"),
            P(("groups", "ep"), None),
            P(("groups", "ep"), None),
            P(("groups", "ep"), None),
            P("groups", None),
            P(("groups", "ep")),
            P(("groups", "ep"), None, None, "sub"),
            P(("groups", "ep"), None, None),
            P(("groups", "ep"), None, "sub"),
            P(("groups", "ep"), None, "sub"),
        ),
        out_specs=(
            P(("groups", "ep"), "sub"),
            P(("groups", "ep"), None),
            P("groups", "ep", "sub"),
            P("groups", "ep", "sub"),
        ),
        check_vma=False,
    )
```

```python
import functools
import math

import jax
import jax.numpy as jnp
from jax import lax
from jax.experimental import pallas as pl
from jax.experimental.pallas import tpu as pltpu
from jax.sharding import PartitionSpec as P

BF = jnp.bfloat16
F32 = jnp.float32
PER = 2
GROUPS = 1


def nt(a, b):
    return lax.dot_general(a, b, (((1,), (1,)), ((), ())), preferred_element_type=F32)


def tn(a, b):
    return lax.dot_general(a, b, (((0,), (0,)), ((), ())), preferred_element_type=F32)


def nn(a, b):
    return jnp.dot(a, b, preferred_element_type=F32)


def whole(shape):
    zeros = (0,) * len(shape)
    return pl.BlockSpec(shape, lambda *_: zeros)


def smem():
    return pl.BlockSpec(memory_space=pltpu.SMEM)


def params(mib):
    return pltpu.CompilerParams(
        vmem_limit_bytes=mib * 1024 * 1024, dimension_semantics=("arbitrary",)
    )


class Sizes:
    def __init__(self, grad_out, routes, replica_slot, saved_input, weight_in, weight_down):
        self.ep = lax.axis_size("ep")
        self.sub = lax.axis_size("sub")
        self.tokens, self.width = grad_out.shape
        self.top = routes.shape[1]
        self.experts, self.reps = replica_slot.shape
        self.local = weight_in.shape[0]
        self.slots = self.ep * self.local
        self.cap = saved_input.shape[2]
        self.rows = self.ep * self.cap
        self.hidden = weight_down.shape[1]
        self.pair = weight_in.shape[1]
        self.all_rows = self.local * self.rows
        self.part = self.all_rows // self.sub
        self.block = math.gcd(self.rows, self.part)
        self.sources = self.block // self.cap
        self.blocks = self.all_rows // self.block
        self.part_blocks = self.part // self.block
        self.slot_blocks = self.rows // self.block
        self.in_cols = self.pair // self.ep
        self.down_cols = self.hidden // self.ep
        self.cols = self.in_cols + self.down_cols
        self.folds = self.width // self.tokens
        self.tail = 2 * self.slots // self.folds
        self.side_folds = self.width // self.part
        self.side_rows = self.down_cols // self.side_folds
        self.side_start = self.tokens + self.tail


def slot_table(z, table_ref, r):
    ids = lax.broadcasted_iota(jnp.int32, (z.slots, z.experts), 0)
    return (table_ref[r : r + 1, :] == ids).astype(F32).astype(BF)


def key_hits(z, count_ref, routes_ref, replica_ref, r, k):
    ids = lax.broadcasted_iota(jnp.int32, (z.experts, z.tokens), 0)
    live = lax.broadcasted_iota(jnp.int32, (1, z.tokens), 1) < count_ref[0]
    key = jnp.where(live & (replica_ref[k : k + 1, :] == r), routes_ref[k : k + 1, :], -1)
    return key == ids


def route_kernel(z, ids_ref, count_ref, *refs):
    grad_ref, weight_ref, routes_ref, replica_ref, table_ref, pair_ref = refs[:6]
    outs, sides = refs[6:-1], refs[-1]
    weights = weight_ref[...].astype(F32)
    hits = jnp.zeros((z.slots, z.tokens), F32)
    loads = jnp.zeros((z.slots, z.tokens), F32)
    for r in range(z.reps):
        hit = jnp.zeros((z.experts, z.tokens), F32)
        load = jnp.zeros((z.experts, z.tokens), F32)
        for k in range(z.top):
            same = key_hits(z, count_ref, routes_ref, replica_ref, r, k)
            hit = jnp.where(same, 1.0, hit)
            load = jnp.where(same, weights[k : k + 1, :], load)
        table = slot_table(z, table_ref, r)
        hits = hits + nn(table, hit.astype(BF))
        loads = loads + nn(table, load.astype(BF))
    before = lax.broadcasted_iota(jnp.int32, (z.tokens, z.tokens), 0)
    after = lax.broadcasted_iota(jnp.int32, (z.tokens, z.tokens), 1)
    earlier = nn(hits.astype(BF), (before < after).astype(F32).astype(BF))
    code = jnp.where(hits > 0.5, earlier, -1.0)
    both = jnp.concatenate([code, loads], axis=0).astype(BF)
    pair = pair_ref[...]
    gate_pre = pair[:, : z.hidden].astype(F32)
    up = pair[:, z.hidden :].astype(F32)
    hidden = (gate_pre * (1.0 / (1.0 + jnp.exp(-gate_pre))) * up).astype(BF).T
    for q in range(z.ep):
        for f in range(z.side_folds):
            lo = q * z.down_cols + f * z.side_rows
            sides[q, :, f * z.part : (f + 1) * z.part] = hidden[lo : lo + z.side_rows, :]
    for k in range(z.ep):
        outs[k][: z.tokens, :] = grad_ref[...]
        for b in range(z.folds):
            outs[k][z.tokens : z.side_start, b * z.tokens : (b + 1) * z.tokens] = both[
                b * z.tail : (b + 1) * z.tail, :
            ]
        outs[k][z.side_start :, :] = sides[ids_ref[0] ^ k]


def block_place(z, block):
    slot = block // z.slot_blocks
    first = (block % z.slot_blocks) * z.sources
    return slot, first


def block_picks(z, codes_ref, slot, first):
    rows = lax.broadcasted_iota(jnp.int32, (z.cap, z.tokens), 0).astype(F32)
    for a in range(z.sources):
        code = codes_ref[first + a, pl.ds(slot, 1), :]
        yield a, rows == code


def block_scale(z, codes_ref, slot, first):
    parts = []
    for a, pick in block_picks(z, codes_ref, slot, first):
        load = codes_ref[first + a, pl.ds(z.slots + slot, 1), :]
        parts.append(jnp.sum(jnp.where(pick, load, 0.0), axis=1, keepdims=True))
    return jnp.concatenate(parts, axis=0)


def local_picks(z, codes_ref, source, me):
    code = codes_ref[source, pl.ds(pl.multiple_of(me * z.local, z.local), z.local), :]
    rows = lax.broadcasted_iota(jnp.int32, (z.local, z.cap, z.tokens), 1).astype(F32)
    pick = (code[:, None, :] == rows).astype(F32)
    return pick.reshape(z.local * z.cap, z.tokens).astype(BF)


def block_slot(z, mine, step):
    place = step // z.part_blocks
    return ((place ^ mine) * z.part_blocks + step % z.part_blocks) // z.slot_blocks


def weight_copy(weight_ref, held, sems, slot):
    return pltpu.make_async_copy(weight_ref.at[slot], held.at[slot], sems.at[slot])


def down_kernel(z, ids_ref, *refs):
    bufs = refs[: z.ep]
    weight_ref = refs[z.ep]
    parts = refs[z.ep + 1 : z.ep + 1 + z.sub]
    grads_ref, codes_ref, rows_ref, held, sems = refs[z.ep + 1 + z.sub :]
    me, mine = ids_ref[0], ids_ref[1]
    step = pl.program_id(0)

    @pl.when(step == 0)
    def _():
        for s in range(z.local):
            weight_copy(weight_ref, held, sems, s).start()
        for k in range(z.ep):
            source = me ^ k
            grads_ref[source] = bufs[k][: z.tokens, :]
            for b in range(z.folds):
                codes_ref[source, b * z.tail : (b + 1) * z.tail, :] = bufs[k][
                    z.tokens : z.side_start, b * z.tokens : (b + 1) * z.tokens
                ].astype(F32)
        for p in range(z.ep):
            rows = nn(local_picks(z, codes_ref, p, me), grads_ref[p]).astype(BF)
            rows_ref[:, p * z.cap : (p + 1) * z.cap, :] = rows.reshape(z.local, z.cap, z.width)

    place = step // z.part_blocks
    block = (place ^ mine) * z.part_blocks + step % z.part_blocks
    slot, first = block_place(z, block)
    start = pl.multiple_of(first * z.cap, z.block)

    @pl.when((step == 0) | (slot != block_slot(z, mine, step - 1)))
    def _():
        weight_copy(weight_ref, held, sems, slot).wait()

    partial = nt(rows_ref[slot, pl.ds(start, z.block), :], held[slot]).astype(BF)
    spot = pl.multiple_of((step % z.part_blocks) * z.block, z.block)
    for k in range(z.sub):

        @pl.when(place == k)
        def _():
            parts[k][pl.ds(spot, z.block), :] = partial


def gate_terms(z, pair, grad, scale):
    gate = pair[:, : z.hidden].astype(F32)
    up = pair[:, z.hidden :].astype(F32)
    sig = 1.0 / (1.0 + jnp.exp(-gate))
    act = gate * sig
    hidden = act * up
    scaled = scale * grad
    grad_gate = scaled * up * sig * (1.0 + gate * (1.0 - sig))
    grad_up = scaled * act
    return hidden, grad_gate.astype(BF), grad_up.astype(BF)


def pre_kernel(z, ids_ref, keep_ref, got_ref, pair_ref, codes_ref, *refs):
    bufs = refs[: z.ep]
    out_ref, grad_ref, down_ref = refs[z.ep :]

    @pl.when(pl.program_id(0) == 0)
    def _():
        for k in range(z.ep):
            for f in range(z.side_folds):
                down_ref[k, f * z.side_rows : (f + 1) * z.side_rows, :] = bufs[k][
                    z.side_start :, f * z.part : (f + 1) * z.part
                ]

    me = ids_ref[0]
    block = ids_ref[1] * z.part_blocks + pl.program_id(0)
    slot, first = block_place(z, block)
    scale = block_scale(z, codes_ref, me * z.local + slot, first)
    grad = keep_ref[...].astype(F32) + got_ref[...].astype(F32)
    grad_ref[...] = grad.astype(BF)
    _, grad_gate, grad_up = gate_terms(z, pair_ref[...], grad, scale)
    pre = jnp.concatenate([grad_gate.T, grad_up.T], axis=0)
    for q in range(z.ep):
        out_ref[q] = pre[q * z.in_cols : (q + 1) * z.in_cols, :]


def row_kernel(z, ids_ref, *refs):
    grads = refs[: z.sub]
    pair_ref, weight_ref, codes_ref, keep_ref, send_ref = refs[z.sub : z.sub + 5]
    rows_ref, marks, held, weights, sems = refs[z.sub + 5 :]
    me, mine = ids_ref[0], ids_ref[1]
    step = pl.program_id(0)
    place = step // z.part_blocks
    block = (place ^ mine) * z.part_blocks + step % z.part_blocks
    slot, first = block_place(z, block)

    @pl.when(step == 0)
    def _():
        for s in range(z.local):
            weight_copy(weight_ref, weights, sems, s).start()
        marks[...] = jnp.zeros_like(marks)

    spot = pl.multiple_of((step % z.part_blocks) * z.block, z.block)
    for k in range(z.sub):

        @pl.when(place == k)
        def _():
            held[...] = grads[k][pl.ds(spot, z.block), :]

    grad = held[...].astype(F32)
    scale = block_scale(z, codes_ref, me * z.local + slot, first)
    hidden, grad_gate, grad_up = gate_terms(z, pair_ref[...], grad, scale)
    route = jnp.sum(hidden * grad, axis=1, keepdims=True).astype(BF).astype(F32)

    @pl.when((step == 0) | (slot != block_slot(z, mine, step - 1)))
    def _():
        weight_copy(weight_ref, weights, sems, slot).wait()

    rows = nn(grad_gate, weights[slot, : z.hidden, :]) + nn(grad_up, weights[slot, z.hidden :, :])
    start = pl.multiple_of(first * z.cap, z.block)
    rows_ref[slot, pl.ds(start, z.block), :] = rows.astype(BF)
    for a, pick in block_picks(z, codes_ref, me * z.local + slot, first):
        marks[first + a, pl.ds(me * z.local + slot, 1), :] = jnp.sum(
            jnp.where(pick, route[a * z.cap : (a + 1) * z.cap, :], 0.0), axis=0, keepdims=True
        )

    @pl.when(step == z.blocks - 1)
    def _():
        blank = jnp.zeros((z.slots, z.width - z.tokens), BF)
        for k in range(z.ep):
            source = me ^ k
            start = pl.multiple_of(source * z.cap, z.cap)
            rows = rows_ref[:, pl.ds(start, z.cap), :].reshape(z.local * z.cap, z.width)
            out_ref = send_ref if k % 2 else keep_ref
            picks = local_picks(z, codes_ref, source, me)
            out_ref[k // 2, : z.tokens, :] = tn(picks, rows).astype(BF)
            out_ref[k // 2, z.tokens :, : z.tokens] = marks[source].astype(BF)
            out_ref[k // 2, z.tokens :, z.tokens :] = blank


def sum_kernel(*refs):
    count = len(refs) // 3
    for i in range(count):
        total = refs[i][...].astype(F32) + refs[count + i][...].astype(F32)
        refs[2 * count + i][...] = total.astype(BF)


def halve_kernel(keep_ref, got_ref, out_keep, out_send):
    for i in range(out_keep.shape[0]):
        for j, out in enumerate((out_keep, out_send)):
            total = keep_ref[2 * i + j].astype(F32) + got_ref[2 * i + j].astype(F32)
            out[i] = total.astype(BF)


def token_kernel(z, count_ref, *refs):
    keep_ref, got_ref, routes_ref, replica_ref, table_ref, tokens_ref, route_ref = refs
    total = keep_ref[0].astype(F32) + got_ref[0].astype(F32)
    tokens_ref[...] = total[: z.tokens, :].astype(BF)
    rows = total[z.tokens :, : z.tokens].astype(BF)
    totals = [jnp.zeros((1, z.tokens), F32)] * z.top
    for r in range(z.reps):
        spread = tn(slot_table(z, table_ref, r), rows)
        for k in range(z.top):
            same = key_hits(z, count_ref, routes_ref, replica_ref, r, k)
            totals[k] += jnp.sum(jnp.where(same, spread, 0.0), axis=0, keepdims=True)
    route_ref[...] = jnp.concatenate(totals, axis=0).astype(BF)


def left_rows(held, part, side, spot, size):
    return held[part, side, :, pl.ds(spot, size)]


def expert_products(z, ids_ref, table_ref, turn, held, right_rows, out_ref, made, out_sems):
    mine = ids_ref[1]

    def out_copy(expert):
        return pltpu.make_async_copy(made.at[expert], out_ref.at[expert], out_sems.at[expert])

    def some(step, carry):
        for i in range(PER):
            expert = step * PER + i
            first = table_ref[0, expert]
            left, right = [], []
            for r in range(z.reps):
                slot_id = table_ref[r, expert]
                source = slot_id // z.local
                for b in range(z.slot_blocks):
                    block = (slot_id % z.local) * z.slot_blocks + b
                    part = (block // z.part_blocks) ^ mine
                    spot = pl.multiple_of((block % z.part_blocks) * z.block, z.block)
                    side = source ^ turn
                    if r:
                        side = jnp.where(slot_id == first, z.ep, side)
                    left.append(functools.partial(left_rows, held, part, side, spot, z.block))
                    right.append(functools.partial(right_rows, slot_id, block, b))
            half = len(left) // 2

            def product(lo, hi):
                return nn(
                    jnp.concatenate([f() for f in left[lo:hi]], axis=1),
                    jnp.concatenate([f() for f in right[lo:hi]], axis=0),
                )

            few = table_ref[z.reps // 2, expert] == first

            @pl.when(few)
            def _():
                made[expert] = product(0, half).astype(BF)

            @pl.when(jnp.logical_not(few))
            def _():
                made[expert] = product(0, 2 * half).astype(BF)

            out_copy(expert).start()
        return carry

    lax.fori_loop(0, z.experts // PER, some, 0)
    for expert in range(z.experts):
        out_copy(expert).wait()


def total_down_kernel(z, ids_ref, table_ref, *refs):
    sides = refs[: z.sub]
    grads_ref, codes_ref, out_ref, token_ref, held, made, out_sems, scaled, sems = refs[z.sub :]
    token_ref[...] = jnp.zeros_like(token_ref)

    def moves(act):
        for k in range(z.sub):
            act(
                pltpu.make_async_copy(
                    sides[k], held.at[k, pl.ds(0, z.ep)], sems.at[k]
                )
            )

    moves(lambda copy: copy.start())
    held[:, z.ep] = jnp.zeros_like(held[:, z.ep])
    rows = lax.broadcasted_iota(jnp.int32, (z.slots, z.cap, z.tokens), 1).astype(F32)
    for p in range(z.ep):
        code = codes_ref[p, : z.slots, :][:, None, :]
        load = codes_ref[p, z.slots :, :][:, None, :]
        pick = jnp.where(rows == code, load, 0.0).reshape(z.slots * z.cap, z.tokens)
        result = nn(pick.astype(BF), grads_ref[p]).astype(BF)
        scaled[:, p * z.cap : (p + 1) * z.cap, :] = result.reshape(z.slots, z.cap, z.width)
    moves(lambda copy: copy.wait())

    def right_rows(slot_id, block, b):
        return scaled[slot_id, b * z.block : (b + 1) * z.block, :]

    expert_products(z, ids_ref, table_ref, ids_ref[0], held, right_rows, out_ref, made, out_sems)


def total_in_kernel(z, ids_ref, table_ref, *refs):
    sides, refs = refs[: GROUPS * z.sub], refs[GROUPS * z.sub :]
    size = z.ep // GROUPS
    gathered_ref, out_ref, token_ref, held, made, out_sems, inputs_ref, sems, in_sems = refs
    token_ref[...] = jnp.zeros_like(token_ref)

    def moves(act):
        for i in range(GROUPS * z.sub):
            g, k = divmod(i, z.sub)
            spots = held.at[k, pl.ds(g * size, size)]
            act(pltpu.make_async_copy(sides[i], spots, sems.at[i]))
        for p in range(z.ep):
            act(pltpu.make_async_copy(gathered_ref.at[p], inputs_ref.at[p], in_sems.at[p]))

    moves(lambda copy: copy.start())
    held[:, z.ep] = jnp.zeros_like(held[:, z.ep])
    moves(lambda copy: copy.wait())

    def right_rows(slot_id, block, b):
        start = pl.multiple_of(block * z.block, z.block)
        return inputs_ref[slot_id // z.local, pl.ds(start, z.block), :]

    expert_products(z, ids_ref, table_ref, 0, held, right_rows, out_ref, made, out_sems)


def swap(x, axis, size, bit):
    return lax.ppermute(x, axis, [(i, i ^ bit) for i in range(size)])


def spread_over(have, axis, size, bit):
    have = dict(have)
    while bit:
        for k in list(have):
            if k | bit not in have:
                have[k | bit] = swap(have[k], axis, size, bit)
        bit //= 2
    return [have[k] for k in range(size)]


def nothing(*refs):
    pass


def gate(values, after):
    anywhere = pl.BlockSpec(memory_space=pl.ANY)
    return pl.pallas_call(
        nothing,
        in_specs=[anywhere] * (len(values) + len(after)),
        out_specs=[anywhere] * len(values),
        out_shape=[jax.ShapeDtypeStruct(v.shape, v.dtype) for v in values],
        input_output_aliases={i: i for i in range(len(values))},
        compiler_params=pltpu.CompilerParams(vmem_limit_bytes=1024 * 1024),
        name="gate",
    )(*values, *after)


def body(
    grad_out,
    route_weight,
    routes,
    replica,
    replica_slot,
    token_count,
    saved_input,
    saved_gate_up,
    weight_in,
    weight_down,
):
    z = Sizes(grad_out, routes, replica_slot, saved_input, weight_in, weight_down)
    n, m = z.ep, z.sub
    ids = jnp.stack([lax.axis_index("ep"), lax.axis_index("sub")]).astype(jnp.int32)
    routes, replica, table = routes.T, replica.T, replica_slot.T
    route_weight = route_weight.T
    pair_rows = saved_gate_up.reshape(z.all_rows, z.pair)
    grad_shape = (z.side_start + z.side_rows, z.width)
    code_shape = (n, 2 * z.slots, z.tokens)
    inputs = saved_input.reshape(z.all_rows, z.width)

    routing = (grad_out, route_weight, routes, replica, table)
    gathered = lax.all_gather(inputs, "ep")
    bufs = pl.pallas_call(
        functools.partial(route_kernel, z),
        grid_spec=pltpu.PrefetchScalarGridSpec(
            num_scalar_prefetch=1,
            grid=(1,),
            in_specs=[smem()]
            + [whole(a.shape) for a in routing]
            + [pl.BlockSpec((z.part, z.pair), lambda i, r: (r[1], 0))],
            out_specs=[whole(grad_shape)] * n,
            scratch_shapes=[pltpu.VMEM((n, z.side_rows, z.width), BF)],
        ),
        out_shape=[jax.ShapeDtypeStruct(grad_shape, BF)] * n,
        compiler_params=params(60),
        name="route",
    )(ids, token_count, *routing, pair_rows)
    bufs = [bufs[0]] + [swap(bufs[k], "ep", n, k) for k in range(1, n)]

    def halve(keep, got):
        half = (keep.shape[0] // 2,) + keep.shape[1:]
        return pl.pallas_call(
            halve_kernel,
            in_specs=[whole(keep.shape)] * 2,
            out_specs=[whole(half)] * 2,
            out_shape=[jax.ShapeDtypeStruct(half, BF)] * 2,
            grid=(1,),
            compiler_params=params(16),
            name="halve",
        )(keep, got)

    def row_block(i, ids_ref):
        place = i // z.part_blocks
        return (place ^ ids_ref[1]) * z.part_blocks + i % z.part_blocks

    part_shape = (z.part, z.hidden)
    outs = pl.pallas_call(
        functools.partial(down_kernel, z),
        grid_spec=pltpu.PrefetchScalarGridSpec(
            num_scalar_prefetch=1,
            grid=(z.blocks,),
            in_specs=[whole(grad_shape)] * n + [pl.BlockSpec(memory_space=pltpu.HBM)],
            out_specs=[whole(part_shape)] * m
            + [whole((n, z.tokens, z.width)), whole(code_shape)],
            scratch_shapes=[
                pltpu.VMEM((z.local, z.rows, z.width), BF),
                pltpu.VMEM((z.local, z.hidden, z.width), BF),
                pltpu.SemaphoreType.DMA((z.local,)),
            ],
        ),
        out_shape=[jax.ShapeDtypeStruct(part_shape, BF)] * m
        + [
            jax.ShapeDtypeStruct((n, z.tokens, z.width), BF),
            jax.ShapeDtypeStruct(code_shape, F32),
        ],
        compiler_params=params(48),
        name="hidden_partials",
    )(ids, *bufs, weight_down)
    parts, (grads_all, codes) = outs[:m], outs[m:]
    bit = 1
    while True:
        keep = parts[::2]
        got = [swap(part, "sub", m, bit) for part in parts[1::2]]
        bit *= 2
        if bit == m:
            break
        count = len(keep)
        parts = pl.pallas_call(
            sum_kernel,
            in_specs=[whole(part_shape)] * 2 * count,
            out_specs=[whole(part_shape)] * count,
            out_shape=[jax.ShapeDtypeStruct(part_shape, BF)] * count,
            grid=(1,),
            compiler_params=params(16),
            name="sum_parts",
        )(*keep, *got)
    pre, grad_part, down_columns = pl.pallas_call(
        functools.partial(pre_kernel, z),
        grid_spec=pltpu.PrefetchScalarGridSpec(
            num_scalar_prefetch=1,
            grid=(z.part_blocks,),
            in_specs=[pl.BlockSpec((z.block, z.hidden), lambda i, r: (i, 0))] * 2
            + [
                pl.BlockSpec((z.block, z.pair), lambda i, r: (r[1] * z.part_blocks + i, 0)),
                whole(code_shape),
            ]
            + [whole(grad_shape)] * n,
            out_specs=[
                pl.BlockSpec((n, z.in_cols, z.block), lambda i, r: (0, 0, i)),
                pl.BlockSpec((z.block, z.hidden), lambda i, r: (i, 0)),
                whole((n, z.down_cols, z.part)),
            ],
        ),
        out_shape=[
            jax.ShapeDtypeStruct((n, z.in_cols, z.part), BF),
            jax.ShapeDtypeStruct((z.part, z.hidden), BF),
            jax.ShapeDtypeStruct((n, z.down_cols, z.part), BF),
        ],
        compiler_params=params(16),
        name="pre_grads",
    )(ids, keep[0], got[0], pair_rows, codes, *bufs)
    columns = lax.all_to_all(pre, "ep", split_axis=0, concat_axis=0, tiled=True)
    down_sides = spread_over({0: down_columns}, "sub", m, m // 2)
    def total_call(kernel, operands, specs, cols, scratch, mib, name):
        return pl.pallas_call(
            functools.partial(kernel, z),
            grid_spec=pltpu.PrefetchScalarGridSpec(
                num_scalar_prefetch=2,
                grid=(1,),
                in_specs=specs,
                out_specs=[pl.BlockSpec(memory_space=pl.ANY), whole((8, 128))],
                scratch_shapes=[
                    pltpu.VMEM((m, n + 1, cols, z.part), BF),
                    pltpu.VMEM((z.experts, cols, z.width), BF),
                    pltpu.SemaphoreType.DMA((z.experts,)),
                ]
                + scratch,
            ),
            out_shape=[
                jax.ShapeDtypeStruct((z.experts, cols, z.width), BF),
                jax.ShapeDtypeStruct((8, 128), F32),
            ],
            compiler_params=params(mib),
            name=name,
        )(ids, table, *operands)

    anywhere = pl.BlockSpec(memory_space=pl.ANY)
    grad_down, down_made = total_call(
        total_down_kernel,
        [*down_sides, grads_all, codes],
        [anywhere] * m + [whole((n, z.tokens, z.width)), whole(code_shape)],
        z.down_cols,
        [pltpu.VMEM((z.slots, z.rows, z.width), BF), pltpu.SemaphoreType.DMA((m,))],
        32,
        "down_grads",
    )
    grad_parts = spread_over({0: grad_part}, "sub", m, m // 2)

    back_shape = (n // 2, z.tokens + z.slots, z.width)
    keep, send = pl.pallas_call(
        functools.partial(row_kernel, z),
        grid_spec=pltpu.PrefetchScalarGridSpec(
            num_scalar_prefetch=1,
            grid=(z.blocks,),
            in_specs=[whole((z.part, z.hidden))] * m
            + [
                pl.BlockSpec((z.block, z.pair), lambda i, r: (row_block(i, r), 0)),
                pl.BlockSpec(memory_space=pltpu.HBM),
                whole(code_shape),
            ],
            out_specs=[whole(back_shape)] * 2,
            scratch_shapes=[
                pltpu.VMEM((z.local, z.rows, z.width), BF),
                pltpu.VMEM((n, z.slots, z.tokens), F32),
                pltpu.VMEM((z.block, z.hidden), BF),
                pltpu.VMEM((z.local, z.pair, z.width), BF),
                pltpu.SemaphoreType.DMA((z.local,)),
            ],
        ),
        out_shape=[jax.ShapeDtypeStruct(back_shape, BF)] * 2,
        compiler_params=params(46),
        name="row_grads",
    )(ids, *grad_parts, pair_rows, weight_in, codes)
    got = swap(send, "ep", n, 1)
    sides = [columns, swap(columns, "sub", m, m // 2)]
    sides = gate(sides, [gathered, keep, down_made])
    sides = spread_over({0: sides[0], m // 2: sides[1]}, "sub", m, m // 4)
    bit = 2
    while bit < n:
        keep, send = halve(keep, got)
        got = swap(send, "ep", n, bit)
        bit *= 2

    grad_in, in_made = total_call(
        total_in_kernel,
        [*sides, gathered],
        [anywhere] * (GROUPS * m) + [pl.BlockSpec(memory_space=pltpu.HBM)],
        z.in_cols,
        [
            pltpu.VMEM((n, z.all_rows, z.width), BF),
            pltpu.SemaphoreType.DMA((GROUPS * m,)),
            pltpu.SemaphoreType.DMA((n,)),
        ],
        44,
        "in_grads",
    )
    got = gate([got], [in_made])[0]
    grad_tokens, grad_routes = pl.pallas_call(
        functools.partial(token_kernel, z),
        out_shape=[
            jax.ShapeDtypeStruct((z.tokens, z.width), BF),
            jax.ShapeDtypeStruct((z.top, z.tokens), BF),
        ],
        in_specs=[smem()] + [whole(a.shape) for a in (keep, got, routes, replica, table)],
        out_specs=[whole((z.tokens, z.width)), whole((z.top, z.tokens))],
        grid=(1,),
        compiler_params=params(16),
        name="token_grads",
    )(token_count, keep, got, routes, replica, table)

    return grad_tokens, grad_routes.T, grad_in, grad_down


def solution(mesh):
    return jax.shard_map(
        body,
        mesh=mesh,
        in_specs=(
            P(("groups", "ep"), "sub"),
            P(("groups", "ep"), None),
            P(("groups", "ep"), None),
            P(("groups", "ep"), None),
            P("groups", None),
            P(("groups", "ep")),
            P(("groups", "ep"), None, None, "sub"),
            P(("groups", "ep"), None, None),
            P(("groups", "ep"), None, "sub"),
            P(("groups", "ep"), None, "sub"),
        ),
        out_specs=(
            P(("groups", "ep"), "sub"),
            P(("groups", "ep"), None),
            P("groups", "ep", "sub"),
            P("groups", "ep", "sub"),
        ),
        check_vma=False,
    )
```

```python
import functools
import math

import jax
import jax.numpy as jnp
from jax import lax
from jax.experimental import pallas as pl
from jax.experimental.pallas import tpu as pltpu
from jax.sharding import PartitionSpec as P

BF = jnp.bfloat16
F32 = jnp.float32
PER = 2


def nt(a, b):
    return lax.dot_general(a, b, (((1,), (1,)), ((), ())), preferred_element_type=F32)


def tn(a, b):
    return lax.dot_general(a, b, (((0,), (0,)), ((), ())), preferred_element_type=F32)


def nn(a, b):
    return jnp.dot(a, b, preferred_element_type=F32)


def whole(shape):
    zeros = (0,) * len(shape)
    return pl.BlockSpec(shape, lambda *_: zeros)


def smem():
    return pl.BlockSpec(memory_space=pltpu.SMEM)


def params(mib):
    return pltpu.CompilerParams(
        vmem_limit_bytes=mib * 1024 * 1024, dimension_semantics=("arbitrary",)
    )


class Sizes:
    def __init__(self, grad_out, routes, replica_slot, saved_input, weight_in, weight_down):
        self.ep = lax.axis_size("ep")
        self.sub = lax.axis_size("sub")
        self.tokens, self.width = grad_out.shape
        self.top = routes.shape[1]
        self.experts, self.reps = replica_slot.shape
        self.local = weight_in.shape[0]
        self.slots = self.ep * self.local
        self.cap = saved_input.shape[2]
        self.rows = self.ep * self.cap
        self.hidden = weight_down.shape[1]
        self.pair = weight_in.shape[1]
        self.all_rows = self.local * self.rows
        self.part = self.all_rows // self.sub
        self.block = math.gcd(self.rows, self.part)
        self.sources = self.block // self.cap
        self.blocks = self.all_rows // self.block
        self.part_blocks = self.part // self.block
        self.slot_blocks = self.rows // self.block
        self.in_cols = self.pair // self.ep
        self.down_cols = self.hidden // self.ep
        self.cols = self.in_cols + self.down_cols
        self.folds = self.width // self.tokens
        self.tail = 2 * self.slots // self.folds


def slot_table(z, table_ref, r):
    ids = lax.broadcasted_iota(jnp.int32, (z.slots, z.experts), 0)
    return (table_ref[r : r + 1, :] == ids).astype(F32).astype(BF)


def key_hits(z, count_ref, routes_ref, replica_ref, r, k):
    ids = lax.broadcasted_iota(jnp.int32, (z.experts, z.tokens), 0)
    live = lax.broadcasted_iota(jnp.int32, (1, z.tokens), 1) < count_ref[0]
    key = jnp.where(live & (replica_ref[k : k + 1, :] == r), routes_ref[k : k + 1, :], -1)
    return key == ids


def route_kernel(z, count_ref, grad_ref, weight_ref, routes_ref, replica_ref, table_ref, out_ref):
    weights = weight_ref[...].astype(F32)
    hits = jnp.zeros((z.slots, z.tokens), F32)
    loads = jnp.zeros((z.slots, z.tokens), F32)
    for r in range(z.reps):
        hit = jnp.zeros((z.experts, z.tokens), F32)
        load = jnp.zeros((z.experts, z.tokens), F32)
        for k in range(z.top):
            same = key_hits(z, count_ref, routes_ref, replica_ref, r, k)
            hit = jnp.where(same, 1.0, hit)
            load = jnp.where(same, weights[k : k + 1, :], load)
        table = slot_table(z, table_ref, r)
        hits = hits + nn(table, hit.astype(BF))
        loads = loads + nn(table, load.astype(BF))
    before = lax.broadcasted_iota(jnp.int32, (z.tokens, z.tokens), 0)
    after = lax.broadcasted_iota(jnp.int32, (z.tokens, z.tokens), 1)
    earlier = nn(hits.astype(BF), (before < after).astype(F32).astype(BF))
    code = jnp.where(hits > 0.5, earlier, -1.0)
    both = jnp.concatenate([code, loads], axis=0).astype(BF)
    out_ref[: z.tokens, :] = grad_ref[...]
    for b in range(z.folds):
        out_ref[z.tokens :, b * z.tokens : (b + 1) * z.tokens] = both[
            b * z.tail : (b + 1) * z.tail, :
        ]


def block_place(z, block):
    slot = block // z.slot_blocks
    first = (block % z.slot_blocks) * z.sources
    return slot, first


def block_picks(z, codes_ref, slot, first):
    rows = lax.broadcasted_iota(jnp.int32, (z.cap, z.tokens), 0).astype(F32)
    for a in range(z.sources):
        code = codes_ref[first + a, pl.ds(slot, 1), :]
        yield a, rows == code


def block_scale(z, codes_ref, slot, first):
    parts = []
    for a, pick in block_picks(z, codes_ref, slot, first):
        load = codes_ref[first + a, pl.ds(z.slots + slot, 1), :]
        parts.append(jnp.sum(jnp.where(pick, load, 0.0), axis=1, keepdims=True))
    return jnp.concatenate(parts, axis=0)


def local_picks(z, codes_ref, source, me):
    code = codes_ref[source, pl.ds(pl.multiple_of(me * z.local, z.local), z.local), :]
    rows = lax.broadcasted_iota(jnp.int32, (z.local, z.cap, z.tokens), 1).astype(F32)
    pick = (code[:, None, :] == rows).astype(F32)
    return pick.reshape(z.local * z.cap, z.tokens).astype(BF)


def block_slot(z, mine, step):
    place = step // z.part_blocks
    return ((place ^ mine) * z.part_blocks + step % z.part_blocks) // z.slot_blocks


def weight_copy(weight_ref, held, sems, slot):
    return pltpu.make_async_copy(weight_ref.at[slot], held.at[slot], sems.at[slot])


def down_kernel(z, ids_ref, *refs):
    bufs = refs[: z.ep]
    weight_ref = refs[z.ep]
    parts = refs[z.ep + 2 : z.ep + 4]
    grads_ref, codes_ref, rows_ref, held, sems = refs[z.ep + 4 :]
    me, mine = ids_ref[0], ids_ref[1]
    step = pl.program_id(0)

    @pl.when(step == 0)
    def _():
        for s in range(z.local):
            weight_copy(weight_ref, held, sems, s).start()
        for k in range(z.ep):
            source = me ^ k
            grads_ref[source] = bufs[k][: z.tokens, :]
            for b in range(z.folds):
                codes_ref[source, b * z.tail : (b + 1) * z.tail, :] = bufs[k][
                    z.tokens :, b * z.tokens : (b + 1) * z.tokens
                ].astype(F32)
        for p in range(z.ep):
            rows = nn(local_picks(z, codes_ref, p, me), grads_ref[p]).astype(BF)
            rows_ref[:, p * z.cap : (p + 1) * z.cap, :] = rows.reshape(z.local, z.cap, z.width)

    place = step // z.part_blocks
    block = (place ^ mine) * z.part_blocks + step % z.part_blocks
    slot, first = block_place(z, block)
    start = pl.multiple_of(first * z.cap, z.block)

    @pl.when((step == 0) | (slot != block_slot(z, mine, step - 1)))
    def _():
        weight_copy(weight_ref, held, sems, slot).wait()

    partial = nt(rows_ref[slot, pl.ds(start, z.block), :], held[slot]).astype(BF)
    spot = pl.multiple_of((step % z.part_blocks) * z.block, z.block)
    for k in range(z.sub):

        @pl.when(place == k)
        def _():
            parts[k % 2][k // 2, pl.ds(spot, z.block), :] = partial


def gate_terms(z, pair, grad, scale):
    gate = pair[:, : z.hidden].astype(F32)
    up = pair[:, z.hidden :].astype(F32)
    sig = 1.0 / (1.0 + jnp.exp(-gate))
    act = gate * sig
    hidden = act * up
    scaled = scale * grad
    grad_gate = scaled * up * sig * (1.0 + gate * (1.0 - sig))
    grad_up = scaled * act
    return hidden, grad_gate.astype(BF), grad_up.astype(BF)


def pre_kernel(z, ids_ref, keep_ref, got_ref, pair_ref, codes_ref, *refs):
    outs, (grad_ref, sides) = refs[: z.ep], refs[z.ep :]
    me = ids_ref[0]
    block = ids_ref[1] * z.part_blocks + pl.program_id(0)
    slot, first = block_place(z, block)
    scale = block_scale(z, codes_ref, me * z.local + slot, first)
    grad = keep_ref[0].astype(F32) + got_ref[0].astype(F32)
    grad_ref[...] = grad.astype(BF)
    _, grad_gate, grad_up = gate_terms(z, pair_ref[...], grad, scale)
    send_columns(z, me, jnp.concatenate([grad_gate.T, grad_up.T], axis=0), sides, outs)


def send_columns(z, me, columns, sides, outs):
    size = columns.shape[0] // z.ep
    for q in range(z.ep):
        sides[q] = columns[q * size : (q + 1) * size, :]
    for k in range(z.ep):
        outs[k][...] = sides[me ^ k]


def hidden_kernel(z, ids_ref, pair_ref, after_ref, other_ref, *refs):
    pair = pair_ref[...]
    gate_pre = pair[:, : z.hidden].astype(F32)
    up = pair[:, z.hidden :].astype(F32)
    hidden = gate_pre * (1.0 / (1.0 + jnp.exp(-gate_pre))) * up
    send_columns(z, ids_ref[0], hidden.astype(BF).T, refs[-1], refs[:-1])


def stack_kernel(z, *refs):
    for k in range(z.ep):
        refs[-1][k] = refs[k][...]


def row_kernel(z, ids_ref, *refs):
    grads = refs[: z.sub]
    pair_ref, weight_ref, codes_ref = refs[z.sub : z.sub + 3]
    outs = refs[z.sub + 3 : z.sub + 3 + z.ep]
    rows_ref, marks, held, weights, sems = refs[z.sub + 3 + z.ep :]
    me, mine = ids_ref[0], ids_ref[1]
    step = pl.program_id(0)
    place = step // z.part_blocks
    block = (place ^ mine) * z.part_blocks + step % z.part_blocks
    slot, first = block_place(z, block)

    @pl.when(step == 0)
    def _():
        for s in range(z.local):
            weight_copy(weight_ref, weights, sems, s).start()
        marks[...] = jnp.zeros_like(marks)

    spot = pl.multiple_of((step % z.part_blocks) * z.block, z.block)
    for k in range(z.sub):

        @pl.when(place == k)
        def _():
            held[...] = grads[k][pl.ds(spot, z.block), :]

    grad = held[...].astype(F32)
    scale = block_scale(z, codes_ref, me * z.local + slot, first)
    hidden, grad_gate, grad_up = gate_terms(z, pair_ref[...], grad, scale)
    route = jnp.sum(hidden * grad, axis=1, keepdims=True).astype(BF).astype(F32)

    @pl.when((step == 0) | (slot != block_slot(z, mine, step - 1)))
    def _():
        weight_copy(weight_ref, weights, sems, slot).wait()

    rows = nn(grad_gate, weights[slot, : z.hidden, :]) + nn(grad_up, weights[slot, z.hidden :, :])
    start = pl.multiple_of(first * z.cap, z.block)
    rows_ref[slot, pl.ds(start, z.block), :] = rows.astype(BF)
    for a, pick in block_picks(z, codes_ref, me * z.local + slot, first):
        marks[first + a, pl.ds(me * z.local + slot, 1), :] = jnp.sum(
            jnp.where(pick, route[a * z.cap : (a + 1) * z.cap, :], 0.0), axis=0, keepdims=True
        )

    @pl.when(step == z.blocks - 1)
    def _():
        blank = jnp.zeros((z.slots, z.width - z.tokens), BF)
        for k in range(z.ep):
            source = me ^ k
            start = pl.multiple_of(source * z.cap, z.cap)
            rows = rows_ref[:, pl.ds(start, z.cap), :].reshape(z.local * z.cap, z.width)
            picks = local_picks(z, codes_ref, source, me)
            outs[k][: z.tokens, :] = tn(picks, rows).astype(BF)
            outs[k][z.tokens :, : z.tokens] = marks[source].astype(BF)
            outs[k][z.tokens :, z.tokens :] = blank


def sum_kernel(*refs):
    count = len(refs) // 3
    for i in range(count):
        total = refs[i][...].astype(F32) + refs[count + i][...].astype(F32)
        refs[2 * count + i][...] = total.astype(BF)


def halve_kernel(keep_ref, got_ref, out_keep, out_send):
    for i in range(out_keep.shape[0]):
        for j, out in enumerate((out_keep, out_send)):
            total = keep_ref[2 * i + j].astype(F32) + got_ref[2 * i + j].astype(F32)
            out[i] = total.astype(BF)


def token_kernel(z, count_ref, *refs):
    keep_ref, got_ref, routes_ref, replica_ref, table_ref, tokens_ref, route_ref = refs
    total = keep_ref[...].astype(F32) + got_ref[...].astype(F32)
    tokens_ref[...] = total[: z.tokens, :].astype(BF)
    rows = total[z.tokens :, : z.tokens].astype(BF)
    totals = [jnp.zeros((1, z.tokens), F32)] * z.top
    for r in range(z.reps):
        spread = tn(slot_table(z, table_ref, r), rows)
        for k in range(z.top):
            same = key_hits(z, count_ref, routes_ref, replica_ref, r, k)
            totals[k] += jnp.sum(jnp.where(same, spread, 0.0), axis=0, keepdims=True)
    route_ref[...] = jnp.concatenate(totals, axis=0).astype(BF)


def input_moves(z, me, own_ref, rights, lefts, inputs_ref, own_sem, right_sems, left_sems, act):
    act(pltpu.make_async_copy(own_ref, inputs_ref.at[me], own_sem))
    for d in range(1, z.ep):

        @pl.when(me >= d)
        def _():
            act(
                pltpu.make_async_copy(
                    rights[d - 1], inputs_ref.at[me - d], right_sems.at[d - 1]
                )
            )

        @pl.when(me + d < z.ep)
        def _():
            act(
                pltpu.make_async_copy(
                    lefts[d - 1], inputs_ref.at[me + d], left_sems.at[d - 1]
                )
            )


def left_rows(held, part, side, spot, size):
    return held[part, side, :, pl.ds(spot, size)]


def expert_products(z, ids_ref, table_ref, turn, held, right_rows, out_ref, made, out_sems):
    mine = ids_ref[1]

    def out_copy(expert):
        return pltpu.make_async_copy(made.at[expert], out_ref.at[expert], out_sems.at[expert])

    def some(step, carry):
        for i in range(PER):
            expert = step * PER + i
            first = table_ref[0, expert]
            left, right = [], []
            for r in range(z.reps):
                slot_id = table_ref[r, expert]
                source = slot_id // z.local
                for b in range(z.slot_blocks):
                    block = (slot_id % z.local) * z.slot_blocks + b
                    part = (block // z.part_blocks) ^ mine
                    spot = pl.multiple_of((block % z.part_blocks) * z.block, z.block)
                    side = source ^ turn
                    if r:
                        side = jnp.where(slot_id == first, z.ep, side)
                    left.append(functools.partial(left_rows, held, part, side, spot, z.block))
                    right.append(functools.partial(right_rows, slot_id, block, b))
            half = len(left) // 2

            def product(lo, hi):
                return nn(
                    jnp.concatenate([f() for f in left[lo:hi]], axis=1),
                    jnp.concatenate([f() for f in right[lo:hi]], axis=0),
                )

            few = table_ref[z.reps // 2, expert] == first

            @pl.when(few)
            def _():
                made[expert] = product(0, half).astype(BF)

            @pl.when(jnp.logical_not(few))
            def _():
                made[expert] = product(0, 2 * half).astype(BF)

            out_copy(expert).start()
        return carry

    lax.fori_loop(0, z.experts // PER, some, 0)
    for expert in range(z.experts):
        out_copy(expert).wait()


def total_down_kernel(z, ids_ref, table_ref, *refs):
    sides = refs[: z.sub]
    grads_ref, codes_ref, out_ref, token_ref, held, made, out_sems, scaled, sems = refs[z.sub :]
    token_ref[...] = jnp.zeros_like(token_ref)

    def moves(act):
        for k in range(z.sub):
            act(
                pltpu.make_async_copy(
                    sides[k], held.at[k, pl.ds(0, z.ep)], sems.at[k]
                )
            )

    moves(lambda copy: copy.start())
    held[:, z.ep] = jnp.zeros_like(held[:, z.ep])
    rows = lax.broadcasted_iota(jnp.int32, (z.slots, z.cap, z.tokens), 1).astype(F32)
    for p in range(z.ep):
        code = codes_ref[p, : z.slots, :][:, None, :]
        load = codes_ref[p, z.slots :, :][:, None, :]
        pick = jnp.where(rows == code, load, 0.0).reshape(z.slots * z.cap, z.tokens)
        result = nn(pick.astype(BF), grads_ref[p]).astype(BF)
        scaled[:, p * z.cap : (p + 1) * z.cap, :] = result.reshape(z.slots, z.cap, z.width)
    moves(lambda copy: copy.wait())

    def right_rows(slot_id, block, b):
        return scaled[slot_id, b * z.block : (b + 1) * z.block, :]

    expert_products(z, ids_ref, table_ref, ids_ref[0], held, right_rows, out_ref, made, out_sems)


def total_in_kernel(z, ids_ref, table_ref, *refs):
    sides, refs = refs[: z.sub], refs[z.sub :]
    own_ref, rights, lefts = refs[0], refs[1 : z.ep], refs[z.ep : 2 * z.ep - 1]
    out_ref, token_ref, held, made, out_sems, inputs_ref, sems, *other_sems = refs[2 * z.ep - 1 :]
    token_ref[...] = jnp.zeros_like(token_ref)

    def moves(act):
        for k in range(z.sub):
            act(pltpu.make_async_copy(sides[k], held.at[k, pl.ds(0, z.ep)], sems.at[k]))
        input_moves(z, ids_ref[0], own_ref, rights, lefts, inputs_ref, *other_sems, act)

    moves(lambda copy: copy.start())
    held[:, z.ep] = jnp.zeros_like(held[:, z.ep])
    moves(lambda copy: copy.wait())

    def right_rows(slot_id, block, b):
        start = pl.multiple_of(block * z.block, z.block)
        return inputs_ref[slot_id // z.local, pl.ds(start, z.block), :]

    expert_products(z, ids_ref, table_ref, ids_ref[0], held, right_rows, out_ref, made, out_sems)


def swap(x, axis, size, bit):
    return lax.ppermute(x, axis, [(i, i ^ bit) for i in range(size)])


def spread_over(have, axis, size, bit):
    have = dict(have)
    while bit:
        for k in list(have):
            if k | bit not in have:
                have[k | bit] = swap(have[k], axis, size, bit)
        bit //= 2
    return [have[k] for k in range(size)]


def nothing(*refs):
    pass


def gate(values, after):
    anywhere = pl.BlockSpec(memory_space=pl.ANY)
    return pl.pallas_call(
        nothing,
        in_specs=[anywhere] * (len(values) + len(after)),
        out_specs=[anywhere] * len(values),
        out_shape=[jax.ShapeDtypeStruct(v.shape, v.dtype) for v in values],
        input_output_aliases={i: i for i in range(len(values))},
        compiler_params=pltpu.CompilerParams(vmem_limit_bytes=1024 * 1024),
        name="gate",
    )(*values, *after)


def pick_kernel(first, ids_ref, go_ref, back_ref, out_ref, sem):
    for condition, ref in ((ids_ref[0] >= first, go_ref), (ids_ref[0] < first, back_ref)):

        @pl.when(condition)
        def _():
            copy = pltpu.make_async_copy(ref, out_ref, sem)
            copy.start()
            copy.wait()


def pick(ids, go, back, first):
    anywhere = pl.BlockSpec(memory_space=pl.ANY)
    return pl.pallas_call(
        functools.partial(pick_kernel, first),
        in_specs=[smem(), anywhere, anywhere],
        out_specs=anywhere,
        out_shape=jax.ShapeDtypeStruct(go.shape, go.dtype),
        scratch_shapes=[pltpu.SemaphoreType.DMA],
        compiler_params=pltpu.CompilerParams(vmem_limit_bytes=1024 * 1024),
        name="pick",
    )(ids, go, back)


def chain_step(go, back, axis, size, d):
    rights = [(i, i + 1) for i in range(d - 1, size - 1)]
    lefts = [(i, i - 1) for i in range(size - d, 0, -1)]
    if d > 1 and go is back:
        got = lax.ppermute(go, axis, rights + lefts)
        return got, got
    return lax.ppermute(go, axis, rights), lax.ppermute(back, axis, lefts)


def body(
    grad_out,
    route_weight,
    routes,
    replica,
    replica_slot,
    token_count,
    saved_input,
    saved_gate_up,
    weight_in,
    weight_down,
):
    z = Sizes(grad_out, routes, replica_slot, saved_input, weight_in, weight_down)
    n, m = z.ep, z.sub
    ids = jnp.stack([lax.axis_index("ep"), lax.axis_index("sub")]).astype(jnp.int32)
    routes, replica, table = routes.T, replica.T, replica_slot.T
    route_weight = route_weight.T
    pair_rows = saved_gate_up.reshape(z.all_rows, z.pair)
    grad_shape = (z.tokens + z.tail, z.width)
    code_shape = (n, 2 * z.slots, z.tokens)
    inputs = saved_input.reshape(z.all_rows, z.width)

    routing = (grad_out, route_weight, routes, replica, table)
    buf = pl.pallas_call(
        functools.partial(route_kernel, z),
        out_shape=jax.ShapeDtypeStruct(grad_shape, BF),
        in_specs=[smem()] + [whole(a.shape) for a in routing],
        out_specs=whole(grad_shape),
        grid=(1,),
        compiler_params=params(60),
        name="route",
    )(token_count, *routing)
    bufs = [buf] + [swap(buf, "ep", n, k) for k in range(1, n)]

    chain = gate([inputs], [buf])
    downs = pl.pallas_call(
        functools.partial(hidden_kernel, z),
        grid_spec=pltpu.PrefetchScalarGridSpec(
            num_scalar_prefetch=1,
            grid=(z.part_blocks,),
            in_specs=[
                pl.BlockSpec((z.block, z.pair), lambda i, r: (r[1] * z.part_blocks + i, 0)),
                pl.BlockSpec(memory_space=pl.ANY),
                pl.BlockSpec(memory_space=pl.ANY),
            ],
            out_specs=[pl.BlockSpec((z.down_cols, z.block), lambda i, r: (0, i))] * n,
            scratch_shapes=[pltpu.VMEM((n, z.down_cols, z.block), BF)],
        ),
        out_shape=[jax.ShapeDtypeStruct((z.down_cols, z.part), BF)] * n,
        compiler_params=params(16),
        name="hidden_columns",
    )(ids, pair_rows, bufs[1], chain[0])
    downs = [downs[0]] + [swap(downs[k], "ep", n, k) for k in range(1, n)]
    chain = gate(chain, bufs[1:] + downs[1:])
    steps = [list(chain_step(chain[0], chain[0], "ep", n, 1))]

    def stack(pieces):
        shape = pieces[0].shape
        return pl.pallas_call(
            functools.partial(stack_kernel, z),
            in_specs=[whole(shape)] * n,
            out_specs=whole((n,) + shape),
            out_shape=jax.ShapeDtypeStruct((n,) + shape, BF),
            grid=(1,),
            compiler_params=params(12),
            name="stack_columns",
        )(*pieces)

    def halve(keep, got):
        half = (keep.shape[0] // 2,) + keep.shape[1:]
        return pl.pallas_call(
            halve_kernel,
            in_specs=[whole(keep.shape)] * 2,
            out_specs=[whole(half)] * 2,
            out_shape=[jax.ShapeDtypeStruct(half, BF)] * 2,
            grid=(1,),
            compiler_params=params(16),
            name="halve",
        )(keep, got)

    def row_block(i, ids_ref):
        place = i // z.part_blocks
        return (place ^ ids_ref[1]) * z.part_blocks + i % z.part_blocks

    part_shape = (m // 2, z.part, z.hidden)
    outs = pl.pallas_call(
        functools.partial(down_kernel, z),
        grid_spec=pltpu.PrefetchScalarGridSpec(
            num_scalar_prefetch=1,
            grid=(z.blocks,),
            in_specs=[whole(grad_shape)] * n
            + [pl.BlockSpec(memory_space=pltpu.HBM), pl.BlockSpec(memory_space=pl.ANY)],
            out_specs=[whole(part_shape)] * 2
            + [whole((n, z.tokens, z.width)), whole(code_shape)],
            scratch_shapes=[
                pltpu.VMEM((z.local, z.rows, z.width), BF),
                pltpu.VMEM((z.local, z.hidden, z.width), BF),
                pltpu.SemaphoreType.DMA((z.local,)),
            ],
        ),
        out_shape=[jax.ShapeDtypeStruct(part_shape, BF)] * 2
        + [
            jax.ShapeDtypeStruct((n, z.tokens, z.width), BF),
            jax.ShapeDtypeStruct(code_shape, F32),
        ],
        compiler_params=params(48),
        name="hidden_partials",
    )(ids, *bufs, weight_down, *downs[:1])
    keep, send, grads_all, codes = outs
    down_sides = spread_over({0: stack(downs)}, "sub", m, m // 2)
    def total_call(kernel, operands, specs, cols, scratch, name):
        return pl.pallas_call(
            functools.partial(kernel, z),
            grid_spec=pltpu.PrefetchScalarGridSpec(
                num_scalar_prefetch=2,
                grid=(1,),
                in_specs=specs,
                out_specs=[pl.BlockSpec(memory_space=pl.ANY), whole((8, 128))],
                scratch_shapes=[
                    pltpu.VMEM((m, n + 1, cols, z.part), BF),
                    pltpu.VMEM((z.experts, cols, z.width), BF),
                    pltpu.SemaphoreType.DMA((z.experts,)),
                ]
                + scratch,
            ),
            out_shape=[
                jax.ShapeDtypeStruct((z.experts, cols, z.width), BF),
                jax.ShapeDtypeStruct((8, 128), F32),
            ],
            compiler_params=params(32),
            name=name,
        )(ids, table, *operands)

    anywhere = pl.BlockSpec(memory_space=pl.ANY)
    grad_down, down_made = total_call(
        total_down_kernel,
        [*down_sides, grads_all, codes],
        [anywhere] * m + [whole((n, z.tokens, z.width)), whole(code_shape)],
        z.down_cols,
        [pltpu.VMEM((z.slots, z.rows, z.width), BF), pltpu.SemaphoreType.DMA((m,))],
        "down_grads",
    )
    steps.append(chain_step(*steps[0], "ep", n, 2))
    got = swap(send, "sub", m, 1)
    after = [*steps[0], down_made]
    bit = 2
    while bit < m:
        keep, send = halve(keep, got)
        send = gate([send], after)[0]
        got = swap(send, "sub", m, bit)
        bit *= 2

    *pieces, grad_part = pl.pallas_call(
        functools.partial(pre_kernel, z),
        grid_spec=pltpu.PrefetchScalarGridSpec(
            num_scalar_prefetch=1,
            grid=(z.part_blocks,),
            in_specs=[pl.BlockSpec((1, z.block, z.hidden), lambda i, r: (0, i, 0))] * 2
            + [
                pl.BlockSpec((z.block, z.pair), lambda i, r: (r[1] * z.part_blocks + i, 0)),
                whole(code_shape),
            ],
            out_specs=[pl.BlockSpec((z.in_cols, z.block), lambda i, r: (0, i))] * n
            + [pl.BlockSpec((z.block, z.hidden), lambda i, r: (i, 0))],
            scratch_shapes=[pltpu.VMEM((n, z.in_cols, z.block), BF)],
        ),
        out_shape=[jax.ShapeDtypeStruct((z.in_cols, z.part), BF)] * n
        + [jax.ShapeDtypeStruct((z.part, z.hidden), BF)],
        compiler_params=params(16),
        name="pre_grads",
    )(ids, keep, got, pair_rows, codes)
    late = gate(pieces[1:], steps[1])
    pieces = pieces[:1] + [swap(a, "ep", n, k) for k, a in enumerate(late, 1)]
    grad_parts = spread_over({0: grad_part}, "sub", m, m // 2)

    back_shape = (z.tokens + z.slots, z.width)
    parts = pl.pallas_call(
        functools.partial(row_kernel, z),
        grid_spec=pltpu.PrefetchScalarGridSpec(
            num_scalar_prefetch=1,
            grid=(z.blocks,),
            in_specs=[whole((z.part, z.hidden))] * m
            + [
                pl.BlockSpec((z.block, z.pair), lambda i, r: (row_block(i, r), 0)),
                pl.BlockSpec(memory_space=pltpu.HBM),
                whole(code_shape),
            ],
            out_specs=[whole(back_shape)] * n,
            scratch_shapes=[
                pltpu.VMEM((z.local, z.rows, z.width), BF),
                pltpu.VMEM((n, z.slots, z.tokens), F32),
                pltpu.VMEM((z.block, z.hidden), BF),
                pltpu.VMEM((z.local, z.pair, z.width), BF),
                pltpu.SemaphoreType.DMA((z.local,)),
            ],
        ),
        out_shape=[jax.ShapeDtypeStruct(back_shape, BF)] * n,
        compiler_params=params(46),
        name="row_grads",
    )(ids, *grad_parts, pair_rows, weight_in, codes)
    steps[1] = go, back = gate(steps[1], pieces[1:])
    picked = []
    for d in range(3, n):
        if 2 * d > n + 1 and go is not back:
            go = back = pick(ids, go, back, d - 1)
            picked.append(go)
        go, back = chain_step(go, back, "ep", n, d)
        steps.append((go, back))
    gathered = [inputs] + [go for go, _ in steps] + [back for _, back in steps]
    got = [swap(part, "ep", n, 1) for part in parts[1::2]]
    pieces[:1] = gate(pieces[:1], [*got, *picked])
    sides = spread_over({0: stack(pieces)}, "sub", m, m // 2)
    keep, bit = parts[::2], 2
    while bit < n:
        count = len(keep)
        parts = pl.pallas_call(
            sum_kernel,
            in_specs=[whole(back_shape)] * 2 * count,
            out_specs=[whole(back_shape)] * count,
            out_shape=[jax.ShapeDtypeStruct(back_shape, BF)] * count,
            grid=(1,),
            compiler_params=params(16),
            name="sum_parts",
        )(*keep, *got)
        keep = parts[::2]
        got = [swap(part, "ep", n, bit) for part in parts[1::2]]
        bit *= 2

    grad_in, in_made = total_call(
        total_in_kernel,
        [*sides, *gathered],
        [anywhere] * (m + 2 * n - 1),
        z.in_cols,
        [
            pltpu.VMEM((n, z.all_rows, z.width), BF),
            pltpu.SemaphoreType.DMA((m,)),
            pltpu.SemaphoreType.DMA,
            pltpu.SemaphoreType.DMA((n - 1,)),
            pltpu.SemaphoreType.DMA((n - 1,)),
        ],
        "in_grads",
    )
    keep, got = keep[0], gate(got, [in_made])[0]
    grad_tokens, grad_routes = pl.pallas_call(
        functools.partial(token_kernel, z),
        out_shape=[
            jax.ShapeDtypeStruct((z.tokens, z.width), BF),
            jax.ShapeDtypeStruct((z.top, z.tokens), BF),
        ],
        in_specs=[smem()] + [whole(a.shape) for a in (keep, got, routes, replica, table)],
        out_specs=[whole((z.tokens, z.width)), whole((z.top, z.tokens))],
        grid=(1,),
        compiler_params=params(16),
        name="token_grads",
    )(token_count, keep, got, routes, replica, table)

    return grad_tokens, grad_routes.T, grad_in, grad_down


def solution(mesh):
    return jax.shard_map(
        body,
        mesh=mesh,
        in_specs=(
            P(("groups", "ep"), "sub"),
            P(("groups", "ep"), None),
            P(("groups", "ep"), None),
            P(("groups", "ep"), None),
            P("groups", None),
            P(("groups", "ep")),
            P(("groups", "ep"), None, None, "sub"),
            P(("groups", "ep"), None, None),
            P(("groups", "ep"), None, "sub"),
            P(("groups", "ep"), None, "sub"),
        ),
        out_specs=(
            P(("groups", "ep"), "sub"),
            P(("groups", "ep"), None),
            P("groups", "ep", "sub"),
            P("groups", "ep", "sub"),
        ),
        check_vma=False,
    )
```

```python
import functools
import math

import jax
import jax.numpy as jnp
from jax import lax
from jax.experimental import pallas as pl
from jax.experimental.pallas import tpu as pltpu
from jax.sharding import PartitionSpec as P

BF = jnp.bfloat16
F32 = jnp.float32
PER = 2


def nt(a, b):
    return lax.dot_general(a, b, (((1,), (1,)), ((), ())), preferred_element_type=F32)


def tn(a, b):
    return lax.dot_general(a, b, (((0,), (0,)), ((), ())), preferred_element_type=F32)


def nn(a, b):
    return jnp.dot(a, b, preferred_element_type=F32)


def whole(shape):
    zeros = (0,) * len(shape)
    return pl.BlockSpec(shape, lambda *_: zeros)


def smem():
    return pl.BlockSpec(memory_space=pltpu.SMEM)


def params(mib):
    return pltpu.CompilerParams(
        vmem_limit_bytes=mib * 1024 * 1024, dimension_semantics=("arbitrary",)
    )


class Sizes:
    def __init__(self, grad_out, routes, replica_slot, saved_input, weight_in, weight_down):
        self.ep = lax.axis_size("ep")
        self.sub = lax.axis_size("sub")
        self.tokens, self.width = grad_out.shape
        self.top = routes.shape[1]
        self.experts, self.reps = replica_slot.shape
        self.local = weight_in.shape[0]
        self.slots = self.ep * self.local
        self.cap = saved_input.shape[2]
        self.rows = self.ep * self.cap
        self.hidden = weight_down.shape[1]
        self.pair = weight_in.shape[1]
        self.all_rows = self.local * self.rows
        self.part = self.all_rows // self.sub
        self.block = math.gcd(self.rows, self.part)
        self.sources = self.block // self.cap
        self.blocks = self.all_rows // self.block
        self.part_blocks = self.part // self.block
        self.slot_blocks = self.rows // self.block
        self.in_cols = self.pair // self.ep
        self.down_cols = self.hidden // self.ep
        self.cols = self.in_cols + self.down_cols
        self.folds = self.width // self.tokens
        self.tail = 2 * self.slots // self.folds


def slot_table(z, table_ref, r):
    ids = lax.broadcasted_iota(jnp.int32, (z.slots, z.experts), 0)
    return (table_ref[r : r + 1, :] == ids).astype(F32).astype(BF)


def key_hits(z, count_ref, routes_ref, replica_ref, r, k):
    ids = lax.broadcasted_iota(jnp.int32, (z.experts, z.tokens), 0)
    live = lax.broadcasted_iota(jnp.int32, (1, z.tokens), 1) < count_ref[0]
    key = jnp.where(live & (replica_ref[k : k + 1, :] == r), routes_ref[k : k + 1, :], -1)
    return key == ids


def route_kernel(z, count_ref, grad_ref, weight_ref, routes_ref, replica_ref, table_ref, out_ref):
    weights = weight_ref[...].astype(F32)
    hits = jnp.zeros((z.slots, z.tokens), F32)
    loads = jnp.zeros((z.slots, z.tokens), F32)
    for r in range(z.reps):
        hit = jnp.zeros((z.experts, z.tokens), F32)
        load = jnp.zeros((z.experts, z.tokens), F32)
        for k in range(z.top):
            same = key_hits(z, count_ref, routes_ref, replica_ref, r, k)
            hit = jnp.where(same, 1.0, hit)
            load = jnp.where(same, weights[k : k + 1, :], load)
        table = slot_table(z, table_ref, r)
        hits = hits + nn(table, hit.astype(BF))
        loads = loads + nn(table, load.astype(BF))
    before = lax.broadcasted_iota(jnp.int32, (z.tokens, z.tokens), 0)
    after = lax.broadcasted_iota(jnp.int32, (z.tokens, z.tokens), 1)
    earlier = nn(hits.astype(BF), (before < after).astype(F32).astype(BF))
    code = jnp.where(hits > 0.5, earlier, -1.0)
    both = jnp.concatenate([code, loads], axis=0).astype(BF)
    out_ref[: z.tokens, :] = grad_ref[...]
    for b in range(z.folds):
        out_ref[z.tokens :, b * z.tokens : (b + 1) * z.tokens] = both[
            b * z.tail : (b + 1) * z.tail, :
        ]


def block_place(z, block):
    slot = block // z.slot_blocks
    first = (block % z.slot_blocks) * z.sources
    return slot, first


def block_picks(z, codes_ref, slot, first):
    rows = lax.broadcasted_iota(jnp.int32, (z.cap, z.tokens), 0).astype(F32)
    for a in range(z.sources):
        code = codes_ref[first + a, pl.ds(slot, 1), :]
        yield a, rows == code


def block_scale(z, codes_ref, slot, first):
    parts = []
    for a, pick in block_picks(z, codes_ref, slot, first):
        load = codes_ref[first + a, pl.ds(z.slots + slot, 1), :]
        parts.append(jnp.sum(jnp.where(pick, load, 0.0), axis=1, keepdims=True))
    return jnp.concatenate(parts, axis=0)


def local_picks(z, codes_ref, source, me):
    code = codes_ref[source, pl.ds(pl.multiple_of(me * z.local, z.local), z.local), :]
    rows = lax.broadcasted_iota(jnp.int32, (z.local, z.cap, z.tokens), 1).astype(F32)
    pick = (code[:, None, :] == rows).astype(F32)
    return pick.reshape(z.local * z.cap, z.tokens).astype(BF)


def block_slot(z, mine, step):
    place = step // z.part_blocks
    return ((place ^ mine) * z.part_blocks + step % z.part_blocks) // z.slot_blocks


def weight_copy(weight_ref, held, sems, slot):
    return pltpu.make_async_copy(weight_ref.at[slot], held.at[slot], sems.at[slot])


def down_kernel(z, ids_ref, *refs):
    bufs = refs[: z.ep]
    weight_ref = refs[z.ep]
    parts = refs[z.ep + 2 : z.ep + 4]
    grads_ref, codes_ref, rows_ref, held, sems = refs[z.ep + 4 :]
    me, mine = ids_ref[0], ids_ref[1]
    step = pl.program_id(0)

    @pl.when(step == 0)
    def _():
        for s in range(z.local):
            weight_copy(weight_ref, held, sems, s).start()
        for k in range(z.ep):
            source = me ^ k
            grads_ref[source] = bufs[k][: z.tokens, :]
            for b in range(z.folds):
                codes_ref[source, b * z.tail : (b + 1) * z.tail, :] = bufs[k][
                    z.tokens :, b * z.tokens : (b + 1) * z.tokens
                ].astype(F32)
        for p in range(z.ep):
            rows = nn(local_picks(z, codes_ref, p, me), grads_ref[p]).astype(BF)
            rows_ref[:, p * z.cap : (p + 1) * z.cap, :] = rows.reshape(z.local, z.cap, z.width)

    place = step // z.part_blocks
    block = (place ^ mine) * z.part_blocks + step % z.part_blocks
    slot, first = block_place(z, block)
    start = pl.multiple_of(first * z.cap, z.block)

    @pl.when((step == 0) | (slot != block_slot(z, mine, step - 1)))
    def _():
        weight_copy(weight_ref, held, sems, slot).wait()

    partial = nt(rows_ref[slot, pl.ds(start, z.block), :], held[slot]).astype(BF)
    spot = pl.multiple_of((step % z.part_blocks) * z.block, z.block)
    for k in range(z.sub):

        @pl.when(place == k)
        def _():
            parts[k % 2][k // 2, pl.ds(spot, z.block), :] = partial


def gate_terms(z, pair, grad, scale):
    gate = pair[:, : z.hidden].astype(F32)
    up = pair[:, z.hidden :].astype(F32)
    sig = 1.0 / (1.0 + jnp.exp(-gate))
    act = gate * sig
    hidden = act * up
    scaled = scale * grad
    grad_gate = scaled * up * sig * (1.0 + gate * (1.0 - sig))
    grad_up = scaled * act
    return hidden, grad_gate.astype(BF), grad_up.astype(BF)


def pre_kernel(z, ids_ref, keep_ref, got_ref, pair_ref, codes_ref, *refs):
    outs, (grad_ref, sides) = refs[: z.ep], refs[z.ep :]
    me = ids_ref[0]
    block = ids_ref[1] * z.part_blocks + pl.program_id(0)
    slot, first = block_place(z, block)
    scale = block_scale(z, codes_ref, me * z.local + slot, first)
    grad = keep_ref[0].astype(F32) + got_ref[0].astype(F32)
    grad_ref[...] = grad.astype(BF)
    _, grad_gate, grad_up = gate_terms(z, pair_ref[...], grad, scale)
    send_columns(z, me, jnp.concatenate([grad_gate.T, grad_up.T], axis=0), sides, outs)


def send_columns(z, me, columns, sides, outs):
    size = columns.shape[0] // z.ep
    for q in range(z.ep):
        sides[q] = columns[q * size : (q + 1) * size, :]
    for k in range(z.ep):
        outs[k][...] = sides[me ^ k]


def hidden_kernel(z, ids_ref, pair_ref, after_ref, other_ref, *refs):
    pair = pair_ref[...]
    gate_pre = pair[:, : z.hidden].astype(F32)
    up = pair[:, z.hidden :].astype(F32)
    hidden = gate_pre * (1.0 / (1.0 + jnp.exp(-gate_pre))) * up
    send_columns(z, ids_ref[0], hidden.astype(BF).T, refs[-1], refs[:-1])


def stack_kernel(z, *refs):
    for k in range(z.ep):
        refs[-1][k] = refs[k][...]


def row_kernel(z, ids_ref, *refs):
    grads = refs[: z.sub]
    pair_ref, weight_ref, codes_ref = refs[z.sub : z.sub + 3]
    outs = refs[z.sub + 3 : z.sub + 3 + z.ep]
    rows_ref, marks, held, weights, sems = refs[z.sub + 3 + z.ep :]
    me, mine = ids_ref[0], ids_ref[1]
    step = pl.program_id(0)
    place = step // z.part_blocks
    block = (place ^ mine) * z.part_blocks + step % z.part_blocks
    slot, first = block_place(z, block)

    @pl.when(step == 0)
    def _():
        for s in range(z.local):
            weight_copy(weight_ref, weights, sems, s).start()
        marks[...] = jnp.zeros_like(marks)

    spot = pl.multiple_of((step % z.part_blocks) * z.block, z.block)
    for k in range(z.sub):

        @pl.when(place == k)
        def _():
            held[...] = grads[k][pl.ds(spot, z.block), :]

    grad = held[...].astype(F32)
    scale = block_scale(z, codes_ref, me * z.local + slot, first)
    hidden, grad_gate, grad_up = gate_terms(z, pair_ref[...], grad, scale)
    route = jnp.sum(hidden * grad, axis=1, keepdims=True).astype(BF).astype(F32)

    @pl.when((step == 0) | (slot != block_slot(z, mine, step - 1)))
    def _():
        weight_copy(weight_ref, weights, sems, slot).wait()

    rows = nn(grad_gate, weights[slot, : z.hidden, :]) + nn(grad_up, weights[slot, z.hidden :, :])
    start = pl.multiple_of(first * z.cap, z.block)
    rows_ref[slot, pl.ds(start, z.block), :] = rows.astype(BF)
    for a, pick in block_picks(z, codes_ref, me * z.local + slot, first):
        marks[first + a, pl.ds(me * z.local + slot, 1), :] = jnp.sum(
            jnp.where(pick, route[a * z.cap : (a + 1) * z.cap, :], 0.0), axis=0, keepdims=True
        )

    @pl.when(step == z.blocks - 1)
    def _():
        blank = jnp.zeros((z.slots, z.width - z.tokens), BF)
        for k in range(z.ep):
            source = me ^ k
            start = pl.multiple_of(source * z.cap, z.cap)
            rows = rows_ref[:, pl.ds(start, z.cap), :].reshape(z.local * z.cap, z.width)
            picks = local_picks(z, codes_ref, source, me)
            outs[k][: z.tokens, :] = tn(picks, rows).astype(BF)
            outs[k][z.tokens :, : z.tokens] = marks[source].astype(BF)
            outs[k][z.tokens :, z.tokens :] = blank


def sum_kernel(*refs):
    count = len(refs) // 3
    for i in range(count):
        total = refs[i][...].astype(F32) + refs[count + i][...].astype(F32)
        refs[2 * count + i][...] = total.astype(BF)


def halve_kernel(keep_ref, got_ref, out_keep, out_send):
    for i in range(out_keep.shape[0]):
        for j, out in enumerate((out_keep, out_send)):
            total = keep_ref[2 * i + j].astype(F32) + got_ref[2 * i + j].astype(F32)
            out[i] = total.astype(BF)


def token_kernel(z, count_ref, *refs):
    keep_ref, got_ref, routes_ref, replica_ref, table_ref, tokens_ref, route_ref = refs
    total = keep_ref[...].astype(F32) + got_ref[...].astype(F32)
    tokens_ref[...] = total[: z.tokens, :].astype(BF)
    rows = total[z.tokens :, : z.tokens].astype(BF)
    totals = [jnp.zeros((1, z.tokens), F32)] * z.top
    for r in range(z.reps):
        spread = tn(slot_table(z, table_ref, r), rows)
        for k in range(z.top):
            same = key_hits(z, count_ref, routes_ref, replica_ref, r, k)
            totals[k] += jnp.sum(jnp.where(same, spread, 0.0), axis=0, keepdims=True)
    route_ref[...] = jnp.concatenate(totals, axis=0).astype(BF)


def input_moves(z, me, own_ref, rights, lefts, inputs_ref, own_sem, right_sems, left_sems, act):
    act(pltpu.make_async_copy(own_ref, inputs_ref.at[me], own_sem))
    for d in range(1, z.ep):

        @pl.when(me >= d)
        def _():
            act(
                pltpu.make_async_copy(
                    rights[d - 1], inputs_ref.at[me - d], right_sems.at[d - 1]
                )
            )

        @pl.when(me + d < z.ep)
        def _():
            act(
                pltpu.make_async_copy(
                    lefts[d - 1], inputs_ref.at[me + d], left_sems.at[d - 1]
                )
            )


def left_rows(held, part, side, spot, size):
    return held[part, side, :, pl.ds(spot, size)]


def expert_products(z, ids_ref, table_ref, turn, held, right_rows, out_ref, made, out_sems):
    mine = ids_ref[1]

    def out_copy(expert):
        return pltpu.make_async_copy(made.at[expert], out_ref.at[expert], out_sems.at[expert])

    def some(step, carry):
        for i in range(PER):
            expert = step * PER + i
            first = table_ref[0, expert]
            left, right = [], []
            for r in range(z.reps):
                slot_id = table_ref[r, expert]
                source = slot_id // z.local
                for b in range(z.slot_blocks):
                    block = (slot_id % z.local) * z.slot_blocks + b
                    part = (block // z.part_blocks) ^ mine
                    spot = pl.multiple_of((block % z.part_blocks) * z.block, z.block)
                    side = source ^ turn
                    if r:
                        side = jnp.where(slot_id == first, z.ep, side)
                    left.append(functools.partial(left_rows, held, part, side, spot, z.block))
                    right.append(functools.partial(right_rows, slot_id, block, b))
            half = len(left) // 2

            def product(lo, hi):
                return nn(
                    jnp.concatenate([f() for f in left[lo:hi]], axis=1),
                    jnp.concatenate([f() for f in right[lo:hi]], axis=0),
                )

            few = table_ref[z.reps // 2, expert] == first

            @pl.when(few)
            def _():
                made[expert] = product(0, half).astype(BF)

            @pl.when(jnp.logical_not(few))
            def _():
                made[expert] = product(0, 2 * half).astype(BF)

            out_copy(expert).start()
        return carry

    lax.fori_loop(0, z.experts // PER, some, 0)
    for expert in range(z.experts):
        out_copy(expert).wait()


def total_down_kernel(z, ids_ref, table_ref, *refs):
    sides = refs[: z.sub]
    grads_ref, codes_ref, out_ref, token_ref, held, made, out_sems, scaled, sems = refs[z.sub :]
    token_ref[...] = jnp.zeros_like(token_ref)

    def moves(act):
        for k in range(z.sub):
            act(
                pltpu.make_async_copy(
                    sides[k], held.at[k, pl.ds(0, z.ep)], sems.at[k]
                )
            )

    moves(lambda copy: copy.start())
    held[:, z.ep] = jnp.zeros_like(held[:, z.ep])
    rows = lax.broadcasted_iota(jnp.int32, (z.slots, z.cap, z.tokens), 1).astype(F32)
    for p in range(z.ep):
        code = codes_ref[p, : z.slots, :][:, None, :]
        load = codes_ref[p, z.slots :, :][:, None, :]
        pick = jnp.where(rows == code, load, 0.0).reshape(z.slots * z.cap, z.tokens)
        result = nn(pick.astype(BF), grads_ref[p]).astype(BF)
        scaled[:, p * z.cap : (p + 1) * z.cap, :] = result.reshape(z.slots, z.cap, z.width)
    moves(lambda copy: copy.wait())

    def right_rows(slot_id, block, b):
        return scaled[slot_id, b * z.block : (b + 1) * z.block, :]

    expert_products(z, ids_ref, table_ref, ids_ref[0], held, right_rows, out_ref, made, out_sems)


def total_in_kernel(z, ids_ref, table_ref, *refs):
    sides, refs = refs[: z.sub], refs[z.sub :]
    own_ref, rights, lefts = refs[0], refs[1 : z.ep], refs[z.ep : 2 * z.ep - 1]
    out_ref, token_ref, held, made, out_sems, inputs_ref, sems, *other_sems = refs[2 * z.ep - 1 :]
    token_ref[...] = jnp.zeros_like(token_ref)

    def moves(act):
        for k in range(z.sub):
            act(pltpu.make_async_copy(sides[k], held.at[k, pl.ds(0, z.ep)], sems.at[k]))
        input_moves(z, ids_ref[0], own_ref, rights, lefts, inputs_ref, *other_sems, act)

    moves(lambda copy: copy.start())
    held[:, z.ep] = jnp.zeros_like(held[:, z.ep])
    moves(lambda copy: copy.wait())

    def right_rows(slot_id, block, b):
        start = pl.multiple_of(block * z.block, z.block)
        return inputs_ref[slot_id // z.local, pl.ds(start, z.block), :]

    expert_products(z, ids_ref, table_ref, ids_ref[0], held, right_rows, out_ref, made, out_sems)


def swap(x, axis, size, bit):
    return lax.ppermute(x, axis, [(i, i ^ bit) for i in range(size)])


def spread_over(have, axis, size, bit):
    have = dict(have)
    while bit:
        for k in list(have):
            if k | bit not in have:
                have[k | bit] = swap(have[k], axis, size, bit)
        bit //= 2
    return [have[k] for k in range(size)]


def nothing(*refs):
    pass


def gate(values, after):
    anywhere = pl.BlockSpec(memory_space=pl.ANY)
    return pl.pallas_call(
        nothing,
        in_specs=[anywhere] * (len(values) + len(after)),
        out_specs=[anywhere] * len(values),
        out_shape=[jax.ShapeDtypeStruct(v.shape, v.dtype) for v in values],
        input_output_aliases={i: i for i in range(len(values))},
        compiler_params=pltpu.CompilerParams(vmem_limit_bytes=1024 * 1024),
        name="gate",
    )(*values, *after)


def pick_kernel(first, ids_ref, go_ref, back_ref, out_ref, sem):
    for condition, ref in ((ids_ref[0] >= first, go_ref), (ids_ref[0] < first, back_ref)):

        @pl.when(condition)
        def _():
            copy = pltpu.make_async_copy(ref, out_ref, sem)
            copy.start()
            copy.wait()


def pick(ids, go, back, first):
    anywhere = pl.BlockSpec(memory_space=pl.ANY)
    return pl.pallas_call(
        functools.partial(pick_kernel, first),
        in_specs=[smem(), anywhere, anywhere],
        out_specs=anywhere,
        out_shape=jax.ShapeDtypeStruct(go.shape, go.dtype),
        scratch_shapes=[pltpu.SemaphoreType.DMA],
        compiler_params=pltpu.CompilerParams(vmem_limit_bytes=1024 * 1024),
        name="pick",
    )(ids, go, back)


def chain_step(go, back, axis, size, d):
    rights = [(i, i + 1) for i in range(d - 1, size - 1)]
    lefts = [(i, i - 1) for i in range(size - d, 0, -1)]
    if d > 1 and go is back:
        got = lax.ppermute(go, axis, rights + lefts)
        return got, got
    return lax.ppermute(go, axis, rights), lax.ppermute(back, axis, lefts)


def body(
    grad_out,
    route_weight,
    routes,
    replica,
    replica_slot,
    token_count,
    saved_input,
    saved_gate_up,
    weight_in,
    weight_down,
):
    z = Sizes(grad_out, routes, replica_slot, saved_input, weight_in, weight_down)
    n, m = z.ep, z.sub
    ids = jnp.stack([lax.axis_index("ep"), lax.axis_index("sub")]).astype(jnp.int32)
    routes, replica, table = routes.T, replica.T, replica_slot.T
    route_weight = route_weight.T
    pair_rows = saved_gate_up.reshape(z.all_rows, z.pair)
    grad_shape = (z.tokens + z.tail, z.width)
    code_shape = (n, 2 * z.slots, z.tokens)
    inputs = saved_input.reshape(z.all_rows, z.width)

    routing = (grad_out, route_weight, routes, replica, table)
    buf = pl.pallas_call(
        functools.partial(route_kernel, z),
        out_shape=jax.ShapeDtypeStruct(grad_shape, BF),
        in_specs=[smem()] + [whole(a.shape) for a in routing],
        out_specs=whole(grad_shape),
        grid=(1,),
        compiler_params=params(60),
        name="route",
    )(token_count, *routing)
    bufs = [buf] + [swap(buf, "ep", n, k) for k in range(1, n)]

    chain = gate([inputs], [buf])
    downs = pl.pallas_call(
        functools.partial(hidden_kernel, z),
        grid_spec=pltpu.PrefetchScalarGridSpec(
            num_scalar_prefetch=1,
            grid=(z.part_blocks,),
            in_specs=[
                pl.BlockSpec((z.block, z.pair), lambda i, r: (r[1] * z.part_blocks + i, 0)),
                pl.BlockSpec(memory_space=pl.ANY),
                pl.BlockSpec(memory_space=pl.ANY),
            ],
            out_specs=[pl.BlockSpec((z.down_cols, z.block), lambda i, r: (0, i))] * n,
            scratch_shapes=[pltpu.VMEM((n, z.down_cols, z.block), BF)],
        ),
        out_shape=[jax.ShapeDtypeStruct((z.down_cols, z.part), BF)] * n,
        compiler_params=params(16),
        name="hidden_columns",
    )(ids, pair_rows, bufs[1], chain[0])
    downs = [downs[0]] + [swap(downs[k], "ep", n, k) for k in range(1, n)]
    chain = gate(chain, bufs[1:] + downs[1:])
    steps = [list(chain_step(chain[0], chain[0], "ep", n, 1))]

    def stack(pieces):
        shape = pieces[0].shape
        return pl.pallas_call(
            functools.partial(stack_kernel, z),
            in_specs=[whole(shape)] * n,
            out_specs=whole((n,) + shape),
            out_shape=jax.ShapeDtypeStruct((n,) + shape, BF),
            grid=(1,),
            compiler_params=params(12),
            name="stack_columns",
        )(*pieces)

    def halve(keep, got):
        half = (keep.shape[0] // 2,) + keep.shape[1:]
        return pl.pallas_call(
            halve_kernel,
            in_specs=[whole(keep.shape)] * 2,
            out_specs=[whole(half)] * 2,
            out_shape=[jax.ShapeDtypeStruct(half, BF)] * 2,
            grid=(1,),
            compiler_params=params(16),
            name="halve",
        )(keep, got)

    def row_block(i, ids_ref):
        place = i // z.part_blocks
        return (place ^ ids_ref[1]) * z.part_blocks + i % z.part_blocks

    part_shape = (m // 2, z.part, z.hidden)
    outs = pl.pallas_call(
        functools.partial(down_kernel, z),
        grid_spec=pltpu.PrefetchScalarGridSpec(
            num_scalar_prefetch=1,
            grid=(z.blocks,),
            in_specs=[whole(grad_shape)] * n
            + [pl.BlockSpec(memory_space=pltpu.HBM), pl.BlockSpec(memory_space=pl.ANY)],
            out_specs=[whole(part_shape)] * 2
            + [whole((n, z.tokens, z.width)), whole(code_shape)],
            scratch_shapes=[
                pltpu.VMEM((z.local, z.rows, z.width), BF),
                pltpu.VMEM((z.local, z.hidden, z.width), BF),
                pltpu.SemaphoreType.DMA((z.local,)),
            ],
        ),
        out_shape=[jax.ShapeDtypeStruct(part_shape, BF)] * 2
        + [
            jax.ShapeDtypeStruct((n, z.tokens, z.width), BF),
            jax.ShapeDtypeStruct(code_shape, F32),
        ],
        compiler_params=params(48),
        name="hidden_partials",
    )(ids, *bufs, weight_down, *downs[:1])
    keep, send, grads_all, codes = outs
    down_sides = spread_over({0: stack(downs)}, "sub", m, m // 2)
    def total_call(kernel, operands, specs, cols, scratch, name):
        return pl.pallas_call(
            functools.partial(kernel, z),
            grid_spec=pltpu.PrefetchScalarGridSpec(
                num_scalar_prefetch=2,
                grid=(1,),
                in_specs=specs,
                out_specs=[pl.BlockSpec(memory_space=pl.ANY), whole((8, 128))],
                scratch_shapes=[
                    pltpu.VMEM((m, n + 1, cols, z.part), BF),
                    pltpu.VMEM((z.experts, cols, z.width), BF),
                    pltpu.SemaphoreType.DMA((z.experts,)),
                ]
                + scratch,
            ),
            out_shape=[
                jax.ShapeDtypeStruct((z.experts, cols, z.width), BF),
                jax.ShapeDtypeStruct((8, 128), F32),
            ],
            compiler_params=params(32),
            name=name,
        )(ids, table, *operands)

    anywhere = pl.BlockSpec(memory_space=pl.ANY)
    grad_down, down_made = total_call(
        total_down_kernel,
        [*down_sides, grads_all, codes],
        [anywhere] * m + [whole((n, z.tokens, z.width)), whole(code_shape)],
        z.down_cols,
        [pltpu.VMEM((z.slots, z.rows, z.width), BF), pltpu.SemaphoreType.DMA((m,))],
        "down_grads",
    )
    steps.append(chain_step(*steps[0], "ep", n, 2))
    got = swap(send, "sub", m, 1)
    after = list(steps[0])
    bit = 2
    while bit < m:
        keep, send = halve(keep, got)
        send = gate([send], after)[0]
        got = swap(send, "sub", m, bit)
        bit *= 2

    got = gate([got], [down_made])[0]
    *pieces, grad_part = pl.pallas_call(
        functools.partial(pre_kernel, z),
        grid_spec=pltpu.PrefetchScalarGridSpec(
            num_scalar_prefetch=1,
            grid=(z.part_blocks,),
            in_specs=[pl.BlockSpec((1, z.block, z.hidden), lambda i, r: (0, i, 0))] * 2
            + [
                pl.BlockSpec((z.block, z.pair), lambda i, r: (r[1] * z.part_blocks + i, 0)),
                whole(code_shape),
            ],
            out_specs=[pl.BlockSpec((z.in_cols, z.block), lambda i, r: (0, i))] * n
            + [pl.BlockSpec((z.block, z.hidden), lambda i, r: (i, 0))],
            scratch_shapes=[pltpu.VMEM((n, z.in_cols, z.block), BF)],
        ),
        out_shape=[jax.ShapeDtypeStruct((z.in_cols, z.part), BF)] * n
        + [jax.ShapeDtypeStruct((z.part, z.hidden), BF)],
        compiler_params=params(16),
        name="pre_grads",
    )(ids, keep, got, pair_rows, codes)
    late = gate(pieces[1:], steps[1])
    pieces = pieces[:1] + [swap(a, "ep", n, k) for k, a in enumerate(late, 1)]
    grad_parts = spread_over({0: grad_part}, "sub", m, m // 2)

    back_shape = (z.tokens + z.slots, z.width)
    parts = pl.pallas_call(
        functools.partial(row_kernel, z),
        grid_spec=pltpu.PrefetchScalarGridSpec(
            num_scalar_prefetch=1,
            grid=(z.blocks,),
            in_specs=[whole((z.part, z.hidden))] * m
            + [
                pl.BlockSpec((z.block, z.pair), lambda i, r: (row_block(i, r), 0)),
                pl.BlockSpec(memory_space=pltpu.HBM),
                whole(code_shape),
            ],
            out_specs=[whole(back_shape)] * n,
            scratch_shapes=[
                pltpu.VMEM((z.local, z.rows, z.width), BF),
                pltpu.VMEM((n, z.slots, z.tokens), F32),
                pltpu.VMEM((z.block, z.hidden), BF),
                pltpu.VMEM((z.local, z.pair, z.width), BF),
                pltpu.SemaphoreType.DMA((z.local,)),
            ],
        ),
        out_shape=[jax.ShapeDtypeStruct(back_shape, BF)] * n,
        compiler_params=params(46),
        name="row_grads",
    )(ids, *grad_parts, pair_rows, weight_in, codes)
    steps[1] = go, back = gate(steps[1], pieces[1:])
    picked = []
    for d in range(3, n):
        if 2 * d > n + 1 and go is not back:
            go = back = pick(ids, go, back, d - 1)
            picked.append(go)
        go, back = chain_step(go, back, "ep", n, d)
        steps.append((go, back))
    gathered = [inputs] + [go for go, _ in steps] + [back for _, back in steps]
    got = [swap(part, "ep", n, 1) for part in parts[1::2]]
    pieces[:1] = gate(pieces[:1], [*got, *picked])
    sides = spread_over({0: stack(pieces)}, "sub", m, m // 2)
    keep, bit = parts[::2], 2
    while bit < n:
        count = len(keep)
        parts = pl.pallas_call(
            sum_kernel,
            in_specs=[whole(back_shape)] * 2 * count,
            out_specs=[whole(back_shape)] * count,
            out_shape=[jax.ShapeDtypeStruct(back_shape, BF)] * count,
            grid=(1,),
            compiler_params=params(16),
            name="sum_parts",
        )(*keep, *got)
        keep = parts[::2]
        send = gate(parts[1::2], gathered[1:])
        got = [swap(part, "ep", n, bit) for part in send]
        bit *= 2

    grad_in, in_made = total_call(
        total_in_kernel,
        [*sides, *gathered],
        [anywhere] * (m + 2 * n - 1),
        z.in_cols,
        [
            pltpu.VMEM((n, z.all_rows, z.width), BF),
            pltpu.SemaphoreType.DMA((m,)),
            pltpu.SemaphoreType.DMA,
            pltpu.SemaphoreType.DMA((n - 1,)),
            pltpu.SemaphoreType.DMA((n - 1,)),
        ],
        "in_grads",
    )
    keep, got = keep[0], gate(got, [in_made])[0]
    grad_tokens, grad_routes = pl.pallas_call(
        functools.partial(token_kernel, z),
        out_shape=[
            jax.ShapeDtypeStruct((z.tokens, z.width), BF),
            jax.ShapeDtypeStruct((z.top, z.tokens), BF),
        ],
        in_specs=[smem()] + [whole(a.shape) for a in (keep, got, routes, replica, table)],
        out_specs=[whole((z.tokens, z.width)), whole((z.top, z.tokens))],
        grid=(1,),
        compiler_params=params(16),
        name="token_grads",
    )(token_count, keep, got, routes, replica, table)

    return grad_tokens, grad_routes.T, grad_in, grad_down


def solution(mesh):
    return jax.shard_map(
        body,
        mesh=mesh,
        in_specs=(
            P(("groups", "ep"), "sub"),
            P(("groups", "ep"), None),
            P(("groups", "ep"), None),
            P(("groups", "ep"), None),
            P("groups", None),
            P(("groups", "ep")),
            P(("groups", "ep"), None, None, "sub"),
            P(("groups", "ep"), None, None),
            P(("groups", "ep"), None, "sub"),
            P(("groups", "ep"), None, "sub"),
        ),
        out_specs=(
            P(("groups", "ep"), "sub"),
            P(("groups", "ep"), None),
            P("groups", "ep", "sub"),
            P("groups", "ep", "sub"),
        ),
        check_vma=False,
    )
```

```python
import functools
import math

import jax
import jax.numpy as jnp
from jax import lax
from jax.experimental import pallas as pl
from jax.experimental.pallas import tpu as pltpu
from jax.sharding import PartitionSpec as P

BF = jnp.bfloat16
F32 = jnp.float32
PER = 2


def nt(a, b):
    return lax.dot_general(a, b, (((1,), (1,)), ((), ())), preferred_element_type=F32)


def tn(a, b):
    return lax.dot_general(a, b, (((0,), (0,)), ((), ())), preferred_element_type=F32)


def nn(a, b):
    return jnp.dot(a, b, preferred_element_type=F32)


def whole(shape):
    zeros = (0,) * len(shape)
    return pl.BlockSpec(shape, lambda *_: zeros)


def smem():
    return pl.BlockSpec(memory_space=pltpu.SMEM)


def params(mib):
    return pltpu.CompilerParams(
        vmem_limit_bytes=mib * 1024 * 1024, dimension_semantics=("arbitrary",)
    )


class Sizes:
    def __init__(self, grad_out, routes, replica_slot, saved_input, weight_in, weight_down):
        self.ep = lax.axis_size("ep")
        self.sub = lax.axis_size("sub")
        self.tokens, self.width = grad_out.shape
        self.top = routes.shape[1]
        self.experts, self.reps = replica_slot.shape
        self.local = weight_in.shape[0]
        self.slots = self.ep * self.local
        self.cap = saved_input.shape[2]
        self.rows = self.ep * self.cap
        self.hidden = weight_down.shape[1]
        self.pair = weight_in.shape[1]
        self.all_rows = self.local * self.rows
        self.part = self.all_rows // self.sub
        self.block = math.gcd(self.rows, self.part)
        self.sources = self.block // self.cap
        self.blocks = self.all_rows // self.block
        self.part_blocks = self.part // self.block
        self.slot_blocks = self.rows // self.block
        self.in_cols = self.pair // self.ep
        self.down_cols = self.hidden // self.ep
        self.cols = self.in_cols + self.down_cols
        self.folds = self.width // self.tokens
        self.tail = 2 * self.slots // self.folds


def slot_table(z, table_ref, r):
    ids = lax.broadcasted_iota(jnp.int32, (z.slots, z.experts), 0)
    return (table_ref[r : r + 1, :] == ids).astype(F32).astype(BF)


def key_hits(z, count_ref, routes_ref, replica_ref, r, k):
    ids = lax.broadcasted_iota(jnp.int32, (z.experts, z.tokens), 0)
    live = lax.broadcasted_iota(jnp.int32, (1, z.tokens), 1) < count_ref[0]
    key = jnp.where(live & (replica_ref[k : k + 1, :] == r), routes_ref[k : k + 1, :], -1)
    return key == ids


def route_kernel(z, count_ref, grad_ref, weight_ref, routes_ref, replica_ref, table_ref, out_ref):
    weights = weight_ref[...].astype(F32)
    hits = jnp.zeros((z.slots, z.tokens), F32)
    loads = jnp.zeros((z.slots, z.tokens), F32)
    for r in range(z.reps):
        hit = jnp.zeros((z.experts, z.tokens), F32)
        load = jnp.zeros((z.experts, z.tokens), F32)
        for k in range(z.top):
            same = key_hits(z, count_ref, routes_ref, replica_ref, r, k)
            hit = jnp.where(same, 1.0, hit)
            load = jnp.where(same, weights[k : k + 1, :], load)
        table = slot_table(z, table_ref, r)
        hits = hits + nn(table, hit.astype(BF))
        loads = loads + nn(table, load.astype(BF))
    before = lax.broadcasted_iota(jnp.int32, (z.tokens, z.tokens), 0)
    after = lax.broadcasted_iota(jnp.int32, (z.tokens, z.tokens), 1)
    earlier = nn(hits.astype(BF), (before < after).astype(F32).astype(BF))
    code = jnp.where(hits > 0.5, earlier, -1.0)
    both = jnp.concatenate([code, loads], axis=0).astype(BF)
    out_ref[: z.tokens, :] = grad_ref[...]
    for b in range(z.folds):
        out_ref[z.tokens :, b * z.tokens : (b + 1) * z.tokens] = both[
            b * z.tail : (b + 1) * z.tail, :
        ]


def block_place(z, block):
    slot = block // z.slot_blocks
    first = (block % z.slot_blocks) * z.sources
    return slot, first


def block_picks(z, codes_ref, slot, first):
    rows = lax.broadcasted_iota(jnp.int32, (z.cap, z.tokens), 0).astype(F32)
    for a in range(z.sources):
        code = codes_ref[first + a, pl.ds(slot, 1), :]
        yield a, rows == code


def block_scale(z, codes_ref, slot, first):
    parts = []
    for a, pick in block_picks(z, codes_ref, slot, first):
        load = codes_ref[first + a, pl.ds(z.slots + slot, 1), :]
        parts.append(jnp.sum(jnp.where(pick, load, 0.0), axis=1, keepdims=True))
    return jnp.concatenate(parts, axis=0)


def local_picks(z, codes_ref, source, me):
    code = codes_ref[source, pl.ds(pl.multiple_of(me * z.local, z.local), z.local), :]
    rows = lax.broadcasted_iota(jnp.int32, (z.local, z.cap, z.tokens), 1).astype(F32)
    pick = (code[:, None, :] == rows).astype(F32)
    return pick.reshape(z.local * z.cap, z.tokens).astype(BF)


def block_slot(z, mine, step):
    place = step // z.part_blocks
    return ((place ^ mine) * z.part_blocks + step % z.part_blocks) // z.slot_blocks


def weight_copy(weight_ref, held, sems, slot):
    return pltpu.make_async_copy(weight_ref.at[slot], held.at[slot], sems.at[slot])


def down_kernel(z, ids_ref, *refs):
    bufs = refs[: z.ep]
    weight_ref = refs[z.ep]
    parts = refs[z.ep + 2 : z.ep + 4]
    grads_ref, codes_ref, rows_ref, held, sems = refs[z.ep + 4 :]
    me, mine = ids_ref[0], ids_ref[1]
    step = pl.program_id(0)

    @pl.when(step == 0)
    def _():
        for s in range(z.local):
            weight_copy(weight_ref, held, sems, s).start()
        for k in range(z.ep):
            source = me ^ k
            grads_ref[source] = bufs[k][: z.tokens, :]
            for b in range(z.folds):
                codes_ref[source, b * z.tail : (b + 1) * z.tail, :] = bufs[k][
                    z.tokens :, b * z.tokens : (b + 1) * z.tokens
                ].astype(F32)
        for p in range(z.ep):
            rows = nn(local_picks(z, codes_ref, p, me), grads_ref[p]).astype(BF)
            rows_ref[:, p * z.cap : (p + 1) * z.cap, :] = rows.reshape(z.local, z.cap, z.width)

    place = step // z.part_blocks
    block = (place ^ mine) * z.part_blocks + step % z.part_blocks
    slot, first = block_place(z, block)
    start = pl.multiple_of(first * z.cap, z.block)

    @pl.when((step == 0) | (slot != block_slot(z, mine, step - 1)))
    def _():
        weight_copy(weight_ref, held, sems, slot).wait()

    partial = nt(rows_ref[slot, pl.ds(start, z.block), :], held[slot]).astype(BF)
    spot = pl.multiple_of((step % z.part_blocks) * z.block, z.block)
    for k in range(z.sub):

        @pl.when(place == k)
        def _():
            parts[k % 2][k // 2, pl.ds(spot, z.block), :] = partial


def gate_terms(z, pair, grad, scale):
    gate = pair[:, : z.hidden].astype(F32)
    up = pair[:, z.hidden :].astype(F32)
    sig = 1.0 / (1.0 + jnp.exp(-gate))
    act = gate * sig
    hidden = act * up
    scaled = scale * grad
    grad_gate = scaled * up * sig * (1.0 + gate * (1.0 - sig))
    grad_up = scaled * act
    return hidden, grad_gate.astype(BF), grad_up.astype(BF)


def pre_kernel(z, ids_ref, keep_ref, got_ref, pair_ref, codes_ref, *refs):
    outs, (grad_ref, sides) = refs[: z.ep], refs[z.ep :]
    me = ids_ref[0]
    block = ids_ref[1] * z.part_blocks + pl.program_id(0)
    slot, first = block_place(z, block)
    scale = block_scale(z, codes_ref, me * z.local + slot, first)
    grad = keep_ref[0].astype(F32) + got_ref[0].astype(F32)
    grad_ref[...] = grad.astype(BF)
    _, grad_gate, grad_up = gate_terms(z, pair_ref[...], grad, scale)
    send_columns(z, me, jnp.concatenate([grad_gate.T, grad_up.T], axis=0), sides, outs)


def send_columns(z, me, columns, sides, outs):
    size = columns.shape[0] // z.ep
    for q in range(z.ep):
        sides[q] = columns[q * size : (q + 1) * size, :]
    for k in range(z.ep):
        outs[k][...] = sides[me ^ k]


def hidden_kernel(z, ids_ref, pair_ref, after_ref, other_ref, *refs):
    pair = pair_ref[...]
    gate_pre = pair[:, : z.hidden].astype(F32)
    up = pair[:, z.hidden :].astype(F32)
    hidden = gate_pre * (1.0 / (1.0 + jnp.exp(-gate_pre))) * up
    send_columns(z, ids_ref[0], hidden.astype(BF).T, refs[-1], refs[:-1])


def stack_kernel(z, *refs):
    for k in range(z.ep):
        refs[-1][k] = refs[k][...]


def row_kernel(z, ids_ref, *refs):
    grads = refs[: z.sub]
    pair_ref, weight_ref, codes_ref = refs[z.sub : z.sub + 3]
    outs = refs[z.sub + 3 : z.sub + 3 + z.ep]
    rows_ref, marks, held, weights, sems = refs[z.sub + 3 + z.ep :]
    me, mine = ids_ref[0], ids_ref[1]
    step = pl.program_id(0)
    place = step // z.part_blocks
    block = (place ^ mine) * z.part_blocks + step % z.part_blocks
    slot, first = block_place(z, block)

    @pl.when(step == 0)
    def _():
        for s in range(z.local):
            weight_copy(weight_ref, weights, sems, s).start()
        marks[...] = jnp.zeros_like(marks)

    spot = pl.multiple_of((step % z.part_blocks) * z.block, z.block)
    for k in range(z.sub):

        @pl.when(place == k)
        def _():
            held[...] = grads[k][pl.ds(spot, z.block), :]

    grad = held[...].astype(F32)
    scale = block_scale(z, codes_ref, me * z.local + slot, first)
    hidden, grad_gate, grad_up = gate_terms(z, pair_ref[...], grad, scale)
    route = jnp.sum(hidden * grad, axis=1, keepdims=True).astype(BF).astype(F32)

    @pl.when((step == 0) | (slot != block_slot(z, mine, step - 1)))
    def _():
        weight_copy(weight_ref, weights, sems, slot).wait()

    rows = nn(grad_gate, weights[slot, : z.hidden, :]) + nn(grad_up, weights[slot, z.hidden :, :])
    start = pl.multiple_of(first * z.cap, z.block)
    rows_ref[slot, pl.ds(start, z.block), :] = rows.astype(BF)
    for a, pick in block_picks(z, codes_ref, me * z.local + slot, first):
        marks[first + a, pl.ds(me * z.local + slot, 1), :] = jnp.sum(
            jnp.where(pick, route[a * z.cap : (a + 1) * z.cap, :], 0.0), axis=0, keepdims=True
        )

    @pl.when(step == z.blocks - 1)
    def _():
        blank = jnp.zeros((z.slots, z.width - z.tokens), BF)
        for k in range(z.ep):
            source = me ^ k
            start = pl.multiple_of(source * z.cap, z.cap)
            rows = rows_ref[:, pl.ds(start, z.cap), :].reshape(z.local * z.cap, z.width)
            picks = local_picks(z, codes_ref, source, me)
            outs[k][: z.tokens, :] = tn(picks, rows).astype(BF)
            outs[k][z.tokens :, : z.tokens] = marks[source].astype(BF)
            outs[k][z.tokens :, z.tokens :] = blank


def sum_kernel(*refs):
    count = len(refs) // 3
    for i in range(count):
        total = refs[i][...].astype(F32) + refs[count + i][...].astype(F32)
        refs[2 * count + i][...] = total.astype(BF)


def halve_kernel(keep_ref, got_ref, out_keep, out_send):
    for i in range(out_keep.shape[0]):
        for j, out in enumerate((out_keep, out_send)):
            total = keep_ref[2 * i + j].astype(F32) + got_ref[2 * i + j].astype(F32)
            out[i] = total.astype(BF)


def token_kernel(z, count_ref, *refs):
    keep_ref, got_ref, routes_ref, replica_ref, table_ref, tokens_ref, route_ref = refs
    total = keep_ref[...].astype(F32) + got_ref[...].astype(F32)
    tokens_ref[...] = total[: z.tokens, :].astype(BF)
    rows = total[z.tokens :, : z.tokens].astype(BF)
    totals = [jnp.zeros((1, z.tokens), F32)] * z.top
    for r in range(z.reps):
        spread = tn(slot_table(z, table_ref, r), rows)
        for k in range(z.top):
            same = key_hits(z, count_ref, routes_ref, replica_ref, r, k)
            totals[k] += jnp.sum(jnp.where(same, spread, 0.0), axis=0, keepdims=True)
    route_ref[...] = jnp.concatenate(totals, axis=0).astype(BF)


def input_moves(z, me, own_ref, rights, lefts, inputs_ref, own_sem, right_sems, left_sems, act):
    act(pltpu.make_async_copy(own_ref, inputs_ref.at[me], own_sem))
    for d in range(1, z.ep):

        @pl.when(me >= d)
        def _():
            act(
                pltpu.make_async_copy(
                    rights[d - 1], inputs_ref.at[me - d], right_sems.at[d - 1]
                )
            )

        @pl.when(me + d < z.ep)
        def _():
            act(
                pltpu.make_async_copy(
                    lefts[d - 1], inputs_ref.at[me + d], left_sems.at[d - 1]
                )
            )


def left_rows(held, part, side, spot, size):
    return held[part, side, :, pl.ds(spot, size)]


def expert_products(z, ids_ref, table_ref, turn, held, right_rows, out_ref, made, out_sems):
    mine = ids_ref[1]

    def out_copy(expert):
        return pltpu.make_async_copy(made.at[expert], out_ref.at[expert], out_sems.at[expert])

    def some(step, carry):
        for i in range(PER):
            expert = step * PER + i
            first = table_ref[0, expert]
            left, right = [], []
            for r in range(z.reps):
                slot_id = table_ref[r, expert]
                source = slot_id // z.local
                for b in range(z.slot_blocks):
                    block = (slot_id % z.local) * z.slot_blocks + b
                    part = (block // z.part_blocks) ^ mine
                    spot = pl.multiple_of((block % z.part_blocks) * z.block, z.block)
                    side = source ^ turn
                    if r:
                        side = jnp.where(slot_id == first, z.ep, side)
                    left.append(functools.partial(left_rows, held, part, side, spot, z.block))
                    right.append(functools.partial(right_rows, slot_id, block, b))
            half = len(left) // 2

            def product(lo, hi):
                return nn(
                    jnp.concatenate([f() for f in left[lo:hi]], axis=1),
                    jnp.concatenate([f() for f in right[lo:hi]], axis=0),
                )

            few = table_ref[z.reps // 2, expert] == first

            @pl.when(few)
            def _():
                made[expert] = product(0, half).astype(BF)

            @pl.when(jnp.logical_not(few))
            def _():
                made[expert] = product(0, 2 * half).astype(BF)

            out_copy(expert).start()
        return carry

    lax.fori_loop(0, z.experts // PER, some, 0)
    for expert in range(z.experts):
        out_copy(expert).wait()


def total_down_kernel(z, ids_ref, table_ref, *refs):
    sides = refs[: z.sub]
    grads_ref, codes_ref, out_ref, token_ref, held, made, out_sems, scaled, sems = refs[z.sub :]
    token_ref[...] = jnp.zeros_like(token_ref)

    def moves(act):
        for k in range(z.sub):
            act(
                pltpu.make_async_copy(
                    sides[k], held.at[k, pl.ds(0, z.ep)], sems.at[k]
                )
            )

    moves(lambda copy: copy.start())
    held[:, z.ep] = jnp.zeros_like(held[:, z.ep])
    rows = lax.broadcasted_iota(jnp.int32, (z.slots, z.cap, z.tokens), 1).astype(F32)
    for p in range(z.ep):
        code = codes_ref[p, : z.slots, :][:, None, :]
        load = codes_ref[p, z.slots :, :][:, None, :]
        pick = jnp.where(rows == code, load, 0.0).reshape(z.slots * z.cap, z.tokens)
        result = nn(pick.astype(BF), grads_ref[p]).astype(BF)
        scaled[:, p * z.cap : (p + 1) * z.cap, :] = result.reshape(z.slots, z.cap, z.width)
    moves(lambda copy: copy.wait())

    def right_rows(slot_id, block, b):
        return scaled[slot_id, b * z.block : (b + 1) * z.block, :]

    expert_products(z, ids_ref, table_ref, ids_ref[0], held, right_rows, out_ref, made, out_sems)


def total_in_kernel(z, ids_ref, table_ref, *refs):
    sides, refs = refs[: z.sub], refs[z.sub :]
    own_ref, rights, lefts = refs[0], refs[1 : z.ep], refs[z.ep : 2 * z.ep - 1]
    out_ref, token_ref, held, made, out_sems, inputs_ref, sems, *other_sems = refs[2 * z.ep - 1 :]
    token_ref[...] = jnp.zeros_like(token_ref)

    def moves(act):
        for k in range(z.sub):
            act(pltpu.make_async_copy(sides[k], held.at[k, pl.ds(0, z.ep)], sems.at[k]))
        input_moves(z, ids_ref[0], own_ref, rights, lefts, inputs_ref, *other_sems, act)

    moves(lambda copy: copy.start())
    held[:, z.ep] = jnp.zeros_like(held[:, z.ep])
    moves(lambda copy: copy.wait())

    def right_rows(slot_id, block, b):
        start = pl.multiple_of(block * z.block, z.block)
        return inputs_ref[slot_id // z.local, pl.ds(start, z.block), :]

    expert_products(z, ids_ref, table_ref, ids_ref[0], held, right_rows, out_ref, made, out_sems)


def swap(x, axis, size, bit):
    return lax.ppermute(x, axis, [(i, i ^ bit) for i in range(size)])


def spread_over(have, axis, size, bit):
    have = dict(have)
    while bit:
        for k in list(have):
            if k | bit not in have:
                have[k | bit] = swap(have[k], axis, size, bit)
        bit //= 2
    return [have[k] for k in range(size)]


def nothing(*refs):
    pass


def gate(values, after):
    anywhere = pl.BlockSpec(memory_space=pl.ANY)
    return pl.pallas_call(
        nothing,
        in_specs=[anywhere] * (len(values) + len(after)),
        out_specs=[anywhere] * len(values),
        out_shape=[jax.ShapeDtypeStruct(v.shape, v.dtype) for v in values],
        input_output_aliases={i: i for i in range(len(values))},
        compiler_params=pltpu.CompilerParams(vmem_limit_bytes=1024 * 1024),
        name="gate",
    )(*values, *after)


def pick_kernel(first, ids_ref, go_ref, back_ref, out_ref, sem):
    for condition, ref in ((ids_ref[0] >= first, go_ref), (ids_ref[0] < first, back_ref)):

        @pl.when(condition)
        def _():
            copy = pltpu.make_async_copy(ref, out_ref, sem)
            copy.start()
            copy.wait()


def pick(ids, go, back, first):
    anywhere = pl.BlockSpec(memory_space=pl.ANY)
    return pl.pallas_call(
        functools.partial(pick_kernel, first),
        in_specs=[smem(), anywhere, anywhere],
        out_specs=anywhere,
        out_shape=jax.ShapeDtypeStruct(go.shape, go.dtype),
        scratch_shapes=[pltpu.SemaphoreType.DMA],
        compiler_params=pltpu.CompilerParams(vmem_limit_bytes=1024 * 1024),
        name="pick",
    )(ids, go, back)


def chain_step(go, back, axis, size, d):
    rights = [(i, i + 1) for i in range(d - 1, size - 1)]
    lefts = [(i, i - 1) for i in range(size - d, 0, -1)]
    if d > 1 and go is back:
        got = lax.ppermute(go, axis, rights + lefts)
        return got, got
    return lax.ppermute(go, axis, rights), lax.ppermute(back, axis, lefts)


def body(
    grad_out,
    route_weight,
    routes,
    replica,
    replica_slot,
    token_count,
    saved_input,
    saved_gate_up,
    weight_in,
    weight_down,
):
    z = Sizes(grad_out, routes, replica_slot, saved_input, weight_in, weight_down)
    n, m = z.ep, z.sub
    ids = jnp.stack([lax.axis_index("ep"), lax.axis_index("sub")]).astype(jnp.int32)
    routes, replica, table = routes.T, replica.T, replica_slot.T
    route_weight = route_weight.T
    pair_rows = saved_gate_up.reshape(z.all_rows, z.pair)
    grad_shape = (z.tokens + z.tail, z.width)
    code_shape = (n, 2 * z.slots, z.tokens)
    inputs = saved_input.reshape(z.all_rows, z.width)

    routing = (grad_out, route_weight, routes, replica, table)
    buf = pl.pallas_call(
        functools.partial(route_kernel, z),
        out_shape=jax.ShapeDtypeStruct(grad_shape, BF),
        in_specs=[smem()] + [whole(a.shape) for a in routing],
        out_specs=whole(grad_shape),
        grid=(1,),
        compiler_params=params(60),
        name="route",
    )(token_count, *routing)
    bufs = [buf] + [swap(buf, "ep", n, k) for k in range(1, n)]

    chain = gate([inputs], [buf])
    downs = pl.pallas_call(
        functools.partial(hidden_kernel, z),
        grid_spec=pltpu.PrefetchScalarGridSpec(
            num_scalar_prefetch=1,
            grid=(z.part_blocks,),
            in_specs=[
                pl.BlockSpec((z.block, z.pair), lambda i, r: (r[1] * z.part_blocks + i, 0)),
                pl.BlockSpec(memory_space=pl.ANY),
                pl.BlockSpec(memory_space=pl.ANY),
            ],
            out_specs=[pl.BlockSpec((z.down_cols, z.block), lambda i, r: (0, i))] * n,
            scratch_shapes=[pltpu.VMEM((n, z.down_cols, z.block), BF)],
        ),
        out_shape=[jax.ShapeDtypeStruct((z.down_cols, z.part), BF)] * n,
        compiler_params=params(16),
        name="hidden_columns",
    )(ids, pair_rows, bufs[1], chain[0])
    downs = [downs[0]] + [swap(downs[k], "ep", n, k) for k in range(1, n)]
    chain = gate(chain, bufs[1:] + downs[1:])
    steps = [list(chain_step(chain[0], chain[0], "ep", n, 1))]

    def stack(pieces):
        shape = pieces[0].shape
        return pl.pallas_call(
            functools.partial(stack_kernel, z),
            in_specs=[whole(shape)] * n,
            out_specs=whole((n,) + shape),
            out_shape=jax.ShapeDtypeStruct((n,) + shape, BF),
            grid=(1,),
            compiler_params=params(12),
            name="stack_columns",
        )(*pieces)

    def halve(keep, got):
        half = (keep.shape[0] // 2,) + keep.shape[1:]
        return pl.pallas_call(
            halve_kernel,
            in_specs=[whole(keep.shape)] * 2,
            out_specs=[whole(half)] * 2,
            out_shape=[jax.ShapeDtypeStruct(half, BF)] * 2,
            grid=(1,),
            compiler_params=params(16),
            name="halve",
        )(keep, got)

    def row_block(i, ids_ref):
        place = i // z.part_blocks
        return (place ^ ids_ref[1]) * z.part_blocks + i % z.part_blocks

    part_shape = (m // 2, z.part, z.hidden)
    outs = pl.pallas_call(
        functools.partial(down_kernel, z),
        grid_spec=pltpu.PrefetchScalarGridSpec(
            num_scalar_prefetch=1,
            grid=(z.blocks,),
            in_specs=[whole(grad_shape)] * n
            + [pl.BlockSpec(memory_space=pltpu.HBM), pl.BlockSpec(memory_space=pl.ANY)],
            out_specs=[whole(part_shape)] * 2
            + [whole((n, z.tokens, z.width)), whole(code_shape)],
            scratch_shapes=[
                pltpu.VMEM((z.local, z.rows, z.width), BF),
                pltpu.VMEM((z.local, z.hidden, z.width), BF),
                pltpu.SemaphoreType.DMA((z.local,)),
            ],
        ),
        out_shape=[jax.ShapeDtypeStruct(part_shape, BF)] * 2
        + [
            jax.ShapeDtypeStruct((n, z.tokens, z.width), BF),
            jax.ShapeDtypeStruct(code_shape, F32),
        ],
        compiler_params=params(48),
        name="hidden_partials",
    )(ids, *bufs, weight_down, *downs[:1])
    keep, send, grads_all, codes = outs
    down_sides = spread_over({0: stack(downs)}, "sub", m, m // 2)
    def total_call(kernel, operands, specs, cols, scratch, name):
        return pl.pallas_call(
            functools.partial(kernel, z),
            grid_spec=pltpu.PrefetchScalarGridSpec(
                num_scalar_prefetch=2,
                grid=(1,),
                in_specs=specs,
                out_specs=[pl.BlockSpec(memory_space=pl.ANY), whole((8, 128))],
                scratch_shapes=[
                    pltpu.VMEM((m, n + 1, cols, z.part), BF),
                    pltpu.VMEM((z.experts, cols, z.width), BF),
                    pltpu.SemaphoreType.DMA((z.experts,)),
                ]
                + scratch,
            ),
            out_shape=[
                jax.ShapeDtypeStruct((z.experts, cols, z.width), BF),
                jax.ShapeDtypeStruct((8, 128), F32),
            ],
            compiler_params=params(32),
            name=name,
        )(ids, table, *operands)

    anywhere = pl.BlockSpec(memory_space=pl.ANY)
    grad_down, down_made = total_call(
        total_down_kernel,
        [*down_sides, grads_all, codes],
        [anywhere] * m + [whole((n, z.tokens, z.width)), whole(code_shape)],
        z.down_cols,
        [pltpu.VMEM((z.slots, z.rows, z.width), BF), pltpu.SemaphoreType.DMA((m,))],
        "down_grads",
    )
    steps.append(chain_step(*steps[0], "ep", n, 2))
    got = swap(send, "sub", m, 1)
    after = list(steps[0])
    bit = 2
    while bit < m:
        keep, send = halve(keep, got)
        send = gate([send], after)[0]
        got = swap(send, "sub", m, bit)
        bit *= 2

    got = gate([got], [down_made])[0]
    *pieces, grad_part = pl.pallas_call(
        functools.partial(pre_kernel, z),
        grid_spec=pltpu.PrefetchScalarGridSpec(
            num_scalar_prefetch=1,
            grid=(z.part_blocks,),
            in_specs=[pl.BlockSpec((1, z.block, z.hidden), lambda i, r: (0, i, 0))] * 2
            + [
                pl.BlockSpec((z.block, z.pair), lambda i, r: (r[1] * z.part_blocks + i, 0)),
                whole(code_shape),
            ],
            out_specs=[pl.BlockSpec((z.in_cols, z.block), lambda i, r: (0, i))] * n
            + [pl.BlockSpec((z.block, z.hidden), lambda i, r: (i, 0))],
            scratch_shapes=[pltpu.VMEM((n, z.in_cols, z.block), BF)],
        ),
        out_shape=[jax.ShapeDtypeStruct((z.in_cols, z.part), BF)] * n
        + [jax.ShapeDtypeStruct((z.part, z.hidden), BF)],
        compiler_params=params(16),
        name="pre_grads",
    )(ids, keep, got, pair_rows, codes)
    late = gate(pieces[2:], steps[1])
    pieces = pieces[:1] + [swap(a, "ep", n, k) for k, a in enumerate([pieces[1], *late], 1)]
    grad_parts = spread_over({0: grad_part}, "sub", m, m // 2)

    back_shape = (z.tokens + z.slots, z.width)
    parts = pl.pallas_call(
        functools.partial(row_kernel, z),
        grid_spec=pltpu.PrefetchScalarGridSpec(
            num_scalar_prefetch=1,
            grid=(z.blocks,),
            in_specs=[whole((z.part, z.hidden))] * m
            + [
                pl.BlockSpec((z.block, z.pair), lambda i, r: (row_block(i, r), 0)),
                pl.BlockSpec(memory_space=pltpu.HBM),
                whole(code_shape),
            ],
            out_specs=[whole(back_shape)] * n,
            scratch_shapes=[
                pltpu.VMEM((z.local, z.rows, z.width), BF),
                pltpu.VMEM((n, z.slots, z.tokens), F32),
                pltpu.VMEM((z.block, z.hidden), BF),
                pltpu.VMEM((z.local, z.pair, z.width), BF),
                pltpu.SemaphoreType.DMA((z.local,)),
            ],
        ),
        out_shape=[jax.ShapeDtypeStruct(back_shape, BF)] * n,
        compiler_params=params(46),
        name="row_grads",
    )(ids, *grad_parts, pair_rows, weight_in, codes)
    steps[1] = go, back = gate(steps[1], pieces[1:])
    picked = []
    for d in range(3, n):
        if 2 * d > n + 1 and go is not back:
            go = back = pick(ids, go, back, d - 1)
            picked.append(go)
        go, back = chain_step(go, back, "ep", n, d)
        steps.append((go, back))
    gathered = [inputs] + [go for go, _ in steps] + [back for _, back in steps]
    got = [swap(part, "ep", n, 1) for part in parts[1::2]]
    pieces[:1] = gate(pieces[:1], [*got, *picked])
    sides = spread_over({0: stack(pieces)}, "sub", m, m // 2)
    keep, bit = parts[::2], 2
    while bit < n:
        count = len(keep)
        parts = pl.pallas_call(
            sum_kernel,
            in_specs=[whole(back_shape)] * 2 * count,
            out_specs=[whole(back_shape)] * count,
            out_shape=[jax.ShapeDtypeStruct(back_shape, BF)] * count,
            grid=(1,),
            compiler_params=params(16),
            name="sum_parts",
        )(*keep, *got)
        keep = parts[::2]
        send = gate(parts[1::2], gathered[1:])
        got = [swap(part, "ep", n, bit) for part in send]
        bit *= 2

    grad_in, in_made = total_call(
        total_in_kernel,
        [*sides, *gathered],
        [anywhere] * (m + 2 * n - 1),
        z.in_cols,
        [
            pltpu.VMEM((n, z.all_rows, z.width), BF),
            pltpu.SemaphoreType.DMA((m,)),
            pltpu.SemaphoreType.DMA,
            pltpu.SemaphoreType.DMA((n - 1,)),
            pltpu.SemaphoreType.DMA((n - 1,)),
        ],
        "in_grads",
    )
    keep, got = keep[0], gate(got, [in_made])[0]
    grad_tokens, grad_routes = pl.pallas_call(
        functools.partial(token_kernel, z),
        out_shape=[
            jax.ShapeDtypeStruct((z.tokens, z.width), BF),
            jax.ShapeDtypeStruct((z.top, z.tokens), BF),
        ],
        in_specs=[smem()] + [whole(a.shape) for a in (keep, got, routes, replica, table)],
        out_specs=[whole((z.tokens, z.width)), whole((z.top, z.tokens))],
        grid=(1,),
        compiler_params=params(16),
        name="token_grads",
    )(token_count, keep, got, routes, replica, table)

    return grad_tokens, grad_routes.T, grad_in, grad_down


def solution(mesh):
    return jax.shard_map(
        body,
        mesh=mesh,
        in_specs=(
            P(("groups", "ep"), "sub"),
            P(("groups", "ep"), None),
            P(("groups", "ep"), None),
            P(("groups", "ep"), None),
            P("groups", None),
            P(("groups", "ep")),
            P(("groups", "ep"), None, None, "sub"),
            P(("groups", "ep"), None, None),
            P(("groups", "ep"), None, "sub"),
            P(("groups", "ep"), None, "sub"),
        ),
        out_specs=(
            P(("groups", "ep"), "sub"),
            P(("groups", "ep"), None),
            P("groups", "ep", "sub"),
            P("groups", "ep", "sub"),
        ),
        check_vma=False,
    )
```

```python
import functools
import math

import jax
import jax.numpy as jnp
from jax import lax
from jax.experimental import pallas as pl
from jax.experimental.pallas import tpu as pltpu
from jax.sharding import PartitionSpec as P

BF = jnp.bfloat16
F32 = jnp.float32
PER = 2


def nt(a, b):
    return lax.dot_general(a, b, (((1,), (1,)), ((), ())), preferred_element_type=F32)


def tn(a, b):
    return lax.dot_general(a, b, (((0,), (0,)), ((), ())), preferred_element_type=F32)


def nn(a, b):
    return jnp.dot(a, b, preferred_element_type=F32)


def whole(shape):
    zeros = (0,) * len(shape)
    return pl.BlockSpec(shape, lambda *_: zeros)


def smem():
    return pl.BlockSpec(memory_space=pltpu.SMEM)


def params(mib):
    return pltpu.CompilerParams(
        vmem_limit_bytes=mib * 1024 * 1024, dimension_semantics=("arbitrary",)
    )


class Sizes:
    def __init__(self, grad_out, routes, replica_slot, saved_input, weight_in, weight_down):
        self.ep = lax.axis_size("ep")
        self.sub = lax.axis_size("sub")
        self.tokens, self.width = grad_out.shape
        self.top = routes.shape[1]
        self.experts, self.reps = replica_slot.shape
        self.local = weight_in.shape[0]
        self.slots = self.ep * self.local
        self.cap = saved_input.shape[2]
        self.rows = self.ep * self.cap
        self.hidden = weight_down.shape[1]
        self.pair = weight_in.shape[1]
        self.all_rows = self.local * self.rows
        self.part = self.all_rows // self.sub
        self.block = math.gcd(self.rows, self.part)
        self.sources = self.block // self.cap
        self.blocks = self.all_rows // self.block
        self.part_blocks = self.part // self.block
        self.slot_blocks = self.rows // self.block
        self.in_cols = self.pair // self.ep
        self.down_cols = self.hidden // self.ep
        self.cols = self.in_cols + self.down_cols
        self.folds = self.width // self.tokens
        self.tail = 2 * self.slots // self.folds


def slot_table(z, table_ref, r):
    ids = lax.broadcasted_iota(jnp.int32, (z.slots, z.experts), 0)
    return (table_ref[r : r + 1, :] == ids).astype(F32).astype(BF)


def key_hits(z, count_ref, routes_ref, replica_ref, r, k):
    ids = lax.broadcasted_iota(jnp.int32, (z.experts, z.tokens), 0)
    live = lax.broadcasted_iota(jnp.int32, (1, z.tokens), 1) < count_ref[0]
    key = jnp.where(live & (replica_ref[k : k + 1, :] == r), routes_ref[k : k + 1, :], -1)
    return key == ids


def route_kernel(z, count_ref, grad_ref, weight_ref, routes_ref, replica_ref, table_ref, out_ref):
    weights = weight_ref[...].astype(F32)
    hits = jnp.zeros((z.slots, z.tokens), F32)
    loads = jnp.zeros((z.slots, z.tokens), F32)
    for r in range(z.reps):
        hit = jnp.zeros((z.experts, z.tokens), F32)
        load = jnp.zeros((z.experts, z.tokens), F32)
        for k in range(z.top):
            same = key_hits(z, count_ref, routes_ref, replica_ref, r, k)
            hit = jnp.where(same, 1.0, hit)
            load = jnp.where(same, weights[k : k + 1, :], load)
        table = slot_table(z, table_ref, r)
        hits = hits + nn(table, hit.astype(BF))
        loads = loads + nn(table, load.astype(BF))
    before = lax.broadcasted_iota(jnp.int32, (z.tokens, z.tokens), 0)
    after = lax.broadcasted_iota(jnp.int32, (z.tokens, z.tokens), 1)
    earlier = nn(hits.astype(BF), (before < after).astype(F32).astype(BF))
    code = jnp.where(hits > 0.5, earlier, -1.0)
    both = jnp.concatenate([code, loads], axis=0).astype(BF)
    out_ref[: z.tokens, :] = grad_ref[...]
    for b in range(z.folds):
        out_ref[z.tokens :, b * z.tokens : (b + 1) * z.tokens] = both[
            b * z.tail : (b + 1) * z.tail, :
        ]


def block_place(z, block):
    slot = block // z.slot_blocks
    first = (block % z.slot_blocks) * z.sources
    return slot, first


def block_picks(z, codes_ref, slot, first):
    rows = lax.broadcasted_iota(jnp.int32, (z.cap, z.tokens), 0).astype(F32)
    for a in range(z.sources):
        code = codes_ref[first + a, pl.ds(slot, 1), :]
        yield a, rows == code


def block_scale(z, codes_ref, slot, first):
    parts = []
    for a, pick in block_picks(z, codes_ref, slot, first):
        load = codes_ref[first + a, pl.ds(z.slots + slot, 1), :]
        parts.append(jnp.sum(jnp.where(pick, load, 0.0), axis=1, keepdims=True))
    return jnp.concatenate(parts, axis=0)


def local_picks(z, codes_ref, source, me):
    code = codes_ref[source, pl.ds(pl.multiple_of(me * z.local, z.local), z.local), :]
    rows = lax.broadcasted_iota(jnp.int32, (z.local, z.cap, z.tokens), 1).astype(F32)
    pick = (code[:, None, :] == rows).astype(F32)
    return pick.reshape(z.local * z.cap, z.tokens).astype(BF)


def block_slot(z, mine, step):
    place = step // z.part_blocks
    return ((place ^ mine) * z.part_blocks + step % z.part_blocks) // z.slot_blocks


def weight_copy(weight_ref, held, sems, slot):
    return pltpu.make_async_copy(weight_ref.at[slot], held.at[slot], sems.at[slot])


def down_kernel(z, ids_ref, *refs):
    bufs = refs[: z.ep]
    weight_ref = refs[z.ep]
    parts = refs[z.ep + 2 : z.ep + 4]
    grads_ref, codes_ref, rows_ref, held, sems = refs[z.ep + 4 :]
    me, mine = ids_ref[0], ids_ref[1]
    step = pl.program_id(0)

    @pl.when(step == 0)
    def _():
        for s in range(z.local):
            weight_copy(weight_ref, held, sems, s).start()
        for k in range(z.ep):
            source = me ^ k
            grads_ref[source] = bufs[k][: z.tokens, :]
            for b in range(z.folds):
                codes_ref[source, b * z.tail : (b + 1) * z.tail, :] = bufs[k][
                    z.tokens :, b * z.tokens : (b + 1) * z.tokens
                ].astype(F32)
        for p in range(z.ep):
            rows = nn(local_picks(z, codes_ref, p, me), grads_ref[p]).astype(BF)
            rows_ref[:, p * z.cap : (p + 1) * z.cap, :] = rows.reshape(z.local, z.cap, z.width)

    place = step // z.part_blocks
    block = (place ^ mine) * z.part_blocks + step % z.part_blocks
    slot, first = block_place(z, block)
    start = pl.multiple_of(first * z.cap, z.block)

    @pl.when((step == 0) | (slot != block_slot(z, mine, step - 1)))
    def _():
        weight_copy(weight_ref, held, sems, slot).wait()

    partial = nt(rows_ref[slot, pl.ds(start, z.block), :], held[slot]).astype(BF)
    spot = pl.multiple_of((step % z.part_blocks) * z.block, z.block)
    for k in range(z.sub):

        @pl.when(place == k)
        def _():
            parts[k % 2][k // 2, pl.ds(spot, z.block), :] = partial


def gate_terms(z, pair, grad, scale):
    gate = pair[:, : z.hidden].astype(F32)
    up = pair[:, z.hidden :].astype(F32)
    sig = 1.0 / (1.0 + jnp.exp(-gate))
    act = gate * sig
    hidden = act * up
    scaled = scale * grad
    grad_gate = scaled * up * sig * (1.0 + gate * (1.0 - sig))
    grad_up = scaled * act
    return hidden, grad_gate.astype(BF), grad_up.astype(BF)


def pre_kernel(z, ids_ref, keep_ref, got_ref, pair_ref, codes_ref, *refs):
    outs, (grad_ref, sides) = refs[: z.ep], refs[z.ep :]
    me = ids_ref[0]
    block = ids_ref[1] * z.part_blocks + pl.program_id(0)
    slot, first = block_place(z, block)
    scale = block_scale(z, codes_ref, me * z.local + slot, first)
    grad = keep_ref[0].astype(F32) + got_ref[0].astype(F32)
    grad_ref[...] = grad.astype(BF)
    _, grad_gate, grad_up = gate_terms(z, pair_ref[...], grad, scale)
    send_columns(z, me, jnp.concatenate([grad_gate.T, grad_up.T], axis=0), sides, outs)


def send_columns(z, me, columns, sides, outs):
    size = columns.shape[0] // z.ep
    for q in range(z.ep):
        sides[q] = columns[q * size : (q + 1) * size, :]
    for k in range(z.ep):
        outs[k][...] = sides[me ^ k]


def hidden_kernel(z, ids_ref, pair_ref, after_ref, other_ref, *refs):
    pair = pair_ref[...]
    gate_pre = pair[:, : z.hidden].astype(F32)
    up = pair[:, z.hidden :].astype(F32)
    hidden = gate_pre * (1.0 / (1.0 + jnp.exp(-gate_pre))) * up
    send_columns(z, ids_ref[0], hidden.astype(BF).T, refs[-1], refs[:-1])


def stack_kernel(z, *refs):
    for k in range(z.ep):
        refs[-1][k] = refs[k][...]


def row_kernel(z, ids_ref, *refs):
    grads = refs[: z.sub]
    pair_ref, weight_ref, codes_ref = refs[z.sub : z.sub + 3]
    outs = refs[z.sub + 3 : z.sub + 3 + z.ep]
    rows_ref, marks, held, weights, sems = refs[z.sub + 3 + z.ep :]
    me, mine = ids_ref[0], ids_ref[1]
    step = pl.program_id(0)
    place = step // z.part_blocks
    block = (place ^ mine) * z.part_blocks + step % z.part_blocks
    slot, first = block_place(z, block)

    @pl.when(step == 0)
    def _():
        for s in range(z.local):
            weight_copy(weight_ref, weights, sems, s).start()
        marks[...] = jnp.zeros_like(marks)

    spot = pl.multiple_of((step % z.part_blocks) * z.block, z.block)
    for k in range(z.sub):

        @pl.when(place == k)
        def _():
            held[...] = grads[k][pl.ds(spot, z.block), :]

    grad = held[...].astype(F32)
    scale = block_scale(z, codes_ref, me * z.local + slot, first)
    hidden, grad_gate, grad_up = gate_terms(z, pair_ref[...], grad, scale)
    route = jnp.sum(hidden * grad, axis=1, keepdims=True).astype(BF).astype(F32)

    @pl.when((step == 0) | (slot != block_slot(z, mine, step - 1)))
    def _():
        weight_copy(weight_ref, weights, sems, slot).wait()

    rows = nn(grad_gate, weights[slot, : z.hidden, :]) + nn(grad_up, weights[slot, z.hidden :, :])
    start = pl.multiple_of(first * z.cap, z.block)
    rows_ref[slot, pl.ds(start, z.block), :] = rows.astype(BF)
    for a, pick in block_picks(z, codes_ref, me * z.local + slot, first):
        marks[first + a, pl.ds(me * z.local + slot, 1), :] = jnp.sum(
            jnp.where(pick, route[a * z.cap : (a + 1) * z.cap, :], 0.0), axis=0, keepdims=True
        )

    @pl.when(step == z.blocks - 1)
    def _():
        blank = jnp.zeros((z.slots, z.width - z.tokens), BF)
        for k in range(z.ep):
            source = me ^ k
            start = pl.multiple_of(source * z.cap, z.cap)
            rows = rows_ref[:, pl.ds(start, z.cap), :].reshape(z.local * z.cap, z.width)
            picks = local_picks(z, codes_ref, source, me)
            outs[k][: z.tokens, :] = tn(picks, rows).astype(BF)
            outs[k][z.tokens :, : z.tokens] = marks[source].astype(BF)
            outs[k][z.tokens :, z.tokens :] = blank


def sum_kernel(*refs):
    count = len(refs) // 3
    for i in range(count):
        total = refs[i][...].astype(F32) + refs[count + i][...].astype(F32)
        refs[2 * count + i][...] = total.astype(BF)


def halve_kernel(keep_ref, got_ref, out_keep, out_send):
    for i in range(out_keep.shape[0]):
        for j, out in enumerate((out_keep, out_send)):
            total = keep_ref[2 * i + j].astype(F32) + got_ref[2 * i + j].astype(F32)
            out[i] = total.astype(BF)


def token_kernel(z, count_ref, *refs):
    keep_ref, got_ref, routes_ref, replica_ref, table_ref, tokens_ref, route_ref = refs
    total = keep_ref[...].astype(F32) + got_ref[...].astype(F32)
    tokens_ref[...] = total[: z.tokens, :].astype(BF)
    rows = total[z.tokens :, : z.tokens].astype(BF)
    totals = [jnp.zeros((1, z.tokens), F32)] * z.top
    for r in range(z.reps):
        spread = tn(slot_table(z, table_ref, r), rows)
        for k in range(z.top):
            same = key_hits(z, count_ref, routes_ref, replica_ref, r, k)
            totals[k] += jnp.sum(jnp.where(same, spread, 0.0), axis=0, keepdims=True)
    route_ref[...] = jnp.concatenate(totals, axis=0).astype(BF)


def input_moves(z, me, own_ref, rights, lefts, inputs_ref, own_sem, right_sems, left_sems, act):
    act(pltpu.make_async_copy(own_ref, inputs_ref.at[me], own_sem))
    for d in range(1, z.ep):

        @pl.when(me >= d)
        def _():
            act(
                pltpu.make_async_copy(
                    rights[d - 1], inputs_ref.at[me - d], right_sems.at[d - 1]
                )
            )

        @pl.when(me + d < z.ep)
        def _():
            act(
                pltpu.make_async_copy(
                    lefts[d - 1], inputs_ref.at[me + d], left_sems.at[d - 1]
                )
            )


def left_rows(held, part, side, spot, size):
    return held[part, side, :, pl.ds(spot, size)]


def expert_products(z, ids_ref, table_ref, turn, held, right_rows, out_ref, made, out_sems):
    mine = ids_ref[1]

    def out_copy(expert):
        return pltpu.make_async_copy(made.at[expert], out_ref.at[expert], out_sems.at[expert])

    def some(step, carry):
        for i in range(PER):
            expert = step * PER + i
            first = table_ref[0, expert]
            left, right = [], []
            for r in range(z.reps):
                slot_id = table_ref[r, expert]
                source = slot_id // z.local
                for b in range(z.slot_blocks):
                    block = (slot_id % z.local) * z.slot_blocks + b
                    part = (block // z.part_blocks) ^ mine
                    spot = pl.multiple_of((block % z.part_blocks) * z.block, z.block)
                    side = source ^ turn
                    if r:
                        side = jnp.where(slot_id == first, z.ep, side)
                    left.append(functools.partial(left_rows, held, part, side, spot, z.block))
                    right.append(functools.partial(right_rows, slot_id, block, b))
            half = len(left) // 2

            def product(lo, hi):
                return nn(
                    jnp.concatenate([f() for f in left[lo:hi]], axis=1),
                    jnp.concatenate([f() for f in right[lo:hi]], axis=0),
                )

            few = table_ref[z.reps // 2, expert] == first

            @pl.when(few)
            def _():
                made[expert] = product(0, half).astype(BF)

            @pl.when(jnp.logical_not(few))
            def _():
                made[expert] = product(0, 2 * half).astype(BF)

            out_copy(expert).start()
        return carry

    lax.fori_loop(0, z.experts // PER, some, 0)
    for expert in range(z.experts):
        out_copy(expert).wait()


def total_down_kernel(z, ids_ref, table_ref, *refs):
    sides = refs[: z.sub]
    grads_ref, codes_ref, out_ref, token_ref, held, made, out_sems, scaled, sems = refs[z.sub :]
    token_ref[...] = jnp.zeros_like(token_ref)

    def moves(act):
        for k in range(z.sub):
            act(
                pltpu.make_async_copy(
                    sides[k], held.at[k, pl.ds(0, z.ep)], sems.at[k]
                )
            )

    moves(lambda copy: copy.start())
    held[:, z.ep] = jnp.zeros_like(held[:, z.ep])
    rows = lax.broadcasted_iota(jnp.int32, (z.slots, z.cap, z.tokens), 1).astype(F32)
    for p in range(z.ep):
        code = codes_ref[p, : z.slots, :][:, None, :]
        load = codes_ref[p, z.slots :, :][:, None, :]
        pick = jnp.where(rows == code, load, 0.0).reshape(z.slots * z.cap, z.tokens)
        result = nn(pick.astype(BF), grads_ref[p]).astype(BF)
        scaled[:, p * z.cap : (p + 1) * z.cap, :] = result.reshape(z.slots, z.cap, z.width)
    moves(lambda copy: copy.wait())

    def right_rows(slot_id, block, b):
        return scaled[slot_id, b * z.block : (b + 1) * z.block, :]

    expert_products(z, ids_ref, table_ref, ids_ref[0], held, right_rows, out_ref, made, out_sems)


def total_in_kernel(z, ids_ref, table_ref, *refs):
    sides, refs = refs[: z.sub], refs[z.sub :]
    own_ref, rights, lefts = refs[0], refs[1 : z.ep], refs[z.ep : 2 * z.ep - 1]
    out_ref, token_ref, held, made, out_sems, inputs_ref, sems, *other_sems = refs[2 * z.ep - 1 :]
    token_ref[...] = jnp.zeros_like(token_ref)

    def moves(act):
        for k in range(z.sub):
            act(pltpu.make_async_copy(sides[k], held.at[k, pl.ds(0, z.ep)], sems.at[k]))
        input_moves(z, ids_ref[0], own_ref, rights, lefts, inputs_ref, *other_sems, act)

    moves(lambda copy: copy.start())
    held[:, z.ep] = jnp.zeros_like(held[:, z.ep])
    moves(lambda copy: copy.wait())

    def right_rows(slot_id, block, b):
        start = pl.multiple_of(block * z.block, z.block)
        return inputs_ref[slot_id // z.local, pl.ds(start, z.block), :]

    expert_products(z, ids_ref, table_ref, ids_ref[0], held, right_rows, out_ref, made, out_sems)


def swap(x, axis, size, bit):
    return lax.ppermute(x, axis, [(i, i ^ bit) for i in range(size)])


def spread_over(have, axis, size, bit):
    have = dict(have)
    while bit:
        for k in list(have):
            if k | bit not in have:
                have[k | bit] = swap(have[k], axis, size, bit)
        bit //= 2
    return [have[k] for k in range(size)]


def nothing(*refs):
    pass


def gate(values, after):
    anywhere = pl.BlockSpec(memory_space=pl.ANY)
    return pl.pallas_call(
        nothing,
        in_specs=[anywhere] * (len(values) + len(after)),
        out_specs=[anywhere] * len(values),
        out_shape=[jax.ShapeDtypeStruct(v.shape, v.dtype) for v in values],
        input_output_aliases={i: i for i in range(len(values))},
        compiler_params=pltpu.CompilerParams(vmem_limit_bytes=1024 * 1024),
        name="gate",
    )(*values, *after)


def pick_kernel(first, ids_ref, go_ref, back_ref, out_ref, sem):
    for condition, ref in ((ids_ref[0] >= first, go_ref), (ids_ref[0] < first, back_ref)):

        @pl.when(condition)
        def _():
            copy = pltpu.make_async_copy(ref, out_ref, sem)
            copy.start()
            copy.wait()


def pick(ids, go, back, first):
    anywhere = pl.BlockSpec(memory_space=pl.ANY)
    return pl.pallas_call(
        functools.partial(pick_kernel, first),
        in_specs=[smem(), anywhere, anywhere],
        out_specs=anywhere,
        out_shape=jax.ShapeDtypeStruct(go.shape, go.dtype),
        scratch_shapes=[pltpu.SemaphoreType.DMA],
        compiler_params=pltpu.CompilerParams(vmem_limit_bytes=1024 * 1024),
        name="pick",
    )(ids, go, back)


def chain_step(go, back, axis, size, d):
    rights = [(i, i + 1) for i in range(d - 1, size - 1)]
    lefts = [(i, i - 1) for i in range(size - d, 0, -1)]
    if d > 1 and go is back:
        got = lax.ppermute(go, axis, rights + lefts)
        return got, got
    return lax.ppermute(go, axis, rights), lax.ppermute(back, axis, lefts)


def body(
    grad_out,
    route_weight,
    routes,
    replica,
    replica_slot,
    token_count,
    saved_input,
    saved_gate_up,
    weight_in,
    weight_down,
):
    z = Sizes(grad_out, routes, replica_slot, saved_input, weight_in, weight_down)
    n, m = z.ep, z.sub
    ids = jnp.stack([lax.axis_index("ep"), lax.axis_index("sub")]).astype(jnp.int32)
    routes, replica, table = routes.T, replica.T, replica_slot.T
    route_weight = route_weight.T
    pair_rows = saved_gate_up.reshape(z.all_rows, z.pair)
    grad_shape = (z.tokens + z.tail, z.width)
    code_shape = (n, 2 * z.slots, z.tokens)
    inputs = saved_input.reshape(z.all_rows, z.width)

    routing = (grad_out, route_weight, routes, replica, table)
    buf = pl.pallas_call(
        functools.partial(route_kernel, z),
        out_shape=jax.ShapeDtypeStruct(grad_shape, BF),
        in_specs=[smem()] + [whole(a.shape) for a in routing],
        out_specs=whole(grad_shape),
        grid=(1,),
        compiler_params=params(60),
        name="route",
    )(token_count, *routing)
    bufs = [buf] + [swap(buf, "ep", n, k) for k in range(1, n)]

    chain = gate([inputs], [buf])
    downs = pl.pallas_call(
        functools.partial(hidden_kernel, z),
        grid_spec=pltpu.PrefetchScalarGridSpec(
            num_scalar_prefetch=1,
            grid=(z.part_blocks,),
            in_specs=[
                pl.BlockSpec((z.block, z.pair), lambda i, r: (r[1] * z.part_blocks + i, 0)),
                pl.BlockSpec(memory_space=pl.ANY),
                pl.BlockSpec(memory_space=pl.ANY),
            ],
            out_specs=[pl.BlockSpec((z.down_cols, z.block), lambda i, r: (0, i))] * n,
            scratch_shapes=[pltpu.VMEM((n, z.down_cols, z.block), BF)],
        ),
        out_shape=[jax.ShapeDtypeStruct((z.down_cols, z.part), BF)] * n,
        compiler_params=params(16),
        name="hidden_columns",
    )(ids, pair_rows, bufs[1], chain[0])
    downs = [downs[0]] + [swap(downs[k], "ep", n, k) for k in range(1, n)]
    chain = gate(chain, bufs[1:] + downs[1:])
    steps = [list(chain_step(chain[0], chain[0], "ep", n, 1))]

    def stack(pieces):
        shape = pieces[0].shape
        return pl.pallas_call(
            functools.partial(stack_kernel, z),
            in_specs=[whole(shape)] * n,
            out_specs=whole((n,) + shape),
            out_shape=jax.ShapeDtypeStruct((n,) + shape, BF),
            grid=(1,),
            compiler_params=params(12),
            name="stack_columns",
        )(*pieces)

    def halve(keep, got):
        half = (keep.shape[0] // 2,) + keep.shape[1:]
        return pl.pallas_call(
            halve_kernel,
            in_specs=[whole(keep.shape)] * 2,
            out_specs=[whole(half)] * 2,
            out_shape=[jax.ShapeDtypeStruct(half, BF)] * 2,
            grid=(1,),
            compiler_params=params(16),
            name="halve",
        )(keep, got)

    def row_block(i, ids_ref):
        place = i // z.part_blocks
        return (place ^ ids_ref[1]) * z.part_blocks + i % z.part_blocks

    part_shape = (m // 2, z.part, z.hidden)
    outs = pl.pallas_call(
        functools.partial(down_kernel, z),
        grid_spec=pltpu.PrefetchScalarGridSpec(
            num_scalar_prefetch=1,
            grid=(z.blocks,),
            in_specs=[whole(grad_shape)] * n
            + [pl.BlockSpec(memory_space=pltpu.HBM), pl.BlockSpec(memory_space=pl.ANY)],
            out_specs=[whole(part_shape)] * 2
            + [whole((n, z.tokens, z.width)), whole(code_shape)],
            scratch_shapes=[
                pltpu.VMEM((z.local, z.rows, z.width), BF),
                pltpu.VMEM((z.local, z.hidden, z.width), BF),
                pltpu.SemaphoreType.DMA((z.local,)),
            ],
        ),
        out_shape=[jax.ShapeDtypeStruct(part_shape, BF)] * 2
        + [
            jax.ShapeDtypeStruct((n, z.tokens, z.width), BF),
            jax.ShapeDtypeStruct(code_shape, F32),
        ],
        compiler_params=params(48),
        name="hidden_partials",
    )(ids, *bufs, weight_down, *downs[:1])
    keep, send, grads_all, codes = outs
    down_sides = spread_over({0: stack(downs)}, "sub", m, m // 2)
    def total_call(kernel, operands, specs, cols, scratch, name):
        return pl.pallas_call(
            functools.partial(kernel, z),
            grid_spec=pltpu.PrefetchScalarGridSpec(
                num_scalar_prefetch=2,
                grid=(1,),
                in_specs=specs,
                out_specs=[pl.BlockSpec(memory_space=pl.ANY), whole((8, 128))],
                scratch_shapes=[
                    pltpu.VMEM((m, n + 1, cols, z.part), BF),
                    pltpu.VMEM((z.experts, cols, z.width), BF),
                    pltpu.SemaphoreType.DMA((z.experts,)),
                ]
                + scratch,
            ),
            out_shape=[
                jax.ShapeDtypeStruct((z.experts, cols, z.width), BF),
                jax.ShapeDtypeStruct((8, 128), F32),
            ],
            compiler_params=params(32),
            name=name,
        )(ids, table, *operands)

    anywhere = pl.BlockSpec(memory_space=pl.ANY)
    grad_down, down_made = total_call(
        total_down_kernel,
        [*down_sides, grads_all, codes],
        [anywhere] * m + [whole((n, z.tokens, z.width)), whole(code_shape)],
        z.down_cols,
        [pltpu.VMEM((z.slots, z.rows, z.width), BF), pltpu.SemaphoreType.DMA((m,))],
        "down_grads",
    )
    steps.append(chain_step(*steps[0], "ep", n, 2))
    got = swap(send, "sub", m, 1)
    after = list(steps[0])
    bit = 2
    while bit < m:
        keep, send = halve(keep, got)
        send = gate([send], after)[0]
        got = swap(send, "sub", m, bit)
        bit *= 2

    got = gate([got], [down_made])[0]
    *pieces, grad_part = pl.pallas_call(
        functools.partial(pre_kernel, z),
        grid_spec=pltpu.PrefetchScalarGridSpec(
            num_scalar_prefetch=1,
            grid=(z.part_blocks,),
            in_specs=[pl.BlockSpec((1, z.block, z.hidden), lambda i, r: (0, i, 0))] * 2
            + [
                pl.BlockSpec((z.block, z.pair), lambda i, r: (r[1] * z.part_blocks + i, 0)),
                whole(code_shape),
            ],
            out_specs=[pl.BlockSpec((z.in_cols, z.block), lambda i, r: (0, i))] * n
            + [pl.BlockSpec((z.block, z.hidden), lambda i, r: (i, 0))],
            scratch_shapes=[pltpu.VMEM((n, z.in_cols, z.block), BF)],
        ),
        out_shape=[jax.ShapeDtypeStruct((z.in_cols, z.part), BF)] * n
        + [jax.ShapeDtypeStruct((z.part, z.hidden), BF)],
        compiler_params=params(16),
        name="pre_grads",
    )(ids, keep, got, pair_rows, codes)
    late = gate(pieces[1:], steps[1])
    pieces = pieces[:1] + [swap(a, "ep", n, k) for k, a in enumerate(late, 1)]
    grad_parts = spread_over({0: grad_part}, "sub", m, m // 2)

    back_shape = (z.tokens + z.slots, z.width)
    parts = pl.pallas_call(
        functools.partial(row_kernel, z),
        grid_spec=pltpu.PrefetchScalarGridSpec(
            num_scalar_prefetch=1,
            grid=(z.blocks,),
            in_specs=[whole((z.part, z.hidden))] * m
            + [
                pl.BlockSpec((z.block, z.pair), lambda i, r: (row_block(i, r), 0)),
                pl.BlockSpec(memory_space=pltpu.HBM),
                whole(code_shape),
            ],
            out_specs=[whole(back_shape)] * n,
            scratch_shapes=[
                pltpu.VMEM((z.local, z.rows, z.width), BF),
                pltpu.VMEM((n, z.slots, z.tokens), F32),
                pltpu.VMEM((z.block, z.hidden), BF),
                pltpu.VMEM((z.local, z.pair, z.width), BF),
                pltpu.SemaphoreType.DMA((z.local,)),
            ],
        ),
        out_shape=[jax.ShapeDtypeStruct(back_shape, BF)] * n,
        compiler_params=params(46),
        name="row_grads",
    )(ids, *grad_parts, pair_rows, weight_in, codes)
    steps[1] = go, back = gate(steps[1], pieces[1:])
    picked = []
    for d in range(3, n):
        if 2 * d > n + 1 and go is not back:
            go = back = pick(ids, go, back, d - 1)
            picked.append(go)
        go, back = chain_step(go, back, "ep", n, d)
        steps.append((go, back))
    gathered = [inputs] + [go for go, _ in steps] + [back for _, back in steps]
    got = [swap(part, "ep", n, 1) for part in parts[1::2]]
    pieces[:1] = gate(pieces[:1], [*got, *picked])
    sides = spread_over({0: stack(pieces)}, "sub", m, m // 2)
    keep, bit = parts[::2], 2
    while bit < n:
        count = len(keep)
        parts = pl.pallas_call(
            sum_kernel,
            in_specs=[whole(back_shape)] * 2 * count,
            out_specs=[whole(back_shape)] * count,
            out_shape=[jax.ShapeDtypeStruct(back_shape, BF)] * count,
            grid=(1,),
            compiler_params=params(16),
            name="sum_parts",
        )(*keep, *got)
        keep = parts[::2]
        send = gate(parts[1::2], sides[1:])
        got = [swap(part, "ep", n, bit) for part in send]
        bit *= 2

    grad_in, in_made = total_call(
        total_in_kernel,
        [*sides, *gathered],
        [anywhere] * (m + 2 * n - 1),
        z.in_cols,
        [
            pltpu.VMEM((n, z.all_rows, z.width), BF),
            pltpu.SemaphoreType.DMA((m,)),
            pltpu.SemaphoreType.DMA,
            pltpu.SemaphoreType.DMA((n - 1,)),
            pltpu.SemaphoreType.DMA((n - 1,)),
        ],
        "in_grads",
    )
    keep, got = keep[0], gate(got, [in_made])[0]
    grad_tokens, grad_routes = pl.pallas_call(
        functools.partial(token_kernel, z),
        out_shape=[
            jax.ShapeDtypeStruct((z.tokens, z.width), BF),
            jax.ShapeDtypeStruct((z.top, z.tokens), BF),
        ],
        in_specs=[smem()] + [whole(a.shape) for a in (keep, got, routes, replica, table)],
        out_specs=[whole((z.tokens, z.width)), whole((z.top, z.tokens))],
        grid=(1,),
        compiler_params=params(16),
        name="token_grads",
    )(token_count, keep, got, routes, replica, table)

    return grad_tokens, grad_routes.T, grad_in, grad_down


def solution(mesh):
    return jax.shard_map(
        body,
        mesh=mesh,
        in_specs=(
            P(("groups", "ep"), "sub"),
            P(("groups", "ep"), None),
            P(("groups", "ep"), None),
            P(("groups", "ep"), None),
            P("groups", None),
            P(("groups", "ep")),
            P(("groups", "ep"), None, None, "sub"),
            P(("groups", "ep"), None, None),
            P(("groups", "ep"), None, "sub"),
            P(("groups", "ep"), None, "sub"),
        ),
        out_specs=(
            P(("groups", "ep"), "sub"),
            P(("groups", "ep"), None),
            P("groups", "ep", "sub"),
            P("groups", "ep", "sub"),
        ),
        check_vma=False,
    )
```

```python
import functools
import math

import jax
import jax.numpy as jnp
from jax import lax
from jax.experimental import pallas as pl
from jax.experimental.pallas import tpu as pltpu
from jax.sharding import PartitionSpec as P

BF = jnp.bfloat16
F32 = jnp.float32
PER = 4


def nt(a, b):
    return lax.dot_general(a, b, (((1,), (1,)), ((), ())), preferred_element_type=F32)


def tn(a, b):
    return lax.dot_general(a, b, (((0,), (0,)), ((), ())), preferred_element_type=F32)


def nn(a, b):
    return jnp.dot(a, b, preferred_element_type=F32)


def whole(shape):
    zeros = (0,) * len(shape)
    return pl.BlockSpec(shape, lambda *_: zeros)


def smem():
    return pl.BlockSpec(memory_space=pltpu.SMEM)


def params(mib):
    return pltpu.CompilerParams(
        vmem_limit_bytes=mib * 1024 * 1024, dimension_semantics=("arbitrary",)
    )


class Sizes:
    def __init__(self, grad_out, routes, replica_slot, saved_input, weight_in, weight_down):
        self.ep = lax.axis_size("ep")
        self.sub = lax.axis_size("sub")
        self.tokens, self.width = grad_out.shape
        self.top = routes.shape[1]
        self.experts, self.reps = replica_slot.shape
        self.local = weight_in.shape[0]
        self.slots = self.ep * self.local
        self.cap = saved_input.shape[2]
        self.rows = self.ep * self.cap
        self.hidden = weight_down.shape[1]
        self.pair = weight_in.shape[1]
        self.all_rows = self.local * self.rows
        self.part = self.all_rows // self.sub
        self.block = math.gcd(self.rows, self.part)
        self.sources = self.block // self.cap
        self.blocks = self.all_rows // self.block
        self.part_blocks = self.part // self.block
        self.slot_blocks = self.rows // self.block
        self.in_cols = self.pair // self.ep
        self.down_cols = self.hidden // self.ep
        self.cols = self.in_cols + self.down_cols
        self.folds = self.width // self.tokens
        self.tail = 2 * self.slots // self.folds
        self.mark_rows = self.slots // self.folds
        self.mark_tail = -(-self.mark_rows // 16) * 16


def slot_table(z, table_ref, r):
    ids = lax.broadcasted_iota(jnp.int32, (z.slots, z.experts), 0)
    return (table_ref[r : r + 1, :] == ids).astype(F32).astype(BF)


def key_hits(z, count_ref, routes_ref, replica_ref, r, k):
    ids = lax.broadcasted_iota(jnp.int32, (z.experts, z.tokens), 0)
    live = lax.broadcasted_iota(jnp.int32, (1, z.tokens), 1) < count_ref[0]
    key = jnp.where(live & (replica_ref[k : k + 1, :] == r), routes_ref[k : k + 1, :], -1)
    return key == ids


def route_kernel(z, count_ref, grad_ref, weight_ref, routes_ref, replica_ref, table_ref, out_ref):
    weights = weight_ref[...].astype(F32)
    hits = jnp.zeros((z.slots, z.tokens), F32)
    loads = jnp.zeros((z.slots, z.tokens), F32)
    for r in range(z.reps):
        hit = jnp.zeros((z.experts, z.tokens), F32)
        load = jnp.zeros((z.experts, z.tokens), F32)
        for k in range(z.top):
            same = key_hits(z, count_ref, routes_ref, replica_ref, r, k)
            hit = jnp.where(same, 1.0, hit)
            load = jnp.where(same, weights[k : k + 1, :], load)
        table = slot_table(z, table_ref, r)
        hits = hits + nn(table, hit.astype(BF))
        loads = loads + nn(table, load.astype(BF))
    before = lax.broadcasted_iota(jnp.int32, (z.tokens, z.tokens), 0)
    after = lax.broadcasted_iota(jnp.int32, (z.tokens, z.tokens), 1)
    earlier = nn(hits.astype(BF), (before < after).astype(F32).astype(BF))
    code = jnp.where(hits > 0.5, earlier, -1.0)
    both = jnp.concatenate([code, loads], axis=0).astype(BF)
    out_ref[: z.tokens, :] = grad_ref[...]
    for b in range(z.folds):
        out_ref[z.tokens :, b * z.tokens : (b + 1) * z.tokens] = both[
            b * z.tail : (b + 1) * z.tail, :
        ]


def block_place(z, block):
    slot = block // z.slot_blocks
    first = (block % z.slot_blocks) * z.sources
    return slot, first


def block_picks(z, codes_ref, slot, first):
    rows = lax.broadcasted_iota(jnp.int32, (z.cap, z.tokens), 0).astype(F32)
    for a in range(z.sources):
        code = codes_ref[first + a, pl.ds(slot, 1), :]
        yield a, rows == code


def block_scale(z, codes_ref, slot, first):
    parts = []
    for a, pick in block_picks(z, codes_ref, slot, first):
        load = codes_ref[first + a, pl.ds(z.slots + slot, 1), :]
        parts.append(jnp.sum(jnp.where(pick, load, 0.0), axis=1, keepdims=True))
    return jnp.concatenate(parts, axis=0)


def local_picks(z, codes_ref, source, me):
    code = codes_ref[source, pl.ds(pl.multiple_of(me * z.local, z.local), z.local), :]
    rows = lax.broadcasted_iota(jnp.int32, (z.local, z.cap, z.tokens), 1).astype(F32)
    pick = (code[:, None, :] == rows).astype(F32)
    return pick.reshape(z.local * z.cap, z.tokens).astype(BF)


def block_slot(z, mine, step):
    place = step // z.part_blocks
    return ((place ^ mine) * z.part_blocks + step % z.part_blocks) // z.slot_blocks


def weight_copy(weight_ref, held, sems, slot):
    return pltpu.make_async_copy(weight_ref.at[slot], held.at[slot], sems.at[slot])


def down_kernel(z, ids_ref, *refs):
    bufs = refs[: z.ep]
    weight_ref = refs[z.ep]
    parts = refs[z.ep + 2 : z.ep + 4]
    grads_ref, codes_ref, rows_ref, held, sems = refs[z.ep + 4 :]
    me, mine = ids_ref[0], ids_ref[1]
    step = pl.program_id(0)

    @pl.when(step == 0)
    def _():
        for s in range(z.local):
            weight_copy(weight_ref, held, sems, s).start()
        for k in range(z.ep):
            source = me ^ k
            grads_ref[source] = bufs[k][: z.tokens, :]
            for b in range(z.folds):
                codes_ref[source, b * z.tail : (b + 1) * z.tail, :] = bufs[k][
                    z.tokens :, b * z.tokens : (b + 1) * z.tokens
                ].astype(F32)
        for p in range(z.ep):
            rows = nn(local_picks(z, codes_ref, p, me), grads_ref[p]).astype(BF)
            rows_ref[:, p * z.cap : (p + 1) * z.cap, :] = rows.reshape(z.local, z.cap, z.width)

    place = step // z.part_blocks
    block = (place ^ mine) * z.part_blocks + step % z.part_blocks
    slot, first = block_place(z, block)
    start = pl.multiple_of(first * z.cap, z.block)

    @pl.when((step == 0) | (slot != block_slot(z, mine, step - 1)))
    def _():
        weight_copy(weight_ref, held, sems, slot).wait()

    partial = nt(rows_ref[slot, pl.ds(start, z.block), :], held[slot]).astype(BF)
    spot = pl.multiple_of((step % z.part_blocks) * z.block, z.block)
    for k in range(z.sub):

        @pl.when(place == k)
        def _():
            parts[k % 2][k // 2, pl.ds(spot, z.block), :] = partial


def gate_terms(z, pair, grad, scale):
    gate = pair[:, : z.hidden].astype(F32)
    up = pair[:, z.hidden :].astype(F32)
    sig = 1.0 / (1.0 + jnp.exp(-gate))
    act = gate * sig
    hidden = act * up
    scaled = scale * grad
    grad_gate = scaled * up * sig * (1.0 + gate * (1.0 - sig))
    grad_up = scaled * act
    return hidden, grad_gate.astype(BF), grad_up.astype(BF)


def pre_kernel(z, ids_ref, keep_ref, got_ref, pair_ref, codes_ref, *refs):
    outs, (grad_ref, sides) = refs[: z.ep], refs[z.ep :]
    me = ids_ref[0]
    block = ids_ref[1] * z.part_blocks + pl.program_id(0)
    slot, first = block_place(z, block)
    scale = block_scale(z, codes_ref, me * z.local + slot, first)
    grad = keep_ref[0].astype(F32) + got_ref[0].astype(F32)
    grad_ref[...] = grad.astype(BF)
    _, grad_gate, grad_up = gate_terms(z, pair_ref[...], grad, scale)
    send_columns(z, me, jnp.concatenate([grad_gate.T, grad_up.T], axis=0), sides, outs)


def send_columns(z, me, columns, sides, outs):
    size = columns.shape[0] // z.ep
    for q in range(z.ep):
        sides[q] = columns[q * size : (q + 1) * size, :]
    for k in range(z.ep):
        outs[k][...] = sides[me ^ k]


def hidden_kernel(z, ids_ref, pair_ref, after_ref, other_ref, *refs):
    pair = pair_ref[...]
    gate_pre = pair[:, : z.hidden].astype(F32)
    up = pair[:, z.hidden :].astype(F32)
    hidden = gate_pre * (1.0 / (1.0 + jnp.exp(-gate_pre))) * up
    send_columns(z, ids_ref[0], hidden.astype(BF).T, refs[-1], refs[:-1])


def stack_kernel(z, *refs):
    for k in range(z.ep):
        refs[-1][k] = refs[k][...]


def row_kernel(z, ids_ref, *refs):
    grads = refs[: z.sub]
    pair_ref, weight_ref, codes_ref = refs[z.sub : z.sub + 3]
    outs = refs[z.sub + 3 : z.sub + 3 + z.ep]
    rows_ref, marks, held, weights, sems = refs[z.sub + 3 + z.ep :]
    me, mine = ids_ref[0], ids_ref[1]
    step = pl.program_id(0)
    place = step // z.part_blocks
    block = (place ^ mine) * z.part_blocks + step % z.part_blocks
    slot, first = block_place(z, block)

    @pl.when(step == 0)
    def _():
        for s in range(z.local):
            weight_copy(weight_ref, weights, sems, s).start()
        marks[...] = jnp.zeros_like(marks)

    spot = pl.multiple_of((step % z.part_blocks) * z.block, z.block)
    for k in range(z.sub):

        @pl.when(place == k)
        def _():
            held[...] = grads[k][pl.ds(spot, z.block), :]

    grad = held[...].astype(F32)
    scale = block_scale(z, codes_ref, me * z.local + slot, first)
    hidden, grad_gate, grad_up = gate_terms(z, pair_ref[...], grad, scale)
    route = jnp.sum(hidden * grad, axis=1, keepdims=True).astype(BF).astype(F32)

    @pl.when((step == 0) | (slot != block_slot(z, mine, step - 1)))
    def _():
        weight_copy(weight_ref, weights, sems, slot).wait()

    rows = nn(grad_gate, weights[slot, : z.hidden, :]) + nn(grad_up, weights[slot, z.hidden :, :])
    start = pl.multiple_of(first * z.cap, z.block)
    rows_ref[slot, pl.ds(start, z.block), :] = rows.astype(BF)
    for a, pick in block_picks(z, codes_ref, me * z.local + slot, first):
        marks[first + a, pl.ds(me * z.local + slot, 1), :] = jnp.sum(
            jnp.where(pick, route[a * z.cap : (a + 1) * z.cap, :], 0.0), axis=0, keepdims=True
        )

    @pl.when(step == z.blocks - 1)
    def _():
        spare = z.mark_tail - z.mark_rows
        blank = jnp.zeros((spare, z.tokens), F32) if spare else None
        for k in range(z.ep):
            source = me ^ k
            start = pl.multiple_of(source * z.cap, z.cap)
            rows = rows_ref[:, pl.ds(start, z.cap), :].reshape(z.local * z.cap, z.width)
            picks = local_picks(z, codes_ref, source, me)
            outs[k][: z.tokens, :] = tn(picks, rows).astype(BF)
            for f in range(z.folds):
                part = marks[source, f * z.mark_rows : (f + 1) * z.mark_rows, :]
                part = jnp.concatenate([part, blank], axis=0) if spare else part
                outs[k][z.tokens :, f * z.tokens : (f + 1) * z.tokens] = part.astype(BF)


def sum_kernel(*refs):
    count = len(refs) // 3
    for i in range(count):
        total = refs[i][...].astype(F32) + refs[count + i][...].astype(F32)
        refs[2 * count + i][...] = total.astype(BF)


def halve_kernel(keep_ref, got_ref, out_keep, out_send):
    for i in range(out_keep.shape[0]):
        for j, out in enumerate((out_keep, out_send)):
            total = keep_ref[2 * i + j].astype(F32) + got_ref[2 * i + j].astype(F32)
            out[i] = total.astype(BF)


def token_kernel(z, count_ref, *refs):
    keep_ref, got_ref, routes_ref, replica_ref, table_ref, tokens_ref, route_ref = refs
    total = keep_ref[...].astype(F32) + got_ref[...].astype(F32)
    tokens_ref[...] = total[: z.tokens, :].astype(BF)
    rows = [
        total[z.tokens : z.tokens + z.mark_rows, f * z.tokens : (f + 1) * z.tokens]
        for f in range(z.folds)
    ]
    rows = jnp.concatenate(rows, axis=0).astype(BF)
    totals = [jnp.zeros((1, z.tokens), F32)] * z.top
    for r in range(z.reps):
        spread = tn(slot_table(z, table_ref, r), rows)
        for k in range(z.top):
            same = key_hits(z, count_ref, routes_ref, replica_ref, r, k)
            totals[k] += jnp.sum(jnp.where(same, spread, 0.0), axis=0, keepdims=True)
    route_ref[...] = jnp.concatenate(totals, axis=0).astype(BF)


def input_moves(z, me, own_ref, rights, lefts, inputs_ref, own_sem, right_sems, left_sems, act):
    act(pltpu.make_async_copy(own_ref, inputs_ref.at[me], own_sem))
    for d in range(1, z.ep):

        @pl.when(me >= d)
        def _():
            act(
                pltpu.make_async_copy(
                    rights[d - 1], inputs_ref.at[me - d], right_sems.at[d - 1]
                )
            )

        @pl.when(me + d < z.ep)
        def _():
            act(
                pltpu.make_async_copy(
                    lefts[d - 1], inputs_ref.at[me + d], left_sems.at[d - 1]
                )
            )


def left_rows(held, part, side, spot, size):
    return held[part, side, :, pl.ds(spot, size)]


def expert_products(z, ids_ref, table_ref, turn, held, right_rows, out_ref, made, out_sems):
    mine = ids_ref[1]

    def out_copy(expert):
        return pltpu.make_async_copy(made.at[expert], out_ref.at[expert], out_sems.at[expert])

    def some(step, carry):
        for i in range(PER):
            expert = step * PER + i
            first = table_ref[0, expert]
            left, right = [], []
            for r in range(z.reps):
                slot_id = table_ref[r, expert]
                source = slot_id // z.local
                for b in range(z.slot_blocks):
                    block = (slot_id % z.local) * z.slot_blocks + b
                    part = (block // z.part_blocks) ^ mine
                    spot = pl.multiple_of((block % z.part_blocks) * z.block, z.block)
                    side = source ^ turn
                    if r:
                        side = jnp.where(slot_id == first, z.ep, side)
                    left.append(functools.partial(left_rows, held, part, side, spot, z.block))
                    right.append(functools.partial(right_rows, slot_id, block, b))
            half = len(left) // 2

            def product(lo, hi):
                return nn(
                    jnp.concatenate([f() for f in left[lo:hi]], axis=1),
                    jnp.concatenate([f() for f in right[lo:hi]], axis=0),
                )

            few = table_ref[z.reps // 2, expert] == first

            @pl.when(few)
            def _():
                made[expert] = product(0, half).astype(BF)

            @pl.when(jnp.logical_not(few))
            def _():
                made[expert] = product(0, 2 * half).astype(BF)

            out_copy(expert).start()
        return carry

    lax.fori_loop(0, z.experts // PER, some, 0)
    for expert in range(z.experts):
        out_copy(expert).wait()


def total_down_kernel(z, ids_ref, table_ref, *refs):
    sides = refs[: z.sub]
    grads_ref, codes_ref, out_ref, token_ref, held, made, out_sems, scaled, sems = refs[z.sub :]
    token_ref[...] = jnp.zeros_like(token_ref)

    def moves(act):
        for k in range(z.sub):
            act(
                pltpu.make_async_copy(
                    sides[k], held.at[k, pl.ds(0, z.ep)], sems.at[k]
                )
            )

    moves(lambda copy: copy.start())
    held[:, z.ep] = jnp.zeros_like(held[:, z.ep])
    rows = lax.broadcasted_iota(jnp.int32, (z.slots, z.cap, z.tokens), 1).astype(F32)
    for p in range(z.ep):
        code = codes_ref[p, : z.slots, :][:, None, :]
        load = codes_ref[p, z.slots :, :][:, None, :]
        pick = jnp.where(rows == code, load, 0.0).reshape(z.slots * z.cap, z.tokens)
        result = nn(pick.astype(BF), grads_ref[p]).astype(BF)
        scaled[:, p * z.cap : (p + 1) * z.cap, :] = result.reshape(z.slots, z.cap, z.width)
    moves(lambda copy: copy.wait())

    def right_rows(slot_id, block, b):
        return scaled[slot_id, b * z.block : (b + 1) * z.block, :]

    expert_products(z, ids_ref, table_ref, ids_ref[0], held, right_rows, out_ref, made, out_sems)


def total_in_kernel(z, ids_ref, table_ref, *refs):
    sides, refs = refs[: z.sub], refs[z.sub :]
    own_ref, rights, lefts = refs[0], refs[1 : z.ep], refs[z.ep : 2 * z.ep - 1]
    out_ref, token_ref, held, made, out_sems, inputs_ref, sems, *other_sems = refs[2 * z.ep - 1 :]
    token_ref[...] = jnp.zeros_like(token_ref)

    def moves(act):
        for k in range(z.sub):
            act(pltpu.make_async_copy(sides[k], held.at[k, pl.ds(0, z.ep)], sems.at[k]))
        input_moves(z, ids_ref[0], own_ref, rights, lefts, inputs_ref, *other_sems, act)

    moves(lambda copy: copy.start())
    held[:, z.ep] = jnp.zeros_like(held[:, z.ep])
    moves(lambda copy: copy.wait())

    def right_rows(slot_id, block, b):
        start = pl.multiple_of(block * z.block, z.block)
        return inputs_ref[slot_id // z.local, pl.ds(start, z.block), :]

    expert_products(z, ids_ref, table_ref, ids_ref[0], held, right_rows, out_ref, made, out_sems)


def swap(x, axis, size, bit):
    return lax.ppermute(x, axis, [(i, i ^ bit) for i in range(size)])


def spread_over(have, axis, size, bit):
    have = dict(have)
    while bit:
        for k in list(have):
            if k | bit not in have:
                have[k | bit] = swap(have[k], axis, size, bit)
        bit //= 2
    return [have[k] for k in range(size)]


def nothing(*refs):
    pass


def gate(values, after):
    anywhere = pl.BlockSpec(memory_space=pl.ANY)
    return pl.pallas_call(
        nothing,
        in_specs=[anywhere] * (len(values) + len(after)),
        out_specs=[anywhere] * len(values),
        out_shape=[jax.ShapeDtypeStruct(v.shape, v.dtype) for v in values],
        input_output_aliases={i: i for i in range(len(values))},
        compiler_params=pltpu.CompilerParams(vmem_limit_bytes=1024 * 1024),
        name="gate",
    )(*values, *after)


def pick_kernel(first, ids_ref, go_ref, back_ref, out_ref, sem):
    for condition, ref in ((ids_ref[0] >= first, go_ref), (ids_ref[0] < first, back_ref)):

        @pl.when(condition)
        def _():
            copy = pltpu.make_async_copy(ref, out_ref, sem)
            copy.start()
            copy.wait()


def pick(ids, go, back, first):
    anywhere = pl.BlockSpec(memory_space=pl.ANY)
    return pl.pallas_call(
        functools.partial(pick_kernel, first),
        in_specs=[smem(), anywhere, anywhere],
        out_specs=anywhere,
        out_shape=jax.ShapeDtypeStruct(go.shape, go.dtype),
        scratch_shapes=[pltpu.SemaphoreType.DMA],
        compiler_params=pltpu.CompilerParams(vmem_limit_bytes=1024 * 1024),
        name="pick",
    )(ids, go, back)


def chain_step(go, back, axis, size, d):
    rights = [(i, i + 1) for i in range(d - 1, size - 1)]
    lefts = [(i, i - 1) for i in range(size - d, 0, -1)]
    if d > 1 and go is back:
        got = lax.ppermute(go, axis, rights + lefts)
        return got, got
    return lax.ppermute(go, axis, rights), lax.ppermute(back, axis, lefts)


def body(
    grad_out,
    route_weight,
    routes,
    replica,
    replica_slot,
    token_count,
    saved_input,
    saved_gate_up,
    weight_in,
    weight_down,
):
    z = Sizes(grad_out, routes, replica_slot, saved_input, weight_in, weight_down)
    n, m = z.ep, z.sub
    ids = jnp.stack([lax.axis_index("ep"), lax.axis_index("sub")]).astype(jnp.int32)
    routes, replica, table = routes.T, replica.T, replica_slot.T
    route_weight = route_weight.T
    pair_rows = saved_gate_up.reshape(z.all_rows, z.pair)
    grad_shape = (z.tokens + z.tail, z.width)
    code_shape = (n, 2 * z.slots, z.tokens)
    inputs = saved_input.reshape(z.all_rows, z.width)

    routing = (grad_out, route_weight, routes, replica, table)
    buf = pl.pallas_call(
        functools.partial(route_kernel, z),
        out_shape=jax.ShapeDtypeStruct(grad_shape, BF),
        in_specs=[smem()] + [whole(a.shape) for a in routing],
        out_specs=whole(grad_shape),
        grid=(1,),
        compiler_params=params(60),
        name="route",
    )(token_count, *routing)
    bufs = [buf] + [swap(buf, "ep", n, k) for k in range(1, n)]

    chain = gate([inputs], [buf])
    downs = pl.pallas_call(
        functools.partial(hidden_kernel, z),
        grid_spec=pltpu.PrefetchScalarGridSpec(
            num_scalar_prefetch=1,
            grid=(z.part_blocks,),
            in_specs=[
                pl.BlockSpec((z.block, z.pair), lambda i, r: (r[1] * z.part_blocks + i, 0)),
                pl.BlockSpec(memory_space=pl.ANY),
                pl.BlockSpec(memory_space=pl.ANY),
            ],
            out_specs=[pl.BlockSpec((z.down_cols, z.block), lambda i, r: (0, i))] * n,
            scratch_shapes=[pltpu.VMEM((n, z.down_cols, z.block), BF)],
        ),
        out_shape=[jax.ShapeDtypeStruct((z.down_cols, z.part), BF)] * n,
        compiler_params=params(16),
        name="hidden_columns",
    )(ids, pair_rows, bufs[1], chain[0])
    downs = [downs[0]] + [swap(downs[k], "ep", n, k) for k in range(1, n)]
    chain = gate(chain, bufs[1:] + downs[1:])
    steps = [list(chain_step(chain[0], chain[0], "ep", n, 1))]

    def stack(pieces):
        shape = pieces[0].shape
        return pl.pallas_call(
            functools.partial(stack_kernel, z),
            in_specs=[whole(shape)] * n,
            out_specs=whole((n,) + shape),
            out_shape=jax.ShapeDtypeStruct((n,) + shape, BF),
            grid=(1,),
            compiler_params=params(12),
            name="stack_columns",
        )(*pieces)

    def halve(keep, got):
        half = (keep.shape[0] // 2,) + keep.shape[1:]
        return pl.pallas_call(
            halve_kernel,
            in_specs=[whole(keep.shape)] * 2,
            out_specs=[whole(half)] * 2,
            out_shape=[jax.ShapeDtypeStruct(half, BF)] * 2,
            grid=(1,),
            compiler_params=params(16),
            name="halve",
        )(keep, got)

    def row_block(i, ids_ref):
        place = i // z.part_blocks
        return (place ^ ids_ref[1]) * z.part_blocks + i % z.part_blocks

    part_shape = (m // 2, z.part, z.hidden)
    outs = pl.pallas_call(
        functools.partial(down_kernel, z),
        grid_spec=pltpu.PrefetchScalarGridSpec(
            num_scalar_prefetch=1,
            grid=(z.blocks,),
            in_specs=[whole(grad_shape)] * n
            + [pl.BlockSpec(memory_space=pltpu.HBM), pl.BlockSpec(memory_space=pl.ANY)],
            out_specs=[whole(part_shape)] * 2
            + [whole((n, z.tokens, z.width)), whole(code_shape)],
            scratch_shapes=[
                pltpu.VMEM((z.local, z.rows, z.width), BF),
                pltpu.VMEM((z.local, z.hidden, z.width), BF),
                pltpu.SemaphoreType.DMA((z.local,)),
            ],
        ),
        out_shape=[jax.ShapeDtypeStruct(part_shape, BF)] * 2
        + [
            jax.ShapeDtypeStruct((n, z.tokens, z.width), BF),
            jax.ShapeDtypeStruct(code_shape, F32),
        ],
        compiler_params=params(48),
        name="hidden_partials",
    )(ids, *bufs, weight_down, *downs[:1])
    keep, send, grads_all, codes = outs
    down_sides = spread_over({0: stack(downs)}, "sub", m, m // 2)
    def total_call(kernel, operands, specs, cols, scratch, name):
        return pl.pallas_call(
            functools.partial(kernel, z),
            grid_spec=pltpu.PrefetchScalarGridSpec(
                num_scalar_prefetch=2,
                grid=(1,),
                in_specs=specs,
                out_specs=[pl.BlockSpec(memory_space=pl.ANY), whole((8, 128))],
                scratch_shapes=[
                    pltpu.VMEM((m, n + 1, cols, z.part), BF),
                    pltpu.VMEM((z.experts, cols, z.width), BF),
                    pltpu.SemaphoreType.DMA((z.experts,)),
                ]
                + scratch,
            ),
            out_shape=[
                jax.ShapeDtypeStruct((z.experts, cols, z.width), BF),
                jax.ShapeDtypeStruct((8, 128), F32),
            ],
            compiler_params=params(32),
            name=name,
        )(ids, table, *operands)

    anywhere = pl.BlockSpec(memory_space=pl.ANY)
    grad_down, down_made = total_call(
        total_down_kernel,
        [*down_sides, grads_all, codes],
        [anywhere] * m + [whole((n, z.tokens, z.width)), whole(code_shape)],
        z.down_cols,
        [pltpu.VMEM((z.slots, z.rows, z.width), BF), pltpu.SemaphoreType.DMA((m,))],
        "down_grads",
    )
    steps.append(chain_step(*steps[0], "ep", n, 2))
    got = swap(send, "sub", m, 1)
    after = list(steps[0])
    bit = 2
    while bit < m:
        keep, send = halve(keep, got)
        send = gate([send], after)[0]
        got = swap(send, "sub", m, bit)
        bit *= 2

    got = gate([got], [down_made])[0]
    *pieces, grad_part = pl.pallas_call(
        functools.partial(pre_kernel, z),
        grid_spec=pltpu.PrefetchScalarGridSpec(
            num_scalar_prefetch=1,
            grid=(z.part_blocks,),
            in_specs=[pl.BlockSpec((1, z.block, z.hidden), lambda i, r: (0, i, 0))] * 2
            + [
                pl.BlockSpec((z.block, z.pair), lambda i, r: (r[1] * z.part_blocks + i, 0)),
                whole(code_shape),
            ],
            out_specs=[pl.BlockSpec((z.in_cols, z.block), lambda i, r: (0, i))] * n
            + [pl.BlockSpec((z.block, z.hidden), lambda i, r: (i, 0))],
            scratch_shapes=[pltpu.VMEM((n, z.in_cols, z.block), BF)],
        ),
        out_shape=[jax.ShapeDtypeStruct((z.in_cols, z.part), BF)] * n
        + [jax.ShapeDtypeStruct((z.part, z.hidden), BF)],
        compiler_params=params(16),
        name="pre_grads",
    )(ids, keep, got, pair_rows, codes)
    late = gate(pieces[1:], steps[1])
    pieces = pieces[:1] + [swap(a, "ep", n, k) for k, a in enumerate(late, 1)]
    grad_parts = spread_over({0: grad_part}, "sub", m, m // 2)

    back_shape = (z.tokens + z.mark_tail, z.width)
    parts = pl.pallas_call(
        functools.partial(row_kernel, z),
        grid_spec=pltpu.PrefetchScalarGridSpec(
            num_scalar_prefetch=1,
            grid=(z.blocks,),
            in_specs=[whole((z.part, z.hidden))] * m
            + [
                pl.BlockSpec((z.block, z.pair), lambda i, r: (row_block(i, r), 0)),
                pl.BlockSpec(memory_space=pltpu.HBM),
                whole(code_shape),
            ],
            out_specs=[whole(back_shape)] * n,
            scratch_shapes=[
                pltpu.VMEM((z.local, z.rows, z.width), BF),
                pltpu.VMEM((n, z.slots, z.tokens), F32),
                pltpu.VMEM((z.block, z.hidden), BF),
                pltpu.VMEM((z.local, z.pair, z.width), BF),
                pltpu.SemaphoreType.DMA((z.local,)),
            ],
        ),
        out_shape=[jax.ShapeDtypeStruct(back_shape, BF)] * n,
        compiler_params=params(46),
        name="row_grads",
    )(ids, *grad_parts, pair_rows, weight_in, codes)
    steps[1] = go, back = gate(steps[1], pieces[1:])
    picked = []
    for d in range(3, n):
        if 2 * d > n + 1 and go is not back:
            go = back = pick(ids, go, back, d - 1)
            picked.append(go)
        go, back = chain_step(go, back, "ep", n, d)
        steps.append((go, back))
    gathered = [inputs] + [go for go, _ in steps] + [back for _, back in steps]
    got = [swap(part, "ep", n, 1) for part in parts[1::2]]
    pieces[:1] = gate(pieces[:1], [*got, *picked])
    sides = spread_over({0: stack(pieces)}, "sub", m, m // 2)
    keep, bit = parts[::2], 2
    while bit < n:
        count = len(keep)
        parts = pl.pallas_call(
            sum_kernel,
            in_specs=[whole(back_shape)] * 2 * count,
            out_specs=[whole(back_shape)] * count,
            out_shape=[jax.ShapeDtypeStruct(back_shape, BF)] * count,
            grid=(1,),
            compiler_params=params(16),
            name="sum_parts",
        )(*keep, *got)
        keep = parts[::2]
        send = gate(parts[1::2], sides[1:])
        got = [swap(part, "ep", n, bit) for part in send]
        bit *= 2

    grad_in, in_made = total_call(
        total_in_kernel,
        [*sides, *gathered],
        [anywhere] * (m + 2 * n - 1),
        z.in_cols,
        [
            pltpu.VMEM((n, z.all_rows, z.width), BF),
            pltpu.SemaphoreType.DMA((m,)),
            pltpu.SemaphoreType.DMA,
            pltpu.SemaphoreType.DMA((n - 1,)),
            pltpu.SemaphoreType.DMA((n - 1,)),
        ],
        "in_grads",
    )
    keep, got = keep[0], gate(got, [in_made])[0]
    grad_tokens, grad_routes = pl.pallas_call(
        functools.partial(token_kernel, z),
        out_shape=[
            jax.ShapeDtypeStruct((z.tokens, z.width), BF),
            jax.ShapeDtypeStruct((z.top, z.tokens), BF),
        ],
        in_specs=[smem()] + [whole(a.shape) for a in (keep, got, routes, replica, table)],
        out_specs=[whole((z.tokens, z.width)), whole((z.top, z.tokens))],
        grid=(1,),
        compiler_params=params(16),
        name="token_grads",
    )(token_count, keep, got, routes, replica, table)

    return grad_tokens, grad_routes.T, grad_in, grad_down


def solution(mesh):
    return jax.shard_map(
        body,
        mesh=mesh,
        in_specs=(
            P(("groups", "ep"), "sub"),
            P(("groups", "ep"), None),
            P(("groups", "ep"), None),
            P(("groups", "ep"), None),
            P("groups", None),
            P(("groups", "ep")),
            P(("groups", "ep"), None, None, "sub"),
            P(("groups", "ep"), None, None),
            P(("groups", "ep"), None, "sub"),
            P(("groups", "ep"), None, "sub"),
        ),
        out_specs=(
            P(("groups", "ep"), "sub"),
            P(("groups", "ep"), None),
            P("groups", "ep", "sub"),
            P("groups", "ep", "sub"),
        ),
        check_vma=False,
    )
```

```python
import functools
import math

import jax
import jax.numpy as jnp
from jax import lax
from jax.experimental import pallas as pl
from jax.experimental.pallas import tpu as pltpu
from jax.sharding import PartitionSpec as P

BF = jnp.bfloat16
F32 = jnp.float32
PER = 2


def nt(a, b):
    return lax.dot_general(a, b, (((1,), (1,)), ((), ())), preferred_element_type=F32)


def tn(a, b):
    return lax.dot_general(a, b, (((0,), (0,)), ((), ())), preferred_element_type=F32)


def nn(a, b):
    return jnp.dot(a, b, preferred_element_type=F32)


def whole(shape):
    zeros = (0,) * len(shape)
    return pl.BlockSpec(shape, lambda *_: zeros)


def smem():
    return pl.BlockSpec(memory_space=pltpu.SMEM)


def params(mib):
    return pltpu.CompilerParams(
        vmem_limit_bytes=mib * 1024 * 1024, dimension_semantics=("arbitrary",)
    )


class Sizes:
    def __init__(self, grad_out, routes, replica_slot, saved_input, weight_in, weight_down):
        self.ep = lax.axis_size("ep")
        self.sub = lax.axis_size("sub")
        self.tokens, self.width = grad_out.shape
        self.top = routes.shape[1]
        self.experts, self.reps = replica_slot.shape
        self.local = weight_in.shape[0]
        self.slots = self.ep * self.local
        self.cap = saved_input.shape[2]
        self.rows = self.ep * self.cap
        self.hidden = weight_down.shape[1]
        self.pair = weight_in.shape[1]
        self.all_rows = self.local * self.rows
        self.part = self.all_rows // self.sub
        self.block = math.gcd(self.rows, self.part)
        self.sources = self.block // self.cap
        self.blocks = self.all_rows // self.block
        self.part_blocks = self.part // self.block
        self.slot_blocks = self.rows // self.block
        self.in_cols = self.pair // self.ep
        self.down_cols = self.hidden // self.ep
        self.cols = self.in_cols + self.down_cols
        self.folds = self.width // self.tokens
        self.tail = 2 * self.slots // self.folds


def slot_table(z, table_ref, r):
    ids = lax.broadcasted_iota(jnp.int32, (z.slots, z.experts), 0)
    return (table_ref[r : r + 1, :] == ids).astype(F32).astype(BF)


def key_hits(z, count_ref, routes_ref, replica_ref, r, k):
    ids = lax.broadcasted_iota(jnp.int32, (z.experts, z.tokens), 0)
    live = lax.broadcasted_iota(jnp.int32, (1, z.tokens), 1) < count_ref[0]
    key = jnp.where(live & (replica_ref[k : k + 1, :] == r), routes_ref[k : k + 1, :], -1)
    return key == ids


def route_kernel(z, count_ref, grad_ref, weight_ref, routes_ref, replica_ref, table_ref, out_ref):
    weights = weight_ref[...].astype(F32)
    hits = jnp.zeros((z.slots, z.tokens), F32)
    loads = jnp.zeros((z.slots, z.tokens), F32)
    for r in range(z.reps):
        hit = jnp.zeros((z.experts, z.tokens), F32)
        load = jnp.zeros((z.experts, z.tokens), F32)
        for k in range(z.top):
            same = key_hits(z, count_ref, routes_ref, replica_ref, r, k)
            hit = jnp.where(same, 1.0, hit)
            load = jnp.where(same, weights[k : k + 1, :], load)
        table = slot_table(z, table_ref, r)
        hits = hits + nn(table, hit.astype(BF))
        loads = loads + nn(table, load.astype(BF))
    before = lax.broadcasted_iota(jnp.int32, (z.tokens, z.tokens), 0)
    after = lax.broadcasted_iota(jnp.int32, (z.tokens, z.tokens), 1)
    earlier = nn(hits.astype(BF), (before < after).astype(F32).astype(BF))
    code = jnp.where(hits > 0.5, earlier, -1.0)
    both = jnp.concatenate([code, loads], axis=0).astype(BF)
    out_ref[: z.tokens, :] = grad_ref[...]
    for b in range(z.folds):
        out_ref[z.tokens :, b * z.tokens : (b + 1) * z.tokens] = both[
            b * z.tail : (b + 1) * z.tail, :
        ]


def block_place(z, block):
    slot = block // z.slot_blocks
    first = (block % z.slot_blocks) * z.sources
    return slot, first


def block_picks(z, codes_ref, slot, first):
    rows = lax.broadcasted_iota(jnp.int32, (z.cap, z.tokens), 0).astype(F32)
    for a in range(z.sources):
        code = codes_ref[first + a, pl.ds(slot, 1), :]
        yield a, rows == code


def block_scale(z, codes_ref, slot, first):
    parts = []
    for a, pick in block_picks(z, codes_ref, slot, first):
        load = codes_ref[first + a, pl.ds(z.slots + slot, 1), :]
        parts.append(jnp.sum(jnp.where(pick, load, 0.0), axis=1, keepdims=True))
    return jnp.concatenate(parts, axis=0)


def local_picks(z, codes_ref, source, me):
    code = codes_ref[source, pl.ds(pl.multiple_of(me * z.local, z.local), z.local), :]
    rows = lax.broadcasted_iota(jnp.int32, (z.local, z.cap, z.tokens), 1).astype(F32)
    pick = (code[:, None, :] == rows).astype(F32)
    return pick.reshape(z.local * z.cap, z.tokens).astype(BF)


def block_slot(z, mine, step):
    place = step // z.part_blocks
    return ((place ^ mine) * z.part_blocks + step % z.part_blocks) // z.slot_blocks


def weight_copy(weight_ref, held, sems, slot):
    return pltpu.make_async_copy(weight_ref.at[slot], held.at[slot], sems.at[slot])


def down_kernel(z, ids_ref, *refs):
    bufs = refs[: z.ep]
    weight_ref = refs[z.ep]
    parts = refs[z.ep + 2 : z.ep + 4]
    grads_ref, codes_ref, rows_ref, held, sems = refs[z.ep + 4 :]
    me, mine = ids_ref[0], ids_ref[1]
    step = pl.program_id(0)

    @pl.when(step == 0)
    def _():
        for s in range(z.local):
            weight_copy(weight_ref, held, sems, s).start()
        for k in range(z.ep):
            source = me ^ k
            grads_ref[source] = bufs[k][: z.tokens, :]
            for b in range(z.folds):
                codes_ref[source, b * z.tail : (b + 1) * z.tail, :] = bufs[k][
                    z.tokens :, b * z.tokens : (b + 1) * z.tokens
                ].astype(F32)
        for p in range(z.ep):
            rows = nn(local_picks(z, codes_ref, p, me), grads_ref[p]).astype(BF)
            rows_ref[:, p * z.cap : (p + 1) * z.cap, :] = rows.reshape(z.local, z.cap, z.width)

    place = step // z.part_blocks
    block = (place ^ mine) * z.part_blocks + step % z.part_blocks
    slot, first = block_place(z, block)
    start = pl.multiple_of(first * z.cap, z.block)

    @pl.when((step == 0) | (slot != block_slot(z, mine, step - 1)))
    def _():
        weight_copy(weight_ref, held, sems, slot).wait()

    partial = nt(rows_ref[slot, pl.ds(start, z.block), :], held[slot]).astype(BF)
    spot = pl.multiple_of((step % z.part_blocks) * z.block, z.block)
    for k in range(z.sub):

        @pl.when(place == k)
        def _():
            parts[k % 2][k // 2, pl.ds(spot, z.block), :] = partial


def gate_terms(z, pair, grad, scale):
    gate = pair[:, : z.hidden].astype(F32)
    up = pair[:, z.hidden :].astype(F32)
    sig = 1.0 / (1.0 + jnp.exp(-gate))
    act = gate * sig
    hidden = act * up
    scaled = scale * grad
    grad_gate = scaled * up * sig * (1.0 + gate * (1.0 - sig))
    grad_up = scaled * act
    return hidden, grad_gate.astype(BF), grad_up.astype(BF)


def pre_kernel(z, ids_ref, keep_ref, got_ref, pair_ref, codes_ref, *refs):
    outs, (grad_ref, sides) = refs[: z.ep], refs[z.ep :]
    me = ids_ref[0]
    block = ids_ref[1] * z.part_blocks + pl.program_id(0)
    slot, first = block_place(z, block)
    scale = block_scale(z, codes_ref, me * z.local + slot, first)
    grad = keep_ref[0].astype(F32) + got_ref[0].astype(F32)
    grad_ref[...] = grad.astype(BF)
    _, grad_gate, grad_up = gate_terms(z, pair_ref[...], grad, scale)
    send_columns(z, me, jnp.concatenate([grad_gate.T, grad_up.T], axis=0), sides, outs)


def send_columns(z, me, columns, sides, outs):
    size = columns.shape[0] // z.ep
    for q in range(z.ep):
        sides[q] = columns[q * size : (q + 1) * size, :]
    for k in range(z.ep):
        outs[k][...] = sides[me ^ k]


def hidden_kernel(z, ids_ref, pair_ref, after_ref, other_ref, *refs):
    pair = pair_ref[...]
    gate_pre = pair[:, : z.hidden].astype(F32)
    up = pair[:, z.hidden :].astype(F32)
    hidden = gate_pre * (1.0 / (1.0 + jnp.exp(-gate_pre))) * up
    send_columns(z, ids_ref[0], hidden.astype(BF).T, refs[-1], refs[:-1])


def stack_kernel(z, *refs):
    for k in range(z.ep):
        refs[-1][k] = refs[k][...]


def row_kernel(z, ids_ref, *refs):
    grads = refs[: z.sub]
    pair_ref, weight_ref, codes_ref = refs[z.sub : z.sub + 3]
    outs = refs[z.sub + 3 : z.sub + 3 + z.ep]
    rows_ref, marks, held, weights, sems = refs[z.sub + 3 + z.ep :]
    me, mine = ids_ref[0], ids_ref[1]
    step = pl.program_id(0)
    place = step // z.part_blocks
    block = (place ^ mine) * z.part_blocks + step % z.part_blocks
    slot, first = block_place(z, block)

    @pl.when(step == 0)
    def _():
        for s in range(z.local):
            weight_copy(weight_ref, weights, sems, s).start()
        marks[...] = jnp.zeros_like(marks)

    spot = pl.multiple_of((step % z.part_blocks) * z.block, z.block)
    for k in range(z.sub):

        @pl.when(place == k)
        def _():
            held[...] = grads[k][pl.ds(spot, z.block), :]

    grad = held[...].astype(F32)
    scale = block_scale(z, codes_ref, me * z.local + slot, first)
    hidden, grad_gate, grad_up = gate_terms(z, pair_ref[...], grad, scale)
    route = jnp.sum(hidden * grad, axis=1, keepdims=True).astype(BF).astype(F32)

    @pl.when((step == 0) | (slot != block_slot(z, mine, step - 1)))
    def _():
        weight_copy(weight_ref, weights, sems, slot).wait()

    rows = nn(grad_gate, weights[slot, : z.hidden, :]) + nn(grad_up, weights[slot, z.hidden :, :])
    start = pl.multiple_of(first * z.cap, z.block)
    rows_ref[slot, pl.ds(start, z.block), :] = rows.astype(BF)
    for a, pick in block_picks(z, codes_ref, me * z.local + slot, first):
        marks[first + a, pl.ds(me * z.local + slot, 1), :] = jnp.sum(
            jnp.where(pick, route[a * z.cap : (a + 1) * z.cap, :], 0.0), axis=0, keepdims=True
        )

    @pl.when(step == z.blocks - 1)
    def _():
        blank = jnp.zeros((z.slots, z.width - z.tokens), BF)
        for k in range(z.ep):
            source = me ^ k
            start = pl.multiple_of(source * z.cap, z.cap)
            rows = rows_ref[:, pl.ds(start, z.cap), :].reshape(z.local * z.cap, z.width)
            picks = local_picks(z, codes_ref, source, me)
            outs[k][: z.tokens, :] = tn(picks, rows).astype(BF)
            outs[k][z.tokens :, : z.tokens] = marks[source].astype(BF)
            outs[k][z.tokens :, z.tokens :] = blank


def sum_kernel(*refs):
    count = len(refs) // 3
    for i in range(count):
        total = refs[i][...].astype(F32) + refs[count + i][...].astype(F32)
        refs[2 * count + i][...] = total.astype(BF)


def halve_kernel(keep_ref, got_ref, out_keep, out_send):
    for i in range(out_keep.shape[0]):
        for j, out in enumerate((out_keep, out_send)):
            total = keep_ref[2 * i + j].astype(F32) + got_ref[2 * i + j].astype(F32)
            out[i] = total.astype(BF)


def token_kernel(z, count_ref, *refs):
    keep_ref, got_ref, routes_ref, replica_ref, table_ref, tokens_ref, route_ref = refs
    total = keep_ref[...].astype(F32) + got_ref[...].astype(F32)
    tokens_ref[...] = total[: z.tokens, :].astype(BF)
    rows = total[z.tokens :, : z.tokens].astype(BF)
    totals = [jnp.zeros((1, z.tokens), F32)] * z.top
    for r in range(z.reps):
        spread = tn(slot_table(z, table_ref, r), rows)
        for k in range(z.top):
            same = key_hits(z, count_ref, routes_ref, replica_ref, r, k)
            totals[k] += jnp.sum(jnp.where(same, spread, 0.0), axis=0, keepdims=True)
    route_ref[...] = jnp.concatenate(totals, axis=0).astype(BF)


def input_moves(z, me, own_ref, rights, lefts, inputs_ref, own_sem, right_sems, left_sems, act):
    act(pltpu.make_async_copy(own_ref, inputs_ref.at[me], own_sem))
    for d in range(1, z.ep):

        @pl.when(me >= d)
        def _():
            act(
                pltpu.make_async_copy(
                    rights[d - 1], inputs_ref.at[me - d], right_sems.at[d - 1]
                )
            )

        @pl.when(me + d < z.ep)
        def _():
            act(
                pltpu.make_async_copy(
                    lefts[d - 1], inputs_ref.at[me + d], left_sems.at[d - 1]
                )
            )


def left_rows(held, part, side, spot, size):
    return held[part, side, :, pl.ds(spot, size)]


def expert_products(z, ids_ref, table_ref, turn, held, right_rows, out_ref, made, out_sems):
    mine = ids_ref[1]

    def out_copy(expert):
        return pltpu.make_async_copy(made.at[expert], out_ref.at[expert], out_sems.at[expert])

    def some(step, carry):
        for i in range(PER):
            expert = step * PER + i
            first = table_ref[0, expert]
            left, right = [], []
            for r in range(z.reps):
                slot_id = table_ref[r, expert]
                source = slot_id // z.local
                for b in range(z.slot_blocks):
                    block = (slot_id % z.local) * z.slot_blocks + b
                    part = (block // z.part_blocks) ^ mine
                    spot = pl.multiple_of((block % z.part_blocks) * z.block, z.block)
                    side = source ^ turn
                    if r:
                        side = jnp.where(slot_id == first, z.ep, side)
                    left.append(functools.partial(left_rows, held, part, side, spot, z.block))
                    right.append(functools.partial(right_rows, slot_id, block, b))
            half = len(left) // 2

            def product(lo, hi):
                return nn(
                    jnp.concatenate([f() for f in left[lo:hi]], axis=1),
                    jnp.concatenate([f() for f in right[lo:hi]], axis=0),
                )

            few = table_ref[z.reps // 2, expert] == first

            @pl.when(few)
            def _():
                made[expert] = product(0, half).astype(BF)

            @pl.when(jnp.logical_not(few))
            def _():
                made[expert] = product(0, 2 * half).astype(BF)

            out_copy(expert).start()
        return carry

    lax.fori_loop(0, z.experts // PER, some, 0)
    for expert in range(z.experts):
        out_copy(expert).wait()


def total_down_kernel(z, ids_ref, table_ref, *refs):
    sides = refs[: z.sub]
    grads_ref, codes_ref, out_ref, token_ref, held, made, out_sems, scaled, sems = refs[z.sub :]
    token_ref[...] = jnp.zeros_like(token_ref)

    def moves(act):
        for k in range(z.sub):
            act(
                pltpu.make_async_copy(
                    sides[k], held.at[k, pl.ds(0, z.ep)], sems.at[k]
                )
            )

    moves(lambda copy: copy.start())
    held[:, z.ep] = jnp.zeros_like(held[:, z.ep])
    rows = lax.broadcasted_iota(jnp.int32, (z.slots, z.cap, z.tokens), 1).astype(F32)
    for p in range(z.ep):
        code = codes_ref[p, : z.slots, :][:, None, :]
        load = codes_ref[p, z.slots :, :][:, None, :]
        pick = jnp.where(rows == code, load, 0.0).reshape(z.slots * z.cap, z.tokens)
        result = nn(pick.astype(BF), grads_ref[p]).astype(BF)
        scaled[:, p * z.cap : (p + 1) * z.cap, :] = result.reshape(z.slots, z.cap, z.width)
    moves(lambda copy: copy.wait())

    def right_rows(slot_id, block, b):
        return scaled[slot_id, b * z.block : (b + 1) * z.block, :]

    expert_products(z, ids_ref, table_ref, ids_ref[0], held, right_rows, out_ref, made, out_sems)


def total_in_kernel(z, ids_ref, table_ref, *refs):
    sides, refs = refs[: z.sub], refs[z.sub :]
    own_ref, rights, lefts = refs[0], refs[1 : z.ep], refs[z.ep : 2 * z.ep - 1]
    out_ref, token_ref, held, made, out_sems, inputs_ref, sems, *other_sems = refs[2 * z.ep - 1 :]
    token_ref[...] = jnp.zeros_like(token_ref)

    def moves(act):
        for k in range(z.sub):
            act(pltpu.make_async_copy(sides[k], held.at[k, pl.ds(0, z.ep)], sems.at[k]))
        input_moves(z, ids_ref[0], own_ref, rights, lefts, inputs_ref, *other_sems, act)

    moves(lambda copy: copy.start())
    held[:, z.ep] = jnp.zeros_like(held[:, z.ep])
    moves(lambda copy: copy.wait())

    def right_rows(slot_id, block, b):
        start = pl.multiple_of(block * z.block, z.block)
        return inputs_ref[slot_id // z.local, pl.ds(start, z.block), :]

    expert_products(z, ids_ref, table_ref, ids_ref[0], held, right_rows, out_ref, made, out_sems)


def swap(x, axis, size, bit):
    return lax.ppermute(x, axis, [(i, i ^ bit) for i in range(size)])


def spread_over(have, axis, size, bit):
    have = dict(have)
    while bit:
        for k in list(have):
            if k | bit not in have:
                have[k | bit] = swap(have[k], axis, size, bit)
        bit //= 2
    return [have[k] for k in range(size)]


def nothing(*refs):
    pass


def gate(values, after):
    anywhere = pl.BlockSpec(memory_space=pl.ANY)
    return pl.pallas_call(
        nothing,
        in_specs=[anywhere] * (len(values) + len(after)),
        out_specs=[anywhere] * len(values),
        out_shape=[jax.ShapeDtypeStruct(v.shape, v.dtype) for v in values],
        input_output_aliases={i: i for i in range(len(values))},
        compiler_params=pltpu.CompilerParams(vmem_limit_bytes=1024 * 1024),
        name="gate",
    )(*values, *after)


def pick_kernel(first, ids_ref, go_ref, back_ref, out_ref, sem):
    for condition, ref in ((ids_ref[0] >= first, go_ref), (ids_ref[0] < first, back_ref)):

        @pl.when(condition)
        def _():
            copy = pltpu.make_async_copy(ref, out_ref, sem)
            copy.start()
            copy.wait()


def pick(ids, go, back, first):
    anywhere = pl.BlockSpec(memory_space=pl.ANY)
    return pl.pallas_call(
        functools.partial(pick_kernel, first),
        in_specs=[smem(), anywhere, anywhere],
        out_specs=anywhere,
        out_shape=jax.ShapeDtypeStruct(go.shape, go.dtype),
        scratch_shapes=[pltpu.SemaphoreType.DMA],
        compiler_params=pltpu.CompilerParams(vmem_limit_bytes=1024 * 1024),
        name="pick",
    )(ids, go, back)


def chain_step(go, back, axis, size, d):
    rights = [(i, i + 1) for i in range(d - 1, size - 1)]
    lefts = [(i, i - 1) for i in range(size - d, 0, -1)]
    if d > 1 and go is back:
        got = lax.ppermute(go, axis, rights + lefts)
        return got, got
    return lax.ppermute(go, axis, rights), lax.ppermute(back, axis, lefts)


def body(
    grad_out,
    route_weight,
    routes,
    replica,
    replica_slot,
    token_count,
    saved_input,
    saved_gate_up,
    weight_in,
    weight_down,
):
    z = Sizes(grad_out, routes, replica_slot, saved_input, weight_in, weight_down)
    n, m = z.ep, z.sub
    ids = jnp.stack([lax.axis_index("ep"), lax.axis_index("sub")]).astype(jnp.int32)
    routes, replica, table = routes.T, replica.T, replica_slot.T
    route_weight = route_weight.T
    pair_rows = saved_gate_up.reshape(z.all_rows, z.pair)
    grad_shape = (z.tokens + z.tail, z.width)
    code_shape = (n, 2 * z.slots, z.tokens)
    inputs = saved_input.reshape(z.all_rows, z.width)

    routing = (grad_out, route_weight, routes, replica, table)
    buf = pl.pallas_call(
        functools.partial(route_kernel, z),
        out_shape=jax.ShapeDtypeStruct(grad_shape, BF),
        in_specs=[smem()] + [whole(a.shape) for a in routing],
        out_specs=whole(grad_shape),
        grid=(1,),
        compiler_params=params(60),
        name="route",
    )(token_count, *routing)
    bufs = [buf] + [swap(buf, "ep", n, k) for k in range(1, n)]

    chain = gate([inputs], [buf])
    downs = pl.pallas_call(
        functools.partial(hidden_kernel, z),
        grid_spec=pltpu.PrefetchScalarGridSpec(
            num_scalar_prefetch=1,
            grid=(z.part_blocks,),
            in_specs=[
                pl.BlockSpec((z.block, z.pair), lambda i, r: (r[1] * z.part_blocks + i, 0)),
                pl.BlockSpec(memory_space=pl.ANY),
                pl.BlockSpec(memory_space=pl.ANY),
            ],
            out_specs=[pl.BlockSpec((z.down_cols, z.block), lambda i, r: (0, i))] * n,
            scratch_shapes=[pltpu.VMEM((n, z.down_cols, z.block), BF)],
        ),
        out_shape=[jax.ShapeDtypeStruct((z.down_cols, z.part), BF)] * n,
        compiler_params=params(16),
        name="hidden_columns",
    )(ids, pair_rows, bufs[1], chain[0])
    downs = [downs[0]] + [swap(downs[k], "ep", n, k) for k in range(1, n)]
    chain = gate(chain, bufs[1:] + downs[1:-1])
    steps = [list(chain_step(chain[0], chain[0], "ep", n, 1))]

    def stack(pieces):
        shape = pieces[0].shape
        return pl.pallas_call(
            functools.partial(stack_kernel, z),
            in_specs=[whole(shape)] * n,
            out_specs=whole((n,) + shape),
            out_shape=jax.ShapeDtypeStruct((n,) + shape, BF),
            grid=(1,),
            compiler_params=params(12),
            name="stack_columns",
        )(*pieces)

    def halve(keep, got):
        half = (keep.shape[0] // 2,) + keep.shape[1:]
        return pl.pallas_call(
            halve_kernel,
            in_specs=[whole(keep.shape)] * 2,
            out_specs=[whole(half)] * 2,
            out_shape=[jax.ShapeDtypeStruct(half, BF)] * 2,
            grid=(1,),
            compiler_params=params(16),
            name="halve",
        )(keep, got)

    def row_block(i, ids_ref):
        place = i // z.part_blocks
        return (place ^ ids_ref[1]) * z.part_blocks + i % z.part_blocks

    part_shape = (m // 2, z.part, z.hidden)
    outs = pl.pallas_call(
        functools.partial(down_kernel, z),
        grid_spec=pltpu.PrefetchScalarGridSpec(
            num_scalar_prefetch=1,
            grid=(z.blocks,),
            in_specs=[whole(grad_shape)] * n
            + [pl.BlockSpec(memory_space=pltpu.HBM), pl.BlockSpec(memory_space=pl.ANY)],
            out_specs=[whole(part_shape)] * 2
            + [whole((n, z.tokens, z.width)), whole(code_shape)],
            scratch_shapes=[
                pltpu.VMEM((z.local, z.rows, z.width), BF),
                pltpu.VMEM((z.local, z.hidden, z.width), BF),
                pltpu.SemaphoreType.DMA((z.local,)),
            ],
        ),
        out_shape=[jax.ShapeDtypeStruct(part_shape, BF)] * 2
        + [
            jax.ShapeDtypeStruct((n, z.tokens, z.width), BF),
            jax.ShapeDtypeStruct(code_shape, F32),
        ],
        compiler_params=params(48),
        name="hidden_partials",
    )(ids, *bufs, weight_down, *downs[:1])
    keep, send, grads_all, codes = outs
    down_sides = spread_over({0: stack(downs)}, "sub", m, m // 2)
    def total_call(kernel, operands, specs, cols, scratch, name):
        return pl.pallas_call(
            functools.partial(kernel, z),
            grid_spec=pltpu.PrefetchScalarGridSpec(
                num_scalar_prefetch=2,
                grid=(1,),
                in_specs=specs,
                out_specs=[pl.BlockSpec(memory_space=pl.ANY), whole((8, 128))],
                scratch_shapes=[
                    pltpu.VMEM((m, n + 1, cols, z.part), BF),
                    pltpu.VMEM((z.experts, cols, z.width), BF),
                    pltpu.SemaphoreType.DMA((z.experts,)),
                ]
                + scratch,
            ),
            out_shape=[
                jax.ShapeDtypeStruct((z.experts, cols, z.width), BF),
                jax.ShapeDtypeStruct((8, 128), F32),
            ],
            compiler_params=params(32),
            name=name,
        )(ids, table, *operands)

    anywhere = pl.BlockSpec(memory_space=pl.ANY)
    grad_down, down_made = total_call(
        total_down_kernel,
        [*down_sides, grads_all, codes],
        [anywhere] * m + [whole((n, z.tokens, z.width)), whole(code_shape)],
        z.down_cols,
        [pltpu.VMEM((z.slots, z.rows, z.width), BF), pltpu.SemaphoreType.DMA((m,))],
        "down_grads",
    )
    steps.append(chain_step(*steps[0], "ep", n, 2))
    got = swap(send, "sub", m, 1)
    after = list(steps[0])
    bit = 2
    while bit < m:
        keep, send = halve(keep, got)
        send = gate([send], after)[0]
        got = swap(send, "sub", m, bit)
        bit *= 2

    got = gate([got], [down_made])[0]
    *pieces, grad_part = pl.pallas_call(
        functools.partial(pre_kernel, z),
        grid_spec=pltpu.PrefetchScalarGridSpec(
            num_scalar_prefetch=1,
            grid=(z.part_blocks,),
            in_specs=[pl.BlockSpec((1, z.block, z.hidden), lambda i, r: (0, i, 0))] * 2
            + [
                pl.BlockSpec((z.block, z.pair), lambda i, r: (r[1] * z.part_blocks + i, 0)),
                whole(code_shape),
            ],
            out_specs=[pl.BlockSpec((z.in_cols, z.block), lambda i, r: (0, i))] * n
            + [pl.BlockSpec((z.block, z.hidden), lambda i, r: (i, 0))],
            scratch_shapes=[pltpu.VMEM((n, z.in_cols, z.block), BF)],
        ),
        out_shape=[jax.ShapeDtypeStruct((z.in_cols, z.part), BF)] * n
        + [jax.ShapeDtypeStruct((z.part, z.hidden), BF)],
        compiler_params=params(16),
        name="pre_grads",
    )(ids, keep, got, pair_rows, codes)
    late = gate(pieces[1:], steps[1])
    pieces = pieces[:1] + [swap(a, "ep", n, k) for k, a in enumerate(late, 1)]
    grad_parts = spread_over({0: grad_part}, "sub", m, m // 2)

    back_shape = (z.tokens + z.slots, z.width)
    parts = pl.pallas_call(
        functools.partial(row_kernel, z),
        grid_spec=pltpu.PrefetchScalarGridSpec(
            num_scalar_prefetch=1,
            grid=(z.blocks,),
            in_specs=[whole((z.part, z.hidden))] * m
            + [
                pl.BlockSpec((z.block, z.pair), lambda i, r: (row_block(i, r), 0)),
                pl.BlockSpec(memory_space=pltpu.HBM),
                whole(code_shape),
            ],
            out_specs=[whole(back_shape)] * n,
            scratch_shapes=[
                pltpu.VMEM((z.local, z.rows, z.width), BF),
                pltpu.VMEM((n, z.slots, z.tokens), F32),
                pltpu.VMEM((z.block, z.hidden), BF),
                pltpu.VMEM((z.local, z.pair, z.width), BF),
                pltpu.SemaphoreType.DMA((z.local,)),
            ],
        ),
        out_shape=[jax.ShapeDtypeStruct(back_shape, BF)] * n,
        compiler_params=params(46),
        name="row_grads",
    )(ids, *grad_parts, pair_rows, weight_in, codes)
    steps[1] = go, back = gate(steps[1], pieces[1:])
    picked = []
    for d in range(3, n):
        if 2 * d > n + 1 and go is not back:
            go = back = pick(ids, go, back, d - 1)
            picked.append(go)
        go, back = chain_step(go, back, "ep", n, d)
        steps.append((go, back))
    gathered = [inputs] + [go for go, _ in steps] + [back for _, back in steps]
    got = [swap(part, "ep", n, 1) for part in parts[1::2]]
    pieces[:1] = gate(pieces[:1], [*got, *picked])
    sides = spread_over({0: stack(pieces)}, "sub", m, m // 2)
    keep, bit = parts[::2], 2
    while bit < n:
        count = len(keep)
        parts = pl.pallas_call(
            sum_kernel,
            in_specs=[whole(back_shape)] * 2 * count,
            out_specs=[whole(back_shape)] * count,
            out_shape=[jax.ShapeDtypeStruct(back_shape, BF)] * count,
            grid=(1,),
            compiler_params=params(16),
            name="sum_parts",
        )(*keep, *got)
        keep = parts[::2]
        send = gate(parts[1::2], gathered[1:])
        got = [swap(part, "ep", n, bit) for part in send]
        bit *= 2

    grad_in, in_made = total_call(
        total_in_kernel,
        [*sides, *gathered],
        [anywhere] * (m + 2 * n - 1),
        z.in_cols,
        [
            pltpu.VMEM((n, z.all_rows, z.width), BF),
            pltpu.SemaphoreType.DMA((m,)),
            pltpu.SemaphoreType.DMA,
            pltpu.SemaphoreType.DMA((n - 1,)),
            pltpu.SemaphoreType.DMA((n - 1,)),
        ],
        "in_grads",
    )
    keep, got = keep[0], gate(got, [in_made])[0]
    grad_tokens, grad_routes = pl.pallas_call(
        functools.partial(token_kernel, z),
        out_shape=[
            jax.ShapeDtypeStruct((z.tokens, z.width), BF),
            jax.ShapeDtypeStruct((z.top, z.tokens), BF),
        ],
        in_specs=[smem()] + [whole(a.shape) for a in (keep, got, routes, replica, table)],
        out_specs=[whole((z.tokens, z.width)), whole((z.top, z.tokens))],
        grid=(1,),
        compiler_params=params(16),
        name="token_grads",
    )(token_count, keep, got, routes, replica, table)

    return grad_tokens, grad_routes.T, grad_in, grad_down


def solution(mesh):
    return jax.shard_map(
        body,
        mesh=mesh,
        in_specs=(
            P(("groups", "ep"), "sub"),
            P(("groups", "ep"), None),
            P(("groups", "ep"), None),
            P(("groups", "ep"), None),
            P("groups", None),
            P(("groups", "ep")),
            P(("groups", "ep"), None, None, "sub"),
            P(("groups", "ep"), None, None),
            P(("groups", "ep"), None, "sub"),
            P(("groups", "ep"), None, "sub"),
        ),
        out_specs=(
            P(("groups", "ep"), "sub"),
            P(("groups", "ep"), None),
            P("groups", "ep", "sub"),
            P("groups", "ep", "sub"),
        ),
        check_vma=False,
    )
```
